32 devices in a mesh: band: 2 (over y), rows: 16 (over z, x, core).
Axes of the slice: x: 2, y: 2, z: 4, core: 2. Of those that a mesh axis runs over, the one named last changes fastest.
Arguments:
- start_iterate: float32 [1024, 16, 128], P(('band', 'rows')), may hold values from 0 to 2
- right_side: float32 [1024, 16, 128], P(('band', 'rows')), as said below
- diag_table: float32 [8, 128, 128], replicated, as said below
- inverse_table: float32 [8, 128, 128], replicated, as said below
- coupling_tiles: float32 [8, 128, 128], replicated, may hold values from 0 to 0.009375
- diag_index: int32 [1024], P(('band', 'rows')), may hold values from 0 to 7
- tile_index: int32 [1024, 4], P(('band', 'rows')), may hold values from 0 to 7
- source_owner: int32 [1024, 2], P(('band', 'rows')), may hold values from 0 to 15, all different within a row; in each aligned block of 32 rows (0 to 31, 32 to 63, ...) at most 8 rows name the same one
- source_local: int32 [1024, 2], P(('band', 'rows')), may hold values from 0 to 31
- aggregate_map: int32 [1024, 1], P(('band', 'rows')), may hold values from 0 to 255
Outputs:
- swept_iterate: float32 [1024, 16, 128], P(('band', 'rows'))
The draws below stay inside these ranges and needn't reach their ends.
Inputs may be any that keep to these rules, and one draw needn't show every extreme that they name: `source_owner`: within each aligned block of 32 rows (the rows of one device) no owner is named by more than 8 entries, a bound that some block reaches; the 2 owners of one row differ. `aggregate_map`: every aggregate is named by at least one block row. `diag_table`: diagonal entries lie from 6 to 10; off-diagonal entries are nonpositive with magnitude at most 5 / 128. `inverse_table`: entries are nonnegative; each block is a first-order approximation of the inverse of the diagonal block of the same index, not its exact inverse. `right_side`: entries are nonnegative.
All inputs are finite; a program needn't handle non-finite values.
Results may differ from the reference program's by a relative error of at most 0.0001.
Values sent between devices are 32-bit elements; how exact they have to be, the bound alone decides.
No kernel may reach another device: no remote copies, remote signals or barrier semaphores. Data moves between devices by JAX's collectives and lax.ppermute only.
A program may use at most 64 MiB of HBM per device.

```python
import math
import jax
import jax.numpy as jnp
import numpy as np
from jax import lax

PH = 128
NV = 16
BR_DEV = 32
K = 2
NT = 8
ND = 8
CAP = 8
NB = 1024
NAGG = 256
N_ROWS = 16


def diagonal_parts(key):
    first_key = jax.random.fold_in(key, 101)
    second_key = jax.random.fold_in(key, 202)
    spread = jax.random.uniform(first_key, (ND, PH), jnp.float32)
    rates = jax.random.uniform(second_key, (ND, PH, PH), jnp.float32)
    diagonal = 6.0 + 4.0 * spread
    rates = 5.0 / PH * rates
    identity = jnp.eye(PH, dtype=jnp.float32)
    rates = rates * (1.0 - identity)
    return (diagonal, rates, identity)


def draw_diag_table(key, part):
    diagonal, rates, identity = diagonal_parts(key)
    return diagonal[:, :, None] * identity - rates


def draw_inverse_table(key, part):
    diagonal, rates, identity = diagonal_parts(key)
    recip = 1.0 / diagonal
    return recip[:, :, None] * identity + rates * recip[:, :, None] * recip[:, None, :]


def draw_right_side(key, part):
    first_key = jax.random.fold_in(key, 303)
    second_key = jax.random.fold_in(key, 404)
    level = jax.random.uniform(first_key, (NB, 1, 1), jnp.float32)
    entries = jax.random.uniform(second_key, (NB, NV, PH), jnp.float32)
    scale = jnp.exp(jnp.log(0.3) + level * jnp.log(10.0))
    values = 2.0 * entries
    return scale * values


def touch_ends(values, stream_key, least, largest):
    extent = values.shape
    spot = [jax.random.randint(jax.random.fold_in(stream_key, axis), (), 0, extent[axis]) for axis in range(len(extent))]
    values = values.at[tuple(spot)].set(least)
    longest = extent.index(max(extent))
    spot[longest] = (spot[longest] + 1) % extent[longest]
    return values.at[tuple(spot)].set(largest)


def block_levels(rng, dims, cuts, smallest, top_value):
    def one(position, parts):
        draws = jax.random.uniform(jax.random.fold_in(jax.random.fold_in(rng, 6), position), (parts,), jnp.float32, smallest / len(cuts), top_value / len(cuts))
        return jnp.repeat(jnp.exp(draws), dims[position] // parts).reshape((-1,) + (1,) * (len(dims) - position - 1))

    loudness = one(*cuts[0])
    for cut in cuts[1:]:
        loudness = loudness * one(*cut)
    return loudness


def choose_distinct(stream_key, rows, amount, top, lift):
    order = jax.random.permutation(jax.random.fold_in(stream_key, 1), amount)
    boost = order
    for power in range(3):
        boost = boost * boost // amount
    boost = boost * lift // amount
    chance = jax.random.randint(jax.random.fold_in(stream_key, 2), (rows, amount), 0, 4096) + boost
    fixed_rows = jax.random.permutation(jax.random.fold_in(stream_key, 3), rows)[jnp.arange(amount) % rows]
    chance = jnp.where(jnp.arange(rows)[:, None] == fixed_rows[None, :], 1 << 14, chance)
    merit = chance * amount + jnp.arange(amount)
    return lax.top_k(merit.astype(jnp.int32), top)[1].astype(jnp.int32)


def shared_out(stream_key, own, number, rows, count, top, reach, lean):
    sequence = jax.random.permutation(stream_key, count)
    crowded, common = load_shares(count, rows * top, reach, lean, True), load_shares(count, rows * top, reach, lean, False)
    places = jnp.arange(count)

    def named(tallies, offset_by):
        used = int((tallies > 0).sum())
        fixed = max(1, used // 4)
        passed = fixed + (places - fixed + offset_by * (used - fixed)) % max(1, count - fixed)
        return jnp.zeros((count,), jnp.int32).at[sequence[jnp.where(places < fixed, places, passed)]].set(jnp.asarray(tallies, jnp.int32))

    tallies = jnp.where(number % 4 == 0, named(crowded, number // 4), named(common, number - number // 4 - 1))
    mixed = jax.random.permutation(jax.random.fold_in(own, 3), count)
    source_of, sink = mixed[0:count // 2 * 2:2], mixed[1:count // 2 * 2:2]
    margin = jnp.minimum(tallies[source_of] - 1, reach - tallies[sink]) // 2
    margin = jnp.where((source_of == sequence[0]) | (sink == sequence[0]) | (tallies[sink] == 0), 0, jnp.maximum(margin, 0))
    passed = jax.random.randint(jax.random.fold_in(own, 4), (count // 2,), 0, 1 << 20) % (margin + 1)
    tallies = tallies.at[source_of].add(-passed).at[sink].add(passed)
    labels = jnp.searchsorted(jnp.cumsum(tallies), jnp.arange(rows * top), side="right").astype(jnp.int32)
    table = labels.reshape(top, rows).T
    table = table[jax.random.permutation(jax.random.fold_in(own, 1), rows)]
    offset_by = jax.random.randint(jax.random.fold_in(own, 2), (rows, 1), 0, top)
    return jnp.take_along_axis(table, (jnp.arange(top)[None, :] + offset_by) % top, axis=1)


def load_shares(amount, total, limit, slope, full):
    weights = [(1 << 20) // math.isqrt(standing ** slope) + 1 for standing in range(1, amount + 1)]
    largest = limit if full else min(limit, max(-(-total // amount), total * weights[0] // sum(weights)))
    least = 1 if total - largest >= amount - 1 else 0
    holding, rest = [largest] + [least] * (amount - 1), total - largest - least * (amount - 1)
    while rest > 0:
        candidates = [i for i in range(1, amount) if holding[i] < largest] or [i for i in range(1, amount) if holding[i] < limit]
        whole, left = sum([weights[i] for i in candidates]), rest
        for i in candidates:
            extra = min(limit - holding[i], max(1, left * weights[i] // whole), rest)
            holding[i] = holding[i] + extra
            rest = rest - extra
    return np.array(holding)


def setup_inputs(seed: int = 0) -> dict:
    arg_keys = jax.random.split(jax.random.key(seed), 11)
    start_iterate = jnp.clip(2.0 * jax.random.uniform(arg_keys[0], (NB, NV, PH), jnp.float32) ** block_levels(arg_keys[0], (NB, NV, PH), ((0, 32),), -0.2, 0.2), 0.0, 2.0)
    right_side = draw_right_side(jax.random.fold_in(arg_keys[10], 71), 0)
    diag_table = draw_diag_table(jax.random.fold_in(arg_keys[10], 71), 0)
    inverse_table = draw_inverse_table(jax.random.fold_in(arg_keys[10], 71), 0)
    coupling_tiles = jnp.clip(jax.random.uniform(arg_keys[4], (NT, PH, PH), jnp.float32, 0.0, 0.009375), 0.0, 0.009375)
    diag_index = touch_ends(jax.random.randint(arg_keys[5], (NB,), 0, ND), jax.random.fold_in(arg_keys[5], 1), 0, ND - 1).astype(jnp.int32)
    tile_index = touch_ends(jax.random.randint(arg_keys[6], (NB, K + 2), 0, NT), jax.random.fold_in(arg_keys[6], 1), 0, NT - 1).astype(jnp.int32)
    source_owner_keys = jax.random.split(jax.random.fold_in(arg_keys[7], 1), NB // BR_DEV)
    source_owner_turns = jax.random.permutation(jax.random.fold_in(arg_keys[7], 3), NB // BR_DEV)
    source_owner = jax.vmap(lambda own, number: shared_out(jax.random.fold_in(arg_keys[7], 2), own, number, BR_DEV, N_ROWS, K, CAP, 2))(source_owner_keys, source_owner_turns).reshape((NB, K))
    source_local = touch_ends(jax.random.randint(arg_keys[8], (NB, K), 0, BR_DEV), jax.random.fold_in(arg_keys[8], 1), 0, BR_DEV - 1).astype(jnp.int32)
    aggregate_map = choose_distinct(arg_keys[9], NB, NAGG, 1, 0)
    return dict(start_iterate=start_iterate, right_side=right_side, diag_table=diag_table, inverse_table=inverse_table, coupling_tiles=coupling_tiles, diag_index=diag_index, tile_index=tile_index, source_owner=source_owner, source_local=source_local, aggregate_map=aggregate_map)


HIGH = lax.Precision.HIGHEST


def blockwise(handler, count, block_rows):
    starts = jnp.arange(count // block_rows, dtype=jnp.int32) * block_rows
    pieces = lax.map(handler, starts)
    return pieces.reshape((count,) + pieces.shape[2:])


def coupling(iterate, tile_index, source_owner, source_local, coupling_tiles):
    band_rows = BR_DEV * N_ROWS
    row_ids = jnp.arange(NB, dtype=jnp.int32)
    band_start = (row_ids // band_rows) * band_rows
    columns = (band_start[:, None] + source_owner * BR_DEV + source_local).astype(jnp.int32)
    padding = jnp.zeros((band_rows, NV, PH), jnp.float32)
    from_lower = jnp.concatenate([padding, iterate[: NB - band_rows]], axis=0)
    from_upper = jnp.concatenate([iterate[band_rows:], padding], axis=0)

    def one_block(start):
        picked = lax.dynamic_slice_in_dim(columns, start, BR_DEV, 0)
        remote = jnp.take(iterate, picked, axis=0)
        below = lax.dynamic_slice_in_dim(from_lower, start, BR_DEV, 0)
        above = lax.dynamic_slice_in_dim(from_upper, start, BR_DEV, 0)
        sources = jnp.concatenate([remote, below[:, None], above[:, None]], axis=1)
        chosen = jnp.take(coupling_tiles, lax.dynamic_slice_in_dim(tile_index, start, BR_DEV, 0), axis=0)
        return jnp.einsum("rkst,rkvt->rvs", chosen, sources, precision=HIGH)

    return blockwise(one_block, NB, BR_DEV)


def apply_table(table, index, iterate):
    def one_block(start):
        chosen = jnp.take(table, lax.dynamic_slice_in_dim(index, start, BR_DEV, 0), axis=0)
        part_rows = lax.dynamic_slice_in_dim(iterate, start, BR_DEV, 0)
        return jnp.einsum("rst,rvt->rvs", chosen, part_rows, precision=HIGH)

    return blockwise(one_block, NB, BR_DEV)


def reference(start_iterate, right_side, diag_table, inverse_table, coupling_tiles, diag_index, tile_index, source_owner, source_local, aggregate_map):
    iterate = start_iterate
    for sweep_pass in range(2):
        coupled = coupling(iterate, tile_index, source_owner, source_local, coupling_tiles)
        iterate = apply_table(inverse_table, diag_index, right_side + coupled)
    coupled = coupling(iterate, tile_index, source_owner, source_local, coupling_tiles)
    residual = right_side + coupled - apply_table(diag_table, diag_index, iterate)
    residual_sums = jnp.sum(residual, axis=2)
    table_sums = jnp.sum(diag_table, axis=(1, 2))
    block_sums = jnp.take(table_sums, diag_index)
    groups = aggregate_map[:, 0]
    coarse_residual = jax.ops.segment_sum(residual_sums, groups, num_segments=NAGG)
    coarse_diag = jax.ops.segment_sum(block_sums, groups, num_segments=NAGG)
    correction = coarse_residual / coarse_diag[:, None]
    return iterate + jnp.take(correction, groups, axis=0)[:, :, None]
```

```python
import functools

import jax
import jax.numpy as jnp
from jax import lax
from jax.experimental import pallas as pl
from jax.experimental.pallas import tpu as pltpu
from jax.sharding import PartitionSpec as P

AGG_DEV = 8
LANES = 128
DENSE_LIMIT = 1 << 19

VMEM = pl.BlockSpec(memory_space=pltpu.VMEM)
SMEM = pl.BlockSpec(memory_space=pltpu.SMEM)
HIGH = lax.Precision.HIGHEST


def params():
    return pltpu.CompilerParams(vmem_limit_bytes=48 * 1024 * 1024)


def call(kernel, out_shape, in_specs, scratch=(), flops=0, moved=0):
    single = not isinstance(out_shape, (tuple, list))
    count = 1 if single else len(out_shape)
    return pl.pallas_call(
        kernel,
        out_shape=out_shape,
        in_specs=in_specs,
        out_specs=VMEM if single else [VMEM] * count,
        scratch_shapes=list(scratch),
        compiler_params=params(),
        cost_estimate=pl.CostEstimate(flops=flops, bytes_accessed=moved, transcendentals=0),
    )


def halves(value):
    high = value.astype(jnp.bfloat16)
    low = (value - high.astype(jnp.float32)).astype(jnp.bfloat16)
    return high, low


def left_operand(value):
    high, low = halves(value)
    return jnp.concatenate([high, low, high], axis=1)


def right_operand(value):
    high, low = halves(value)
    return jnp.concatenate([high, high, low], axis=1)


def dot_nt(left, right):
    return lax.dot_general(
        left, right, (((1,), (1,)), ((), ())), preferred_element_type=jnp.float32
    )


def table_products(value, table_ref, out_ref):
    left = left_operand(value)
    count, width = table_ref.shape[0], table_ref.shape[1]
    for first in range(0, count, 2):
        last = min(first + 2, count)
        right = right_operand(table_ref[first:last].reshape((last - first) * width, -1))
        product = dot_nt(left, right)
        for t in range(first, last):
            out_ref[t] = product[:, (t - first) * width : (t - first + 1) * width]


def dot_exact(left, value):
    high, low = halves(value)
    return jnp.dot(left, high, preferred_element_type=jnp.float32) + jnp.dot(
        left, low, preferred_element_type=jnp.float32
    )


def request_kernel(
    sizes, owner_ref, local_ref, tile_ref, diag_ref, group_ref, payload_ref, slot_ref
):
    rows, width_k, n_rows, cap, n_tiles = sizes
    entries = rows * width_k

    def column(ref, k):
        return ref[:, k : k + 1]

    def stacked(ref):
        return jnp.concatenate([column(ref, k) for k in range(width_k)], axis=0)

    owner, local, tile = stacked(owner_ref), stacked(local_ref), stacked(tile_ref)
    group = jnp.concatenate([group_ref[:, 0:1]] * width_k, axis=0)
    code = local + rows * (tile + n_tiles * group) + 1
    row_of = lax.broadcasted_iota(jnp.int32, (entries, entries), 0)
    col_of = lax.broadcasted_iota(jnp.int32, (entries, entries), 1)

    def as_row(col):
        return jnp.sum(jnp.where(row_of == col_of, col, 0), axis=0, keepdims=True)

    owner_row = as_row(owner)
    earlier = jnp.where((owner == owner_row) & (col_of < row_of), 1, 0)
    rank = jnp.sum(earlier, axis=1, keepdims=True)
    slot_ref[...] = as_row(owner * cap + rank)
    lane = lax.broadcasted_iota(jnp.int32, (entries, LANES), 1)
    by_rank = jnp.where(lane == rank, code, 0).astype(jnp.float32)
    owners = lax.broadcasted_iota(jnp.int32, (n_rows, entries), 0)
    mine = jnp.where(owners == owner_row, 1.0, 0.0)
    lists = jnp.dot(mine, by_rank, precision=HIGH, preferred_element_type=jnp.float32)
    lists = (lists + 0.5).astype(jnp.int32)
    wide = payload_ref.shape[2] - LANES
    row_of = lax.broadcasted_iota(jnp.int32, (rows, wide), 0)
    col_of = lax.broadcasted_iota(jnp.int32, (rows, wide), 1)
    common = jnp.zeros((rows, wide), jnp.int32)
    parts = (
        group_ref[:, 0:1],
        diag_ref[...],
        column(tile_ref, width_k),
        column(tile_ref, width_k + 1),
    )
    for q, part in enumerate(parts):
        common = jnp.where(col_of == row_of + q * rows, part, common)
    common = jnp.sum(common, axis=0, keepdims=True)
    whole = jnp.concatenate([lists, jnp.broadcast_to(common, (n_rows, wide))], axis=1)
    for band in range(payload_ref.shape[0]):
        payload_ref[band] = whole


def pack(sizes, product_ref, request_ref, tiles_ref, send_ref, band_refs):
    rows, n_rows, cap, n_tiles, n_rhs = sizes
    for owner in range(n_rows):
        for rank in range(cap):
            code = jnp.maximum(request_ref[owner, rank] - 1, 0)
            tile = lax.rem(lax.div(code, rows), n_tiles)
            start = pl.multiple_of(lax.rem(code, rows) * n_rhs, n_rhs)
            send_ref[owner, rank] = product_ref[tile, pl.ds(start, n_rhs), :]
    for way, band_ref in enumerate(band_refs):
        for row in range(rows):
            tile = tiles_ref[way, row]
            band_ref[row] = product_ref[tile, pl.ds(row * n_rhs, n_rhs), :]


def first_kernel(sizes, start_ref, tile_ref, request_ref, tiles_ref, send_ref, *rest):
    product_ref, band_refs = rest[-1], rest[:-1]
    table_products(start_ref[...].reshape(product_ref.shape[1:]), tile_ref, product_ref)
    pack(sizes, product_ref, request_ref, tiles_ref, send_ref, band_refs)


def gather_solve(
    sizes, slot_ref, diag_ref, arrived_ref, band_refs, right_ref, inverse_ref, sum_ref, product_ref
):
    rows, n_rows, cap, n_tiles, n_rhs = sizes
    for row in range(rows):
        total = right_ref[row]
        for entry in range(row, slot_ref.shape[1], rows):
            slot = slot_ref[0, entry]
            total = total + arrived_ref[lax.div(slot, cap), lax.rem(slot, cap)]
        for band_ref in band_refs:
            total = total + band_ref[row]
        sum_ref[pl.ds(row * n_rhs, n_rhs), :] = total
    table_products(sum_ref[...], inverse_ref, product_ref)
    for row in range(rows):
        place = pl.ds(row * n_rhs, n_rhs)
        sum_ref[place, :] = product_ref[diag_ref[0, row], place, :]


def middle_kernel(sizes, n_band, *refs):
    slot_ref, diag_ref, request_ref, tiles_ref, arrived_ref = refs[:5]
    band_in = refs[5 : 5 + n_band]
    right_ref, inverse_ref, tile_ref, send_ref = refs[5 + n_band : 9 + n_band]
    band_out = refs[9 + n_band : 9 + 2 * n_band]
    sum_ref, product_ref = refs[9 + 2 * n_band :]
    gather_solve(
        sizes, slot_ref, diag_ref, arrived_ref, band_in, right_ref, inverse_ref, sum_ref, product_ref
    )
    table_products(sum_ref[...], tile_ref, product_ref)
    pack(sizes, product_ref, request_ref, tiles_ref, send_ref, band_out)


def last_kernel(sizes, n_band, dense, *refs):
    slot_ref, diag_ref, arrived_ref = refs[:3]
    band_in = refs[3 : 3 + n_band]
    refs = refs[3 + n_band :]
    right_ref, inverse_ref = refs[:2]
    if dense:
        tile_ref, table_ref, count_ref, place_ref, second_ref, part_ref = refs[2:8]
    else:
        second_ref = refs[2]
    sum_ref, product_ref = refs[-2:]
    rows, n_rhs = sizes[0], sizes[4]
    gather_solve(
        sizes, slot_ref, diag_ref, arrived_ref, band_in, right_ref, inverse_ref, sum_ref, product_ref
    )
    second = sum_ref[...]
    second_ref[...] = second.reshape(second_ref.shape)
    if not dense:
        return
    functionals = jnp.concatenate(
        [jnp.sum(tile_ref[...], axis=1), -jnp.sum(table_ref[...], axis=1)], axis=0
    )
    weights = dot_nt(right_operand(functionals), left_operand(second))
    ones = jnp.ones((8, right_ref.shape[2]), jnp.bfloat16)
    high, low = halves(right_ref[...].reshape(second.shape))
    rights = dot_nt(ones, high) + dot_nt(ones, low)
    per_tile = LANES // n_rhs
    n_func = functionals.shape[0]
    lane = lax.broadcasted_iota(jnp.int32, (n_func + 8, LANES), 1)
    weights = jnp.concatenate([weights, rights], axis=0)
    pieces = []
    for row in range(rows):
        tile, spot = row // per_tile, row % per_tile
        piece = weights[:, tile * LANES : (tile + 1) * LANES]
        pieces.append(jnp.where(lax.div(lane, n_rhs) == spot, piece, 0.0))
    spread = jnp.concatenate(pieces, axis=0)
    partial = dot_exact(count_ref[...], spread)
    source = lax.broadcasted_iota(jnp.int32, (LANES, LANES), 0)
    target = lax.broadcasted_iota(jnp.int32, (LANES, LANES), 1)
    same = jnp.where(lax.rem(source, n_rhs) == lax.rem(target, n_rhs), 1.0, 0.0)
    same = same.astype(jnp.bfloat16)
    high, low = halves(partial)
    partial = jnp.dot(high, same, preferred_element_type=jnp.float32) + jnp.dot(
        low, same, preferred_element_type=jnp.float32
    )
    high, low = halves(partial)
    both = jnp.concatenate([high, low], axis=1)
    depth = part_ref.shape[0]
    lane = lax.broadcasted_iota(jnp.int32, (depth, LANES), 1)
    result = jnp.zeros((depth, LANES), jnp.float32)
    for spot in range(per_tile):
        chosen = jnp.dot(
            place_ref[spot * depth : (spot + 1) * depth, :],
            both,
            preferred_element_type=jnp.float32,
        )
        chosen = chosen[:, :LANES] + chosen[:, LANES:]
        result = jnp.where(lax.div(lane, n_rhs) == spot, chosen, result)
    part_ref[...] = result


def final_kernel(sizes, part_ref, scale_ref, second_ref, out_ref):
    rows, n_rhs = sizes[0], sizes[4]
    depth = scale_ref.shape[0]
    total = part_ref[0]
    for source in range(1, part_ref.shape[0]):
        total = total + part_ref[source]
    correction = total / scale_ref[...]
    padded = jnp.concatenate([correction, jnp.zeros((8 - depth, LANES), jnp.float32)], axis=0)
    turned = padded.T
    for row in range(rows):
        spot, place = row // depth, row % depth
        column = turned[spot * n_rhs : (spot + 1) * n_rhs, place : place + 1]
        out_ref[row] = second_ref[row] + column


def shifted(value, axis, steps):
    count = lax.axis_size(axis)
    initial, last = (max(0, -steps), min(count, count - steps))
    return lax.ppermute(value, axis, [(source, source + steps) for source in range(initial, last)])


def to_bands(sends):
    if len(sends) == 1:
        return (lax.ppermute(sends[0], "band", [(0, 1), (1, 0)]),)
    return shifted(sends[0], "band", 1), shifted(sends[1], "band", -1)


def on_device(
    start_iterate,
    right_side,
    diag_table,
    inverse_table,
    coupling_tiles,
    diag_index,
    tile_index,
    source_owner,
    source_local,
    aggregate_map,
):
    rows, n_rhs, states = start_iterate.shape
    width_k = source_owner.shape[1]
    n_tiles, n_diag = coupling_tiles.shape[0], inverse_table.shape[0]
    n_rows, n_bands = lax.axis_size("rows"), lax.axis_size("band")
    n_dev = n_rows * n_bands
    cap = max(2, 2 * width_k * rows // n_rows)
    slots = n_rows * cap
    total_groups = AGG_DEV * n_dev
    dense = n_dev * rows * total_groups <= DENSE_LIMIT and LANES % n_rhs == 0
    sizes = (rows, n_rows, cap, n_tiles, n_rhs)
    f32, i32 = jnp.float32, jnp.int32
    my_band = lax.axis_index("band")
    my_row = lax.axis_index("rows")

    wide = -(-4 * rows // LANES) * LANES
    payload, slot_place = call(
        functools.partial(request_kernel, (rows, width_k, n_rows, cap, n_tiles)),
        (
            jax.ShapeDtypeStruct((n_bands, n_rows, LANES + wide), i32),
            jax.ShapeDtypeStruct((1, width_k * rows), i32),
        ),
        [VMEM] * 5,
    )(source_owner, source_local, tile_index, diag_index[:, None], aggregate_map)
    arrived = lax.all_to_all(
        payload.reshape(n_dev, LANES + wide), ("band", "rows"), split_axis=0, concat_axis=0, tiled=True
    ).reshape(n_bands, n_rows, LANES + wide)
    requests = lax.dynamic_index_in_dim(arrived[:, :, :LANES], my_band, 0, keepdims=False)
    common = arrived[:, :, LANES:]
    groups_all = common[:, :, :rows]
    diags_all = common[:, :, rows : 2 * rows]

    def neighbour(steps):
        other = lax.rem(my_band + steps + n_bands, n_bands)
        part = lax.dynamic_index_in_dim(common, other, 0, keepdims=False)
        return lax.dynamic_index_in_dim(part, my_row, 0, keepdims=False)

    above, below = neighbour(1), neighbour(-1)
    has_above, has_below = my_band + 1 < n_bands, my_band > 0
    tiles_above, tiles_below = above[2 * rows : 3 * rows], below[3 * rows : 4 * rows]
    if n_bands == 2:
        band_tiles = jnp.where(has_above, tiles_above, tiles_below)[None]
        band_groups = jnp.where(has_above, above[:rows], below[:rows])[None]
        band_valid = jnp.ones((1, rows), bool)
    else:
        band_tiles = jnp.stack([tiles_above, tiles_below])
        band_groups = jnp.stack([above[:rows], below[:rows]])
        band_valid = jnp.stack(
            [jnp.broadcast_to(has_above, (rows,)), jnp.broadcast_to(has_below, (rows,))]
        )
    n_ways = band_tiles.shape[0]

    block = (rows, n_rhs, states)
    send_shapes = (
        jax.ShapeDtypeStruct((n_rows, cap, n_rhs, states), f32),
        *[jax.ShapeDtypeStruct(block, f32)] * n_ways,
    )
    flat = rows * n_rhs
    sums = pltpu.VMEM((flat, states), f32)
    products = pltpu.VMEM((max(n_tiles, n_diag), flat, states), f32)
    work = 6 * flat * states * states
    sends = call(
        functools.partial(first_kernel, sizes),
        send_shapes,
        [VMEM, VMEM, SMEM, SMEM],
        [products],
        work * n_tiles,
        4 << 20,
    )(start_iterate, coupling_tiles, requests, band_tiles)

    def exchange(sends):
        arrived = lax.all_to_all(sends[0], "rows", split_axis=0, concat_axis=0, tiled=True)
        return arrived, to_bands(sends[1:])

    diag_row = diag_index[None]
    arrived_blocks, arrived_bands = exchange(sends)
    sends = call(
        functools.partial(middle_kernel, sizes, n_ways),
        send_shapes,
        [SMEM] * 4 + [VMEM] * (4 + n_ways),
        [sums, products],
        work * (n_tiles + n_diag),
        4 << 20,
    )(
        slot_place,
        diag_row,
        requests,
        band_tiles,
        arrived_blocks,
        *arrived_bands,
        right_side,
        inverse_table,
        coupling_tiles,
    )
    arrived_blocks, arrived_bands = exchange(sends)

    n_func = n_tiles + n_diag + 8
    codes = requests[:, :cap].reshape(-1)
    code = jnp.maximum(codes - 1, 0)
    own = jnp.arange(rows, dtype=i32)
    groups = aggregate_map[:, 0]
    entry_group = jnp.concatenate(
        [code // (rows * n_tiles), band_groups.reshape(-1), groups, groups]
    )
    entry_func = jnp.concatenate(
        [
            (code % rows) * n_func + (code // rows) % n_tiles,
            (own[None] * n_func + band_tiles).reshape(-1),
            own * n_func + n_tiles + diag_index,
            own * n_func + n_tiles + n_diag,
        ]
    )
    entry_valid = jnp.concatenate(
        [codes > 0, band_valid.reshape(-1), jnp.ones((2 * rows,), bool)]
    )
    table_sums = jnp.sum(diag_table, axis=(1, 2))
    diag_onehot = diags_all.reshape(-1, 1) == jnp.arange(n_diag, dtype=i32)[None]
    block_sums = jnp.sum(jnp.where(diag_onehot, table_sums[None], 0.0), axis=1)
    all_groups = groups_all.reshape(-1)
    whole_diag = jnp.sum(
        jnp.where(groups[:, None] == all_groups[None], block_sums[None], 0.0), axis=1
    )
    if dense:
        per_tile = LANES // n_rhs
        depth = rows // per_tile
        group_ids = jnp.arange(total_groups, dtype=i32)
        left = (group_ids[:, None] == entry_group[None]).astype(jnp.bfloat16)
        right = (
            (entry_func[:, None] == jnp.arange(rows * n_func, dtype=i32)[None]) & entry_valid[:, None]
        ).astype(jnp.bfloat16)
        counts = jnp.dot(left, right, preferred_element_type=f32).astype(jnp.bfloat16)
        order = all_groups.reshape(n_dev, per_tile, depth).transpose(1, 0, 2).reshape(-1)
        placing = (order[:, None] == group_ids[None]).astype(jnp.bfloat16)
        scale = jnp.repeat(whole_diag.reshape(per_tile, depth).T, n_rhs, axis=1)
        second, parts = call(
            functools.partial(last_kernel, sizes, n_ways, True),
            (
                jax.ShapeDtypeStruct(block, f32),
                jax.ShapeDtypeStruct((n_dev * depth, LANES), f32),
            ),
            [SMEM] * 2 + [VMEM] * (7 + n_ways),
            [sums, products],
            2 * work * n_diag,
            4 << 20,
        )(
            slot_place,
            diag_row,
            arrived_blocks,
            *arrived_bands,
            right_side,
            inverse_table,
            coupling_tiles,
            diag_table,
            counts,
            placing,
        )
        parts = lax.all_to_all(
            parts.reshape(n_dev, depth, LANES), ("band", "rows"), split_axis=0, concat_axis=0, tiled=True
        )
        return call(
            functools.partial(final_kernel, sizes), jax.ShapeDtypeStruct(block, f32), [VMEM] * 3
        )(parts, scale, second)

    second = call(
        functools.partial(last_kernel, sizes, n_ways, False),
        jax.ShapeDtypeStruct(block, f32),
        [SMEM] * 2 + [VMEM] * (3 + n_ways),
        [sums, products],
        work * n_diag,
        4 << 20,
    )(slot_place, diag_row, arrived_blocks, *arrived_bands, right_side, inverse_table)
    functionals = jnp.concatenate(
        [jnp.sum(coupling_tiles, axis=1), -jnp.sum(diag_table, axis=1)], axis=0
    )
    weights = jnp.einsum("fp,rcp->rfc", functionals, second, precision=HIGH)
    rights = jnp.sum(right_side, axis=2)[:, None]
    weights = jnp.concatenate([weights, jnp.broadcast_to(rights, (rows, 8, n_rhs))], axis=1)
    chosen = jnp.take(weights.reshape(rows * n_func, n_rhs), entry_func, axis=0)
    chosen = jnp.where(entry_valid[:, None], chosen, 0.0)
    partial = jax.ops.segment_sum(chosen, entry_group, num_segments=total_groups)
    whole = lax.psum(partial, ("band", "rows"))
    correction = jnp.take(whole, groups, axis=0) / whole_diag[:, None]
    return second + correction[:, :, None]


def solution(mesh):
    in_specs = (
        P(("band", "rows"), None, None),
        P(("band", "rows"), None, None),
        P(),
        P(),
        P(),
        P(("band", "rows")),
        P(("band", "rows"), None),
        P(("band", "rows"), None),
        P(("band", "rows"), None),
        P(("band", "rows"), None),
    )
    out_specs = P(("band", "rows"), None, None)
    return jax.shard_map(
        on_device, mesh=mesh, in_specs=in_specs, out_specs=out_specs, check_vma=False
    )
```

```python
import functools

import jax
import jax.numpy as jnp
from jax import lax
from jax.experimental import pallas as pl
from jax.experimental.pallas import tpu as pltpu
from jax.sharding import PartitionSpec as P

AGG_DEV = 8
LANES = 128
DENSE_LIMIT = 1 << 19

VMEM = pl.BlockSpec(memory_space=pltpu.VMEM)
SMEM = pl.BlockSpec(memory_space=pltpu.SMEM)
HIGH = lax.Precision.HIGHEST


def params():
    return pltpu.CompilerParams(vmem_limit_bytes=16 * 1024 * 1024)


def call(kernel, out_shape, in_specs, scratch=(), flops=0, moved=0):
    single = not isinstance(out_shape, (tuple, list))
    count = 1 if single else len(out_shape)
    return pl.pallas_call(
        kernel,
        out_shape=out_shape,
        in_specs=in_specs,
        out_specs=VMEM if single else [VMEM] * count,
        scratch_shapes=list(scratch),
        compiler_params=params(),
        cost_estimate=pl.CostEstimate(flops=flops, bytes_accessed=moved, transcendentals=0),
    )


def halves(value):
    high = value.astype(jnp.bfloat16)
    low = (value - high.astype(jnp.float32)).astype(jnp.bfloat16)
    return high, low


def left_operand(value):
    high, low = halves(value)
    return jnp.concatenate([high, low, high], axis=1)


def right_operand(value):
    high, low = halves(value)
    return jnp.concatenate([high, high, low], axis=1)


def dot_nt(left, right):
    return lax.dot_general(
        left, right, (((1,), (1,)), ((), ())), preferred_element_type=jnp.float32
    )


def table_products(value, table_ref, out_ref):
    left = left_operand(value)
    count, width = table_ref.shape[0], table_ref.shape[1]
    for first in range(0, count, 2):
        last = min(first + 2, count)
        right = right_operand(table_ref[first:last].reshape((last - first) * width, -1))
        product = dot_nt(left, right)
        for t in range(first, last):
            out_ref[t] = product[:, (t - first) * width : (t - first + 1) * width]


def dot_exact(left, value):
    high, low = halves(value)
    return jnp.dot(left, high, preferred_element_type=jnp.float32) + jnp.dot(
        left, low, preferred_element_type=jnp.float32
    )


def request_kernel(
    sizes, owner_ref, local_ref, tile_ref, diag_ref, group_ref, payload_ref, slot_ref
):
    rows, n_rows, cap, n_tiles = sizes
    width_k = owner_ref.shape[0]
    half = n_rows // 2
    row_of = lax.broadcasted_iota(jnp.int32, (rows, rows), 0)
    col_of = lax.broadcasted_iota(jnp.int32, (rows, rows), 1)
    lane = lax.broadcasted_iota(jnp.int32, (rows, LANES), 1)
    owners = lax.broadcasted_iota(jnp.int32, (n_rows, rows), 0)

    def column(row):
        return jnp.sum(jnp.where(row_of == col_of, row, 0), axis=1, keepdims=True)

    def owner_row(k):
        return owner_ref[k : k + 1, :]

    owner_columns = [column(owner_row(k)) for k in range(width_k)]
    lists = jnp.zeros((n_rows, LANES), jnp.float32)
    for k in range(width_k):
        rank = jnp.zeros((1, rows), jnp.int32)
        for other in range(k + 1):
            match = owner_columns[other] == owner_row(k)
            if other == k:
                match = match & (row_of < col_of)
            rank = rank + jnp.sum(jnp.where(match, 1, 0), axis=0, keepdims=True)
        slot_ref[k : k + 1, :] = owner_row(k) * cap + rank
        code = local_ref[k : k + 1, :] + rows * (
            tile_ref[k : k + 1, :] + n_tiles * group_ref[...]
        )
        code, rank = column(code + 1), column(rank)
        mirror = jnp.where(owner_row(k) >= half, owner_row(k) - half, owner_row(k) + half)
        for owner, base in ((owner_row(k), 0), (mirror, LANES // 2)):
            by_rank = jnp.where(lane == rank + base, code, 0).astype(jnp.float32)
            mine = jnp.where(owners == owner, 1.0, 0.0)
            lists = lists + jnp.dot(
                mine, by_rank, precision=HIGH, preferred_element_type=jnp.float32
            )
    lists = (lists + 0.5).astype(jnp.int32)
    common = [group_ref[...], diag_ref[...], tile_ref[width_k : width_k + 1, :]]
    common.append(tile_ref[width_k + 1 : width_k + 2, :])
    spare = payload_ref.shape[2] - LANES - len(common) * rows
    if spare:
        common.append(jnp.zeros((1, spare), jnp.int32))
    common = jnp.concatenate(common, axis=1)
    for device in range(n_rows):
        line = jnp.concatenate([lists[device : device + 1, :], common], axis=1)
        for band in range(payload_ref.shape[0] // n_rows):
            payload_ref[band * n_rows + device] = line


def chosen_product(sizes, product_ref, code, base):
    rows, n_rows, cap, n_tiles, n_rhs = sizes
    code = jnp.maximum(code - 1, 0)
    tile = lax.rem(lax.div(code, rows), n_tiles)
    start = pl.multiple_of((lax.rem(code, rows) + base) * n_rhs, n_rhs)
    return product_ref[tile, pl.ds(start, n_rhs), :]


def pack_bands(sizes, product_ref, tiles_ref, band_refs):
    rows, n_rhs = sizes[0], sizes[4]
    for way, band_ref in enumerate(band_refs):
        for row in range(rows):
            band_ref[row] = product_ref[tiles_ref[way, row], pl.ds(row * n_rhs, n_rhs), :]


def first_kernel(
    sizes, start_ref, mirror_ref, tile_ref, request_ref, tiles_ref, send_ref, *rest
):
    rows, n_rows, cap, n_tiles, n_rhs = sizes
    product_ref, band_refs = rest[-1], rest[:-1]
    flat = rows * n_rhs
    values = [ref[...].reshape(flat, -1) for ref in (start_ref, mirror_ref)]
    table_products(jnp.concatenate(values, axis=0), tile_ref, product_ref)
    half = n_rows // 2
    base = lax.div(lax.axis_index("rows"), half) * half
    for device in range(half):
        for slot in range(2 * cap):
            side, rank = slot // cap, slot % cap
            code = request_ref[base + device, side * (LANES // 2) + rank]
            send_ref[device, slot] = chosen_product(sizes, product_ref, code, side * rows)
    pack_bands(sizes, product_ref, tiles_ref, band_refs)


def gather_solve(
    sizes, slot_ref, diag_ref, arrived_ref, band_refs, right_ref, inverse_ref, sum_ref, product_ref
):
    rows, n_rows, cap, n_tiles, n_rhs = sizes
    for row in range(rows):
        total = right_ref[row]
        for k in range(slot_ref.shape[0]):
            total = total + arrived_ref[slot_ref[k, row]]
        for band_ref in band_refs:
            total = total + band_ref[row]
        sum_ref[pl.ds(row * n_rhs, n_rhs), :] = total
    table_products(sum_ref[...], inverse_ref, product_ref)
    for row in range(rows):
        place = pl.ds(row * n_rhs, n_rhs)
        sum_ref[place, :] = product_ref[diag_ref[0, row], place, :]


def middle_kernel(sizes, n_band, *refs):
    slot_ref, diag_ref, request_ref, tiles_ref, arrived_ref = refs[:5]
    band_in = refs[5 : 5 + n_band]
    right_ref, inverse_ref, tile_ref, send_ref = refs[5 + n_band : 9 + n_band]
    band_out = refs[9 + n_band : 9 + 2 * n_band]
    sum_ref, product_ref = refs[9 + 2 * n_band :]
    gather_solve(
        sizes, slot_ref, diag_ref, arrived_ref, band_in, right_ref, inverse_ref, sum_ref, product_ref
    )
    table_products(sum_ref[...], tile_ref, product_ref)
    rows, n_rows, cap, n_tiles, n_rhs = sizes
    for owner in range(n_rows):
        for rank in range(cap):
            send_ref[owner, rank] = chosen_product(sizes, product_ref, request_ref[owner, rank], 0)
    pack_bands(sizes, product_ref, tiles_ref, band_out)


def last_kernel(sizes, n_band, dense, *refs):
    slot_ref, diag_ref, arrived_ref = refs[:3]
    band_in = refs[3 : 3 + n_band]
    refs = refs[3 + n_band :]
    right_ref, inverse_ref = refs[:2]
    if dense:
        tile_ref, table_ref, count_ref, place_ref, second_ref, part_ref = refs[2:8]
    else:
        second_ref = refs[2]
    sum_ref, product_ref = refs[-2:]
    rows, n_rhs = sizes[0], sizes[4]
    gather_solve(
        sizes, slot_ref, diag_ref, arrived_ref, band_in, right_ref, inverse_ref, sum_ref, product_ref
    )
    second = sum_ref[...]
    second_ref[...] = second.reshape(second_ref.shape)
    if not dense:
        return
    functionals = jnp.concatenate(
        [jnp.sum(tile_ref[...], axis=1), -jnp.sum(table_ref[...], axis=1)], axis=0
    )
    weights = dot_nt(right_operand(functionals), left_operand(second))
    ones = jnp.ones((8, right_ref.shape[2]), jnp.bfloat16)
    high, low = halves(right_ref[...].reshape(second.shape))
    rights = dot_nt(ones, high) + dot_nt(ones, low)
    per_tile = LANES // n_rhs
    n_func = functionals.shape[0]
    lane = lax.broadcasted_iota(jnp.int32, (n_func + 8, LANES), 1)
    weights = jnp.concatenate([weights, rights], axis=0)
    pieces = []
    for row in range(rows):
        tile, spot = row // per_tile, row % per_tile
        piece = weights[:, tile * LANES : (tile + 1) * LANES]
        pieces.append(jnp.where(lax.div(lane, n_rhs) == spot, piece, 0.0))
    spread = jnp.concatenate(pieces, axis=0)
    partial = dot_exact(count_ref[...], spread)
    source = lax.broadcasted_iota(jnp.int32, (LANES, LANES), 0)
    target = lax.broadcasted_iota(jnp.int32, (LANES, LANES), 1)
    same = jnp.where(lax.rem(source, n_rhs) == lax.rem(target, n_rhs), 1.0, 0.0)
    same = same.astype(jnp.bfloat16)
    high, low = halves(partial)
    partial = jnp.dot(high, same, preferred_element_type=jnp.float32) + jnp.dot(
        low, same, preferred_element_type=jnp.float32
    )
    high, low = halves(partial)
    both = jnp.concatenate([high, low], axis=1)
    depth = part_ref.shape[0]
    lane = lax.broadcasted_iota(jnp.int32, (depth, LANES), 1)
    result = jnp.zeros((depth, LANES), jnp.float32)
    for spot in range(per_tile):
        chosen = jnp.dot(
            place_ref[spot * depth : (spot + 1) * depth, :],
            both,
            preferred_element_type=jnp.float32,
        )
        chosen = chosen[:, :LANES] + chosen[:, LANES:]
        result = jnp.where(lax.div(lane, n_rhs) == spot, chosen, result)
    part_ref[...] = result


def final_kernel(sizes, part_ref, scale_ref, second_ref, out_ref):
    rows, n_rhs = sizes[0], sizes[4]
    depth = scale_ref.shape[0]
    total = part_ref[0]
    for source in range(1, part_ref.shape[0]):
        total = total + part_ref[source]
    correction = total / scale_ref[...]
    padded = jnp.concatenate([correction, jnp.zeros((8 - depth, LANES), jnp.float32)], axis=0)
    turned = padded.T
    for row in range(rows):
        spot, place = row // depth, row % depth
        column = turned[spot * n_rhs : (spot + 1) * n_rhs, place : place + 1]
        out_ref[row] = second_ref[row] + column


def shifted(value, axis, steps):
    count = lax.axis_size(axis)
    initial, last = (max(0, -steps), min(count, count - steps))
    return lax.ppermute(value, axis, [(source, source + steps) for source in range(initial, last)])


def to_bands(sends):
    if len(sends) == 1:
        return (lax.ppermute(sends[0], "band", [(0, 1), (1, 0)]),)
    return shifted(sends[0], "band", 1), shifted(sends[1], "band", -1)


def on_device(
    start_iterate,
    right_side,
    diag_table,
    inverse_table,
    coupling_tiles,
    diag_index,
    tile_index,
    source_owner,
    source_local,
    aggregate_map,
):
    rows, n_rhs, states = start_iterate.shape
    width_k = source_owner.shape[1]
    n_tiles, n_diag = coupling_tiles.shape[0], inverse_table.shape[0]
    n_rows, n_bands = lax.axis_size("rows"), lax.axis_size("band")
    n_dev = n_rows * n_bands
    cap = max(2, 2 * width_k * rows // n_rows)
    slots = n_rows * cap
    total_groups = AGG_DEV * n_dev
    dense = n_dev * rows * total_groups <= DENSE_LIMIT and LANES % n_rhs == 0
    sizes = (rows, n_rows, cap, n_tiles, n_rhs)
    f32, i32 = jnp.float32, jnp.int32
    my_band = lax.axis_index("band")
    my_row = lax.axis_index("rows")

    half = n_rows // 2
    mirror = lax.ppermute(start_iterate, "rows", [(i, (i + half) % n_rows) for i in range(n_rows)])
    wide = -(-4 * rows // LANES) * LANES
    payload, slot_place = call(
        functools.partial(request_kernel, (rows, n_rows, cap, n_tiles)),
        (
            jax.ShapeDtypeStruct((n_dev, 1, LANES + wide), i32),
            jax.ShapeDtypeStruct((width_k, rows), i32),
        ),
        [VMEM] * 5,
    )(source_owner.T, source_local.T, tile_index.T, diag_index[None], aggregate_map.T)
    arrived = lax.all_to_all(
        payload, ("band", "rows"), split_axis=0, concat_axis=0, tiled=True
    ).reshape(n_bands, n_rows, LANES + wide)
    owner = slot_place // cap
    half_place = (owner % half) * 2 * cap + slot_place % cap
    half_place = half_place + jnp.where(owner // half == my_row // half, 0, cap)
    requests = lax.dynamic_index_in_dim(arrived[:, :, :LANES], my_band, 0, keepdims=False)
    common = arrived[:, :, LANES:]
    groups_all = common[:, :, :rows]
    diags_all = common[:, :, rows : 2 * rows]

    def neighbour(steps):
        other = lax.rem(my_band + steps + n_bands, n_bands)
        part = lax.dynamic_index_in_dim(common, other, 0, keepdims=False)
        return lax.dynamic_index_in_dim(part, my_row, 0, keepdims=False)

    above, below = neighbour(1), neighbour(-1)
    has_above, has_below = my_band + 1 < n_bands, my_band > 0
    tiles_above, tiles_below = above[2 * rows : 3 * rows], below[3 * rows : 4 * rows]
    if n_bands == 2:
        band_tiles = jnp.where(has_above, tiles_above, tiles_below)[None]
        band_groups = jnp.where(has_above, above[:rows], below[:rows])[None]
        band_valid = jnp.ones((1, rows), bool)
    else:
        band_tiles = jnp.stack([tiles_above, tiles_below])
        band_groups = jnp.stack([above[:rows], below[:rows]])
        band_valid = jnp.stack(
            [jnp.broadcast_to(has_above, (rows,)), jnp.broadcast_to(has_below, (rows,))]
        )
    n_ways = band_tiles.shape[0]

    block = (rows, n_rhs, states)
    band_shapes = [jax.ShapeDtypeStruct(block, f32)] * n_ways
    flat = rows * n_rhs
    sums = pltpu.VMEM((flat, states), f32)
    products = pltpu.VMEM((max(n_tiles, n_diag), flat, states), f32)
    work = 6 * flat * states * states
    sends = call(
        functools.partial(first_kernel, sizes),
        (jax.ShapeDtypeStruct((half, 2 * cap, n_rhs, states), f32), *band_shapes),
        [VMEM, VMEM, VMEM, SMEM, SMEM],
        [pltpu.VMEM((n_tiles, 2 * flat, states), f32)],
        2 * work * n_tiles,
        4 << 20,
    )(start_iterate, mirror, coupling_tiles, requests, band_tiles)
    halves_of_rows = [list(range(half)), list(range(half, n_rows))]

    def exchange(sends, groups=None):
        arrived = lax.all_to_all(
            sends[0], "rows", split_axis=0, concat_axis=0, tiled=True, axis_index_groups=groups
        )
        return arrived.reshape(slots, n_rhs, states), to_bands(sends[1:])

    diag_row = diag_index[None]
    arrived_blocks, arrived_bands = exchange(sends, halves_of_rows)
    sends = call(
        functools.partial(middle_kernel, sizes, n_ways),
        (jax.ShapeDtypeStruct((n_rows, cap, n_rhs, states), f32), *band_shapes),
        [SMEM] * 4 + [VMEM] * (4 + n_ways),
        [sums, products],
        work * (n_tiles + n_diag),
        4 << 20,
    )(
        half_place,
        diag_row,
        requests,
        band_tiles,
        arrived_blocks,
        *arrived_bands,
        right_side,
        inverse_table,
        coupling_tiles,
    )
    arrived_blocks, arrived_bands = exchange(sends)

    n_func = n_tiles + n_diag + 8
    codes = requests[:, :cap].reshape(-1)
    code = jnp.maximum(codes - 1, 0)
    own = jnp.arange(rows, dtype=i32)
    groups = aggregate_map[:, 0]
    entry_group = jnp.concatenate(
        [code // (rows * n_tiles), band_groups.reshape(-1), groups, groups]
    )
    entry_func = jnp.concatenate(
        [
            (code % rows) * n_func + (code // rows) % n_tiles,
            (own[None] * n_func + band_tiles).reshape(-1),
            own * n_func + n_tiles + diag_index,
            own * n_func + n_tiles + n_diag,
        ]
    )
    entry_valid = jnp.concatenate(
        [codes > 0, band_valid.reshape(-1), jnp.ones((2 * rows,), bool)]
    )
    table_sums = jnp.sum(diag_table, axis=(1, 2))
    diag_onehot = diags_all.reshape(-1, 1) == jnp.arange(n_diag, dtype=i32)[None]
    block_sums = jnp.sum(jnp.where(diag_onehot, table_sums[None], 0.0), axis=1)
    all_groups = groups_all.reshape(-1)
    whole_diag = jnp.sum(
        jnp.where(groups[:, None] == all_groups[None], block_sums[None], 0.0), axis=1
    )
    if dense:
        per_tile = LANES // n_rhs
        depth = rows // per_tile
        group_ids = jnp.arange(total_groups, dtype=i32)
        left = (group_ids[:, None] == entry_group[None]).astype(jnp.bfloat16)
        right = (
            (entry_func[:, None] == jnp.arange(rows * n_func, dtype=i32)[None]) & entry_valid[:, None]
        ).astype(jnp.bfloat16)
        counts = jnp.dot(left, right, preferred_element_type=f32).astype(jnp.bfloat16)
        order = all_groups.reshape(n_dev, per_tile, depth).transpose(1, 0, 2).reshape(-1)
        placing = (order[:, None] == group_ids[None]).astype(jnp.bfloat16)
        scale = jnp.repeat(whole_diag.reshape(per_tile, depth).T, n_rhs, axis=1)
        second, parts = call(
            functools.partial(last_kernel, sizes, n_ways, True),
            (
                jax.ShapeDtypeStruct(block, f32),
                jax.ShapeDtypeStruct((n_dev * depth, LANES), f32),
            ),
            [SMEM] * 2 + [VMEM] * (7 + n_ways),
            [sums, products],
            2 * work * n_diag,
            4 << 20,
        )(
            slot_place,
            diag_row,
            arrived_blocks,
            *arrived_bands,
            right_side,
            inverse_table,
            coupling_tiles,
            diag_table,
            counts,
            placing,
        )
        parts = lax.all_to_all(
            parts.reshape(n_dev, depth, LANES), ("band", "rows"), split_axis=0, concat_axis=0, tiled=True
        )
        return call(
            functools.partial(final_kernel, sizes), jax.ShapeDtypeStruct(block, f32), [VMEM] * 3
        )(parts, scale, second)

    second = call(
        functools.partial(last_kernel, sizes, n_ways, False),
        jax.ShapeDtypeStruct(block, f32),
        [SMEM] * 2 + [VMEM] * (3 + n_ways),
        [sums, products],
        work * n_diag,
        4 << 20,
    )(slot_place, diag_row, arrived_blocks, *arrived_bands, right_side, inverse_table)
    functionals = jnp.concatenate(
        [jnp.sum(coupling_tiles, axis=1), -jnp.sum(diag_table, axis=1)], axis=0
    )
    weights = jnp.einsum("fp,rcp->rfc", functionals, second, precision=HIGH)
    rights = jnp.sum(right_side, axis=2)[:, None]
    weights = jnp.concatenate([weights, jnp.broadcast_to(rights, (rows, 8, n_rhs))], axis=1)
    chosen = jnp.take(weights.reshape(rows * n_func, n_rhs), entry_func, axis=0)
    chosen = jnp.where(entry_valid[:, None], chosen, 0.0)
    partial = jax.ops.segment_sum(chosen, entry_group, num_segments=total_groups)
    whole = lax.psum(partial, ("band", "rows"))
    correction = jnp.take(whole, groups, axis=0) / whole_diag[:, None]
    return second + correction[:, :, None]


def solution(mesh):
    in_specs = (
        P(("band", "rows"), None, None),
        P(("band", "rows"), None, None),
        P(),
        P(),
        P(),
        P(("band", "rows")),
        P(("band", "rows"), None),
        P(("band", "rows"), None),
        P(("band", "rows"), None),
        P(("band", "rows"), None),
    )
    out_specs = P(("band", "rows"), None, None)
    return jax.shard_map(
        on_device, mesh=mesh, in_specs=in_specs, out_specs=out_specs, check_vma=False
    )
```

```python
import functools

import jax
import jax.numpy as jnp
from jax import lax
from jax.experimental import pallas as pl
from jax.experimental.pallas import tpu as pltpu
from jax.sharding import PartitionSpec as P

AGG_DEV = 8
LANES = 128
DENSE_LIMIT = 1 << 19

VMEM = pl.BlockSpec(memory_space=pltpu.VMEM)
SMEM = pl.BlockSpec(memory_space=pltpu.SMEM)
HIGH = lax.Precision.HIGHEST


def params():
    return pltpu.CompilerParams(vmem_limit_bytes=16 * 1024 * 1024)


def call(kernel, out_shape, in_specs, scratch=(), flops=0, moved=0):
    single = not isinstance(out_shape, (tuple, list))
    count = 1 if single else len(out_shape)
    return pl.pallas_call(
        kernel,
        out_shape=out_shape,
        in_specs=in_specs,
        out_specs=VMEM if single else [VMEM] * count,
        scratch_shapes=list(scratch),
        compiler_params=params(),
        cost_estimate=pl.CostEstimate(flops=flops, bytes_accessed=moved, transcendentals=0),
    )


def halves(value):
    high = value.astype(jnp.bfloat16)
    low = (value - high.astype(jnp.float32)).astype(jnp.bfloat16)
    return high, low


def left_operand(value):
    high, low = halves(value)
    return jnp.concatenate([high, low, high], axis=1)


def right_operand(value):
    high, low = halves(value)
    return jnp.concatenate([high, high, low], axis=1)


def dot_nt(left, right):
    return lax.dot_general(
        left, right, (((1,), (1,)), ((), ())), preferred_element_type=jnp.float32
    )


def table_products(value, table_ref, out_ref):
    left = left_operand(value)
    count, width = table_ref.shape[0], table_ref.shape[1]
    for first in range(0, count, 2):
        last = min(first + 2, count)
        right = right_operand(table_ref[first:last].reshape((last - first) * width, -1))
        product = dot_nt(left, right)
        for t in range(first, last):
            out_ref[t] = product[:, (t - first) * width : (t - first + 1) * width]


def dot_exact(left, value):
    high, low = halves(value)
    return jnp.dot(left, high, preferred_element_type=jnp.float32) + jnp.dot(
        left, low, preferred_element_type=jnp.float32
    )


def request_kernel(
    sizes, owner_ref, local_ref, tile_ref, diag_ref, group_ref, payload_ref, slot_ref
):
    rows, n_rows, cap, n_tiles = sizes
    width_k = owner_ref.shape[0]
    half = n_rows // 2
    row_of = lax.broadcasted_iota(jnp.int32, (rows, rows), 0)
    col_of = lax.broadcasted_iota(jnp.int32, (rows, rows), 1)
    lane = lax.broadcasted_iota(jnp.int32, (rows, LANES), 1)
    owners = lax.broadcasted_iota(jnp.int32, (n_rows, rows), 0)

    def column(row):
        return jnp.sum(jnp.where(row_of == col_of, row, 0), axis=1, keepdims=True)

    def owner_row(k):
        return owner_ref[k : k + 1, :]

    row_ids = lax.broadcasted_iota(jnp.int32, (1, rows), 1)
    owner_columns = [column(owner_row(k)) for k in range(width_k)]
    lists = jnp.zeros((n_rows, LANES), jnp.float32)
    for k in range(width_k):
        rank = jnp.zeros((1, rows), jnp.int32)
        for other in range(k + 1):
            match = owner_columns[other] == owner_row(k)
            if other == k:
                match = match & (row_of < col_of)
            rank = rank + jnp.sum(jnp.where(match, 1, 0), axis=0, keepdims=True)
        slot_ref[k : k + 1, :] = owner_row(k) * cap + rank
        code = local_ref[k : k + 1, :] + rows * (
            tile_ref[k : k + 1, :] + n_tiles * row_ids
        )
        code, rank = column(code + 1), column(rank)
        mirror = jnp.where(owner_row(k) >= half, owner_row(k) - half, owner_row(k) + half)
        for owner, base in ((owner_row(k), 0), (mirror, LANES // 2)):
            by_rank = jnp.where(lane == rank + base, code, 0).astype(jnp.float32)
            mine = jnp.where(owners == owner, 1.0, 0.0)
            lists = lists + jnp.dot(
                mine, by_rank, precision=HIGH, preferred_element_type=jnp.float32
            )
    lists = (lists + 0.5).astype(jnp.int32)
    common = [group_ref[...], diag_ref[...]]
    common += [tile_ref[k : k + 1, :] for k in range(width_k + 2)]
    common += [owner_row(k) * rows + local_ref[k : k + 1, :] for k in range(width_k)]
    spare = payload_ref.shape[2] - LANES - len(common) * rows
    if spare:
        common.append(jnp.zeros((1, spare), jnp.int32))
    common = jnp.concatenate(common, axis=1)
    for device in range(n_rows):
        line = jnp.concatenate([lists[device : device + 1, :], common], axis=1)
        for band in range(payload_ref.shape[0] // n_rows):
            payload_ref[band * n_rows + device] = line


def chosen_product(sizes, product_ref, code, base):
    rows, n_rows, cap, n_tiles, n_rhs = sizes
    code = jnp.maximum(code - 1, 0)
    tile = lax.rem(lax.div(code, rows), n_tiles)
    start = pl.multiple_of((lax.rem(code, rows) + base) * n_rhs, n_rhs)
    return product_ref[tile, pl.ds(start, n_rhs), :]


def pack_bands(sizes, product_ref, tiles_ref, band_refs):
    rows, n_rhs = sizes[0], sizes[4]
    for way, band_ref in enumerate(band_refs):
        for row in range(rows):
            band_ref[row] = product_ref[tiles_ref[way, row], pl.ds(row * n_rhs, n_rhs), :]


def product_kernel(start_ref, mirror_ref, tile_ref, product_ref):
    flat = product_ref.shape[1] // 2
    values = [ref[...].reshape(flat, -1) for ref in (start_ref, mirror_ref)]
    table_products(jnp.concatenate(values, axis=0), tile_ref, product_ref)


def first_kernel(sizes, product_ref, request_ref, tiles_ref, send_ref, *band_refs):
    rows, n_rows, cap, n_tiles, n_rhs = sizes
    half = n_rows // 2
    base = lax.div(lax.axis_index("rows"), half) * half
    for device in range(half):
        for slot in range(2 * cap):
            side, rank = slot // cap, slot % cap
            code = request_ref[base + device, side * (LANES // 2) + rank]
            block = chosen_product(sizes, product_ref, code, side * rows)
            send_ref[device, slot * n_rhs : (slot + 1) * n_rhs, :] = block
    pack_bands(sizes, product_ref, tiles_ref, band_refs)


def count_kernel(n_func, *refs):
    *sides, group_ref, own_ref, tile_ref, table_ref, inverse_ref, count_ref, functional_ref = refs
    n_tiles, n_groups = tile_ref.shape[0], count_ref.shape[1]
    pieces = []
    for code_ref, source_ref, target_ref in (sides[:3], sides[3:]):
        hits = jnp.where(target_ref[...] == source_ref[...], 1.0, 0.0).astype(jnp.bfloat16)
        pieces.append((code_ref, hits))
    for t in range(n_tiles):
        found = []
        for code_ref, hits in pieces:
            ids = lax.broadcasted_iota(jnp.int32, (n_groups, code_ref.shape[1]), 0) + t * n_groups
            takes = jnp.where(ids == code_ref[...], 1.0, 0.0).astype(jnp.bfloat16)
            found.append(dot_nt(takes, hits))
        count_ref[t] = jnp.concatenate(found, axis=1).astype(jnp.bfloat16)
    ids = lax.broadcasted_iota(jnp.int32, count_ref.shape[1:], 0)
    count_ref[n_tiles] = jnp.where(ids == group_ref[...], 1.0, 0.0).astype(jnp.bfloat16)
    count_ref[n_tiles + 1] = jnp.where(ids == own_ref[...], 1.0, 0.0).astype(jnp.bfloat16)
    sums = jnp.sum(tile_ref[...], axis=1)
    line = lax.broadcasted_iota(jnp.int32, (n_func, sums.shape[1]), 0)
    sums = jnp.concatenate([sums, jnp.zeros((n_func - n_tiles, sums.shape[1]), jnp.float32)], axis=0)
    for d in range(inverse_ref.shape[0]):
        minus = -jnp.sum(table_ref[d], axis=0, keepdims=True)
        wanted = jnp.where(line == n_tiles, minus, sums)
        high, low = halves(inverse_ref[d])
        right = jnp.concatenate([high, high, low], axis=0)
        solved = jnp.dot(left_operand(wanted), right, preferred_element_type=jnp.float32)
        solved = jnp.where(line == n_tiles + 1, 1.0, solved)
        functional_ref[d * n_func : (d + 1) * n_func, :] = left_operand(solved)


def gather_solve(
    sizes, slot_ref, diag_ref, arrived_ref, band_refs, right_ref, inverse_ref, sum_ref, product_ref
):
    rows, n_rows, cap, n_tiles, n_rhs = sizes
    per = n_rows * cap // arrived_ref.shape[0]
    for row in range(rows):
        total = right_ref[row]
        for k in range(slot_ref.shape[0]):
            slot = slot_ref[k, row]
            start = pl.multiple_of(lax.rem(slot, per) * n_rhs, n_rhs)
            total = total + arrived_ref[lax.div(slot, per), pl.ds(start, n_rhs), :]
        for band_ref in band_refs:
            total = total + band_ref[row]
        sum_ref[pl.ds(row * n_rhs, n_rhs), :] = total
    table_products(sum_ref[...], inverse_ref, product_ref)
    for row in range(rows):
        place = pl.ds(row * n_rhs, n_rhs)
        sum_ref[place, :] = product_ref[diag_ref[0, row], place, :]


def middle_kernel(sizes, n_band, dense, *refs):
    slot_ref, diag_ref, request_ref, tiles_ref, arrived_ref = refs[:5]
    band_in = refs[5 : 5 + n_band]
    right_ref, inverse_ref, tile_ref = refs[5 + n_band : 8 + n_band]
    refs = refs[8 + n_band :]
    extra, refs = (refs[:4], refs[4:]) if dense else ((), refs)
    send_ref, band_out = refs[0], refs[1 : 1 + n_band]
    sum_ref, product_ref = refs[1 + n_band : 3 + n_band]
    gather_solve(
        sizes, slot_ref, diag_ref, arrived_ref, band_in, right_ref, inverse_ref, sum_ref, product_ref
    )
    table_products(sum_ref[...], tile_ref, product_ref)
    rows, n_rows, cap, n_tiles, n_rhs = sizes
    for owner in range(n_rows):
        for rank in range(cap):
            block = chosen_product(sizes, product_ref, request_ref[owner, rank], 0)
            send_ref[owner, rank * n_rhs : (rank + 1) * n_rhs, :] = block
    pack_bands(sizes, product_ref, tiles_ref, band_out)
    if dense:
        value_ref, spread_ref = refs[3 + n_band :]
        coarse_parts(sizes, extra, right_ref, send_ref, band_out, value_ref, spread_ref)


def coarse_parts(sizes, extra, right_ref, send_ref, band_out, value_ref, spread_ref):
    kind_ref, functional_ref, count_ref, place_ref = extra
    rows, n_rows, cap, n_tiles, n_rhs = sizes
    body = cap * n_rhs
    n_func = spread_ref.shape[0] // count_ref.shape[2]
    per_tile = LANES // n_rhs
    functional = functional_ref[...]
    done = 0
    for owner in range(0, n_rows, 2):
        values = [send_ref[owner + more, :body, :] for more in range(2)]
        values = jnp.concatenate(values, axis=0)
        value_ref[:, done : done + 2 * body] = dot_nt(functional, right_operand(values))
        done += 2 * body
    for ref in (right_ref, *band_out):
        values = ref[...].reshape(rows * n_rhs, -1)
        value_ref[:, done : done + rows * n_rhs] = dot_nt(functional, right_operand(values))
        done += rows * n_rhs
    lane = lax.broadcasted_iota(jnp.int32, (n_func, LANES), 1)
    for block in range(done // n_rhs):
        tile, spot = block // per_tile, block % per_tile
        start = pl.multiple_of(kind_ref[0, block] * n_func, n_func)
        piece = value_ref[pl.ds(start, n_func), tile * LANES : (tile + 1) * LANES]
        piece = jnp.where((lane >= spot * n_rhs) & (lane < (spot + 1) * n_rhs), piece, 0.0)
        spread_ref[block * n_func : (block + 1) * n_func, :] = piece
    partial = jnp.zeros((count_ref.shape[1], 2 * LANES), jnp.float32)
    for t in range(count_ref.shape[0]):
        values = spread_ref[pl.ds(t, done // n_rhs, stride=n_func), :]
        partial = partial + jnp.dot(
            count_ref[t],
            jnp.concatenate(halves(values), axis=1),
            preferred_element_type=jnp.float32,
        )
    partial = partial[:, :LANES] + partial[:, LANES:]
    source = lax.broadcasted_iota(jnp.int32, (LANES, LANES), 0)
    target = lax.broadcasted_iota(jnp.int32, (LANES, LANES), 1)
    same = jnp.where(lax.rem(source, n_rhs) == lax.rem(target, n_rhs), 1.0, 0.0)
    same = same.astype(jnp.bfloat16)
    same = jnp.concatenate([same, same], axis=0)
    partial = jnp.dot(
        jnp.concatenate(halves(partial), axis=1), same, preferred_element_type=jnp.float32
    )
    both = jnp.concatenate(halves(partial), axis=1)
    length = place_ref.shape[0] // per_tile
    lane = lax.broadcasted_iota(jnp.int32, (length, LANES), 1)
    result = jnp.zeros((length, LANES), jnp.float32)
    for spot in range(per_tile):
        chosen = jnp.dot(
            place_ref[spot * length : (spot + 1) * length, :],
            both,
            preferred_element_type=jnp.float32,
        )
        chosen = chosen[:, :LANES] + chosen[:, LANES:]
        result = jnp.where((lane >= spot * n_rhs) & (lane < (spot + 1) * n_rhs), chosen, result)
    depth = length // n_rows
    for owner in range(n_rows):
        send_ref[owner, body:, :] = result[owner * depth : (owner + 1) * depth, :]


def part_kernel(arrived_ref, mine_ref, other_ref):
    depth = mine_ref.shape[0]
    body = arrived_ref.shape[1] - 2 * depth
    total = arrived_ref[0, body:, :]
    for source in range(1, arrived_ref.shape[0]):
        total = total + arrived_ref[source, body:, :]
    upper = lax.axis_index("band") == 0
    mine_ref[...] = jnp.where(upper, total[:depth], total[depth:])
    other_ref[...] = jnp.where(upper, total[depth:], total[:depth])


def last_kernel(sizes, n_band, *refs):
    slot_ref, diag_ref, arrived_ref = refs[:3]
    band_in = refs[3 : 3 + n_band]
    right_ref, inverse_ref, second_ref, sum_ref, product_ref = refs[3 + n_band :]
    gather_solve(
        sizes, slot_ref, diag_ref, arrived_ref, band_in, right_ref, inverse_ref, sum_ref, product_ref
    )
    second_ref[...] = sum_ref[...].reshape(second_ref.shape)


def final_kernel(sizes, mine_ref, other_ref, scale_ref, second_ref, out_ref):
    rows, n_rhs = sizes[0], sizes[4]
    depth = scale_ref.shape[0]
    correction = (mine_ref[...] + other_ref[...]) / scale_ref[...]
    padded = jnp.concatenate([correction, jnp.zeros((8 - depth, LANES), jnp.float32)], axis=0)
    turned = padded.T
    for row in range(rows):
        spot, place = row // depth, row % depth
        column = turned[spot * n_rhs : (spot + 1) * n_rhs, place : place + 1]
        out_ref[row] = second_ref[row] + column


def shifted(value, axis, steps):
    count = lax.axis_size(axis)
    initial, last = (max(0, -steps), min(count, count - steps))
    return lax.ppermute(value, axis, [(source, source + steps) for source in range(initial, last)])


def to_bands(sends):
    if len(sends) == 1:
        return (lax.ppermute(sends[0], "band", [(0, 1), (1, 0)]),)
    return shifted(sends[0], "band", 1), shifted(sends[1], "band", -1)


def on_device(
    start_iterate,
    right_side,
    diag_table,
    inverse_table,
    coupling_tiles,
    diag_index,
    tile_index,
    source_owner,
    source_local,
    aggregate_map,
):
    rows, n_rhs, states = start_iterate.shape
    width_k = source_owner.shape[1]
    n_tiles, n_diag = coupling_tiles.shape[0], inverse_table.shape[0]
    n_rows, n_bands = lax.axis_size("rows"), lax.axis_size("band")
    n_dev = n_rows * n_bands
    cap = max(2, 2 * width_k * rows // n_rows)
    slots = n_rows * cap
    total_groups = AGG_DEV * n_dev
    per_tile = LANES // n_rhs
    depth = rows // per_tile
    n_func = 16
    dense = (
        n_bands == 2
        and n_dev * rows * total_groups <= DENSE_LIMIT
        and depth == 4
        and n_diag * n_func == LANES
        and n_tiles + 2 <= n_func
    )
    sizes = (rows, n_rows, cap, n_tiles, n_rhs)
    f32, i32 = jnp.float32, jnp.int32
    my_band = lax.axis_index("band")
    my_row = lax.axis_index("rows")

    half = n_rows // 2
    mirror = lax.ppermute(start_iterate, "rows", [(i, (i + half) % n_rows) for i in range(n_rows)])
    wide = -(-(4 + 2 * width_k) * rows // LANES) * LANES
    payload, slot_place = call(
        functools.partial(request_kernel, (rows, n_rows, cap, n_tiles)),
        (
            jax.ShapeDtypeStruct((n_dev, 1, LANES + wide), i32),
            jax.ShapeDtypeStruct((width_k, rows), i32),
        ),
        [VMEM] * 5,
    )(source_owner.T, source_local.T, tile_index.T, diag_index[None], aggregate_map.T)
    arrived = lax.all_to_all(
        payload, ("band", "rows"), split_axis=0, concat_axis=0, tiled=True
    ).reshape(n_bands, n_rows, LANES + wide)
    owner = slot_place // cap
    half_place = (owner % half) * 2 * cap + slot_place % cap
    half_place = half_place + jnp.where(owner // half == my_row // half, 0, cap)
    requests = lax.dynamic_index_in_dim(arrived[:, :, :LANES], my_band, 0, keepdims=False)
    common = arrived[:, :, LANES:]
    groups_all = common[:, :, :rows]
    diags_all = common[:, :, rows : 2 * rows]

    def neighbour(steps):
        other = lax.rem(my_band + steps + n_bands, n_bands)
        part = lax.dynamic_index_in_dim(common, other, 0, keepdims=False)
        return lax.dynamic_index_in_dim(part, my_row, 0, keepdims=False)

    above, below = neighbour(1), neighbour(-1)
    has_above, has_below = my_band + 1 < n_bands, my_band > 0
    field = (2 + width_k) * rows
    tiles_above = above[field : field + rows]
    tiles_below = below[field + rows : field + 2 * rows]
    if n_bands == 2:
        band_tiles = jnp.where(has_above, tiles_above, tiles_below)[None]
        band_groups = jnp.where(has_above, above[:rows], below[:rows])[None]
        band_valid = jnp.ones((1, rows), bool)
    else:
        band_tiles = jnp.stack([tiles_above, tiles_below])
        band_groups = jnp.stack([above[:rows], below[:rows]])
        band_valid = jnp.stack(
            [jnp.broadcast_to(has_above, (rows,)), jnp.broadcast_to(has_below, (rows,))]
        )
    n_ways = band_tiles.shape[0]

    block = (rows, n_rhs, states)
    band_shapes = [jax.ShapeDtypeStruct(block, f32)] * n_ways
    flat = rows * n_rhs
    sums = pltpu.VMEM((flat, states), f32)
    products = pltpu.VMEM((max(n_tiles, n_diag), flat, states), f32)
    work = 6 * flat * states * states
    made = call(
        product_kernel,
        jax.ShapeDtypeStruct((n_tiles, 2 * flat, states), f32),
        [VMEM] * 3,
        (),
        2 * work * n_tiles,
        4 << 20,
    )(start_iterate, mirror, coupling_tiles)
    sends = call(
        functools.partial(first_kernel, sizes),
        (jax.ShapeDtypeStruct((half, 2 * cap * n_rhs, states), f32), *band_shapes),
        [VMEM, SMEM, SMEM],
        (),
        0,
        4 << 20,
    )(made, requests, band_tiles)
    halves_of_rows = [list(range(half)), list(range(half, n_rows))]

    def exchange(sends, groups=None):
        arrived = lax.all_to_all(
            sends[0], "rows", split_axis=0, concat_axis=0, tiled=True, axis_index_groups=groups
        )
        return arrived, to_bands(sends[1:])

    diag_row = diag_index[None]
    arrived_blocks, arrived_bands = exchange(sends, halves_of_rows)

    groups = aggregate_map[:, 0]
    own = jnp.arange(rows, dtype=i32)
    codes = requests[:, :cap]
    asked = lax.broadcasted_iota(i32, codes.shape, 0) * rows + (codes - 1) // (rows * n_tiles)
    asked = jnp.where(codes > 0, asked, -1).reshape(-1)
    own_rows = my_row * rows + own
    table_sums = jnp.sum(diag_table, axis=(1, 2))
    diag_onehot = diags_all.reshape(-1, 1) == jnp.arange(n_diag, dtype=i32)[None]
    block_sums = jnp.sum(jnp.where(diag_onehot, table_sums[None], 0.0), axis=1)
    all_groups = groups_all.reshape(-1)
    whole_diag = jnp.sum(
        jnp.where(groups[:, None] == all_groups[None], block_sums[None], 0.0), axis=1
    )
    extra, extra_specs, extra_scratch, tail = (), [], [], 0
    if dense:
        fields = common.reshape(n_bands, n_rows, -1, rows).transpose(2, 0, 1, 3)
        fields = fields.reshape(-1, n_bands, n_rows * rows)
        by_group, by_diag = fields[0], fields[1]
        tiles_of, sources_of = fields[2 : 4 + width_k], fields[4 + width_k : 4 + 2 * width_k]
        across = jnp.stack([tiles_of[width_k, 1], tiles_of[width_k + 1, 0]])
        taken = [tiles_of[k] * total_groups + by_group for k in range(width_k)]
        taken = jnp.concatenate([*taken, across * total_groups + by_group[::-1]], axis=1)
        band_row_ids = jnp.broadcast_to(jnp.arange(n_rows * rows, dtype=i32)[None], by_group.shape)
        origin = jnp.concatenate([*sources_of, band_row_ids], axis=1)

        def pick(table, band):
            return lax.dynamic_index_in_dim(table, band, 0, keepdims=True)

        near, far = my_band, 1 - my_band
        near_targets = jnp.concatenate([asked, own_rows])
        targets = jnp.maximum(near_targets, 0)
        target_groups = jnp.concatenate([jnp.take(pick(by_group, near)[0], targets), band_groups[0]])
        target_kinds = jnp.concatenate(
            [jnp.take(pick(by_diag, near)[0], targets), pick(by_diag, far)[0][own_rows]]
        )
        target_groups = jnp.where(jnp.concatenate([near_targets, own_rows]) >= 0, target_groups, -1)
        nobody = jnp.full((slots,), -1, i32)
        own_groups = jnp.concatenate([nobody, groups, jnp.full((rows,), -1, i32)])
        n_blocks = slots + 2 * rows
        counts, functionals = call(
            functools.partial(count_kernel, n_func),
            (
                jax.ShapeDtypeStruct((n_tiles + 2, total_groups, n_blocks), jnp.bfloat16),
                jax.ShapeDtypeStruct((n_diag * n_func, 3 * states), jnp.bfloat16),
            ),
            [VMEM] * 11,
            (),
            4 * total_groups * n_tiles * n_dev * rows * n_blocks,
            4 << 20,
        )(
            pick(taken, near),
            pick(origin, near),
            near_targets[:, None],
            pick(taken, far),
            pick(origin, far),
            own_rows[:, None],
            target_groups[None],
            own_groups[None],
            coupling_tiles,
            diag_table,
            inverse_table,
        )
        order = groups_all.reshape(n_bands, n_rows, per_tile, depth).transpose(2, 1, 0, 3)
        group_ids = jnp.arange(total_groups, dtype=i32)
        placing = (order.reshape(-1, 1) == group_ids[None]).astype(jnp.bfloat16)
        scale = jnp.repeat(whole_diag.reshape(per_tile, depth).T, n_rhs, axis=1)
        extra = (target_kinds[None], functionals, counts, placing)
        extra_specs = [SMEM, VMEM, VMEM, VMEM]
        extra_scratch = [
            pltpu.VMEM((n_diag * n_func, n_blocks * n_rhs), f32),
            pltpu.VMEM((n_blocks * n_func, LANES), f32),
        ]
        tail = n_bands * depth

    sends = call(
        functools.partial(middle_kernel, sizes, n_ways, dense),
        (jax.ShapeDtypeStruct((n_rows, cap * n_rhs + tail, states), f32), *band_shapes),
        [SMEM] * 4 + [VMEM] * (4 + n_ways) + extra_specs,
        [sums, products, *extra_scratch],
        work * (n_tiles + n_diag),
        4 << 20,
    )(
        half_place,
        diag_row,
        requests,
        band_tiles,
        arrived_blocks,
        *arrived_bands,
        right_side,
        inverse_table,
        coupling_tiles,
        *extra,
    )
    arrived_blocks, arrived_bands = exchange(sends)

    if dense:
        part = jax.ShapeDtypeStruct((depth, LANES), f32)
        mine, other = call(part_kernel, (part, part), [VMEM])(arrived_blocks)
        other = lax.ppermute(other, "band", [(0, 1), (1, 0)])
    second = call(
        functools.partial(last_kernel, sizes, n_ways),
        jax.ShapeDtypeStruct(block, f32),
        [SMEM] * 2 + [VMEM] * (3 + n_ways),
        [sums, products],
        work * n_diag,
        4 << 20,
    )(slot_place, diag_row, arrived_blocks, *arrived_bands, right_side, inverse_table)
    if dense:
        return call(
            functools.partial(final_kernel, sizes), jax.ShapeDtypeStruct(block, f32), [VMEM] * 4
        )(mine, other, scale, second)

    n_all = n_tiles + n_diag + 1
    code = jnp.maximum(codes.reshape(-1) - 1, 0)
    band_of_mine = lax.dynamic_index_in_dim(groups_all, my_band, 0, keepdims=False).reshape(-1)
    entry_group = jnp.concatenate(
        [jnp.take(band_of_mine, jnp.maximum(asked, 0)), band_groups.reshape(-1), groups, groups]
    )
    entry_func = jnp.concatenate(
        [
            (code % rows) * n_all + (code // rows) % n_tiles,
            (own[None] * n_all + band_tiles).reshape(-1),
            own * n_all + n_tiles + diag_index,
            own * n_all + n_tiles + n_diag,
        ]
    )
    entry_valid = jnp.concatenate([asked >= 0, band_valid.reshape(-1), jnp.ones((2 * rows,), bool)])
    functionals = jnp.concatenate(
        [jnp.sum(coupling_tiles, axis=1), -jnp.sum(diag_table, axis=1)], axis=0
    )
    weights = jnp.einsum("fp,rcp->rfc", functionals, second, precision=HIGH)
    weights = jnp.concatenate([weights, jnp.sum(right_side, axis=2)[:, None]], axis=1)
    chosen = jnp.take(weights.reshape(rows * n_all, n_rhs), entry_func, axis=0)
    chosen = jnp.where(entry_valid[:, None], chosen, 0.0)
    partial = jax.ops.segment_sum(chosen, entry_group, num_segments=total_groups)
    whole = lax.psum(partial, ("band", "rows"))
    correction = jnp.take(whole, groups, axis=0) / whole_diag[:, None]
    return second + correction[:, :, None]


def solution(mesh):
    in_specs = (
        P(("band", "rows"), None, None),
        P(("band", "rows"), None, None),
        P(),
        P(),
        P(),
        P(("band", "rows")),
        P(("band", "rows"), None),
        P(("band", "rows"), None),
        P(("band", "rows"), None),
        P(("band", "rows"), None),
    )
    out_specs = P(("band", "rows"), None, None)
    return jax.shard_map(
        on_device, mesh=mesh, in_specs=in_specs, out_specs=out_specs, check_vma=False
    )
```

```python
import functools

import jax
import jax.numpy as jnp
from jax import lax
from jax.experimental import pallas as pl
from jax.experimental.pallas import tpu as pltpu
from jax.sharding import PartitionSpec as P

AGG_DEV = 8
LANES = 128
DENSE_LIMIT = 1 << 19

VMEM = pl.BlockSpec(memory_space=pltpu.VMEM)
SMEM = pl.BlockSpec(memory_space=pltpu.SMEM)
HBM = pl.BlockSpec(memory_space=pltpu.HBM)
ANY = pl.BlockSpec(memory_space=pl.ANY)
HIGH = lax.Precision.HIGHEST


def params():
    return pltpu.CompilerParams(vmem_limit_bytes=24 * 1024 * 1024)


def call(kernel, out_shape, in_specs, out_specs, scratch=(), flops=0, moved=0):
    def shaped(shape, spec):
        return pltpu.HBM(shape.shape, shape.dtype) if spec is HBM else shape

    if isinstance(out_shape, (tuple, list)):
        out_shape = [shaped(*pair) for pair in zip(out_shape, out_specs)]
    else:
        out_shape = shaped(out_shape, out_specs)
    run = pl.pallas_call(
        kernel,
        out_shape=out_shape,
        in_specs=in_specs,
        out_specs=out_specs,
        scratch_shapes=list(scratch),
        compiler_params=params(),
        cost_estimate=pl.CostEstimate(flops=flops, bytes_accessed=moved, transcendentals=0),
    )

    def apply(*args):
        pinned = [
            pltpu.with_memory_space_constraint(arg, pltpu.HBM) if spec is HBM else arg
            for arg, spec in zip(args, in_specs)
        ]
        return run(*pinned)

    return apply


def below(value, bound):
    return value & (bound - 1) if bound & (bound - 1) == 0 else lax.rem(value, bound)


def over(value, bound):
    if bound & (bound - 1) == 0:
        return lax.shift_right_logical(value, bound.bit_length() - 1)
    return lax.div(value, bound)


def halves(value):
    high = value.astype(jnp.bfloat16)
    low = (value - high.astype(jnp.float32)).astype(jnp.bfloat16)
    return high, low


def left_operand(value):
    high, low = halves(value)
    return jnp.concatenate([high, low, high], axis=1)


def right_operand(value):
    high, low = halves(value)
    return jnp.concatenate([high, high, low], axis=1)


def dot_nt(left, right):
    return lax.dot_general(
        left, right, (((1,), (1,)), ((), ())), preferred_element_type=jnp.float32
    )


def table_products(value, table_ref, out_ref, done=None):
    left = left_operand(value)
    count, width = table_ref.shape[0], table_ref.shape[1]
    n_rhs = out_ref.shape[1]
    rows = left.shape[0] // n_rhs
    for first in range(0, count, 2):
        last = min(first + 2, count)
        right = right_operand(table_ref[first:last].reshape((last - first) * width, -1))
        product = dot_nt(left, right)
        for t in range(first, last):
            part = product[:, (t - first) * width : (t - first + 1) * width]
            out_ref[t * rows : (t + 1) * rows] = part.reshape(rows, n_rhs, width)
        if done is not None:
            done(first * rows, (last - first) * rows)


def started(copies):
    for copy in copies:
        copy.start()
    return copies


def finish(copies):
    for copy in copies:
        copy.wait()


def request_kernel(sizes, *refs):
    rows, n_rows, cap, n_tiles, n_diag = sizes
    inputs, payload_ref, held, sems = refs[:5], refs[5], refs[6:11], refs[11]
    finish(
        started([pltpu.make_async_copy(i, h, sems.at[n]) for n, (i, h) in enumerate(zip(inputs, held))])
    )
    owner_ref, local_ref, tile_ref, diag_ref, group_ref = held
    width_k = owner_ref.shape[0]
    half = n_rows // 2
    row_of = lax.broadcasted_iota(jnp.int32, (rows, rows), 0)
    col_of = lax.broadcasted_iota(jnp.int32, (rows, rows), 1)
    lane = lax.broadcasted_iota(jnp.int32, (rows, LANES), 1)
    owners = lax.broadcasted_iota(jnp.int32, (n_rows, rows), 0)

    def column(row):
        return jnp.sum(jnp.where(row_of == col_of, row, 0), axis=1, keepdims=True)

    def owner_row(k):
        return owner_ref[k : k + 1, :]

    row_ids = lax.broadcasted_iota(jnp.int32, (1, rows), 1)
    owner_columns = [column(owner_row(k)) for k in range(width_k)]
    lists = jnp.zeros((n_rows, LANES), jnp.float32)
    places, half_places = [], []
    for k in range(width_k):
        rank = jnp.zeros((1, rows), jnp.int32)
        for other in range(k + 1):
            match = owner_columns[other] == owner_row(k)
            if other == k:
                match = match & (row_of < col_of)
            rank = rank + jnp.sum(jnp.where(match, 1, 0), axis=0, keepdims=True)
        places.append(owner_row(k) * cap + rank)
        same = (owner_row(k) >= half) == (lax.axis_index("rows") >= half)
        holder = jnp.where(owner_row(k) >= half, owner_row(k) - half, owner_row(k))
        half_places.append(holder * (2 * cap) + rank + jnp.where(same, 0, cap))
        taker = row_ids + rows * (diag_ref[...] + n_diag)
        code = local_ref[k : k + 1, :] + rows * (tile_ref[k : k + 1, :] + n_tiles * taker)
        code, rank = column(code), column(rank)
        mirror = jnp.where(owner_row(k) >= half, owner_row(k) - half, owner_row(k) + half)
        for owner, base in ((owner_row(k), 0), (mirror, LANES // 2)):
            by_rank = jnp.where(lane == rank + base, code, 0).astype(jnp.float32)
            mine = jnp.where(owners == owner, 1.0, 0.0)
            lists = lists + jnp.dot(
                mine, by_rank, precision=HIGH, preferred_element_type=jnp.float32
            )
    lists = (lists + 0.5).astype(jnp.int32)
    common = [group_ref[...], diag_ref[...]]
    common += [tile_ref[k : k + 1, :] for k in range(width_k + 2)]
    common += [owner_row(k) * rows + local_ref[k : k + 1, :] for k in range(width_k)]
    common += half_places + places
    spare = payload_ref.shape[2] - LANES - len(common) * rows
    if spare:
        common.append(jnp.zeros((1, spare), jnp.int32))
    common = jnp.concatenate(common, axis=1)
    for device in range(n_rows):
        line = jnp.concatenate([lists[device : device + 1, :], common], axis=1)
        for band in range(payload_ref.shape[0] // n_rows):
            payload_ref[band * n_rows + device] = line


def metadata_copies(meta_ref, request_ref, near_ref, sems):
    n_rows, n_near = request_ref.shape[0], near_ref.shape[0]
    band, row = lax.axis_index("band"), lax.axis_index("rows")
    last = meta_ref.shape[0] // n_rows - 1
    if n_near == 1:
        nexts = [last - band]
    else:
        nexts = [jnp.minimum(band + 1, last), jnp.maximum(band - 1, 0)]
    copies = [
        pltpu.make_async_copy(meta_ref.at[pl.ds(band * n_rows, n_rows)], request_ref, sems.at[0])
    ]
    for n, other in enumerate(nexts):
        source = meta_ref.at[pl.ds(other * n_rows + row, 1)]
        copies.append(pltpu.make_async_copy(source, near_ref.at[pl.ds(n, 1)], sems.at[1 + n]))
    return copies


def band_field(rows, width_k, way, n_ways):
    field = LANES + (2 + width_k) * rows
    if n_ways == 1:
        return field + jnp.where(lax.axis_index("band") == 0, 0, rows)
    return field + way * rows


def pack_bands(sizes, width_k, product_ref, near_ref, band_refs):
    rows = sizes[0]
    for way, band_ref in enumerate(band_refs):
        field = band_field(rows, width_k, way, len(band_refs))
        for row in range(rows):
            band_ref[row] = product_ref[near_ref[way, 0, field + row] * rows + row]


def product_kernel(start_ref, mirror_ref, tile_ref, product_out, product_ref, sems):
    copies = []
    for side, ref in enumerate((start_ref, mirror_ref)):
        held = product_ref.at[side]

        def done(first, count):
            place = pl.ds(first, count)
            copy = pltpu.make_async_copy(
                held.at[place], product_out.at[side, place], sems.at[len(copies)]
            )
            copies.extend(started([copy]))

        rows, n_rhs, states = ref.shape
        table_products(ref[...].reshape(rows * n_rhs, states), tile_ref, held, done)
    finish(copies)


def first_kernel(sizes, width_k, n_band, *refs):
    rows, n_rows, cap, n_tiles, n_rhs = sizes
    product_ref, meta_ref, send_out = refs[:3]
    band_out, refs = refs[3 : 3 + n_band], refs[3 + n_band :]
    request_ref, near_ref, meta_sems, send_sems = refs
    finish(started(metadata_copies(meta_ref, request_ref, near_ref, meta_sems)))
    half = n_rows // 2
    base = jnp.where(lax.axis_index("rows") >= half, half, 0)
    for device in range(half):
        for slot in range(2 * cap):
            side, rank = slot // cap, slot % cap
            code = request_ref[base + device, 0, side * (LANES // 2) + rank]
            pltpu.make_async_copy(
                product_ref.at[side, below(code, rows * n_tiles)],
                send_out.at[device, slot],
                send_sems.at[0],
            ).start()
    for way, out in enumerate(band_out):
        field = band_field(rows, width_k, way, n_band)
        for row in range(rows):
            block = near_ref[way, 0, field + row] * rows + row
            pltpu.make_async_copy(
                product_ref.at[0, block], out.at[row], send_sems.at[1 + way]
            ).start()
    for n, out in enumerate((send_out, *band_out)):
        pltpu.make_async_copy(out, out, send_sems.at[n]).wait()


def place(place_ref, values, n_rhs):
    per_tile = LANES // n_rhs
    length = place_ref.shape[0] // per_tile
    parts, rest = [], values
    for _ in range(3):
        part = rest.astype(jnp.bfloat16)
        rest = rest - part.astype(jnp.float32)
        parts.append(part)
    parts = jnp.concatenate(parts, axis=1)
    lane = lax.broadcasted_iota(jnp.int32, (length, LANES), 1)
    result = jnp.zeros((length, LANES), jnp.float32)
    for spot in range(per_tile):
        chosen = jnp.dot(
            place_ref[spot * length : (spot + 1) * length, :],
            parts,
            preferred_element_type=jnp.float32,
        )
        chosen = chosen[:, :LANES] + chosen[:, LANES : 2 * LANES] + chosen[:, 2 * LANES :]
        result = jnp.where((lane >= spot * n_rhs) & (lane < (spot + 1) * n_rhs), chosen, result)
    return result


def one_hot(ids, row):
    return jnp.where(ids == row, 1.0, 0.0).astype(jnp.bfloat16)


def count_kernel(sizes, width_k, n_func, *refs):
    rows, n_rows, cap, n_tiles, n_rhs = sizes
    field_ref, list_ref, tile_ref, table_ref, inverse_ref = refs[:5]
    count_out, functional_out, placing_out, scale_ref = refs[5:9]
    count_ref, functional_ref, placing_ref, sems = refs[9:]
    n_groups, n_blocks = count_ref.shape[1:]
    slots, band_rows = n_rows * cap, n_rows * rows
    copies = []

    def send(source, target):
        copies.extend(started([pltpu.make_async_copy(source, target, sems.at[len(copies)])]))

    sums = jnp.sum(tile_ref[...], axis=1)
    line = lax.broadcasted_iota(jnp.int32, (n_func, sums.shape[1]), 0)
    sums = jnp.concatenate([sums, jnp.zeros((n_func - n_tiles, sums.shape[1]), jnp.float32)], axis=0)
    n_diag = inverse_ref.shape[0]
    totals = []
    for d in range(n_diag):
        minus = -jnp.sum(table_ref[d], axis=0, keepdims=True)
        totals.append(-jnp.sum(minus, axis=1, keepdims=True))
        wanted = jnp.where(line == n_tiles, minus, sums)
        high, low = halves(inverse_ref[d])
        right = jnp.concatenate([high, high, low], axis=0)
        solved = jnp.dot(left_operand(wanted), right, preferred_element_type=jnp.float32)
        solved = jnp.where(line == n_tiles + 1, 1.0, solved)
        functional_ref[d * n_func : (d + 1) * n_func, :] = left_operand(solved)
    send(functional_ref, functional_out)

    lists = list_ref[...]
    asker = lax.broadcasted_iota(jnp.int32, lists.shape, 0)
    codes = asker * rows + below(over(lists, rows * n_tiles), rows)
    codes = jnp.where(lists > 0, codes, -1).astype(jnp.float32)
    spread = lax.broadcasted_iota(jnp.int32, (slots, n_rows), 0)
    spread = lax.div(spread, cap) == lax.broadcasted_iota(jnp.int32, (slots, n_rows), 1)
    codes = jnp.dot(
        jnp.where(spread, 1.0, 0.0), codes, precision=HIGH, preferred_element_type=jnp.float32
    )
    rank = lax.rem(lax.broadcasted_iota(jnp.int32, codes.shape, 0), cap)
    lane = lax.broadcasted_iota(jnp.int32, codes.shape, 1)
    asked = jnp.sum(jnp.where(rank == lane, codes, 0.0), axis=1, keepdims=True)
    asked = jnp.where(asked < 0.0, asked - 0.5, asked + 0.5).astype(jnp.int32)
    own = lax.axis_index("rows") * rows + lax.broadcasted_iota(jnp.int32, (rows, 1), 0)
    band = lax.axis_index("band")

    def field(n, which):
        return field_ref[n, pl.ds(which, 1), :]

    row_ids = lax.broadcasted_iota(jnp.int32, (1, band_rows), 1)
    sides = []
    for which, targets in ((band, jnp.concatenate([asked, own], axis=0)), (1 - band, own)):
        across = jnp.where(which == 0, field(2 + width_k, 1), field(3 + width_k, 0))
        takers = [field(2 + k, which) * n_groups + field(0, which) for k in range(width_k)]
        takers.append(across * n_groups + field(0, 1 - which))
        takers = jnp.concatenate(takers, axis=1)
        origins = [field(4 + width_k + k, which) for k in range(width_k)] + [row_ids]
        hits = one_hot(targets, jnp.concatenate(origins, axis=1))
        sides.append((takers, hits, field(0, which)))
    for t in range(n_tiles):
        found = []
        for takers, hits, _ in sides:
            ids = lax.broadcasted_iota(jnp.int32, (n_groups, takers.shape[1]), 0) + t * n_groups
            found.append(dot_nt(one_hot(ids, takers), hits))
        count_ref[t] = jnp.concatenate(found, axis=1).astype(jnp.bfloat16)
        send(count_ref.at[t], count_out.at[t])
    ids = lax.broadcasted_iota(jnp.int32, (n_groups, band_rows), 0)
    found = [dot_nt(one_hot(ids, groups), hits[:, -band_rows:]) for _, hits, groups in sides]
    found = jnp.concatenate(found, axis=1)
    count_ref[n_tiles] = found.astype(jnp.bfloat16)
    send(count_ref.at[n_tiles], count_out.at[n_tiles])
    block = lax.broadcasted_iota(jnp.int32, found.shape, 1)
    mine = (block >= slots) & (block < slots + rows)
    count_ref[n_tiles + 1] = jnp.where(mine, found, 0.0).astype(jnp.bfloat16)
    send(count_ref.at[n_tiles + 1], count_out.at[n_tiles + 1])

    per_tile = LANES // n_rhs
    depth = rows // per_tile
    length = n_rows * 2 * depth
    order = lax.broadcasted_iota(jnp.int32, (per_tile * length, 1), 0)
    spot, order = lax.div(order, length), lax.rem(order, length)
    device, order = lax.div(order, 2 * depth), lax.rem(order, 2 * depth)
    side, order = lax.div(order, depth), lax.rem(order, depth)
    order = side * band_rows + device * rows + spot * depth + order
    member = [one_hot(ids, field(0, which)) for which in range(2)]
    placing = jnp.zeros(placing_ref.shape, jnp.float32)
    for which in range(2):
        placing = placing + dot_nt(one_hot(order, row_ids + which * band_rows), member[which])
    placing_ref[...] = placing.astype(jnp.bfloat16)
    send(placing_ref, placing_out)
    whole = jnp.zeros((n_groups, 1), jnp.float32)
    for which in range(2):
        sums = jnp.zeros((1, band_rows), jnp.float32)
        for d in range(n_diag):
            sums = jnp.where(field(1, which) == d, totals[d], sums)
        weighted = jnp.where(ids == field(0, which), sums, 0.0)
        whole = whole + jnp.sum(weighted, axis=1, keepdims=True)
    scale = place(placing_ref, jnp.broadcast_to(whole, (n_groups, LANES)), n_rhs)
    mine = jnp.zeros(scale_ref.shape, jnp.float32)
    here = lax.axis_index("rows") * 2 + band
    for n in range(2 * n_rows):
        mine = jnp.where(here == n, scale[n * depth : (n + 1) * depth, :], mine)
    scale_ref[...] = mine
    finish(copies)


def gather_solve(
    sizes, slots, diags, arrived_ref, later, terms, inverse_ref, sum_ref, product_ref
):
    rows, n_rows, cap, n_tiles, n_rhs = sizes
    per = n_rows * cap // arrived_ref.shape[0]
    for row in range(rows):
        total = None
        for slot in slots(row):
            start = pl.multiple_of(below(slot, per) * n_rhs, n_rhs)
            block = arrived_ref[over(slot, per), pl.ds(start, n_rhs), :]
            total = block if total is None else total + block
        sum_ref[pl.ds(row * n_rhs, n_rhs), :] = total
    finish(later)
    total = sum_ref[...]
    for term in terms:
        total = total + term[...].reshape(total.shape)
    table_products(total, inverse_ref, product_ref)
    for row in range(rows):
        sum_ref[pl.ds(row * n_rhs, n_rhs), :] = product_ref[diags(row) * rows + row]


def middle_kernel(sizes, width_k, n_band, dense, *refs):
    meta_ref, arrived_ref, inverse_ref, tile_ref = refs[:4]
    terms_in, refs = refs[4 : 5 + n_band], refs[5 + n_band :]
    extra, refs = (refs[:3], refs[3:]) if dense else ((), refs)
    send_out, band_out, refs = refs[0], refs[1 : 1 + n_band], refs[1 + n_band :]
    sum_ref, product_ref, request_ref, near_ref, send_ref = refs[:5]
    terms, band_refs, refs = refs[5 : 6 + n_band], refs[6 + n_band : 6 + 2 * n_band], refs[6 + 2 * n_band :]
    term_sems, meta_sems, send_sems, refs = *refs[:3], refs[3:]
    right_ref = terms[0]
    rows, n_rows, cap, n_tiles, n_rhs = sizes
    body = cap * n_rhs
    metadata = started(metadata_copies(meta_ref, request_ref, near_ref, meta_sems))
    pairs = enumerate(zip(terms_in, terms))
    later = started([pltpu.make_async_copy(i, h, term_sems.at[n]) for n, (i, h) in pairs])
    fetched = []
    if dense:
        held, extra_sems, value_ref, spread_ref = refs[:3], refs[3], refs[4], refs[5]
        n_diag = inverse_ref.shape[0]
        pairs = enumerate(zip(extra, held))
        fetched = started([pltpu.make_async_copy(i, h, extra_sems.at[n]) for n, (i, h) in pairs])
    finish(metadata)
    mine = lax.axis_index("rows")

    def slots(row):
        field = LANES + (4 + 2 * width_k) * rows + row
        return [request_ref[mine, 0, field + k * rows] for k in range(width_k)]

    def diags(row):
        return request_ref[mine, 0, LANES + rows + row]

    gather_solve(sizes, slots, diags, arrived_ref, later, terms, inverse_ref, sum_ref, product_ref)
    table_products(sum_ref[...], tile_ref, product_ref)
    copies = []

    def send(source, target):
        copies.extend(started([pltpu.make_async_copy(source, target, send_sems.at[len(copies)])]))

    for owner in range(n_rows):
        for rank in range(cap):
            block = product_ref[below(request_ref[owner, 0, rank], rows * n_tiles)]
            send_ref[owner, rank * n_rhs : (rank + 1) * n_rhs, :] = block
        if not dense:
            send(send_ref.at[owner], send_out.at[owner])
        else:
            send(send_ref.at[owner, pl.ds(0, body)], send_out.at[owner, pl.ds(0, body)])
    pack_bands(sizes, width_k, product_ref, near_ref, band_refs)
    for ref, out in zip(band_refs, band_out):
        send(ref, out)
    if dense:
        finish(fetched)
        kinds = []
        for owner in range(n_rows):
            for rank in range(cap):
                code = over(request_ref[owner, 0, rank], rows * n_tiles * rows)
                kinds.append(below(code, n_diag))
        kinds += [diags(row) for row in range(rows)]
        kinds += [near_ref[0, 0, LANES + rows + row] for row in range(rows)]
        result = coarse_parts(
            sizes, kinds, held, right_ref, send_ref, band_refs, value_ref, spread_ref
        )
        depth = result.shape[0] // n_rows
        for owner in range(n_rows):
            send_ref[owner, body:, :] = result[owner * depth : (owner + 1) * depth, :]
        send(send_ref.at[:, pl.ds(body, depth)], send_out.at[:, pl.ds(body, depth)])
    finish(copies)


def coarse_parts(sizes, kinds, held, right_ref, send_ref, band_refs, value_ref, spread_ref):
    functional_ref, count_ref, place_ref = held
    rows, n_rows, cap, n_tiles, n_rhs = sizes
    body = cap * n_rhs
    n_func = spread_ref.shape[0] // count_ref.shape[2]
    per_tile = LANES // n_rhs
    functional = functional_ref[...]
    done = 0
    for owner in range(0, n_rows, 2):
        values = [send_ref[owner + more, :body, :] for more in range(2)]
        values = jnp.concatenate(values, axis=0)
        value_ref[:, done : done + 2 * body] = dot_nt(functional, right_operand(values))
        done += 2 * body
    for ref in (right_ref, *band_refs):
        values = ref[...].reshape(rows * n_rhs, -1)
        value_ref[:, done : done + rows * n_rhs] = dot_nt(functional, right_operand(values))
        done += rows * n_rhs
    lane = lax.broadcasted_iota(jnp.int32, (n_func, LANES), 1)
    for block, kind in enumerate(kinds):
        tile, spot = block // per_tile, block % per_tile
        start = pl.multiple_of(kind * n_func, n_func)
        piece = value_ref[pl.ds(start, n_func), tile * LANES : (tile + 1) * LANES]
        piece = jnp.where((lane >= spot * n_rhs) & (lane < (spot + 1) * n_rhs), piece, 0.0)
        spread_ref[block * n_func : (block + 1) * n_func, :] = piece
    partial = jnp.zeros((count_ref.shape[1], 2 * LANES), jnp.float32)
    for t in range(count_ref.shape[0]):
        values = spread_ref[pl.ds(t, done // n_rhs, stride=n_func), :]
        partial = partial + jnp.dot(
            count_ref[t],
            jnp.concatenate(halves(values), axis=1),
            preferred_element_type=jnp.float32,
        )
    partial = partial[:, :LANES] + partial[:, LANES:]
    source = lax.broadcasted_iota(jnp.int32, (LANES, LANES), 0)
    target = lax.broadcasted_iota(jnp.int32, (LANES, LANES), 1)
    same = jnp.where(lax.rem(source, n_rhs) == lax.rem(target, n_rhs), 1.0, 0.0)
    same = same.astype(jnp.bfloat16)
    same = jnp.concatenate([same, same], axis=0)
    partial = jnp.dot(
        jnp.concatenate(halves(partial), axis=1), same, preferred_element_type=jnp.float32
    )
    return place(place_ref, partial, n_rhs)


def part_kernel(arrived_ref, mine_ref, other_ref):
    depth = mine_ref.shape[0]
    body = arrived_ref.shape[1] - 2 * depth
    total = arrived_ref[0, body:, :]
    for source in range(1, arrived_ref.shape[0]):
        total = total + arrived_ref[source, body:, :]
    upper = lax.axis_index("band") == 0
    mine_ref[...] = jnp.where(upper, total[:depth], total[depth:])
    other_ref[...] = jnp.where(upper, total[depth:], total[:depth])


def last_kernel(sizes, width_k, n_band, *refs):
    meta_ref, arrived_ref, inverse_ref = refs[:3]
    terms_in, refs = refs[3 : 4 + n_band], refs[4 + n_band :]
    second_ref, sum_ref, product_ref, mine_ref = refs[:4]
    terms, (term_sems, meta_sem) = refs[4 : 5 + n_band], refs[5 + n_band :]
    rows, n_rows = sizes[:2]
    place = lax.axis_index("band") * n_rows + lax.axis_index("rows")
    metadata = pltpu.make_async_copy(meta_ref.at[pl.ds(place, 1)], mine_ref, meta_sem)
    metadata.start()
    pairs = enumerate(zip(terms_in, terms))
    later = started([pltpu.make_async_copy(i, h, term_sems.at[n]) for n, (i, h) in pairs])
    metadata.wait()

    def slots(row):
        field = LANES + (4 + 3 * width_k) * rows + row
        return [mine_ref[0, 0, field + k * rows] for k in range(width_k)]

    def diags(row):
        return mine_ref[0, 0, LANES + rows + row]

    gather_solve(sizes, slots, diags, arrived_ref, later, terms, inverse_ref, sum_ref, product_ref)
    second_ref[...] = sum_ref[...].reshape(second_ref.shape)


def final_kernel(sizes, mine_ref, other_ref, scale_ref, second_ref, out_ref):
    rows, n_rhs = sizes[0], sizes[4]
    depth = scale_ref.shape[0]
    correction = (mine_ref[...] + other_ref[...]) / scale_ref[...]
    padded = jnp.concatenate([correction, jnp.zeros((8 - depth, LANES), jnp.float32)], axis=0)
    turned = padded.T
    for row in range(rows):
        spot, place = row // depth, row % depth
        column = turned[spot * n_rhs : (spot + 1) * n_rhs, place : place + 1]
        out_ref[row] = second_ref[row] + column


def shifted(value, axis, steps):
    count = lax.axis_size(axis)
    initial, last = (max(0, -steps), min(count, count - steps))
    return lax.ppermute(value, axis, [(source, source + steps) for source in range(initial, last)])


def to_bands(sends):
    if len(sends) == 1:
        return (lax.ppermute(sends[0], "band", [(0, 1), (1, 0)]),)
    return shifted(sends[0], "band", 1), shifted(sends[1], "band", -1)


def on_device(
    start_iterate,
    right_side,
    diag_table,
    inverse_table,
    coupling_tiles,
    diag_index,
    tile_index,
    source_owner,
    source_local,
    aggregate_map,
):
    rows, n_rhs, states = start_iterate.shape
    width_k = source_owner.shape[1]
    n_tiles, n_diag = coupling_tiles.shape[0], inverse_table.shape[0]
    n_rows, n_bands = lax.axis_size("rows"), lax.axis_size("band")
    n_dev = n_rows * n_bands
    cap = max(2, 2 * width_k * rows // n_rows)
    slots = n_rows * cap
    total_groups = AGG_DEV * n_dev
    per_tile = LANES // n_rhs
    depth = rows // per_tile
    n_func = 16
    dense = (
        n_bands == 2
        and n_dev * rows * total_groups <= DENSE_LIMIT
        and depth == 4
        and n_diag * n_func == LANES
        and n_tiles + 2 <= n_func
    )
    sizes = (rows, n_rows, cap, n_tiles, n_rhs)
    f32, i32 = jnp.float32, jnp.int32
    my_band = lax.axis_index("band")
    my_row = lax.axis_index("rows")

    half = n_rows // 2
    mirror = lax.ppermute(start_iterate, "rows", [(i, (i + half) % n_rows) for i in range(n_rows)])
    wide = LANES + -(-(4 + 4 * width_k) * rows // LANES) * LANES
    index_shapes = [(width_k, rows), (width_k, rows), (width_k + 2, rows), (1, rows), (1, rows)]
    payload = call(
        functools.partial(request_kernel, (rows, n_rows, cap, n_tiles, n_diag)),
        jax.ShapeDtypeStruct((n_dev, 1, wide), i32),
        [HBM] * 5,
        VMEM,
        [*[pltpu.VMEM(shape, i32) for shape in index_shapes], pltpu.SemaphoreType.DMA((5,))],
    )(source_owner.T, source_local.T, tile_index.T, diag_index[None], aggregate_map.T)
    meta = lax.all_to_all(payload, ("band", "rows"), split_axis=0, concat_axis=0, tiled=True)

    n_ways = 1 if n_bands == 2 else 2
    block = (rows, n_rhs, states)
    band_shapes = [jax.ShapeDtypeStruct(block, f32)] * n_ways
    band_scratch = [pltpu.VMEM(block, f32)] * n_ways
    term_scratch = [pltpu.VMEM(block, f32)] * (1 + n_ways)
    term_sems = pltpu.SemaphoreType.DMA((1 + n_ways,))
    meta_scratch = [pltpu.SMEM((n_rows, 1, wide), i32), pltpu.SMEM((n_ways, 1, wide), i32)]
    meta_sems = pltpu.SemaphoreType.DMA((1 + n_ways,))
    flat = rows * n_rhs
    sums = pltpu.VMEM((flat, states), f32)
    products = pltpu.VMEM((max(n_tiles, n_diag) * rows, n_rhs, states), f32)
    work = 6 * flat * states * states
    made_shape = (2, n_tiles * rows, n_rhs, states)
    made = call(
        product_kernel,
        jax.ShapeDtypeStruct(made_shape, f32),
        [VMEM] * 3,
        HBM,
        [pltpu.VMEM(made_shape, f32), pltpu.SemaphoreType.DMA((2 * n_tiles,))],
        2 * work * n_tiles,
        4 << 20,
    )(start_iterate, mirror, coupling_tiles)
    packed, *bands = call(
        functools.partial(first_kernel, sizes, width_k, n_ways),
        (jax.ShapeDtypeStruct((half, 2 * cap, n_rhs, states), f32), *band_shapes),
        [HBM, ANY],
        [HBM] * (1 + n_ways),
        [*meta_scratch, meta_sems, pltpu.SemaphoreType.DMA((1 + n_ways,))],
        0,
        4 << 20,
    )(made, meta)
    sends = (packed.reshape(half, 2 * cap * n_rhs, states), *bands)
    halves_of_rows = [list(range(half)), list(range(half, n_rows))]
    late, *sends = lax.optimization_barrier((meta, *sends))

    def exchange(sends, groups=None):
        arrived = lax.all_to_all(
            sends[0], "rows", split_axis=0, concat_axis=0, tiled=True, axis_index_groups=groups
        )
        return arrived, to_bands(sends[1:])

    arrived_blocks, arrived_bands = exchange(sends, halves_of_rows)

    late = late.reshape(n_bands, n_rows, wide)
    requests = lax.dynamic_index_in_dim(late[:, :, :LANES], my_band, 0, keepdims=False)
    common = late[:, :, LANES:]
    extra, extra_scratch, tail = (), [], 0
    if dense:
        fields = common[:, :, : (4 + 2 * width_k) * rows].reshape(n_bands, n_rows, -1, rows).transpose(2, 0, 1, 3)
        fields = fields.reshape(-1, n_bands, n_rows * rows)
        n_blocks = slots + 2 * rows
        length = n_dev * depth
        extra_shapes = [
            ((n_diag * n_func, 3 * states), jnp.bfloat16),
            ((n_tiles + 2, total_groups, n_blocks), jnp.bfloat16),
            ((per_tile * length, total_groups), jnp.bfloat16),
        ]
        functional_shape, count_shape, placing_shape = extra_shapes
        counts, functionals, placing, scale = call(
            functools.partial(count_kernel, sizes, width_k, n_func),
            (
                jax.ShapeDtypeStruct(*count_shape),
                jax.ShapeDtypeStruct(*functional_shape),
                jax.ShapeDtypeStruct(*placing_shape),
                jax.ShapeDtypeStruct((depth, LANES), f32),
            ),
            [VMEM] * 5,
            [HBM, HBM, HBM, VMEM],
            [
                pltpu.VMEM(*count_shape),
                pltpu.VMEM(*functional_shape),
                pltpu.VMEM(*placing_shape),
                pltpu.SemaphoreType.DMA((n_tiles + 4,)),
            ],
            4 * total_groups * n_tiles * n_dev * rows * n_blocks,
            4 << 20,
        )(fields, requests, coupling_tiles, diag_table, inverse_table)
        extra = (functionals, counts, placing)
        extra_scratch = [
            *[pltpu.VMEM(*shape) for shape in extra_shapes],
            pltpu.SemaphoreType.DMA((3,)),
            pltpu.VMEM((n_diag * n_func, n_blocks * n_rhs), f32),
            pltpu.VMEM((n_blocks * n_func, LANES), f32),
        ]
        tail = n_bands * depth

    send_shape = (n_rows, cap * n_rhs + tail, states)
    sends = call(
        functools.partial(middle_kernel, sizes, width_k, n_ways, dense),
        (jax.ShapeDtypeStruct(send_shape, f32), *band_shapes),
        [HBM] + [VMEM] * 3 + [HBM] + [ANY] * n_ways + [HBM] * len(extra),
        [HBM] * (1 + n_ways),
        [
            sums,
            products,
            *meta_scratch,
            pltpu.VMEM(send_shape, f32),
            *term_scratch,
            *band_scratch,
            term_sems,
            meta_sems,
            pltpu.SemaphoreType.DMA((n_rows + n_ways + 1,)),
            *extra_scratch,
        ],
        work * (n_tiles + n_diag),
        4 << 20,
    )(
        meta,
        arrived_blocks,
        inverse_table,
        coupling_tiles,
        right_side,
        *arrived_bands,
        *extra,
    )
    arrived_blocks, arrived_bands = exchange(sends)

    if dense:
        part = jax.ShapeDtypeStruct((depth, LANES), f32)
        mine, other = call(part_kernel, (part, part), [VMEM], [VMEM] * 2)(arrived_blocks)
        other = lax.ppermute(other, "band", [(0, 1), (1, 0)])
    second = call(
        functools.partial(last_kernel, sizes, width_k, n_ways),
        jax.ShapeDtypeStruct(block, f32),
        [HBM] + [VMEM] * 2 + [HBM] + [ANY] * n_ways,
        VMEM,
        [
            sums,
            products,
            pltpu.SMEM((1, 1, wide), i32),
            *term_scratch,
            term_sems,
            pltpu.SemaphoreType.DMA,
        ],
        work * n_diag,
        4 << 20,
    )(meta, arrived_blocks, inverse_table, right_side, *arrived_bands)
    if dense:
        return call(
            functools.partial(final_kernel, sizes),
            jax.ShapeDtypeStruct(block, f32),
            [VMEM] * 4,
            VMEM,
        )(mine, other, scale, second)

    groups = aggregate_map[:, 0]
    own = jnp.arange(rows, dtype=i32)
    groups_all = common[:, :, :rows]
    diags_all = common[:, :, rows : 2 * rows]
    codes = requests[:, :cap]
    asked = lax.broadcasted_iota(i32, codes.shape, 0) * rows + codes // (rows * n_tiles) % rows
    asked = jnp.where(codes > 0, asked, -1).reshape(-1)
    table_sums = jnp.sum(diag_table, axis=(1, 2))
    diag_onehot = diags_all.reshape(-1, 1) == jnp.arange(n_diag, dtype=i32)[None]
    block_sums = jnp.sum(jnp.where(diag_onehot, table_sums[None], 0.0), axis=1)
    whole_diag = jnp.sum(
        jnp.where(groups[:, None] == groups_all.reshape(-1)[None], block_sums[None], 0.0), axis=1
    )
    here = lax.dynamic_index_in_dim(common, my_row, 1, keepdims=False)
    above = lax.dynamic_index_in_dim(here, jnp.minimum(my_band + 1, n_bands - 1), 0, keepdims=False)
    below = lax.dynamic_index_in_dim(here, jnp.maximum(my_band - 1, 0), 0, keepdims=False)
    place_of = (2 + width_k) * rows
    band_tiles = jnp.stack([above[place_of : place_of + rows], below[place_of + rows : place_of + 2 * rows]])
    band_groups = jnp.stack([above[:rows], below[:rows]])
    band_valid = jnp.stack([my_band + 1 < n_bands, my_band > 0])
    band_valid = jnp.broadcast_to(band_valid[:, None], (2, rows))
    n_all = n_tiles + n_diag + 1
    code = codes.reshape(-1)
    band_of_mine = lax.dynamic_index_in_dim(groups_all, my_band, 0, keepdims=False).reshape(-1)
    entry_group = jnp.concatenate(
        [jnp.take(band_of_mine, jnp.maximum(asked, 0)), band_groups.reshape(-1), groups, groups]
    )
    entry_func = jnp.concatenate(
        [
            (code % rows) * n_all + (code // rows) % n_tiles,
            (own[None] * n_all + band_tiles).reshape(-1),
            own * n_all + n_tiles + diag_index,
            own * n_all + n_tiles + n_diag,
        ]
    )
    entry_valid = jnp.concatenate([asked >= 0, band_valid.reshape(-1), jnp.ones((2 * rows,), bool)])
    functionals = jnp.concatenate(
        [jnp.sum(coupling_tiles, axis=1), -jnp.sum(diag_table, axis=1)], axis=0
    )
    weights = jnp.einsum("fp,rcp->rfc", functionals, second, precision=HIGH)
    weights = jnp.concatenate([weights, jnp.sum(right_side, axis=2)[:, None]], axis=1)
    chosen = jnp.take(weights.reshape(rows * n_all, n_rhs), entry_func, axis=0)
    chosen = jnp.where(entry_valid[:, None], chosen, 0.0)
    partial = jax.ops.segment_sum(chosen, entry_group, num_segments=total_groups)
    whole = lax.psum(partial, ("band", "rows"))
    correction = jnp.take(whole, groups, axis=0) / whole_diag[:, None]
    return second + correction[:, :, None]


def solution(mesh):
    in_specs = (
        P(("band", "rows"), None, None),
        P(("band", "rows"), None, None),
        P(),
        P(),
        P(),
        P(("band", "rows")),
        P(("band", "rows"), None),
        P(("band", "rows"), None),
        P(("band", "rows"), None),
        P(("band", "rows"), None),
    )
    out_specs = P(("band", "rows"), None, None)
    return jax.shard_map(
        on_device, mesh=mesh, in_specs=in_specs, out_specs=out_specs, check_vma=False
    )
```

```python
import functools

import jax
import jax.numpy as jnp
from jax import lax
from jax.experimental import pallas as pl
from jax.experimental.pallas import tpu as pltpu
from jax.sharding import PartitionSpec as P

AGG_DEV = 8
LANES = 128
DENSE_LIMIT = 1 << 19

VMEM = pl.BlockSpec(memory_space=pltpu.VMEM)
SMEM = pl.BlockSpec(memory_space=pltpu.SMEM)
HBM = pl.BlockSpec(memory_space=pltpu.HBM)
ANY = pl.BlockSpec(memory_space=pl.ANY)
HIGH = lax.Precision.HIGHEST


def params():
    return pltpu.CompilerParams(vmem_limit_bytes=24 * 1024 * 1024)


def call(kernel, out_shape, in_specs, out_specs, scratch=(), flops=0, moved=0):
    def shaped(shape, spec):
        return pltpu.HBM(shape.shape, shape.dtype) if spec is HBM else shape

    if isinstance(out_shape, (tuple, list)):
        out_shape = [shaped(*pair) for pair in zip(out_shape, out_specs)]
    else:
        out_shape = shaped(out_shape, out_specs)
    run = pl.pallas_call(
        kernel,
        out_shape=out_shape,
        in_specs=in_specs,
        out_specs=out_specs,
        scratch_shapes=list(scratch),
        compiler_params=params(),
        cost_estimate=pl.CostEstimate(flops=flops, bytes_accessed=moved, transcendentals=0),
    )

    def apply(*args):
        pinned = [
            pltpu.with_memory_space_constraint(arg, pltpu.HBM) if spec is HBM else arg
            for arg, spec in zip(args, in_specs)
        ]
        return run(*pinned)

    return apply


def below(value, bound):
    return value & (bound - 1) if bound & (bound - 1) == 0 else lax.rem(value, bound)


def over(value, bound):
    if bound & (bound - 1) == 0:
        return lax.shift_right_logical(value, bound.bit_length() - 1)
    return lax.div(value, bound)


def halves(value):
    high = value.astype(jnp.bfloat16)
    low = (value - high.astype(jnp.float32)).astype(jnp.bfloat16)
    return high, low


def left_operand(value):
    high, low = halves(value)
    return jnp.concatenate([high, low, high], axis=1)


def right_operand(value):
    high, low = halves(value)
    return jnp.concatenate([high, high, low], axis=1)


def dot_nt(left, right):
    return lax.dot_general(
        left, right, (((1,), (1,)), ((), ())), preferred_element_type=jnp.float32
    )


def table_products(value, table_ref, out_ref, done=None):
    left = left_operand(value)
    count, width = table_ref.shape[0], table_ref.shape[1]
    n_rhs = out_ref.shape[1]
    rows = left.shape[0] // n_rhs
    for first in range(0, count, 2):
        last = min(first + 2, count)
        right = right_operand(table_ref[first:last].reshape((last - first) * width, -1))
        product = dot_nt(left, right)
        for t in range(first, last):
            part = product[:, (t - first) * width : (t - first + 1) * width]
            out_ref[t * rows : (t + 1) * rows] = part.reshape(rows, n_rhs, width)
        if done is not None:
            done(first * rows, (last - first) * rows)


def started(copies):
    for copy in copies:
        copy.start()
    return copies


def finish(copies):
    for copy in copies:
        copy.wait()


def request_kernel(sizes, *refs):
    rows, n_rows, cap, n_tiles, n_diag = sizes
    inputs, payload_ref, held, sems = refs[:5], refs[5], refs[6:11], refs[11]
    finish(
        started([pltpu.make_async_copy(i, h, sems.at[n]) for n, (i, h) in enumerate(zip(inputs, held))])
    )
    owner_ref, local_ref, tile_ref, diag_ref, group_ref = held
    width_k = owner_ref.shape[0]
    half = n_rows // 2
    row_of = lax.broadcasted_iota(jnp.int32, (rows, rows), 0)
    col_of = lax.broadcasted_iota(jnp.int32, (rows, rows), 1)
    lane = lax.broadcasted_iota(jnp.int32, (rows, LANES), 1)
    owners = lax.broadcasted_iota(jnp.int32, (n_rows, rows), 0)

    def column(row):
        return jnp.sum(jnp.where(row_of == col_of, row, 0), axis=1, keepdims=True)

    def owner_row(k):
        return owner_ref[k : k + 1, :]

    row_ids = lax.broadcasted_iota(jnp.int32, (1, rows), 1)
    owner_columns = [column(owner_row(k)) for k in range(width_k)]
    lists = jnp.zeros((n_rows, LANES), jnp.float32)
    places, half_places = [], []
    for k in range(width_k):
        rank = jnp.zeros((1, rows), jnp.int32)
        for other in range(k + 1):
            match = owner_columns[other] == owner_row(k)
            if other == k:
                match = match & (row_of < col_of)
            rank = rank + jnp.sum(jnp.where(match, 1, 0), axis=0, keepdims=True)
        places.append(owner_row(k) * cap + rank)
        same = (owner_row(k) >= half) == (lax.axis_index("rows") >= half)
        holder = jnp.where(owner_row(k) >= half, owner_row(k) - half, owner_row(k))
        half_places.append(holder * (2 * cap) + rank + jnp.where(same, 0, cap))
        taker = row_ids + rows * (diag_ref[...] + n_diag)
        code = local_ref[k : k + 1, :] + rows * (tile_ref[k : k + 1, :] + n_tiles * taker)
        code, rank = column(code), column(rank)
        mirror = jnp.where(owner_row(k) >= half, owner_row(k) - half, owner_row(k) + half)
        for owner, base in ((owner_row(k), 0), (mirror, LANES // 2)):
            by_rank = jnp.where(lane == rank + base, code, 0).astype(jnp.float32)
            mine = jnp.where(owners == owner, 1.0, 0.0)
            lists = lists + jnp.dot(
                mine, by_rank, precision=HIGH, preferred_element_type=jnp.float32
            )
    lists = (lists + 0.5).astype(jnp.int32)
    common = [group_ref[...], diag_ref[...]]
    common += [tile_ref[k : k + 1, :] for k in range(width_k + 2)]
    common += [owner_row(k) * rows + local_ref[k : k + 1, :] for k in range(width_k)]
    common += half_places + places
    spare = payload_ref.shape[2] - LANES - len(common) * rows
    if spare:
        common.append(jnp.zeros((1, spare), jnp.int32))
    common = jnp.concatenate(common, axis=1)
    for device in range(n_rows):
        line = jnp.concatenate([lists[device : device + 1, :], common], axis=1)
        for band in range(payload_ref.shape[0] // n_rows):
            payload_ref[band * n_rows + device] = line


def metadata_copies(meta_ref, request_ref, near_ref, sems):
    n_rows, n_near = request_ref.shape[0], near_ref.shape[0]
    band, row = lax.axis_index("band"), lax.axis_index("rows")
    last = meta_ref.shape[0] // n_rows - 1
    if n_near == 1:
        nexts = [last - band]
    else:
        nexts = [jnp.minimum(band + 1, last), jnp.maximum(band - 1, 0)]
    copies = [
        pltpu.make_async_copy(meta_ref.at[pl.ds(band * n_rows, n_rows)], request_ref, sems.at[0])
    ]
    for n, other in enumerate(nexts):
        source = meta_ref.at[pl.ds(other * n_rows + row, 1)]
        copies.append(pltpu.make_async_copy(source, near_ref.at[pl.ds(n, 1)], sems.at[1 + n]))
    return copies


def band_field(rows, width_k, way, n_ways):
    field = LANES + (2 + width_k) * rows
    if n_ways == 1:
        return field + jnp.where(lax.axis_index("band") == 0, 0, rows)
    return field + way * rows


def pack_bands(sizes, width_k, product_ref, near_ref, band_refs):
    rows = sizes[0]
    for way, band_ref in enumerate(band_refs):
        field = band_field(rows, width_k, way, len(band_refs))
        for row in range(rows):
            band_ref[row] = product_ref[near_ref[way, 0, field + row] * rows + row]


def product_kernel(start_ref, mirror_ref, tile_ref, product_out, product_ref, sems):
    copies = []
    for side, ref in enumerate((start_ref, mirror_ref)):
        held = product_ref.at[side]

        def done(first, count):
            place = pl.ds(first, count)
            copy = pltpu.make_async_copy(
                held.at[place], product_out.at[side, place], sems.at[len(copies)]
            )
            copies.extend(started([copy]))

        rows, n_rhs, states = ref.shape
        table_products(ref[...].reshape(rows * n_rhs, states), tile_ref, held, done)
    finish(copies)


def first_kernel(sizes, width_k, n_band, *refs):
    rows, n_rows, cap, n_tiles, n_rhs = sizes
    product_in, meta_ref, send_out = refs[:3]
    band_out, refs = refs[3 : 3 + n_band], refs[3 + n_band :]
    product_ref, request_ref, near_ref, send_ref = refs[:4]
    band_refs, (load_sems, meta_sems, send_sems) = refs[4 : 4 + n_band], refs[4 + n_band :]
    loads = []
    for side in range(2):
        for tile in range(n_tiles):
            place = pl.ds(tile * rows, rows)
            source, target = product_in.at[side, place], product_ref.at[side, place]
            loads.append(pltpu.make_async_copy(source, target, load_sems.at[len(loads)]))
    started(loads)
    finish(started(metadata_copies(meta_ref, request_ref, near_ref, meta_sems)))
    finish(loads)
    half = n_rows // 2
    base = jnp.where(lax.axis_index("rows") >= half, half, 0)
    copies = []
    for device in range(half):
        for slot in range(2 * cap):
            side, rank = slot // cap, slot % cap
            code = request_ref[base + device, 0, side * (LANES // 2) + rank]
            send_ref[device, slot] = product_ref[side, below(code, rows * n_tiles)]
        copy = pltpu.make_async_copy(send_ref.at[device], send_out.at[device], send_sems.at[device])
        copies += started([copy])
    pack_bands(sizes, width_k, product_ref.at[0], near_ref, band_refs)
    for n, (ref, out) in enumerate(zip(band_refs, band_out)):
        copies += started([pltpu.make_async_copy(ref, out, send_sems.at[half + n])])
    finish(copies)


def place(place_ref, values, n_rhs):
    per_tile = LANES // n_rhs
    length = place_ref.shape[0] // per_tile
    parts, rest = [], values
    for _ in range(3):
        part = rest.astype(jnp.bfloat16)
        rest = rest - part.astype(jnp.float32)
        parts.append(part)
    parts = jnp.concatenate(parts, axis=1)
    lane = lax.broadcasted_iota(jnp.int32, (length, LANES), 1)
    result = jnp.zeros((length, LANES), jnp.float32)
    for spot in range(per_tile):
        chosen = jnp.dot(
            place_ref[spot * length : (spot + 1) * length, :],
            parts,
            preferred_element_type=jnp.float32,
        )
        chosen = chosen[:, :LANES] + chosen[:, LANES : 2 * LANES] + chosen[:, 2 * LANES :]
        result = jnp.where((lane >= spot * n_rhs) & (lane < (spot + 1) * n_rhs), chosen, result)
    return result


def one_hot(ids, row):
    return jnp.where(ids == row, 1.0, 0.0).astype(jnp.bfloat16)


def count_kernel(sizes, width_k, n_func, *refs):
    rows, n_rows, cap, n_tiles, n_rhs = sizes
    field_ref, list_ref, tile_ref, table_ref, inverse_ref = refs[:5]
    count_out, functional_out, placing_out, scale_ref = refs[5:9]
    count_ref, functional_ref, placing_ref, sems = refs[9:]
    n_groups, n_blocks = count_ref.shape[1:]
    slots, band_rows = n_rows * cap, n_rows * rows
    copies = []

    def send(source, target):
        copies.extend(started([pltpu.make_async_copy(source, target, sems.at[len(copies)])]))

    sums = jnp.sum(tile_ref[...], axis=1)
    line = lax.broadcasted_iota(jnp.int32, (n_func, sums.shape[1]), 0)
    sums = jnp.concatenate([sums, jnp.zeros((n_func - n_tiles, sums.shape[1]), jnp.float32)], axis=0)
    n_diag = inverse_ref.shape[0]
    totals = []
    for d in range(n_diag):
        minus = -jnp.sum(table_ref[d], axis=0, keepdims=True)
        totals.append(-jnp.sum(minus, axis=1, keepdims=True))
        wanted = jnp.where(line == n_tiles, minus, sums)
        high, low = halves(inverse_ref[d])
        right = jnp.concatenate([high, high, low], axis=0)
        solved = jnp.dot(left_operand(wanted), right, preferred_element_type=jnp.float32)
        solved = jnp.where(line == n_tiles + 1, 1.0, solved)
        functional_ref[d * n_func : (d + 1) * n_func, :] = left_operand(solved)
    send(functional_ref, functional_out)

    lists = list_ref[...]
    asker = lax.broadcasted_iota(jnp.int32, lists.shape, 0)
    codes = asker * rows + below(over(lists, rows * n_tiles), rows)
    codes = jnp.where(lists > 0, codes, -1).astype(jnp.float32)
    spread = lax.broadcasted_iota(jnp.int32, (slots, n_rows), 0)
    spread = lax.div(spread, cap) == lax.broadcasted_iota(jnp.int32, (slots, n_rows), 1)
    codes = jnp.dot(
        jnp.where(spread, 1.0, 0.0), codes, precision=HIGH, preferred_element_type=jnp.float32
    )
    rank = lax.rem(lax.broadcasted_iota(jnp.int32, codes.shape, 0), cap)
    lane = lax.broadcasted_iota(jnp.int32, codes.shape, 1)
    asked = jnp.sum(jnp.where(rank == lane, codes, 0.0), axis=1, keepdims=True)
    asked = jnp.where(asked < 0.0, asked - 0.5, asked + 0.5).astype(jnp.int32)
    own = lax.axis_index("rows") * rows + lax.broadcasted_iota(jnp.int32, (rows, 1), 0)
    band = lax.axis_index("band")

    def field(n, which):
        return field_ref[n, pl.ds(which, 1), :]

    row_ids = lax.broadcasted_iota(jnp.int32, (1, band_rows), 1)
    sides = []
    for which, targets in ((band, jnp.concatenate([asked, own], axis=0)), (1 - band, own)):
        across = jnp.where(which == 0, field(2 + width_k, 1), field(3 + width_k, 0))
        takers = [field(2 + k, which) * n_groups + field(0, which) for k in range(width_k)]
        takers.append(across * n_groups + field(0, 1 - which))
        takers = jnp.concatenate(takers, axis=1)
        origins = [field(4 + width_k + k, which) for k in range(width_k)] + [row_ids]
        hits = one_hot(targets, jnp.concatenate(origins, axis=1))
        sides.append((takers, hits, field(0, which)))
    for t in range(n_tiles):
        found = []
        for takers, hits, _ in sides:
            ids = lax.broadcasted_iota(jnp.int32, (n_groups, takers.shape[1]), 0) + t * n_groups
            found.append(dot_nt(one_hot(ids, takers), hits))
        count_ref[t] = jnp.concatenate(found, axis=1).astype(jnp.bfloat16)
        send(count_ref.at[t], count_out.at[t])
    ids = lax.broadcasted_iota(jnp.int32, (n_groups, band_rows), 0)
    found = [dot_nt(one_hot(ids, groups), hits[:, -band_rows:]) for _, hits, groups in sides]
    found = jnp.concatenate(found, axis=1)
    count_ref[n_tiles] = found.astype(jnp.bfloat16)
    send(count_ref.at[n_tiles], count_out.at[n_tiles])
    block = lax.broadcasted_iota(jnp.int32, found.shape, 1)
    mine = (block >= slots) & (block < slots + rows)
    count_ref[n_tiles + 1] = jnp.where(mine, found, 0.0).astype(jnp.bfloat16)
    send(count_ref.at[n_tiles + 1], count_out.at[n_tiles + 1])

    per_tile = LANES // n_rhs
    depth = rows // per_tile
    length = n_rows * 2 * depth
    order = lax.broadcasted_iota(jnp.int32, (per_tile * length, 1), 0)
    spot, order = lax.div(order, length), lax.rem(order, length)
    device, order = lax.div(order, 2 * depth), lax.rem(order, 2 * depth)
    side, order = lax.div(order, depth), lax.rem(order, depth)
    order = side * band_rows + device * rows + spot * depth + order
    member = [one_hot(ids, field(0, which)) for which in range(2)]
    placing = jnp.zeros(placing_ref.shape, jnp.float32)
    for which in range(2):
        placing = placing + dot_nt(one_hot(order, row_ids + which * band_rows), member[which])
    placing_ref[...] = placing.astype(jnp.bfloat16)
    send(placing_ref, placing_out)
    whole = jnp.zeros((n_groups, 1), jnp.float32)
    for which in range(2):
        sums = jnp.zeros((1, band_rows), jnp.float32)
        for d in range(n_diag):
            sums = jnp.where(field(1, which) == d, totals[d], sums)
        weighted = jnp.where(ids == field(0, which), sums, 0.0)
        whole = whole + jnp.sum(weighted, axis=1, keepdims=True)
    scale = place(placing_ref, jnp.broadcast_to(whole, (n_groups, LANES)), n_rhs)
    mine = jnp.zeros(scale_ref.shape, jnp.float32)
    here = lax.axis_index("rows") * 2 + band
    for n in range(2 * n_rows):
        mine = jnp.where(here == n, scale[n * depth : (n + 1) * depth, :], mine)
    scale_ref[...] = mine
    finish(copies)


def gather_solve(
    sizes, slots, diags, arrived_ref, later, terms, inverse_ref, sum_ref, product_ref
):
    rows, n_rows, cap, n_tiles, n_rhs = sizes
    per = n_rows * cap // arrived_ref.shape[0]
    for row in range(rows):
        total = None
        for slot in slots(row):
            start = pl.multiple_of(below(slot, per) * n_rhs, n_rhs)
            block = arrived_ref[over(slot, per), pl.ds(start, n_rhs), :]
            total = block if total is None else total + block
        sum_ref[pl.ds(row * n_rhs, n_rhs), :] = total
    finish(later)
    total = sum_ref[...]
    for term in terms:
        total = total + term[...].reshape(total.shape)
    table_products(total, inverse_ref, product_ref)
    for row in range(rows):
        sum_ref[pl.ds(row * n_rhs, n_rhs), :] = product_ref[diags(row) * rows + row]


def middle_kernel(sizes, width_k, n_band, dense, *refs):
    meta_ref, arrived_ref, inverse_ref, tile_ref = refs[:4]
    terms_in, refs = refs[4 : 5 + n_band], refs[5 + n_band :]
    extra, refs = (refs[:3], refs[3:]) if dense else ((), refs)
    send_out, band_out, refs = refs[0], refs[1 : 1 + n_band], refs[1 + n_band :]
    sum_ref, product_ref, request_ref, near_ref, send_ref = refs[:5]
    terms, band_refs, refs = refs[5 : 6 + n_band], refs[6 + n_band : 6 + 2 * n_band], refs[6 + 2 * n_band :]
    term_sems, meta_sems, send_sems, refs = *refs[:3], refs[3:]
    right_ref = terms[0]
    rows, n_rows, cap, n_tiles, n_rhs = sizes
    body = cap * n_rhs
    metadata = started(metadata_copies(meta_ref, request_ref, near_ref, meta_sems))
    pairs = enumerate(zip(terms_in, terms))
    later = started([pltpu.make_async_copy(i, h, term_sems.at[n]) for n, (i, h) in pairs])
    fetched = []
    if dense:
        held, extra_sems, value_ref, spread_ref = refs[:3], refs[3], refs[4], refs[5]
        n_diag = inverse_ref.shape[0]
        pairs = enumerate(zip(extra, held))
        fetched = started([pltpu.make_async_copy(i, h, extra_sems.at[n]) for n, (i, h) in pairs])
    finish(metadata)
    mine = lax.axis_index("rows")

    def slots(row):
        field = LANES + (4 + 2 * width_k) * rows + row
        return [request_ref[mine, 0, field + k * rows] for k in range(width_k)]

    def diags(row):
        return request_ref[mine, 0, LANES + rows + row]

    gather_solve(sizes, slots, diags, arrived_ref, later, terms, inverse_ref, sum_ref, product_ref)
    table_products(sum_ref[...], tile_ref, product_ref)
    copies = []

    def send(source, target):
        copies.extend(started([pltpu.make_async_copy(source, target, send_sems.at[len(copies)])]))

    for owner in range(n_rows):
        for rank in range(cap):
            block = product_ref[below(request_ref[owner, 0, rank], rows * n_tiles)]
            send_ref[owner, rank * n_rhs : (rank + 1) * n_rhs, :] = block
        if not dense:
            send(send_ref.at[owner], send_out.at[owner])
        else:
            send(send_ref.at[owner, pl.ds(0, body)], send_out.at[owner, pl.ds(0, body)])
    pack_bands(sizes, width_k, product_ref, near_ref, band_refs)
    for ref, out in zip(band_refs, band_out):
        send(ref, out)
    if dense:
        finish(fetched)
        kinds = []
        for owner in range(n_rows):
            for rank in range(cap):
                code = over(request_ref[owner, 0, rank], rows * n_tiles * rows)
                kinds.append(below(code, n_diag))
        kinds += [diags(row) for row in range(rows)]
        kinds += [near_ref[0, 0, LANES + rows + row] for row in range(rows)]
        result = coarse_parts(
            sizes, kinds, held, right_ref, send_ref, band_refs, value_ref, spread_ref
        )
        depth = result.shape[0] // n_rows
        for owner in range(n_rows):
            send_ref[owner, body:, :] = result[owner * depth : (owner + 1) * depth, :]
        send(send_ref.at[:, pl.ds(body, depth)], send_out.at[:, pl.ds(body, depth)])
    finish(copies)


def coarse_parts(sizes, kinds, held, right_ref, send_ref, band_refs, value_ref, spread_ref):
    functional_ref, count_ref, place_ref = held
    rows, n_rows, cap, n_tiles, n_rhs = sizes
    body = cap * n_rhs
    n_func = spread_ref.shape[0] // count_ref.shape[2]
    per_tile = LANES // n_rhs
    functional = functional_ref[...]
    done = 0
    for owner in range(0, n_rows, 2):
        values = [send_ref[owner + more, :body, :] for more in range(2)]
        values = jnp.concatenate(values, axis=0)
        value_ref[:, done : done + 2 * body] = dot_nt(functional, right_operand(values))
        done += 2 * body
    for ref in (right_ref, *band_refs):
        values = ref[...].reshape(rows * n_rhs, -1)
        value_ref[:, done : done + rows * n_rhs] = dot_nt(functional, right_operand(values))
        done += rows * n_rhs
    lane = lax.broadcasted_iota(jnp.int32, (n_func, LANES), 1)
    for block, kind in enumerate(kinds):
        tile, spot = block // per_tile, block % per_tile
        start = pl.multiple_of(kind * n_func, n_func)
        piece = value_ref[pl.ds(start, n_func), tile * LANES : (tile + 1) * LANES]
        piece = jnp.where((lane >= spot * n_rhs) & (lane < (spot + 1) * n_rhs), piece, 0.0)
        spread_ref[block * n_func : (block + 1) * n_func, :] = piece
    partial = jnp.zeros((count_ref.shape[1], 2 * LANES), jnp.float32)
    for t in range(count_ref.shape[0]):
        values = spread_ref[pl.ds(t, done // n_rhs, stride=n_func), :]
        partial = partial + jnp.dot(
            count_ref[t],
            jnp.concatenate(halves(values), axis=1),
            preferred_element_type=jnp.float32,
        )
    partial = partial[:, :LANES] + partial[:, LANES:]
    source = lax.broadcasted_iota(jnp.int32, (LANES, LANES), 0)
    target = lax.broadcasted_iota(jnp.int32, (LANES, LANES), 1)
    same = jnp.where(lax.rem(source, n_rhs) == lax.rem(target, n_rhs), 1.0, 0.0)
    same = same.astype(jnp.bfloat16)
    same = jnp.concatenate([same, same], axis=0)
    partial = jnp.dot(
        jnp.concatenate(halves(partial), axis=1), same, preferred_element_type=jnp.float32
    )
    return place(place_ref, partial, n_rhs)


def part_kernel(arrived_ref, mine_ref, other_ref):
    depth = mine_ref.shape[0]
    body = arrived_ref.shape[1] - 2 * depth
    total = arrived_ref[0, body:, :]
    for source in range(1, arrived_ref.shape[0]):
        total = total + arrived_ref[source, body:, :]
    upper = lax.axis_index("band") == 0
    mine_ref[...] = jnp.where(upper, total[:depth], total[depth:])
    other_ref[...] = jnp.where(upper, total[depth:], total[:depth])


def last_kernel(sizes, width_k, n_band, *refs):
    meta_ref, arrived_ref, inverse_ref = refs[:3]
    terms_in, refs = refs[3 : 4 + n_band], refs[4 + n_band :]
    second_ref, sum_ref, product_ref, mine_ref = refs[:4]
    terms, (term_sems, meta_sem) = refs[4 : 5 + n_band], refs[5 + n_band :]
    rows, n_rows = sizes[:2]
    place = lax.axis_index("band") * n_rows + lax.axis_index("rows")
    metadata = pltpu.make_async_copy(meta_ref.at[pl.ds(place, 1)], mine_ref, meta_sem)
    metadata.start()
    pairs = enumerate(zip(terms_in, terms))
    later = started([pltpu.make_async_copy(i, h, term_sems.at[n]) for n, (i, h) in pairs])
    metadata.wait()

    def slots(row):
        field = LANES + (4 + 3 * width_k) * rows + row
        return [mine_ref[0, 0, field + k * rows] for k in range(width_k)]

    def diags(row):
        return mine_ref[0, 0, LANES + rows + row]

    gather_solve(sizes, slots, diags, arrived_ref, later, terms, inverse_ref, sum_ref, product_ref)
    second_ref[...] = sum_ref[...].reshape(second_ref.shape)


def final_kernel(sizes, mine_ref, other_ref, scale_ref, second_ref, out_ref):
    rows, n_rhs = sizes[0], sizes[4]
    depth = scale_ref.shape[0]
    correction = (mine_ref[...] + other_ref[...]) / scale_ref[...]
    padded = jnp.concatenate([correction, jnp.zeros((8 - depth, LANES), jnp.float32)], axis=0)
    turned = padded.T
    for row in range(rows):
        spot, place = row // depth, row % depth
        column = turned[spot * n_rhs : (spot + 1) * n_rhs, place : place + 1]
        out_ref[row] = second_ref[row] + column


def shifted(value, axis, steps):
    count = lax.axis_size(axis)
    initial, last = (max(0, -steps), min(count, count - steps))
    return lax.ppermute(value, axis, [(source, source + steps) for source in range(initial, last)])


def to_bands(sends):
    if len(sends) == 1:
        return (lax.ppermute(sends[0], "band", [(0, 1), (1, 0)]),)
    return shifted(sends[0], "band", 1), shifted(sends[1], "band", -1)


def on_device(
    start_iterate,
    right_side,
    diag_table,
    inverse_table,
    coupling_tiles,
    diag_index,
    tile_index,
    source_owner,
    source_local,
    aggregate_map,
):
    rows, n_rhs, states = start_iterate.shape
    width_k = source_owner.shape[1]
    n_tiles, n_diag = coupling_tiles.shape[0], inverse_table.shape[0]
    n_rows, n_bands = lax.axis_size("rows"), lax.axis_size("band")
    n_dev = n_rows * n_bands
    cap = max(2, 2 * width_k * rows // n_rows)
    slots = n_rows * cap
    total_groups = AGG_DEV * n_dev
    per_tile = LANES // n_rhs
    depth = rows // per_tile
    n_func = 16
    dense = (
        n_bands == 2
        and n_dev * rows * total_groups <= DENSE_LIMIT
        and depth == 4
        and n_diag * n_func == LANES
        and n_tiles + 2 <= n_func
    )
    sizes = (rows, n_rows, cap, n_tiles, n_rhs)
    f32, i32 = jnp.float32, jnp.int32
    my_band = lax.axis_index("band")
    my_row = lax.axis_index("rows")

    half = n_rows // 2
    mirror = lax.ppermute(start_iterate, "rows", [(i, (i + half) % n_rows) for i in range(n_rows)])
    wide = LANES + -(-(4 + 4 * width_k) * rows // LANES) * LANES
    index_shapes = [(width_k, rows), (width_k, rows), (width_k + 2, rows), (1, rows), (1, rows)]
    payload = call(
        functools.partial(request_kernel, (rows, n_rows, cap, n_tiles, n_diag)),
        jax.ShapeDtypeStruct((n_dev, 1, wide), i32),
        [HBM] * 5,
        VMEM,
        [*[pltpu.VMEM(shape, i32) for shape in index_shapes], pltpu.SemaphoreType.DMA((5,))],
    )(source_owner.T, source_local.T, tile_index.T, diag_index[None], aggregate_map.T)
    meta = lax.all_to_all(payload, ("band", "rows"), split_axis=0, concat_axis=0, tiled=True)

    n_ways = 1 if n_bands == 2 else 2
    block = (rows, n_rhs, states)
    band_shapes = [jax.ShapeDtypeStruct(block, f32)] * n_ways
    band_scratch = [pltpu.VMEM(block, f32)] * n_ways
    term_scratch = [pltpu.VMEM(block, f32)] * (1 + n_ways)
    term_sems = pltpu.SemaphoreType.DMA((1 + n_ways,))
    meta_scratch = [pltpu.SMEM((n_rows, 1, wide), i32), pltpu.SMEM((n_ways, 1, wide), i32)]
    meta_sems = pltpu.SemaphoreType.DMA((1 + n_ways,))
    flat = rows * n_rhs
    sums = pltpu.VMEM((flat, states), f32)
    products = pltpu.VMEM((max(n_tiles, n_diag) * rows, n_rhs, states), f32)
    work = 6 * flat * states * states
    made_shape = (2, n_tiles * rows, n_rhs, states)
    made = call(
        product_kernel,
        jax.ShapeDtypeStruct(made_shape, f32),
        [VMEM] * 3,
        HBM,
        [pltpu.VMEM(made_shape, f32), pltpu.SemaphoreType.DMA((2 * n_tiles,))],
        2 * work * n_tiles,
        4 << 20,
    )(start_iterate, mirror, coupling_tiles)
    packed, *bands = call(
        functools.partial(first_kernel, sizes, width_k, n_ways),
        (jax.ShapeDtypeStruct((half, 2 * cap, n_rhs, states), f32), *band_shapes),
        [HBM, ANY],
        [HBM] * (1 + n_ways),
        [
            pltpu.VMEM(made_shape, f32),
            *meta_scratch,
            pltpu.VMEM((half, 2 * cap, n_rhs, states), f32),
            *band_scratch,
            pltpu.SemaphoreType.DMA((2 * n_tiles,)),
            meta_sems,
            pltpu.SemaphoreType.DMA((half + n_ways,)),
        ],
        0,
        4 << 20,
    )(made, meta)
    sends = (packed.reshape(half, 2 * cap * n_rhs, states), *bands)
    halves_of_rows = [list(range(half)), list(range(half, n_rows))]
    late, *sends = lax.optimization_barrier((meta, *sends))

    def exchange(sends, groups=None):
        arrived = lax.all_to_all(
            sends[0], "rows", split_axis=0, concat_axis=0, tiled=True, axis_index_groups=groups
        )
        return arrived, to_bands(sends[1:])

    arrived_blocks, arrived_bands = exchange(sends, halves_of_rows)

    late = late.reshape(n_bands, n_rows, wide)
    requests = lax.dynamic_index_in_dim(late[:, :, :LANES], my_band, 0, keepdims=False)
    common = late[:, :, LANES:]
    extra, extra_scratch, tail = (), [], 0
    if dense:
        fields = common[:, :, : (4 + 2 * width_k) * rows].reshape(n_bands, n_rows, -1, rows).transpose(2, 0, 1, 3)
        fields = fields.reshape(-1, n_bands, n_rows * rows)
        n_blocks = slots + 2 * rows
        length = n_dev * depth
        extra_shapes = [
            ((n_diag * n_func, 3 * states), jnp.bfloat16),
            ((n_tiles + 2, total_groups, n_blocks), jnp.bfloat16),
            ((per_tile * length, total_groups), jnp.bfloat16),
        ]
        functional_shape, count_shape, placing_shape = extra_shapes
        counts, functionals, placing, scale = call(
            functools.partial(count_kernel, sizes, width_k, n_func),
            (
                jax.ShapeDtypeStruct(*count_shape),
                jax.ShapeDtypeStruct(*functional_shape),
                jax.ShapeDtypeStruct(*placing_shape),
                jax.ShapeDtypeStruct((depth, LANES), f32),
            ),
            [VMEM] * 5,
            [HBM, HBM, HBM, VMEM],
            [
                pltpu.VMEM(*count_shape),
                pltpu.VMEM(*functional_shape),
                pltpu.VMEM(*placing_shape),
                pltpu.SemaphoreType.DMA((n_tiles + 4,)),
            ],
            4 * total_groups * n_tiles * n_dev * rows * n_blocks,
            4 << 20,
        )(fields, requests, coupling_tiles, diag_table, inverse_table)
        extra = (functionals, counts, placing)
        extra_scratch = [
            *[pltpu.VMEM(*shape) for shape in extra_shapes],
            pltpu.SemaphoreType.DMA((3,)),
            pltpu.VMEM((n_diag * n_func, n_blocks * n_rhs), f32),
            pltpu.VMEM((n_blocks * n_func, LANES), f32),
        ]
        tail = n_bands * depth

    send_shape = (n_rows, cap * n_rhs + tail, states)
    sends = call(
        functools.partial(middle_kernel, sizes, width_k, n_ways, dense),
        (jax.ShapeDtypeStruct(send_shape, f32), *band_shapes),
        [HBM] + [VMEM] * 3 + [HBM] + [ANY] * n_ways + [HBM] * len(extra),
        [HBM] * (1 + n_ways),
        [
            sums,
            products,
            *meta_scratch,
            pltpu.VMEM(send_shape, f32),
            *term_scratch,
            *band_scratch,
            term_sems,
            meta_sems,
            pltpu.SemaphoreType.DMA((n_rows + n_ways + 1,)),
            *extra_scratch,
        ],
        work * (n_tiles + n_diag),
        4 << 20,
    )(
        meta,
        arrived_blocks,
        inverse_table,
        coupling_tiles,
        right_side,
        *arrived_bands,
        *extra,
    )
    arrived_blocks, arrived_bands = exchange(sends)

    if dense:
        part = jax.ShapeDtypeStruct((depth, LANES), f32)
        mine, other = call(part_kernel, (part, part), [VMEM], [VMEM] * 2)(arrived_blocks)
        other = lax.ppermute(other, "band", [(0, 1), (1, 0)])
    second = call(
        functools.partial(last_kernel, sizes, width_k, n_ways),
        jax.ShapeDtypeStruct(block, f32),
        [HBM] + [VMEM] * 2 + [HBM] + [ANY] * n_ways,
        VMEM,
        [
            sums,
            products,
            pltpu.SMEM((1, 1, wide), i32),
            *term_scratch,
            term_sems,
            pltpu.SemaphoreType.DMA,
        ],
        work * n_diag,
        4 << 20,
    )(meta, arrived_blocks, inverse_table, right_side, *arrived_bands)
    if dense:
        return call(
            functools.partial(final_kernel, sizes),
            jax.ShapeDtypeStruct(block, f32),
            [VMEM] * 4,
            VMEM,
        )(mine, other, scale, second)

    groups = aggregate_map[:, 0]
    own = jnp.arange(rows, dtype=i32)
    groups_all = common[:, :, :rows]
    diags_all = common[:, :, rows : 2 * rows]
    codes = requests[:, :cap]
    asked = lax.broadcasted_iota(i32, codes.shape, 0) * rows + codes // (rows * n_tiles) % rows
    asked = jnp.where(codes > 0, asked, -1).reshape(-1)
    table_sums = jnp.sum(diag_table, axis=(1, 2))
    diag_onehot = diags_all.reshape(-1, 1) == jnp.arange(n_diag, dtype=i32)[None]
    block_sums = jnp.sum(jnp.where(diag_onehot, table_sums[None], 0.0), axis=1)
    whole_diag = jnp.sum(
        jnp.where(groups[:, None] == groups_all.reshape(-1)[None], block_sums[None], 0.0), axis=1
    )
    here = lax.dynamic_index_in_dim(common, my_row, 1, keepdims=False)
    above = lax.dynamic_index_in_dim(here, jnp.minimum(my_band + 1, n_bands - 1), 0, keepdims=False)
    below = lax.dynamic_index_in_dim(here, jnp.maximum(my_band - 1, 0), 0, keepdims=False)
    place_of = (2 + width_k) * rows
    band_tiles = jnp.stack([above[place_of : place_of + rows], below[place_of + rows : place_of + 2 * rows]])
    band_groups = jnp.stack([above[:rows], below[:rows]])
    band_valid = jnp.stack([my_band + 1 < n_bands, my_band > 0])
    band_valid = jnp.broadcast_to(band_valid[:, None], (2, rows))
    n_all = n_tiles + n_diag + 1
    code = codes.reshape(-1)
    band_of_mine = lax.dynamic_index_in_dim(groups_all, my_band, 0, keepdims=False).reshape(-1)
    entry_group = jnp.concatenate(
        [jnp.take(band_of_mine, jnp.maximum(asked, 0)), band_groups.reshape(-1), groups, groups]
    )
    entry_func = jnp.concatenate(
        [
            (code % rows) * n_all + (code // rows) % n_tiles,
            (own[None] * n_all + band_tiles).reshape(-1),
            own * n_all + n_tiles + diag_index,
            own * n_all + n_tiles + n_diag,
        ]
    )
    entry_valid = jnp.concatenate([asked >= 0, band_valid.reshape(-1), jnp.ones((2 * rows,), bool)])
    functionals = jnp.concatenate(
        [jnp.sum(coupling_tiles, axis=1), -jnp.sum(diag_table, axis=1)], axis=0
    )
    weights = jnp.einsum("fp,rcp->rfc", functionals, second, precision=HIGH)
    weights = jnp.concatenate([weights, jnp.sum(right_side, axis=2)[:, None]], axis=1)
    chosen = jnp.take(weights.reshape(rows * n_all, n_rhs), entry_func, axis=0)
    chosen = jnp.where(entry_valid[:, None], chosen, 0.0)
    partial = jax.ops.segment_sum(chosen, entry_group, num_segments=total_groups)
    whole = lax.psum(partial, ("band", "rows"))
    correction = jnp.take(whole, groups, axis=0) / whole_diag[:, None]
    return second + correction[:, :, None]


def solution(mesh):
    in_specs = (
        P(("band", "rows"), None, None),
        P(("band", "rows"), None, None),
        P(),
        P(),
        P(),
        P(("band", "rows")),
        P(("band", "rows"), None),
        P(("band", "rows"), None),
        P(("band", "rows"), None),
        P(("band", "rows"), None),
    )
    out_specs = P(("band", "rows"), None, None)
    return jax.shard_map(
        on_device, mesh=mesh, in_specs=in_specs, out_specs=out_specs, check_vma=False
    )
```

```python
import functools

import jax
import jax.numpy as jnp
from jax import lax
from jax.experimental import pallas as pl
from jax.experimental.pallas import tpu as pltpu
from jax.sharding import PartitionSpec as P

AGG_DEV = 8
LANES = 128
DENSE_LIMIT = 1 << 19

VMEM = pl.BlockSpec(memory_space=pltpu.VMEM)
SMEM = pl.BlockSpec(memory_space=pltpu.SMEM)
HBM = pl.BlockSpec(memory_space=pltpu.HBM)
ANY = pl.BlockSpec(memory_space=pl.ANY)
HIGH = lax.Precision.HIGHEST


def params():
    return pltpu.CompilerParams(vmem_limit_bytes=24 * 1024 * 1024)


def call(kernel, out_shape, in_specs, out_specs, scratch=(), flops=0, moved=0):
    def shaped(shape, spec):
        return pltpu.HBM(shape.shape, shape.dtype) if spec is HBM else shape

    if isinstance(out_shape, (tuple, list)):
        out_shape = [shaped(*pair) for pair in zip(out_shape, out_specs)]
    else:
        out_shape = shaped(out_shape, out_specs)
    run = pl.pallas_call(
        kernel,
        out_shape=out_shape,
        in_specs=in_specs,
        out_specs=out_specs,
        scratch_shapes=list(scratch),
        compiler_params=params(),
        cost_estimate=pl.CostEstimate(flops=flops, bytes_accessed=moved, transcendentals=0),
    )

    def apply(*args):
        pinned = [
            pltpu.with_memory_space_constraint(arg, pltpu.HBM) if spec is HBM else arg
            for arg, spec in zip(args, in_specs)
        ]
        return run(*pinned)

    return apply


def below(value, bound):
    return value & (bound - 1) if bound & (bound - 1) == 0 else lax.rem(value, bound)


def over(value, bound):
    if bound & (bound - 1) == 0:
        return lax.shift_right_logical(value, bound.bit_length() - 1)
    return lax.div(value, bound)


def halves(value):
    high = value.astype(jnp.bfloat16)
    low = (value - high.astype(jnp.float32)).astype(jnp.bfloat16)
    return high, low


def left_operand(value):
    high, low = halves(value)
    return jnp.concatenate([high, low, high], axis=1)


def right_operand(value):
    high, low = halves(value)
    return jnp.concatenate([high, high, low], axis=1)


def dot_nt(left, right):
    return lax.dot_general(
        left, right, (((1,), (1,)), ((), ())), preferred_element_type=jnp.float32
    )


def table_products(value, table_ref, out_ref, done=None, loads=None):
    left = left_operand(value)
    count, width = table_ref.shape[0], table_ref.shape[1]
    n_rhs = out_ref.shape[1]
    rows = left.shape[0] // n_rhs
    for first in range(0, count, 2):
        last = min(first + 2, count)
        if loads is not None:
            loads[first // 2].wait()
        right = right_operand(table_ref[first:last].reshape((last - first) * width, -1))
        product = dot_nt(left, right)
        for t in range(first, last):
            part = product[:, (t - first) * width : (t - first + 1) * width]
            out_ref[t * rows : (t + 1) * rows] = part.reshape(rows, n_rhs, width)
        if done is not None:
            done(first * rows, (last - first) * rows)


def started(copies):
    for copy in copies:
        copy.start()
    return copies


def finish(copies):
    for copy in copies:
        copy.wait()


def request_kernel(sizes, *refs):
    rows, n_rows, cap, n_tiles, n_diag = sizes
    inputs, payload_ref, held, sems = refs[:5], refs[5], refs[6:11], refs[11]
    finish(
        started([pltpu.make_async_copy(i, h, sems.at[n]) for n, (i, h) in enumerate(zip(inputs, held))])
    )
    owner_ref, local_ref, tile_ref, diag_ref, group_ref = held
    width_k = owner_ref.shape[0]
    half = n_rows // 2
    row_of = lax.broadcasted_iota(jnp.int32, (rows, rows), 0)
    col_of = lax.broadcasted_iota(jnp.int32, (rows, rows), 1)
    lane = lax.broadcasted_iota(jnp.int32, (rows, LANES), 1)
    owners = lax.broadcasted_iota(jnp.int32, (n_rows, rows), 0)

    def column(row):
        return jnp.sum(jnp.where(row_of == col_of, row, 0), axis=1, keepdims=True)

    def owner_row(k):
        return owner_ref[k : k + 1, :]

    row_ids = lax.broadcasted_iota(jnp.int32, (1, rows), 1)
    owner_columns = [column(owner_row(k)) for k in range(width_k)]
    lists = jnp.zeros((n_rows, LANES), jnp.float32)
    places, half_places = [], []
    for k in range(width_k):
        rank = jnp.zeros((1, rows), jnp.int32)
        for other in range(k + 1):
            match = owner_columns[other] == owner_row(k)
            if other == k:
                match = match & (row_of < col_of)
            rank = rank + jnp.sum(jnp.where(match, 1, 0), axis=0, keepdims=True)
        places.append(owner_row(k) * cap + rank)
        same = (owner_row(k) >= half) == (lax.axis_index("rows") >= half)
        holder = jnp.where(owner_row(k) >= half, owner_row(k) - half, owner_row(k))
        half_places.append(holder * (2 * cap) + rank + jnp.where(same, 0, cap))
        taker = row_ids + rows * (diag_ref[...] + n_diag)
        code = local_ref[k : k + 1, :] + rows * (tile_ref[k : k + 1, :] + n_tiles * taker)
        code, rank = column(code), column(rank)
        mirror = jnp.where(owner_row(k) >= half, owner_row(k) - half, owner_row(k) + half)
        for owner, base in ((owner_row(k), 0), (mirror, LANES // 2)):
            by_rank = jnp.where(lane == rank + base, code, 0).astype(jnp.float32)
            mine = jnp.where(owners == owner, 1.0, 0.0)
            lists = lists + jnp.dot(
                mine, by_rank, precision=HIGH, preferred_element_type=jnp.float32
            )
    lists = (lists + 0.5).astype(jnp.int32)
    common = [group_ref[...], diag_ref[...]]
    common += [tile_ref[k : k + 1, :] for k in range(width_k + 2)]
    common += [owner_row(k) * rows + local_ref[k : k + 1, :] for k in range(width_k)]
    common += half_places + places
    spare = payload_ref.shape[2] - LANES - len(common) * rows
    if spare:
        common.append(jnp.zeros((1, spare), jnp.int32))
    common = jnp.concatenate(common, axis=1)
    for device in range(n_rows):
        line = jnp.concatenate([lists[device : device + 1, :], common], axis=1)
        for band in range(payload_ref.shape[0] // n_rows):
            payload_ref[band * n_rows + device] = line


def metadata_copies(meta_ref, request_ref, near_ref, sems):
    n_rows, n_near = request_ref.shape[0], near_ref.shape[0]
    band, row = lax.axis_index("band"), lax.axis_index("rows")
    last = meta_ref.shape[0] // n_rows - 1
    if n_near == 1:
        nexts = [last - band]
    else:
        nexts = [jnp.minimum(band + 1, last), jnp.maximum(band - 1, 0)]
    copies = [
        pltpu.make_async_copy(meta_ref.at[pl.ds(band * n_rows, n_rows)], request_ref, sems.at[0])
    ]
    for n, other in enumerate(nexts):
        source = meta_ref.at[pl.ds(other * n_rows + row, 1)]
        copies.append(pltpu.make_async_copy(source, near_ref.at[pl.ds(n, 1)], sems.at[1 + n]))
    return copies


def band_field(rows, width_k, way, n_ways):
    field = LANES + (2 + width_k) * rows
    if n_ways == 1:
        return field + jnp.where(lax.axis_index("band") == 0, 0, rows)
    return field + way * rows


def pack_bands(sizes, width_k, product_ref, near_ref, band_refs):
    rows = sizes[0]
    for way, band_ref in enumerate(band_refs):
        field = band_field(rows, width_k, way, len(band_refs))
        for row in range(rows):
            band_ref[row] = product_ref[near_ref[way, 0, field + row] * rows + row]


def table_loads(table_in, table_ref, sems):
    copies = []
    for first in range(0, table_in.shape[0], 2):
        place = pl.ds(first, min(2, table_in.shape[0] - first))
        source, target = table_in.at[place], table_ref.at[place]
        copies.append(pltpu.make_async_copy(source, target, sems.at[first // 2]))
    return started(copies)


def product_kernel(start_in, tile_in, product_out, start_ref, tile_ref, product_ref, sems, tile_sems):
    start = pltpu.make_async_copy(start_in, start_ref, sems.at[0])
    start.start()
    loads = table_loads(tile_in, tile_ref, tile_sems)
    start.wait()
    copies = []

    def done(first, count):
        place = pl.ds(first, count)
        source, target = product_ref.at[place], product_out.at[place]
        copies.extend(started([pltpu.make_async_copy(source, target, sems.at[1 + len(copies)])]))

    rows, n_rhs, states = start_ref.shape
    values = start_ref[...].reshape(rows * n_rhs, states)
    table_products(values, tile_ref, product_ref, done, loads)
    finish(copies)


def first_kernel(sizes, width_k, n_band, *refs):
    rows, n_rows, cap, n_tiles, n_rhs = sizes
    product_in, mirror_ref, tile_in, meta_ref, send_out = refs[:5]
    band_out, refs = refs[5 : 5 + n_band], refs[5 + n_band :]
    product_ref, tile_ref, request_ref, near_ref, send_ref = refs[:5]
    band_refs, (load_sems, tile_sems, meta_sems, send_sems) = refs[5 : 5 + n_band], refs[5 + n_band :]
    tile_loads = table_loads(tile_in, tile_ref, tile_sems)
    metadata = started(metadata_copies(meta_ref, request_ref, near_ref, meta_sems))
    loads = []
    for tile in range(n_tiles):
        place = pl.ds(tile * rows, rows)
        source, target = product_in.at[place], product_ref.at[0, place]
        loads.append(pltpu.make_async_copy(source, target, load_sems.at[tile]))
    started(loads)
    values = mirror_ref[...].reshape(rows * n_rhs, -1)
    table_products(values, tile_ref, product_ref.at[1], None, tile_loads)
    finish(metadata)
    finish(loads)
    half = n_rows // 2
    base = jnp.where(lax.axis_index("rows") >= half, half, 0)
    copies = []
    for device in range(half):
        for slot in range(2 * cap):
            side, rank = slot // cap, slot % cap
            code = request_ref[base + device, 0, side * (LANES // 2) + rank]
            send_ref[device, slot] = product_ref[side, below(code, rows * n_tiles)]
        copy = pltpu.make_async_copy(send_ref.at[device], send_out.at[device], send_sems.at[device])
        copies += started([copy])
    pack_bands(sizes, width_k, product_ref.at[0], near_ref, band_refs)
    for n, (ref, out) in enumerate(zip(band_refs, band_out)):
        copies += started([pltpu.make_async_copy(ref, out, send_sems.at[half + n])])
    finish(copies)


def place(place_ref, values, n_rhs):
    per_tile = LANES // n_rhs
    length = place_ref.shape[0] // per_tile
    parts, rest = [], values
    for _ in range(3):
        part = rest.astype(jnp.bfloat16)
        rest = rest - part.astype(jnp.float32)
        parts.append(part)
    parts = jnp.concatenate(parts, axis=1)
    lane = lax.broadcasted_iota(jnp.int32, (length, LANES), 1)
    result = jnp.zeros((length, LANES), jnp.float32)
    for spot in range(per_tile):
        chosen = jnp.dot(
            place_ref[spot * length : (spot + 1) * length, :],
            parts,
            preferred_element_type=jnp.float32,
        )
        chosen = chosen[:, :LANES] + chosen[:, LANES : 2 * LANES] + chosen[:, 2 * LANES :]
        result = jnp.where((lane >= spot * n_rhs) & (lane < (spot + 1) * n_rhs), chosen, result)
    return result


def one_hot(ids, row):
    return jnp.where(ids == row, 1.0, 0.0).astype(jnp.bfloat16)


def count_kernel(sizes, width_k, n_func, *refs):
    rows, n_rows, cap, n_tiles, n_rhs = sizes
    field_ref, list_ref, tile_ref, table_ref, inverse_ref = refs[:5]
    count_out, functional_out, placing_out, scale_ref = refs[5:9]
    count_ref, functional_ref, placing_ref, sems = refs[9:]
    n_groups, n_blocks = count_ref.shape[1:]
    slots, band_rows = n_rows * cap, n_rows * rows
    copies = []

    def send(source, target):
        copies.extend(started([pltpu.make_async_copy(source, target, sems.at[len(copies)])]))

    sums = jnp.sum(tile_ref[...], axis=1)
    line = lax.broadcasted_iota(jnp.int32, (n_func, sums.shape[1]), 0)
    sums = jnp.concatenate([sums, jnp.zeros((n_func - n_tiles, sums.shape[1]), jnp.float32)], axis=0)
    n_diag = inverse_ref.shape[0]
    totals = []
    for d in range(n_diag):
        minus = -jnp.sum(table_ref[d], axis=0, keepdims=True)
        totals.append(-jnp.sum(minus, axis=1, keepdims=True))
        wanted = jnp.where(line == n_tiles, minus, sums)
        high, low = halves(inverse_ref[d])
        right = jnp.concatenate([high, high, low], axis=0)
        solved = jnp.dot(left_operand(wanted), right, preferred_element_type=jnp.float32)
        solved = jnp.where(line == n_tiles + 1, 1.0, solved)
        functional_ref[d * n_func : (d + 1) * n_func, :] = left_operand(solved)
    send(functional_ref, functional_out)

    lists = list_ref[...]
    asker = lax.broadcasted_iota(jnp.int32, lists.shape, 0)
    codes = asker * rows + below(over(lists, rows * n_tiles), rows)
    codes = jnp.where(lists > 0, codes, -1).astype(jnp.float32)
    spread = lax.broadcasted_iota(jnp.int32, (slots, n_rows), 0)
    spread = lax.div(spread, cap) == lax.broadcasted_iota(jnp.int32, (slots, n_rows), 1)
    codes = jnp.dot(
        jnp.where(spread, 1.0, 0.0), codes, precision=HIGH, preferred_element_type=jnp.float32
    )
    rank = lax.rem(lax.broadcasted_iota(jnp.int32, codes.shape, 0), cap)
    lane = lax.broadcasted_iota(jnp.int32, codes.shape, 1)
    asked = jnp.sum(jnp.where(rank == lane, codes, 0.0), axis=1, keepdims=True)
    asked = jnp.where(asked < 0.0, asked - 0.5, asked + 0.5).astype(jnp.int32)
    own = lax.axis_index("rows") * rows + lax.broadcasted_iota(jnp.int32, (rows, 1), 0)
    band = lax.axis_index("band")

    def field(n, which):
        return field_ref[n, pl.ds(which, 1), :]

    row_ids = lax.broadcasted_iota(jnp.int32, (1, band_rows), 1)
    sides = []
    for which, targets in ((band, jnp.concatenate([asked, own], axis=0)), (1 - band, own)):
        across = jnp.where(which == 0, field(2 + width_k, 1), field(3 + width_k, 0))
        takers = [field(2 + k, which) * n_groups + field(0, which) for k in range(width_k)]
        takers.append(across * n_groups + field(0, 1 - which))
        takers = jnp.concatenate(takers, axis=1)
        origins = [field(4 + width_k + k, which) for k in range(width_k)] + [row_ids]
        hits = one_hot(targets, jnp.concatenate(origins, axis=1))
        sides.append((takers, hits, field(0, which)))
    for t in range(n_tiles):
        found = []
        for takers, hits, _ in sides:
            ids = lax.broadcasted_iota(jnp.int32, (n_groups, takers.shape[1]), 0) + t * n_groups
            found.append(dot_nt(one_hot(ids, takers), hits))
        count_ref[t] = jnp.concatenate(found, axis=1).astype(jnp.bfloat16)
        send(count_ref.at[t], count_out.at[t])
    ids = lax.broadcasted_iota(jnp.int32, (n_groups, band_rows), 0)
    found = [dot_nt(one_hot(ids, groups), hits[:, -band_rows:]) for _, hits, groups in sides]
    found = jnp.concatenate(found, axis=1)
    count_ref[n_tiles] = found.astype(jnp.bfloat16)
    send(count_ref.at[n_tiles], count_out.at[n_tiles])
    block = lax.broadcasted_iota(jnp.int32, found.shape, 1)
    mine = (block >= slots) & (block < slots + rows)
    count_ref[n_tiles + 1] = jnp.where(mine, found, 0.0).astype(jnp.bfloat16)
    send(count_ref.at[n_tiles + 1], count_out.at[n_tiles + 1])

    per_tile = LANES // n_rhs
    depth = rows // per_tile
    length = n_rows * 2 * depth
    order = lax.broadcasted_iota(jnp.int32, (per_tile * length, 1), 0)
    spot, order = lax.div(order, length), lax.rem(order, length)
    device, order = lax.div(order, 2 * depth), lax.rem(order, 2 * depth)
    side, order = lax.div(order, depth), lax.rem(order, depth)
    order = side * band_rows + device * rows + spot * depth + order
    member = [one_hot(ids, field(0, which)) for which in range(2)]
    placing = jnp.zeros(placing_ref.shape, jnp.float32)
    for which in range(2):
        placing = placing + dot_nt(one_hot(order, row_ids + which * band_rows), member[which])
    placing_ref[...] = placing.astype(jnp.bfloat16)
    send(placing_ref, placing_out)
    whole = jnp.zeros((n_groups, 1), jnp.float32)
    for which in range(2):
        sums = jnp.zeros((1, band_rows), jnp.float32)
        for d in range(n_diag):
            sums = jnp.where(field(1, which) == d, totals[d], sums)
        weighted = jnp.where(ids == field(0, which), sums, 0.0)
        whole = whole + jnp.sum(weighted, axis=1, keepdims=True)
    scale = place(placing_ref, jnp.broadcast_to(whole, (n_groups, LANES)), n_rhs)
    mine = jnp.zeros(scale_ref.shape, jnp.float32)
    here = lax.axis_index("rows") * 2 + band
    for n in range(2 * n_rows):
        mine = jnp.where(here == n, scale[n * depth : (n + 1) * depth, :], mine)
    scale_ref[...] = mine
    finish(copies)


def gather_solve(
    sizes, slots, diags, arrived_ref, later, terms, inverse_ref, sum_ref, product_ref
):
    rows, n_rows, cap, n_tiles, n_rhs = sizes
    per = n_rows * cap // arrived_ref.shape[0]
    for row in range(rows):
        total = None
        for slot in slots(row):
            start = pl.multiple_of(below(slot, per) * n_rhs, n_rhs)
            block = arrived_ref[over(slot, per), pl.ds(start, n_rhs), :]
            total = block if total is None else total + block
        sum_ref[pl.ds(row * n_rhs, n_rhs), :] = total
    finish(later)
    total = sum_ref[...]
    for term in terms:
        total = total + term[...].reshape(total.shape)
    table_products(total, inverse_ref, product_ref)
    for row in range(rows):
        sum_ref[pl.ds(row * n_rhs, n_rhs), :] = product_ref[diags(row) * rows + row]


def middle_kernel(sizes, width_k, n_band, dense, *refs):
    meta_ref, arrived_ref, inverse_ref, tile_ref = refs[:4]
    terms_in, refs = refs[4 : 5 + n_band], refs[5 + n_band :]
    extra, refs = (refs[:3], refs[3:]) if dense else ((), refs)
    send_out, band_out, refs = refs[0], refs[1 : 1 + n_band], refs[1 + n_band :]
    sum_ref, product_ref, request_ref, near_ref, send_ref = refs[:5]
    terms, band_refs, refs = refs[5 : 6 + n_band], refs[6 + n_band : 6 + 2 * n_band], refs[6 + 2 * n_band :]
    term_sems, meta_sems, send_sems, refs = *refs[:3], refs[3:]
    right_ref = terms[0]
    rows, n_rows, cap, n_tiles, n_rhs = sizes
    body = cap * n_rhs
    metadata = started(metadata_copies(meta_ref, request_ref, near_ref, meta_sems))
    pairs = enumerate(zip(terms_in, terms))
    later = started([pltpu.make_async_copy(i, h, term_sems.at[n]) for n, (i, h) in pairs])
    fetched = []
    if dense:
        held, extra_sems, value_ref, spread_ref = refs[:3], refs[3], refs[4], refs[5]
        n_diag = inverse_ref.shape[0]
        pairs = enumerate(zip(extra, held))
        fetched = started([pltpu.make_async_copy(i, h, extra_sems.at[n]) for n, (i, h) in pairs])
    finish(metadata)
    mine = lax.axis_index("rows")

    def slots(row):
        field = LANES + (4 + 2 * width_k) * rows + row
        return [request_ref[mine, 0, field + k * rows] for k in range(width_k)]

    def diags(row):
        return request_ref[mine, 0, LANES + rows + row]

    gather_solve(sizes, slots, diags, arrived_ref, later, terms, inverse_ref, sum_ref, product_ref)
    table_products(sum_ref[...], tile_ref, product_ref)
    copies = []

    def send(source, target):
        copies.extend(started([pltpu.make_async_copy(source, target, send_sems.at[len(copies)])]))

    for owner in range(n_rows):
        for rank in range(cap):
            block = product_ref[below(request_ref[owner, 0, rank], rows * n_tiles)]
            send_ref[owner, rank * n_rhs : (rank + 1) * n_rhs, :] = block
        if not dense:
            send(send_ref.at[owner], send_out.at[owner])
        else:
            send(send_ref.at[owner, pl.ds(0, body)], send_out.at[owner, pl.ds(0, body)])
    pack_bands(sizes, width_k, product_ref, near_ref, band_refs)
    for ref, out in zip(band_refs, band_out):
        send(ref, out)
    if dense:
        finish(fetched)
        kinds = []
        for owner in range(n_rows):
            for rank in range(cap):
                code = over(request_ref[owner, 0, rank], rows * n_tiles * rows)
                kinds.append(below(code, n_diag))
        kinds += [diags(row) for row in range(rows)]
        kinds += [near_ref[0, 0, LANES + rows + row] for row in range(rows)]
        result = coarse_parts(
            sizes, kinds, held, right_ref, send_ref, band_refs, value_ref, spread_ref
        )
        depth = result.shape[0] // n_rows
        for owner in range(n_rows):
            send_ref[owner, body:, :] = result[owner * depth : (owner + 1) * depth, :]
        send(send_ref.at[:, pl.ds(body, depth)], send_out.at[:, pl.ds(body, depth)])
    finish(copies)


def coarse_parts(sizes, kinds, held, right_ref, send_ref, band_refs, value_ref, spread_ref):
    functional_ref, count_ref, place_ref = held
    rows, n_rows, cap, n_tiles, n_rhs = sizes
    body = cap * n_rhs
    n_func = spread_ref.shape[0] // count_ref.shape[2]
    per_tile = LANES // n_rhs
    functional = functional_ref[...]
    done = 0
    for owner in range(0, n_rows, 2):
        values = [send_ref[owner + more, :body, :] for more in range(2)]
        values = jnp.concatenate(values, axis=0)
        value_ref[:, done : done + 2 * body] = dot_nt(functional, right_operand(values))
        done += 2 * body
    for ref in (right_ref, *band_refs):
        values = ref[...].reshape(rows * n_rhs, -1)
        value_ref[:, done : done + rows * n_rhs] = dot_nt(functional, right_operand(values))
        done += rows * n_rhs
    lane = lax.broadcasted_iota(jnp.int32, (n_func, LANES), 1)
    for block, kind in enumerate(kinds):
        tile, spot = block // per_tile, block % per_tile
        start = pl.multiple_of(kind * n_func, n_func)
        piece = value_ref[pl.ds(start, n_func), tile * LANES : (tile + 1) * LANES]
        piece = jnp.where((lane >= spot * n_rhs) & (lane < (spot + 1) * n_rhs), piece, 0.0)
        spread_ref[block * n_func : (block + 1) * n_func, :] = piece
    partial = jnp.zeros((count_ref.shape[1], 2 * LANES), jnp.float32)
    for t in range(count_ref.shape[0]):
        values = spread_ref[pl.ds(t, done // n_rhs, stride=n_func), :]
        partial = partial + jnp.dot(
            count_ref[t],
            jnp.concatenate(halves(values), axis=1),
            preferred_element_type=jnp.float32,
        )
    partial = partial[:, :LANES] + partial[:, LANES:]
    source = lax.broadcasted_iota(jnp.int32, (LANES, LANES), 0)
    target = lax.broadcasted_iota(jnp.int32, (LANES, LANES), 1)
    same = jnp.where(lax.rem(source, n_rhs) == lax.rem(target, n_rhs), 1.0, 0.0)
    same = same.astype(jnp.bfloat16)
    same = jnp.concatenate([same, same], axis=0)
    partial = jnp.dot(
        jnp.concatenate(halves(partial), axis=1), same, preferred_element_type=jnp.float32
    )
    return place(place_ref, partial, n_rhs)


def part_kernel(arrived_ref, mine_ref, other_ref):
    depth = mine_ref.shape[0]
    body = arrived_ref.shape[1] - 2 * depth
    total = arrived_ref[0, body:, :]
    for source in range(1, arrived_ref.shape[0]):
        total = total + arrived_ref[source, body:, :]
    upper = lax.axis_index("band") == 0
    mine_ref[...] = jnp.where(upper, total[:depth], total[depth:])
    other_ref[...] = jnp.where(upper, total[depth:], total[:depth])


def last_kernel(sizes, width_k, n_band, *refs):
    meta_ref, arrived_ref, inverse_ref = refs[:3]
    terms_in, refs = refs[3 : 4 + n_band], refs[4 + n_band :]
    second_ref, sum_ref, product_ref, mine_ref = refs[:4]
    terms, (term_sems, meta_sem) = refs[4 : 5 + n_band], refs[5 + n_band :]
    rows, n_rows = sizes[:2]
    place = lax.axis_index("band") * n_rows + lax.axis_index("rows")
    metadata = pltpu.make_async_copy(meta_ref.at[pl.ds(place, 1)], mine_ref, meta_sem)
    metadata.start()
    pairs = enumerate(zip(terms_in, terms))
    later = started([pltpu.make_async_copy(i, h, term_sems.at[n]) for n, (i, h) in pairs])
    metadata.wait()

    def slots(row):
        field = LANES + (4 + 3 * width_k) * rows + row
        return [mine_ref[0, 0, field + k * rows] for k in range(width_k)]

    def diags(row):
        return mine_ref[0, 0, LANES + rows + row]

    gather_solve(sizes, slots, diags, arrived_ref, later, terms, inverse_ref, sum_ref, product_ref)
    second_ref[...] = sum_ref[...].reshape(second_ref.shape)


def final_kernel(sizes, mine_ref, other_ref, scale_ref, second_ref, out_ref):
    rows, n_rhs = sizes[0], sizes[4]
    depth = scale_ref.shape[0]
    correction = (mine_ref[...] + other_ref[...]) / scale_ref[...]
    padded = jnp.concatenate([correction, jnp.zeros((8 - depth, LANES), jnp.float32)], axis=0)
    turned = padded.T
    for row in range(rows):
        spot, place = row // depth, row % depth
        column = turned[spot * n_rhs : (spot + 1) * n_rhs, place : place + 1]
        out_ref[row] = second_ref[row] + column


def shifted(value, axis, steps):
    count = lax.axis_size(axis)
    initial, last = (max(0, -steps), min(count, count - steps))
    return lax.ppermute(value, axis, [(source, source + steps) for source in range(initial, last)])


def to_bands(sends):
    if len(sends) == 1:
        return (lax.ppermute(sends[0], "band", [(0, 1), (1, 0)]),)
    return shifted(sends[0], "band", 1), shifted(sends[1], "band", -1)


def on_device(
    start_iterate,
    right_side,
    diag_table,
    inverse_table,
    coupling_tiles,
    diag_index,
    tile_index,
    source_owner,
    source_local,
    aggregate_map,
):
    rows, n_rhs, states = start_iterate.shape
    width_k = source_owner.shape[1]
    n_tiles, n_diag = coupling_tiles.shape[0], inverse_table.shape[0]
    n_rows, n_bands = lax.axis_size("rows"), lax.axis_size("band")
    n_dev = n_rows * n_bands
    cap = max(2, 2 * width_k * rows // n_rows)
    slots = n_rows * cap
    total_groups = AGG_DEV * n_dev
    per_tile = LANES // n_rhs
    depth = rows // per_tile
    n_func = 16
    dense = (
        n_bands == 2
        and n_dev * rows * total_groups <= DENSE_LIMIT
        and depth == 4
        and n_diag * n_func == LANES
        and n_tiles + 2 <= n_func
    )
    sizes = (rows, n_rows, cap, n_tiles, n_rhs)
    f32, i32 = jnp.float32, jnp.int32
    my_band = lax.axis_index("band")
    my_row = lax.axis_index("rows")

    half = n_rows // 2
    wide = LANES + -(-(4 + 4 * width_k) * rows // LANES) * LANES
    index_shapes = [(width_k, rows), (width_k, rows), (width_k + 2, rows), (1, rows), (1, rows)]
    payload = call(
        functools.partial(request_kernel, (rows, n_rows, cap, n_tiles, n_diag)),
        jax.ShapeDtypeStruct((n_dev, 1, wide), i32),
        [HBM] * 5,
        VMEM,
        [*[pltpu.VMEM(shape, i32) for shape in index_shapes], pltpu.SemaphoreType.DMA((5,))],
    )(source_owner.T, source_local.T, tile_index.T, diag_index[None], aggregate_map.T)
    payload, to_mirror = lax.optimization_barrier((payload, start_iterate))
    mirror = lax.ppermute(to_mirror, "rows", [(i, (i + half) % n_rows) for i in range(n_rows)])
    meta = lax.all_to_all(payload, ("band", "rows"), split_axis=0, concat_axis=0, tiled=True)

    n_ways = 1 if n_bands == 2 else 2
    block = (rows, n_rhs, states)
    band_shapes = [jax.ShapeDtypeStruct(block, f32)] * n_ways
    band_scratch = [pltpu.VMEM(block, f32)] * n_ways
    term_scratch = [pltpu.VMEM(block, f32)] * (1 + n_ways)
    term_sems = pltpu.SemaphoreType.DMA((1 + n_ways,))
    meta_scratch = [pltpu.SMEM((n_rows, 1, wide), i32), pltpu.SMEM((n_ways, 1, wide), i32)]
    meta_sems = pltpu.SemaphoreType.DMA((1 + n_ways,))
    flat = rows * n_rhs
    sums = pltpu.VMEM((flat, states), f32)
    products = pltpu.VMEM((max(n_tiles, n_diag) * rows, n_rhs, states), f32)
    work = 6 * flat * states * states
    made_shape = (n_tiles * rows, n_rhs, states)
    table_scratch = [pltpu.VMEM(coupling_tiles.shape, f32)]
    table_sems = pltpu.SemaphoreType.DMA((-(-n_tiles // 2),))
    made = call(
        product_kernel,
        jax.ShapeDtypeStruct(made_shape, f32),
        [HBM, HBM],
        HBM,
        [
            pltpu.VMEM(block, f32),
            *table_scratch,
            pltpu.VMEM(made_shape, f32),
            pltpu.SemaphoreType.DMA((1 + n_tiles,)),
            table_sems,
        ],
        work * n_tiles,
        4 << 20,
    )(start_iterate, coupling_tiles)
    packed, *bands = call(
        functools.partial(first_kernel, sizes, width_k, n_ways),
        (jax.ShapeDtypeStruct((half, 2 * cap, n_rhs, states), f32), *band_shapes),
        [HBM, VMEM, HBM, ANY],
        [HBM] * (1 + n_ways),
        [
            pltpu.VMEM((2, *made_shape), f32),
            *table_scratch,
            *meta_scratch,
            pltpu.VMEM((half, 2 * cap, n_rhs, states), f32),
            *band_scratch,
            pltpu.SemaphoreType.DMA((n_tiles,)),
            table_sems,
            meta_sems,
            pltpu.SemaphoreType.DMA((half + n_ways,)),
        ],
        work * n_tiles,
        4 << 20,
    )(made, mirror, coupling_tiles, meta)
    sends = (packed.reshape(half, 2 * cap * n_rhs, states), *bands)
    halves_of_rows = [list(range(half)), list(range(half, n_rows))]
    late, *sends = lax.optimization_barrier((meta, *sends))

    def exchange(sends, groups=None):
        arrived = lax.all_to_all(
            sends[0], "rows", split_axis=0, concat_axis=0, tiled=True, axis_index_groups=groups
        )
        return arrived, to_bands(sends[1:])

    arrived_blocks, arrived_bands = exchange(sends, halves_of_rows)

    late = late.reshape(n_bands, n_rows, wide)
    requests = lax.dynamic_index_in_dim(late[:, :, :LANES], my_band, 0, keepdims=False)
    common = late[:, :, LANES:]
    extra, extra_scratch, tail = (), [], 0
    if dense:
        fields = common[:, :, : (4 + 2 * width_k) * rows].reshape(n_bands, n_rows, -1, rows).transpose(2, 0, 1, 3)
        fields = fields.reshape(-1, n_bands, n_rows * rows)
        n_blocks = slots + 2 * rows
        length = n_dev * depth
        extra_shapes = [
            ((n_diag * n_func, 3 * states), jnp.bfloat16),
            ((n_tiles + 2, total_groups, n_blocks), jnp.bfloat16),
            ((per_tile * length, total_groups), jnp.bfloat16),
        ]
        functional_shape, count_shape, placing_shape = extra_shapes
        counts, functionals, placing, scale = call(
            functools.partial(count_kernel, sizes, width_k, n_func),
            (
                jax.ShapeDtypeStruct(*count_shape),
                jax.ShapeDtypeStruct(*functional_shape),
                jax.ShapeDtypeStruct(*placing_shape),
                jax.ShapeDtypeStruct((depth, LANES), f32),
            ),
            [VMEM] * 5,
            [HBM, HBM, HBM, VMEM],
            [
                pltpu.VMEM(*count_shape),
                pltpu.VMEM(*functional_shape),
                pltpu.VMEM(*placing_shape),
                pltpu.SemaphoreType.DMA((n_tiles + 4,)),
            ],
            4 * total_groups * n_tiles * n_dev * rows * n_blocks,
            4 << 20,
        )(fields, requests, coupling_tiles, diag_table, inverse_table)
        extra = (functionals, counts, placing)
        extra_scratch = [
            *[pltpu.VMEM(*shape) for shape in extra_shapes],
            pltpu.SemaphoreType.DMA((3,)),
            pltpu.VMEM((n_diag * n_func, n_blocks * n_rhs), f32),
            pltpu.VMEM((n_blocks * n_func, LANES), f32),
        ]
        tail = n_bands * depth

    send_shape = (n_rows, cap * n_rhs + tail, states)
    sends = call(
        functools.partial(middle_kernel, sizes, width_k, n_ways, dense),
        (jax.ShapeDtypeStruct(send_shape, f32), *band_shapes),
        [HBM] + [VMEM] * 3 + [HBM] + [ANY] * n_ways + [HBM] * len(extra),
        [HBM] * (1 + n_ways),
        [
            sums,
            products,
            *meta_scratch,
            pltpu.VMEM(send_shape, f32),
            *term_scratch,
            *band_scratch,
            term_sems,
            meta_sems,
            pltpu.SemaphoreType.DMA((n_rows + n_ways + 1,)),
            *extra_scratch,
        ],
        work * (n_tiles + n_diag),
        4 << 20,
    )(
        meta,
        arrived_blocks,
        inverse_table,
        coupling_tiles,
        right_side,
        *arrived_bands,
        *extra,
    )
    arrived_blocks, arrived_bands = exchange(sends)

    if dense:
        part = jax.ShapeDtypeStruct((depth, LANES), f32)
        mine, other = call(part_kernel, (part, part), [VMEM], [VMEM] * 2)(arrived_blocks)
        other = lax.ppermute(other, "band", [(0, 1), (1, 0)])
    second = call(
        functools.partial(last_kernel, sizes, width_k, n_ways),
        jax.ShapeDtypeStruct(block, f32),
        [HBM] + [VMEM] * 2 + [HBM] + [ANY] * n_ways,
        VMEM,
        [
            sums,
            products,
            pltpu.SMEM((1, 1, wide), i32),
            *term_scratch,
            term_sems,
            pltpu.SemaphoreType.DMA,
        ],
        work * n_diag,
        4 << 20,
    )(meta, arrived_blocks, inverse_table, right_side, *arrived_bands)
    if dense:
        return call(
            functools.partial(final_kernel, sizes),
            jax.ShapeDtypeStruct(block, f32),
            [VMEM] * 4,
            VMEM,
        )(mine, other, scale, second)

    groups = aggregate_map[:, 0]
    own = jnp.arange(rows, dtype=i32)
    groups_all = common[:, :, :rows]
    diags_all = common[:, :, rows : 2 * rows]
    codes = requests[:, :cap]
    asked = lax.broadcasted_iota(i32, codes.shape, 0) * rows + codes // (rows * n_tiles) % rows
    asked = jnp.where(codes > 0, asked, -1).reshape(-1)
    table_sums = jnp.sum(diag_table, axis=(1, 2))
    diag_onehot = diags_all.reshape(-1, 1) == jnp.arange(n_diag, dtype=i32)[None]
    block_sums = jnp.sum(jnp.where(diag_onehot, table_sums[None], 0.0), axis=1)
    whole_diag = jnp.sum(
        jnp.where(groups[:, None] == groups_all.reshape(-1)[None], block_sums[None], 0.0), axis=1
    )
    here = lax.dynamic_index_in_dim(common, my_row, 1, keepdims=False)
    above = lax.dynamic_index_in_dim(here, jnp.minimum(my_band + 1, n_bands - 1), 0, keepdims=False)
    below = lax.dynamic_index_in_dim(here, jnp.maximum(my_band - 1, 0), 0, keepdims=False)
    place_of = (2 + width_k) * rows
    band_tiles = jnp.stack([above[place_of : place_of + rows], below[place_of + rows : place_of + 2 * rows]])
    band_groups = jnp.stack([above[:rows], below[:rows]])
    band_valid = jnp.stack([my_band + 1 < n_bands, my_band > 0])
    band_valid = jnp.broadcast_to(band_valid[:, None], (2, rows))
    n_all = n_tiles + n_diag + 1
    code = codes.reshape(-1)
    band_of_mine = lax.dynamic_index_in_dim(groups_all, my_band, 0, keepdims=False).reshape(-1)
    entry_group = jnp.concatenate(
        [jnp.take(band_of_mine, jnp.maximum(asked, 0)), band_groups.reshape(-1), groups, groups]
    )
    entry_func = jnp.concatenate(
        [
            (code % rows) * n_all + (code // rows) % n_tiles,
            (own[None] * n_all + band_tiles).reshape(-1),
            own * n_all + n_tiles + diag_index,
            own * n_all + n_tiles + n_diag,
        ]
    )
    entry_valid = jnp.concatenate([asked >= 0, band_valid.reshape(-1), jnp.ones((2 * rows,), bool)])
    functionals = jnp.concatenate(
        [jnp.sum(coupling_tiles, axis=1), -jnp.sum(diag_table, axis=1)], axis=0
    )
    weights = jnp.einsum("fp,rcp->rfc", functionals, second, precision=HIGH)
    weights = jnp.concatenate([weights, jnp.sum(right_side, axis=2)[:, None]], axis=1)
    chosen = jnp.take(weights.reshape(rows * n_all, n_rhs), entry_func, axis=0)
    chosen = jnp.where(entry_valid[:, None], chosen, 0.0)
    partial = jax.ops.segment_sum(chosen, entry_group, num_segments=total_groups)
    whole = lax.psum(partial, ("band", "rows"))
    correction = jnp.take(whole, groups, axis=0) / whole_diag[:, None]
    return second + correction[:, :, None]


def solution(mesh):
    in_specs = (
        P(("band", "rows"), None, None),
        P(("band", "rows"), None, None),
        P(),
        P(),
        P(),
        P(("band", "rows")),
        P(("band", "rows"), None),
        P(("band", "rows"), None),
        P(("band", "rows"), None),
        P(("band", "rows"), None),
    )
    out_specs = P(("band", "rows"), None, None)
    return jax.shard_map(
        on_device, mesh=mesh, in_specs=in_specs, out_specs=out_specs, check_vma=False
    )
```

```python
import functools

import jax
import jax.numpy as jnp
from jax import lax
from jax.experimental import pallas as pl
from jax.experimental.pallas import tpu as pltpu
from jax.sharding import PartitionSpec as P

AGG_DEV = 8
LANES = 128
DENSE_LIMIT = 1 << 19

VMEM = pl.BlockSpec(memory_space=pltpu.VMEM)
SMEM = pl.BlockSpec(memory_space=pltpu.SMEM)
HBM = pl.BlockSpec(memory_space=pltpu.HBM)
ANY = pl.BlockSpec(memory_space=pl.ANY)
HIGH = lax.Precision.HIGHEST


def params():
    return pltpu.CompilerParams(vmem_limit_bytes=24 * 1024 * 1024)


def call(kernel, out_shape, in_specs, out_specs, scratch=(), flops=0, moved=0):
    def shaped(shape, spec):
        return pltpu.HBM(shape.shape, shape.dtype) if spec is HBM else shape

    if isinstance(out_shape, (tuple, list)):
        out_shape = [shaped(*pair) for pair in zip(out_shape, out_specs)]
    else:
        out_shape = shaped(out_shape, out_specs)
    run = pl.pallas_call(
        kernel,
        out_shape=out_shape,
        in_specs=in_specs,
        out_specs=out_specs,
        scratch_shapes=list(scratch),
        compiler_params=params(),
        cost_estimate=pl.CostEstimate(flops=flops, bytes_accessed=moved, transcendentals=0),
    )

    def apply(*args):
        pinned = [
            pltpu.with_memory_space_constraint(arg, pltpu.HBM) if spec is HBM else arg
            for arg, spec in zip(args, in_specs)
        ]
        return run(*pinned)

    return apply


def below(value, bound):
    return value & (bound - 1) if bound & (bound - 1) == 0 else lax.rem(value, bound)


def over(value, bound):
    if bound & (bound - 1) == 0:
        return lax.shift_right_logical(value, bound.bit_length() - 1)
    return lax.div(value, bound)


def halves(value):
    high = value.astype(jnp.bfloat16)
    low = (value - high.astype(jnp.float32)).astype(jnp.bfloat16)
    return high, low


def left_operand(value):
    high, low = halves(value)
    return jnp.concatenate([high, low, high], axis=1)


def right_operand(value):
    high, low = halves(value)
    return jnp.concatenate([high, high, low], axis=1)


def dot_nt(left, right):
    return lax.dot_general(
        left, right, (((1,), (1,)), ((), ())), preferred_element_type=jnp.float32
    )


def table_products(value, table_ref, out_ref, done=None, loads=None):
    left = left_operand(value)
    count, width = table_ref.shape[0], table_ref.shape[1]
    n_rhs = out_ref.shape[1]
    rows = left.shape[0] // n_rhs
    for first in range(0, count, 2):
        last = min(first + 2, count)
        if loads is not None:
            loads[first // 2].wait()
        right = right_operand(table_ref[first:last].reshape((last - first) * width, -1))
        product = dot_nt(left, right)
        for t in range(first, last):
            part = product[:, (t - first) * width : (t - first + 1) * width]
            out_ref[t * rows : (t + 1) * rows] = part.reshape(rows, n_rhs, width)
        if done is not None:
            done(first * rows, (last - first) * rows)


def started(copies):
    for copy in copies:
        copy.start()
    return copies


def finish(copies):
    for copy in copies:
        copy.wait()


def request_kernel(sizes, *refs):
    rows, n_rows, cap, n_tiles, n_diag = sizes
    inputs, (list_ref, index_ref, place_ref), held, sems = refs[:5], refs[5:8], refs[8:13], refs[13]
    finish(
        started([pltpu.make_async_copy(i, h, sems.at[n]) for n, (i, h) in enumerate(zip(inputs, held))])
    )
    owner_ref, local_ref, tile_ref, diag_ref, group_ref = held
    width_k = owner_ref.shape[0]
    half = n_rows // 2
    row_of = lax.broadcasted_iota(jnp.int32, (rows, rows), 0)
    col_of = lax.broadcasted_iota(jnp.int32, (rows, rows), 1)
    lane = lax.broadcasted_iota(jnp.int32, (rows, LANES), 1)
    owners = lax.broadcasted_iota(jnp.int32, (n_rows, rows), 0)

    def column(row):
        return jnp.sum(jnp.where(row_of == col_of, row, 0), axis=1, keepdims=True)

    def owner_row(k):
        return owner_ref[k : k + 1, :]

    row_ids = lax.broadcasted_iota(jnp.int32, (1, rows), 1)
    owner_columns = [column(owner_row(k)) for k in range(width_k)]
    lists = jnp.zeros((n_rows, LANES), jnp.float32)
    places, half_places = [], []
    for k in range(width_k):
        rank = jnp.zeros((1, rows), jnp.int32)
        for other in range(k + 1):
            match = owner_columns[other] == owner_row(k)
            if other == k:
                match = match & (row_of < col_of)
            rank = rank + jnp.sum(jnp.where(match, 1, 0), axis=0, keepdims=True)
        places.append(owner_row(k) * cap + rank)
        same = (owner_row(k) >= half) == (lax.axis_index("rows") >= half)
        holder = jnp.where(owner_row(k) >= half, owner_row(k) - half, owner_row(k))
        half_places.append(holder * (2 * cap) + rank + jnp.where(same, 0, cap))
        taker = row_ids + rows * (diag_ref[...] + n_diag)
        code = local_ref[k : k + 1, :] + rows * (tile_ref[k : k + 1, :] + n_tiles * taker)
        code, rank = column(code), column(rank)
        mirror = jnp.where(owner_row(k) >= half, owner_row(k) - half, owner_row(k) + half)
        for owner, base in ((owner_row(k), 0), (mirror, LANES // 2)):
            by_rank = jnp.where(lane == rank + base, code, 0).astype(jnp.float32)
            mine = jnp.where(owners == owner, 1.0, 0.0)
            lists = lists + jnp.dot(
                mine, by_rank, precision=HIGH, preferred_element_type=jnp.float32
            )
    lists = (lists + 0.5).astype(jnp.int32)
    upper = lax.axis_index("rows") >= half
    lists = jnp.where(upper, lists[half:], lists[:half])

    def joined(parts, wide):
        spare = wide - len(parts) * rows
        if spare:
            parts = [*parts, jnp.zeros((1, spare), jnp.int32)]
        return jnp.concatenate(parts, axis=1)

    index = [group_ref[...], diag_ref[...]]
    index += [tile_ref[k : k + 1, :] for k in range(width_k + 2)]
    index += [owner_row(k) * rows + local_ref[k : k + 1, :] for k in range(width_k)]
    index = joined(index, index_ref.shape[2])
    index_ref[0] = index
    place_ref[0] = joined(half_places + places, place_ref.shape[2])
    for device in range(half):
        list_ref[device] = jnp.concatenate([lists[device : device + 1, :], index], axis=1)


def copies_of(pairs, sems):
    return started([pltpu.make_async_copy(i, h, sems.at[n]) for n, (i, h) in enumerate(pairs)])


def band_field(rows, width_k, way, n_ways):
    field = (2 + width_k) * rows
    if n_ways == 1:
        return field + jnp.where(lax.axis_index("band") == 0, 0, rows)
    return field + way * rows


def pack_bands(sizes, width_k, product_ref, near_ref, band_refs):
    rows = sizes[0]
    for way, band_ref in enumerate(band_refs):
        field = band_field(rows, width_k, way, len(band_refs))
        for row in range(rows):
            band_ref[row] = product_ref[near_ref[way, 0, field + row] * rows + row]


def table_loads(table_in, table_ref, sems):
    copies = []
    for first in range(0, table_in.shape[0], 2):
        place = pl.ds(first, min(2, table_in.shape[0] - first))
        source, target = table_in.at[place], table_ref.at[place]
        copies.append(pltpu.make_async_copy(source, target, sems.at[first // 2]))
    return started(copies)


def product_kernel(start_in, tile_in, product_out, start_ref, tile_ref, product_ref, sems, tile_sems):
    start = pltpu.make_async_copy(start_in, start_ref, sems.at[0])
    start.start()
    loads = table_loads(tile_in, tile_ref, tile_sems)
    start.wait()
    copies = []

    def done(first, count):
        place = pl.ds(first, count)
        source, target = product_ref.at[place], product_out.at[place]
        copies.extend(started([pltpu.make_async_copy(source, target, sems.at[1 + len(copies)])]))

    rows, n_rhs, states = start_ref.shape
    values = start_ref[...].reshape(rows * n_rhs, states)
    table_products(values, tile_ref, product_ref, done, loads)
    finish(copies)


def first_kernel(sizes, width_k, n_band, *refs):
    rows, n_rows, cap, n_tiles, n_rhs = sizes
    product_in, mirror_ref, tile_ref, list_in, near_in, send_out = refs[:6]
    band_out, refs = refs[6 : 6 + n_band], refs[6 + n_band :]
    product_ref, list_ref, near_ref, send_ref = refs[:4]
    band_refs, (load_sems, meta_sems, send_sems) = refs[4 : 4 + n_band], refs[4 + n_band :]
    list_in = list_in.at[:, :, pl.ds(0, LANES)]
    metadata = copies_of(((list_in, list_ref), (near_in, near_ref)), meta_sems)
    places = [pl.ds(tile * rows, rows) for tile in range(n_tiles)]
    loads = [(product_in.at[place], product_ref.at[0, place]) for place in places]
    loads = copies_of(loads, load_sems)
    values = mirror_ref[...].reshape(rows * n_rhs, -1)
    table_products(values, tile_ref, product_ref.at[1])
    finish(metadata)
    finish(loads)
    copies = []
    pack_bands(sizes, width_k, product_ref.at[0], near_ref, band_refs)
    half = n_rows // 2
    for n, (ref, out) in enumerate(zip(band_refs, band_out)):
        copies += started([pltpu.make_async_copy(ref, out, send_sems.at[half + n])])
    for device in range(half):
        for slot in range(2 * cap):
            side, rank = slot // cap, slot % cap
            code = list_ref[device, 0, side * (LANES // 2) + rank]
            send_ref[device, slot] = product_ref[side, below(code, rows * n_tiles)]
        copy = pltpu.make_async_copy(send_ref.at[device], send_out.at[device], send_sems.at[device])
        copies += started([copy])
    finish(copies)


def place(place_ref, values, n_rhs, n_parts):
    per_tile = LANES // n_rhs
    length = place_ref.shape[0] // per_tile
    parts, rest = [], values
    for _ in range(n_parts):
        part = rest.astype(jnp.bfloat16)
        rest = rest - part.astype(jnp.float32)
        parts.append(part)
    parts = jnp.concatenate(parts, axis=1)
    lane = lax.broadcasted_iota(jnp.int32, (length, LANES), 1)
    result = jnp.zeros((length, LANES), jnp.float32)
    for spot in range(per_tile):
        chosen = jnp.dot(
            place_ref[spot * length : (spot + 1) * length, :],
            parts,
            preferred_element_type=jnp.float32,
        )
        chosen = sum(chosen[:, n * LANES : (n + 1) * LANES] for n in range(n_parts))
        result = jnp.where((lane >= spot * n_rhs) & (lane < (spot + 1) * n_rhs), chosen, result)
    return result


def one_hot(ids, row):
    return jnp.where(ids == row, 1.0, 0.0).astype(jnp.bfloat16)


def count_kernel(sizes, width_k, n_func, *refs):
    rows, n_rows, cap, n_tiles, n_rhs = sizes
    field_ref, list_ref, mirror_list_ref, tile_ref, table_ref, inverse_ref = refs[:6]
    count_out, functional_out, placing_out, scale_ref = refs[6:10]
    count_ref, functional_ref, placing_ref, sems = refs[10:]
    n_groups, n_blocks = count_ref.shape[1:]
    slots, band_rows = n_rows * cap, n_rows * rows
    copies = []

    def send(source, target):
        copies.extend(started([pltpu.make_async_copy(source, target, sems.at[len(copies)])]))

    sums = jnp.sum(tile_ref[...], axis=1)
    line = lax.broadcasted_iota(jnp.int32, (n_func, sums.shape[1]), 0)
    sums = jnp.concatenate([sums, jnp.zeros((n_func - n_tiles, sums.shape[1]), jnp.float32)], axis=0)
    n_diag = inverse_ref.shape[0]
    totals = []
    for d in range(n_diag):
        minus = -jnp.sum(table_ref[d], axis=0, keepdims=True)
        totals.append(-jnp.sum(minus, axis=1, keepdims=True))
        wanted = jnp.where(line == n_tiles, minus, sums)
        high, low = halves(inverse_ref[d])
        right = jnp.concatenate([high, high, low], axis=0)
        solved = jnp.dot(left_operand(wanted), right, preferred_element_type=jnp.float32)
        solved = jnp.where(line == n_tiles + 1, 1.0, solved)
        functional_ref[d * n_func : (d + 1) * n_func, :] = left_operand(solved)
    send(functional_ref, functional_out)

    half = n_rows // 2
    upper = lax.axis_index("rows") >= half
    asked = []
    for ref, first, lanes in (
        (list_ref, jnp.where(upper, half, 0), 0),
        (mirror_list_ref, jnp.where(upper, 0, half), LANES // 2),
    ):
        lists = ref[...]
        asker = first + lax.broadcasted_iota(jnp.int32, lists.shape, 0)
        codes = asker * rows + below(over(lists, rows * n_tiles), rows)
        codes = jnp.where(lists > 0, codes, -1).astype(jnp.float32)
        spread = lax.broadcasted_iota(jnp.int32, (slots // 2, half), 0)
        spread = lax.div(spread, cap) == lax.broadcasted_iota(jnp.int32, (slots // 2, half), 1)
        codes = jnp.dot(
            jnp.where(spread, 1.0, 0.0), codes, precision=HIGH, preferred_element_type=jnp.float32
        )
        rank = lax.rem(lax.broadcasted_iota(jnp.int32, codes.shape, 0), cap)
        lane = lax.broadcasted_iota(jnp.int32, codes.shape, 1)
        codes = jnp.sum(jnp.where(rank + lanes == lane, codes, 0.0), axis=1, keepdims=True)
        asked.append(jnp.where(codes < 0.0, codes - 0.5, codes + 0.5).astype(jnp.int32))
    asked = jnp.concatenate(asked, axis=0)
    own = lax.axis_index("rows") * rows + lax.broadcasted_iota(jnp.int32, (rows, 1), 0)
    band = lax.axis_index("band")

    def field(n, side):
        return field_ref[n, side : side + 1, :]

    row_ids = lax.broadcasted_iota(jnp.int32, (1, band_rows), 1)
    sides = []
    for side, targets in ((0, jnp.concatenate([asked, own], axis=0)), (1, own)):
        first = band == side
        across = jnp.where(first, field(2 + width_k, 1 - side), field(3 + width_k, 1 - side))
        takers = [field(2 + k, side) * n_groups + field(0, side) for k in range(width_k)]
        takers.append(across * n_groups + field(0, 1 - side))
        takers = jnp.concatenate(takers, axis=1)
        origins = [field(4 + width_k + k, side) for k in range(width_k)] + [row_ids]
        hits = one_hot(targets, jnp.concatenate(origins, axis=1))
        sides.append((takers, hits, field(0, side)))
    for t in range(n_tiles):
        found = []
        for takers, hits, _ in sides:
            ids = lax.broadcasted_iota(jnp.int32, (n_groups, takers.shape[1]), 0) + t * n_groups
            found.append(dot_nt(one_hot(ids, takers), hits))
        count_ref[t] = jnp.concatenate(found, axis=1).astype(jnp.bfloat16)
        send(count_ref.at[t], count_out.at[t])
    ids = lax.broadcasted_iota(jnp.int32, (n_groups, band_rows), 0)
    found = [dot_nt(one_hot(ids, groups), hits[:, -band_rows:]) for _, hits, groups in sides]
    found = jnp.concatenate(found, axis=1)
    count_ref[n_tiles] = found.astype(jnp.bfloat16)
    send(count_ref.at[n_tiles], count_out.at[n_tiles])
    block = lax.broadcasted_iota(jnp.int32, found.shape, 1)
    mine = (block >= slots) & (block < slots + rows)
    count_ref[n_tiles + 1] = jnp.where(mine, found, 0.0).astype(jnp.bfloat16)
    send(count_ref.at[n_tiles + 1], count_out.at[n_tiles + 1])

    per_tile = LANES // n_rhs
    depth = rows // per_tile
    length = n_rows * 2 * depth
    order = lax.broadcasted_iota(jnp.int32, (per_tile * length, 1), 0)
    spot, order = lax.div(order, length), lax.rem(order, length)
    device, order = lax.div(order, 2 * depth), lax.rem(order, 2 * depth)
    side, order = lax.div(order, depth), lax.rem(order, depth)
    order = side * band_rows + device * rows + spot * depth + order
    member = [
        one_hot(ids, jnp.where(band == which, field(0, 0), field(0, 1))) for which in range(2)
    ]
    placing = jnp.zeros(placing_ref.shape, jnp.float32)
    for which in range(2):
        placing = placing + dot_nt(one_hot(order, row_ids + which * band_rows), member[which])
    placing_ref[...] = placing.astype(jnp.bfloat16)
    send(placing_ref, placing_out)
    whole = jnp.zeros((n_groups, 1), jnp.float32)
    for side in range(2):
        sums = jnp.zeros((1, band_rows), jnp.float32)
        for d in range(n_diag):
            sums = jnp.where(field(1, side) == d, totals[d], sums)
        weighted = jnp.where(ids == field(0, side), sums, 0.0)
        whole = whole + jnp.sum(weighted, axis=1, keepdims=True)
    scale = place(placing_ref, jnp.broadcast_to(whole, (n_groups, LANES)), n_rhs, 3)
    mine = jnp.zeros(scale_ref.shape, jnp.float32)
    here = lax.axis_index("rows") * 2 + band
    for n in range(2 * n_rows):
        mine = jnp.where(here == n, scale[n * depth : (n + 1) * depth, :], mine)
    scale_ref[...] = mine
    finish(copies)


def gather_solve(
    sizes, slots, diags, arrived_ref, later, terms, inverse_ref, sum_ref, product_ref
):
    rows, n_rows, cap, n_tiles, n_rhs = sizes
    per = n_rows * cap // arrived_ref.shape[0]
    for row in range(rows):
        total = None
        for slot in slots(row):
            start = pl.multiple_of(below(slot, per) * n_rhs, n_rhs)
            block = arrived_ref[over(slot, per), pl.ds(start, n_rhs), :]
            total = block if total is None else total + block
        sum_ref[pl.ds(row * n_rhs, n_rhs), :] = total
    finish(later)
    total = sum_ref[...]
    for term in terms:
        total = total + term[...].reshape(total.shape)
    table_products(total, inverse_ref, product_ref)
    for row in range(rows):
        sum_ref[pl.ds(row * n_rhs, n_rhs), :] = product_ref[diags(row) * rows + row]


def middle_kernel(sizes, width_k, n_band, dense, *refs):
    metadata_in, arrived_ref, inverse_ref, tile_ref = list(refs[:5]), *refs[5:8]
    for n in (2, 3):
        metadata_in[n] = metadata_in[n].at[:, :, pl.ds(0, LANES)]
    terms_in, refs = refs[8 : 9 + n_band], refs[9 + n_band :]
    extra, refs = (refs[:3], refs[3:]) if dense else ((), refs)
    send_out, band_out, refs = refs[0], refs[1 : 1 + n_band], refs[1 + n_band :]
    metadata, sum_ref, product_ref, send_ref = refs[:5], *refs[5:8]
    place_ref, index_ref, list_ref, mirror_list_ref, near_ref = metadata
    terms, band_refs, refs = refs[8 : 9 + n_band], refs[9 + n_band : 9 + 2 * n_band], refs[9 + 2 * n_band :]
    term_sems, meta_sems, send_sems, refs = *refs[:3], refs[3:]
    right_ref = terms[0]
    rows, n_rows, cap, n_tiles, n_rhs = sizes
    body, half = cap * n_rhs, n_rows // 2
    metadata = copies_of(zip(metadata_in, metadata), meta_sems)
    later = copies_of(zip(terms_in, terms), term_sems)
    fetched = []
    if dense:
        held, extra_sems, value_ref, spread_ref, result_ref = refs[:3], *refs[3:]
        n_diag = inverse_ref.shape[0]
        fetched = copies_of(zip(extra, held), extra_sems)
    finish(metadata)

    def slots(row):
        return [place_ref[0, 0, k * rows + row] for k in range(width_k)]

    def diags(row):
        return index_ref[0, 0, rows + row]

    gather_solve(sizes, slots, diags, arrived_ref, later, terms, inverse_ref, sum_ref, product_ref)
    table_products(sum_ref[...], tile_ref, product_ref)
    copies = []

    def send(source, target):
        copies.extend(started([pltpu.make_async_copy(source, target, send_sems.at[len(copies)])]))

    pack_bands(sizes, width_k, product_ref, near_ref, band_refs)
    for ref, out in zip(band_refs, band_out):
        send(ref, out)
    upper = lax.axis_index("rows") >= half
    codes, order = [], 0
    for ref, first, lanes in (
        (list_ref, jnp.where(upper, half, 0), 0),
        (mirror_list_ref, jnp.where(upper, 0, half), LANES // 2),
    ):
        for device in range(half):
            for rank in range(cap):
                code = ref[device, 0, lanes + rank]
                codes.append(code)
                block = product_ref[below(code, rows * n_tiles)]
                send_ref[order, rank * n_rhs : (rank + 1) * n_rhs, :] = block
            target = send_out.at[first + device]
            send(send_ref.at[order], target.at[pl.ds(0, body)] if dense else target)
            order += 1
    if dense:
        finish(fetched)
        kinds = [below(over(code, rows * n_tiles * rows), n_diag) for code in codes]
        kinds += [diags(row) for row in range(rows)]
        kinds += [near_ref[0, 0, rows + row] for row in range(rows)]
        result = coarse_parts(
            sizes, kinds, held, right_ref, send_ref, band_refs, value_ref, spread_ref
        )
        result_ref[...] = result.reshape(result_ref.shape)
        send(result_ref, send_out.at[:, pl.ds(body, result_ref.shape[1])])
    finish(copies)


def coarse_parts(sizes, kinds, held, right_ref, send_ref, band_refs, value_ref, spread_ref):
    functional_ref, count_ref, place_ref = held
    rows, n_rows, cap, n_tiles, n_rhs = sizes
    body = cap * n_rhs
    n_func = spread_ref.shape[0] // count_ref.shape[2]
    per_tile = LANES // n_rhs
    functional = functional_ref[...]
    done = 0
    for owner in range(0, n_rows, 2):
        values = [send_ref[owner + more] for more in range(2)]
        values = jnp.concatenate(values, axis=0)
        value_ref[:, done : done + 2 * body] = dot_nt(functional, right_operand(values))
        done += 2 * body
    for ref in (right_ref, *band_refs):
        values = ref[...].reshape(rows * n_rhs, -1)
        value_ref[:, done : done + rows * n_rhs] = dot_nt(functional, right_operand(values))
        done += rows * n_rhs
    lane = lax.broadcasted_iota(jnp.int32, (n_func, LANES), 1)
    for block, kind in enumerate(kinds):
        tile, spot = block // per_tile, block % per_tile
        start = pl.multiple_of(kind * n_func, n_func)
        piece = value_ref[pl.ds(start, n_func), tile * LANES : (tile + 1) * LANES]
        piece = jnp.where((lane >= spot * n_rhs) & (lane < (spot + 1) * n_rhs), piece, 0.0)
        spread_ref[block * n_func : (block + 1) * n_func, :] = piece
    partial = jnp.zeros((count_ref.shape[1], 2 * LANES), jnp.float32)
    for t in range(count_ref.shape[0]):
        values = spread_ref[pl.ds(t, done // n_rhs, stride=n_func), :]
        partial = partial + jnp.dot(
            count_ref[t],
            jnp.concatenate(halves(values), axis=1),
            preferred_element_type=jnp.float32,
        )
    partial = partial[:, :LANES] + partial[:, LANES:]
    source = lax.broadcasted_iota(jnp.int32, (LANES, LANES), 0)
    target = lax.broadcasted_iota(jnp.int32, (LANES, LANES), 1)
    same = jnp.where(lax.rem(source, n_rhs) == lax.rem(target, n_rhs), 1.0, 0.0)
    same = same.astype(jnp.bfloat16)
    same = jnp.concatenate([same, same], axis=0)
    partial = jnp.dot(
        jnp.concatenate(halves(partial), axis=1), same, preferred_element_type=jnp.float32
    )
    return place(place_ref, partial, n_rhs, 2)


def part_kernel(arrived_ref, mine_ref, other_ref):
    depth = mine_ref.shape[0]
    body = arrived_ref.shape[1] - 2 * depth
    total = arrived_ref[0, body:, :]
    for source in range(1, arrived_ref.shape[0]):
        total = total + arrived_ref[source, body:, :]
    upper = lax.axis_index("band") == 0
    mine_ref[...] = jnp.where(upper, total[:depth], total[depth:])
    other_ref[...] = jnp.where(upper, total[depth:], total[:depth])


def last_kernel(sizes, width_k, n_band, *refs):
    metadata_in, arrived_ref, inverse_ref = refs[:2], *refs[2:4]
    terms_in, refs = refs[4 : 5 + n_band], refs[5 + n_band :]
    second_ref, metadata, sum_ref, product_ref = refs[0], refs[1:3], *refs[3:5]
    place_ref, index_ref = metadata
    terms, (term_sems, meta_sems) = refs[5 : 6 + n_band], refs[6 + n_band :]
    rows = sizes[0]
    metadata = copies_of(zip(metadata_in, metadata), meta_sems)
    later = copies_of(zip(terms_in, terms), term_sems)
    finish(metadata)

    def slots(row):
        return [place_ref[0, 0, (width_k + k) * rows + row] for k in range(width_k)]

    def diags(row):
        return index_ref[0, 0, rows + row]

    gather_solve(sizes, slots, diags, arrived_ref, later, terms, inverse_ref, sum_ref, product_ref)
    second_ref[...] = sum_ref[...].reshape(second_ref.shape)


def final_kernel(sizes, mine_ref, other_ref, scale_ref, second_ref, out_ref):
    rows, n_rhs = sizes[0], sizes[4]
    depth = scale_ref.shape[0]
    correction = (mine_ref[...] + other_ref[...]) / scale_ref[...]
    padded = jnp.concatenate([correction, jnp.zeros((8 - depth, LANES), jnp.float32)], axis=0)
    turned = padded.T
    for row in range(rows):
        spot, place = row // depth, row % depth
        column = turned[spot * n_rhs : (spot + 1) * n_rhs, place : place + 1]
        out_ref[row] = second_ref[row] + column


def shifted(value, axis, steps):
    count = lax.axis_size(axis)
    initial, last = (max(0, -steps), min(count, count - steps))
    return lax.ppermute(value, axis, [(source, source + steps) for source in range(initial, last)])


def to_bands(sends):
    if len(sends) == 1:
        return (lax.ppermute(sends[0], "band", [(0, 1), (1, 0)]),)
    return shifted(sends[0], "band", 1), shifted(sends[1], "band", -1)


def on_device(
    start_iterate,
    right_side,
    diag_table,
    inverse_table,
    coupling_tiles,
    diag_index,
    tile_index,
    source_owner,
    source_local,
    aggregate_map,
):
    rows, n_rhs, states = start_iterate.shape
    width_k = source_owner.shape[1]
    n_tiles, n_diag = coupling_tiles.shape[0], inverse_table.shape[0]
    n_rows, n_bands = lax.axis_size("rows"), lax.axis_size("band")
    n_dev = n_rows * n_bands
    cap = max(2, 2 * width_k * rows // n_rows)
    slots = n_rows * cap
    total_groups = AGG_DEV * n_dev
    per_tile = LANES // n_rhs
    depth = rows // per_tile
    n_func = 16
    dense = (
        n_bands == 2
        and n_dev * rows * total_groups <= DENSE_LIMIT
        and depth == 4
        and n_diag * n_func == LANES
        and n_tiles + 2 <= n_func
    )
    sizes = (rows, n_rows, cap, n_tiles, n_rhs)
    f32, i32 = jnp.float32, jnp.int32
    my_band = lax.axis_index("band")
    my_row = lax.axis_index("rows")

    half = n_rows // 2
    wide = -(-(4 + 2 * width_k) * rows // LANES) * LANES
    place_wide = -(-2 * width_k * rows // LANES) * LANES
    index_shapes = [(width_k, rows), (width_k, rows), (width_k + 2, rows), (1, rows), (1, rows)]
    halves_of_rows = [list(range(half)), list(range(half, n_rows))]
    to_mirror = [(i, (i + half) % n_rows) for i in range(n_rows)]
    mirror = lax.ppermute(start_iterate, "rows", to_mirror)
    lists, index, places = call(
        functools.partial(request_kernel, (rows, n_rows, cap, n_tiles, n_diag)),
        (
            jax.ShapeDtypeStruct((half, 1, LANES + wide), i32),
            jax.ShapeDtypeStruct((1, 1, wide), i32),
            jax.ShapeDtypeStruct((1, 1, place_wide), i32),
        ),
        [HBM] * 5,
        [VMEM] * 3,
        [*[pltpu.VMEM(shape, i32) for shape in index_shapes], pltpu.SemaphoreType.DMA((5,))],
    )(source_owner.T, source_local.T, tile_index.T, diag_index[None], aggregate_map.T)
    lists = lax.all_to_all(
        lists, "rows", split_axis=0, concat_axis=0, tiled=True, axis_index_groups=halves_of_rows
    )
    if n_bands == 2:
        near = lax.ppermute(index, "band", [(0, 1), (1, 0)])
    else:
        ways = [[(b, (b + step) % n_bands) for b in range(n_bands)] for step in (-1, 1)]
        near = jnp.concatenate([lax.ppermute(index, "band", way) for way in ways], axis=0)

    n_ways = 1 if n_bands == 2 else 2
    block = (rows, n_rhs, states)
    band_shapes = [jax.ShapeDtypeStruct(block, f32)] * n_ways
    band_scratch = [pltpu.VMEM(block, f32)] * n_ways
    term_scratch = [pltpu.VMEM(block, f32)] * (1 + n_ways)
    term_sems = pltpu.SemaphoreType.DMA((1 + n_ways,))
    list_scratch = pltpu.SMEM((half, 1, LANES), i32)
    near_scratch = pltpu.SMEM((n_ways, 1, wide), i32)
    row_scratch = [pltpu.SMEM((1, 1, place_wide), i32), pltpu.SMEM((1, 1, wide), i32)]
    flat = rows * n_rhs
    sums = pltpu.VMEM((flat, states), f32)
    products = pltpu.VMEM((max(n_tiles, n_diag) * rows, n_rhs, states), f32)
    work = 6 * flat * states * states
    made_shape = (n_tiles * rows, n_rhs, states)
    table_scratch = [pltpu.VMEM(coupling_tiles.shape, f32)]
    table_sems = pltpu.SemaphoreType.DMA((-(-n_tiles // 2),))
    made = call(
        product_kernel,
        jax.ShapeDtypeStruct(made_shape, f32),
        [HBM, HBM],
        HBM,
        [
            pltpu.VMEM(block, f32),
            *table_scratch,
            pltpu.VMEM(made_shape, f32),
            pltpu.SemaphoreType.DMA((1 + n_tiles,)),
            table_sems,
        ],
        work * n_tiles,
        4 << 20,
    )(start_iterate, coupling_tiles)
    packed, *bands = call(
        functools.partial(first_kernel, sizes, width_k, n_ways),
        (jax.ShapeDtypeStruct((half, 2 * cap, n_rhs, states), f32), *band_shapes),
        [HBM, VMEM, VMEM, ANY, ANY],
        [HBM] * (1 + n_ways),
        [
            pltpu.VMEM((2, *made_shape), f32),
            list_scratch,
            near_scratch,
            pltpu.VMEM((half, 2 * cap, n_rhs, states), f32),
            *band_scratch,
            pltpu.SemaphoreType.DMA((n_tiles,)),
            pltpu.SemaphoreType.DMA((2,)),
            pltpu.SemaphoreType.DMA((half + n_ways,)),
        ],
        work * n_tiles,
        4 << 20,
    )(made, mirror, coupling_tiles, lists, near)
    packed, late = lax.optimization_barrier((packed, lists))
    sends = (packed.reshape(half, 2 * cap * n_rhs, states), *bands)
    halves_of_rows = [list(range(half)), list(range(half, n_rows))]
    def exchange(sends, groups=None):
        arrived = lax.all_to_all(
            sends[0], "rows", split_axis=0, concat_axis=0, tiled=True, axis_index_groups=groups
        )
        return arrived, to_bands(sends[1:])

    arrived_blocks, arrived_bands = exchange(sends, halves_of_rows)

    mirror_lists = lax.ppermute(late, "rows", to_mirror)
    extra, extra_scratch, tail = (), [], 0
    if dense:
        across = lax.ppermute(late, "band", [(0, 1), (1, 0)])
        corner = [(b * n_rows + i, (1 - b) * n_rows + j) for b in range(2) for i, j in to_mirror]
        corner = lax.ppermute(late, ("band", "rows"), corner)
        near_half = jnp.stack([late, across])[:, :, 0, LANES:]
        far_half = jnp.stack([mirror_lists, corner])[:, :, 0, LANES:]
        upper = my_row >= half
        fields = [jnp.where(upper, far_half, near_half), jnp.where(upper, near_half, far_half)]
        fields = jnp.concatenate(fields, axis=1).reshape(2, n_rows, -1, rows).transpose(2, 0, 1, 3)
        fields = fields.reshape(-1, 2, n_rows * rows)
        n_blocks = slots + 2 * rows
        length = n_dev * depth
        extra_shapes = [
            ((n_diag * n_func, 3 * states), jnp.bfloat16),
            ((n_tiles + 2, total_groups, n_blocks), jnp.bfloat16),
            ((per_tile * length, total_groups), jnp.bfloat16),
        ]
        functional_shape, count_shape, placing_shape = extra_shapes
        counts, functionals, placing, scale = call(
            functools.partial(count_kernel, sizes, width_k, n_func),
            (
                jax.ShapeDtypeStruct(*count_shape),
                jax.ShapeDtypeStruct(*functional_shape),
                jax.ShapeDtypeStruct(*placing_shape),
                jax.ShapeDtypeStruct((depth, LANES), f32),
            ),
            [VMEM] * 6,
            [HBM, HBM, HBM, VMEM],
            [
                pltpu.VMEM(*count_shape),
                pltpu.VMEM(*functional_shape),
                pltpu.VMEM(*placing_shape),
                pltpu.SemaphoreType.DMA((n_tiles + 4,)),
            ],
            4 * total_groups * n_tiles * n_dev * rows * n_blocks,
            4 << 20,
        )(fields, late[:, 0, :LANES], mirror_lists[:, 0, :LANES], coupling_tiles, diag_table, inverse_table)
        extra = (functionals, counts, placing)
        extra_scratch = [
            *[pltpu.VMEM(*shape) for shape in extra_shapes],
            pltpu.SemaphoreType.DMA((3,)),
            pltpu.VMEM((n_diag * n_func, n_blocks * n_rhs), f32),
            pltpu.VMEM((n_blocks * n_func, LANES), f32),
            pltpu.VMEM((n_rows, n_bands * depth, LANES), f32),
        ]
        tail = n_bands * depth

    send_shape = (n_rows, cap * n_rhs + tail, states)
    sends = call(
        functools.partial(middle_kernel, sizes, width_k, n_ways, dense),
        (jax.ShapeDtypeStruct(send_shape, f32), *band_shapes),
        [ANY] * 5 + [VMEM] * 3 + [HBM] + [ANY] * n_ways + [HBM] * len(extra),
        [HBM] * (1 + n_ways),
        [
            *row_scratch,
            list_scratch,
            list_scratch,
            near_scratch,
            sums,
            products,
            pltpu.VMEM((n_rows, cap * n_rhs, states), f32),
            *term_scratch,
            *band_scratch,
            term_sems,
            pltpu.SemaphoreType.DMA((5,)),
            pltpu.SemaphoreType.DMA((n_rows + n_ways + 1,)),
            *extra_scratch,
        ],
        work * (n_tiles + n_diag),
        4 << 20,
    )(
        places,
        index,
        lists,
        mirror_lists,
        near,
        arrived_blocks,
        inverse_table,
        coupling_tiles,
        right_side,
        *arrived_bands,
        *extra,
    )
    arrived_blocks, arrived_bands = exchange(sends)

    if dense:
        part = jax.ShapeDtypeStruct((depth, LANES), f32)
        mine, other = call(part_kernel, (part, part), [VMEM], [VMEM] * 2)(arrived_blocks)
        other = lax.ppermute(other, "band", [(0, 1), (1, 0)])
    second = call(
        functools.partial(last_kernel, sizes, width_k, n_ways),
        jax.ShapeDtypeStruct(block, f32),
        [ANY] * 2 + [VMEM] * 2 + [HBM] + [ANY] * n_ways,
        VMEM,
        [
            *row_scratch,
            sums,
            products,
            *term_scratch,
            term_sems,
            pltpu.SemaphoreType.DMA((2,)),
        ],
        work * n_diag,
        4 << 20,
    )(places, index, arrived_blocks, inverse_table, right_side, *arrived_bands)
    if dense:
        return call(
            functools.partial(final_kernel, sizes),
            jax.ShapeDtypeStruct(block, f32),
            [VMEM] * 4,
            VMEM,
        )(mine, other, scale, second)

    groups = aggregate_map[:, 0]
    own = jnp.arange(rows, dtype=i32)
    index_all = lax.all_gather(index, ("band", "rows"), axis=0, tiled=True)
    index_all = index_all.reshape(n_bands, n_rows, wide)
    groups_all, diags_all = index_all[:, :, :rows], index_all[:, :, rows : 2 * rows]
    lanes = LANES // 2
    codes = jnp.concatenate([lists[:, 0, :cap], mirror_lists[:, 0, lanes : lanes + cap]], axis=0)
    asker = jnp.arange(n_rows, dtype=i32)
    asker = jnp.where(my_row < half, asker, (asker + half) % n_rows)
    asked = asker[:, None] * rows + codes // (rows * n_tiles) % rows
    asked = jnp.where(codes > 0, asked, -1).reshape(-1)
    table_sums = jnp.sum(diag_table, axis=(1, 2))
    diag_onehot = diags_all.reshape(-1, 1) == jnp.arange(n_diag, dtype=i32)[None]
    block_sums = jnp.sum(jnp.where(diag_onehot, table_sums[None], 0.0), axis=1)
    whole_diag = jnp.sum(
        jnp.where(groups[:, None] == groups_all.reshape(-1)[None], block_sums[None], 0.0), axis=1
    )
    above, below = near[0, 0], near[-1, 0]
    place_of = (2 + width_k) * rows
    band_tiles = jnp.stack([above[place_of : place_of + rows], below[place_of + rows : place_of + 2 * rows]])
    band_groups = jnp.stack([above[:rows], below[:rows]])
    band_valid = jnp.stack([my_band + 1 < n_bands, my_band > 0])
    band_valid = jnp.broadcast_to(band_valid[:, None], (2, rows))
    n_all = n_tiles + n_diag + 1
    code = codes.reshape(-1)
    band_of_mine = lax.dynamic_index_in_dim(groups_all, my_band, 0, keepdims=False).reshape(-1)
    entry_group = jnp.concatenate(
        [jnp.take(band_of_mine, jnp.maximum(asked, 0)), band_groups.reshape(-1), groups, groups]
    )
    entry_func = jnp.concatenate(
        [
            (code % rows) * n_all + (code // rows) % n_tiles,
            (own[None] * n_all + band_tiles).reshape(-1),
            own * n_all + n_tiles + diag_index,
            own * n_all + n_tiles + n_diag,
        ]
    )
    entry_valid = jnp.concatenate([asked >= 0, band_valid.reshape(-1), jnp.ones((2 * rows,), bool)])
    functionals = jnp.concatenate(
        [jnp.sum(coupling_tiles, axis=1), -jnp.sum(diag_table, axis=1)], axis=0
    )
    weights = jnp.einsum("fp,rcp->rfc", functionals, second, precision=HIGH)
    weights = jnp.concatenate([weights, jnp.sum(right_side, axis=2)[:, None]], axis=1)
    chosen = jnp.take(weights.reshape(rows * n_all, n_rhs), entry_func, axis=0)
    chosen = jnp.where(entry_valid[:, None], chosen, 0.0)
    partial = jax.ops.segment_sum(chosen, entry_group, num_segments=total_groups)
    whole = lax.psum(partial, ("band", "rows"))
    correction = jnp.take(whole, groups, axis=0) / whole_diag[:, None]
    return second + correction[:, :, None]


def solution(mesh):
    in_specs = (
        P(("band", "rows"), None, None),
        P(("band", "rows"), None, None),
        P(),
        P(),
        P(),
        P(("band", "rows")),
        P(("band", "rows"), None),
        P(("band", "rows"), None),
        P(("band", "rows"), None),
        P(("band", "rows"), None),
    )
    out_specs = P(("band", "rows"), None, None)
    return jax.shard_map(
        on_device, mesh=mesh, in_specs=in_specs, out_specs=out_specs, check_vma=False
    )
```

```python
import functools

import jax
import jax.numpy as jnp
from jax import lax
from jax.experimental import pallas as pl
from jax.experimental.pallas import tpu as pltpu
from jax.sharding import PartitionSpec as P

AGG_DEV = 8
LANES = 128
DENSE_LIMIT = 1 << 19

VMEM = pl.BlockSpec(memory_space=pltpu.VMEM)
SMEM = pl.BlockSpec(memory_space=pltpu.SMEM)
HBM = pl.BlockSpec(memory_space=pltpu.HBM)
ANY = pl.BlockSpec(memory_space=pl.ANY)
HIGH = lax.Precision.HIGHEST


def params():
    return pltpu.CompilerParams(vmem_limit_bytes=24 * 1024 * 1024)


def call(kernel, out_shape, in_specs, out_specs, scratch=(), flops=0, moved=0):
    def shaped(shape, spec):
        return pltpu.HBM(shape.shape, shape.dtype) if spec is HBM else shape

    if isinstance(out_shape, (tuple, list)):
        out_shape = [shaped(*pair) for pair in zip(out_shape, out_specs)]
    else:
        out_shape = shaped(out_shape, out_specs)
    run = pl.pallas_call(
        kernel,
        out_shape=out_shape,
        in_specs=in_specs,
        out_specs=out_specs,
        scratch_shapes=list(scratch),
        compiler_params=params(),
        cost_estimate=pl.CostEstimate(flops=flops, bytes_accessed=moved, transcendentals=0),
    )

    def apply(*args):
        pinned = [
            pltpu.with_memory_space_constraint(arg, pltpu.HBM) if spec is HBM else arg
            for arg, spec in zip(args, in_specs)
        ]
        return run(*pinned)

    return apply


def below(value, bound):
    return value & (bound - 1) if bound & (bound - 1) == 0 else lax.rem(value, bound)


def over(value, bound):
    if bound & (bound - 1) == 0:
        return lax.shift_right_logical(value, bound.bit_length() - 1)
    return lax.div(value, bound)


def halves(value):
    high = value.astype(jnp.bfloat16)
    low = (value - high.astype(jnp.float32)).astype(jnp.bfloat16)
    return high, low


def left_operand(value):
    high, low = halves(value)
    return jnp.concatenate([high, low, high], axis=1)


def right_operand(value):
    high, low = halves(value)
    return jnp.concatenate([high, high, low], axis=1)


def dot_nt(left, right):
    return lax.dot_general(
        left, right, (((1,), (1,)), ((), ())), preferred_element_type=jnp.float32
    )


def table_products(value, table_ref, out_ref, done=None, loads=None):
    left = left_operand(value)
    count, width = table_ref.shape[0], table_ref.shape[1]
    n_rhs = out_ref.shape[1]
    rows = left.shape[0] // n_rhs
    for first in range(0, count, 2):
        last = min(first + 2, count)
        if loads is not None:
            loads[first // 2].wait()
        right = right_operand(table_ref[first:last].reshape((last - first) * width, -1))
        product = dot_nt(left, right)
        for t in range(first, last):
            part = product[:, (t - first) * width : (t - first + 1) * width]
            out_ref[t * rows : (t + 1) * rows] = part.reshape(rows, n_rhs, width)
        if done is not None:
            done(first * rows, (last - first) * rows)


def started(copies):
    for copy in copies:
        copy.start()
    return copies


def finish(copies):
    for copy in copies:
        copy.wait()


def request_kernel(sizes, *refs):
    rows, n_rows, cap, n_tiles, n_diag = sizes
    inputs, (list_ref, index_ref, place_ref), held, sems = refs[:5], refs[5:8], refs[8:13], refs[13]
    finish(
        started([pltpu.make_async_copy(i, h, sems.at[n]) for n, (i, h) in enumerate(zip(inputs, held))])
    )
    owner_ref, local_ref, tile_ref, diag_ref, group_ref = held
    width_k = owner_ref.shape[0]
    half = n_rows // 2
    row_of = lax.broadcasted_iota(jnp.int32, (rows, rows), 0)
    col_of = lax.broadcasted_iota(jnp.int32, (rows, rows), 1)
    lane = lax.broadcasted_iota(jnp.int32, (rows, LANES), 1)
    owners = lax.broadcasted_iota(jnp.int32, (n_rows, rows), 0)

    def column(row):
        return jnp.sum(jnp.where(row_of == col_of, row, 0), axis=1, keepdims=True)

    def owner_row(k):
        return owner_ref[k : k + 1, :]

    row_ids = lax.broadcasted_iota(jnp.int32, (1, rows), 1)
    owner_columns = [column(owner_row(k)) for k in range(width_k)]
    lists = jnp.zeros((n_rows, LANES), jnp.float32)
    places, half_places = [], []
    for k in range(width_k):
        rank = jnp.zeros((1, rows), jnp.int32)
        for other in range(k + 1):
            match = owner_columns[other] == owner_row(k)
            if other == k:
                match = match & (row_of < col_of)
            rank = rank + jnp.sum(jnp.where(match, 1, 0), axis=0, keepdims=True)
        places.append(owner_row(k) * cap + rank)
        same = (owner_row(k) >= half) == (lax.axis_index("rows") >= half)
        holder = jnp.where(owner_row(k) >= half, owner_row(k) - half, owner_row(k))
        half_places.append(holder * (2 * cap) + rank + jnp.where(same, 0, cap))
        taker = row_ids + rows * (diag_ref[...] + n_diag)
        code = local_ref[k : k + 1, :] + rows * (tile_ref[k : k + 1, :] + n_tiles * taker)
        code, rank = column(code), column(rank)
        mirror = jnp.where(owner_row(k) >= half, owner_row(k) - half, owner_row(k) + half)
        for owner, base in ((owner_row(k), 0), (mirror, LANES // 2)):
            by_rank = jnp.where(lane == rank + base, code, 0).astype(jnp.float32)
            mine = jnp.where(owners == owner, 1.0, 0.0)
            lists = lists + jnp.dot(
                mine, by_rank, precision=HIGH, preferred_element_type=jnp.float32
            )
    lists = (lists + 0.5).astype(jnp.int32)
    upper = lax.axis_index("rows") >= half
    lists = jnp.where(upper, lists[half:], lists[:half])

    def joined(parts, wide):
        spare = wide - len(parts) * rows
        if spare:
            parts = [*parts, jnp.zeros((1, spare), jnp.int32)]
        return jnp.concatenate(parts, axis=1)

    index = [group_ref[...], diag_ref[...]]
    index += [tile_ref[k : k + 1, :] for k in range(width_k + 2)]
    index += [owner_row(k) * rows + local_ref[k : k + 1, :] for k in range(width_k)]
    index = joined(index, index_ref.shape[2])
    index_ref[0] = index
    place_ref[0] = joined(half_places + places, place_ref.shape[2])
    for device in range(half):
        list_ref[device] = jnp.concatenate([lists[device : device + 1, :], index], axis=1)


def copies_of(pairs, sems):
    return started([pltpu.make_async_copy(i, h, sems.at[n]) for n, (i, h) in enumerate(pairs)])


def near_rows(near_in, near_ref):
    if near_ref.shape[0] != 1:
        return near_in
    row = lax.rem(lax.axis_index("rows"), near_in.shape[0])
    return near_in.at[pl.ds(row, 1), :, pl.ds(LANES, near_ref.shape[2])]


def band_field(rows, width_k, way, n_ways):
    field = (2 + width_k) * rows
    if n_ways == 1:
        return field + jnp.where(lax.axis_index("band") == 0, 0, rows)
    return field + way * rows


def pack_bands(sizes, width_k, product_ref, near_ref, band_refs):
    rows = sizes[0]
    for way, band_ref in enumerate(band_refs):
        field = band_field(rows, width_k, way, len(band_refs))
        for row in range(rows):
            band_ref[row] = product_ref[near_ref[way, 0, field + row] * rows + row]


def table_loads(table_in, table_ref, sems):
    copies = []
    for first in range(0, table_in.shape[0], 2):
        place = pl.ds(first, min(2, table_in.shape[0] - first))
        source, target = table_in.at[place], table_ref.at[place]
        copies.append(pltpu.make_async_copy(source, target, sems.at[first // 2]))
    return started(copies)


def product_kernel(start_in, tile_in, product_out, start_ref, tile_ref, product_ref, sems, tile_sems):
    start = pltpu.make_async_copy(start_in, start_ref, sems.at[0])
    start.start()
    loads = table_loads(tile_in, tile_ref, tile_sems)
    start.wait()
    copies = []

    def done(first, count):
        place = pl.ds(first, count)
        source, target = product_ref.at[place], product_out.at[place]
        copies.extend(started([pltpu.make_async_copy(source, target, sems.at[1 + len(copies)])]))

    rows, n_rhs, states = start_ref.shape
    values = start_ref[...].reshape(rows * n_rhs, states)
    table_products(values, tile_ref, product_ref, done, loads)
    finish(copies)


def first_kernel(sizes, width_k, n_band, *refs):
    rows, n_rows, cap, n_tiles, n_rhs = sizes
    product_in, mirror_ref, tile_ref, list_in, near_in, send_out = refs[:6]
    band_out, refs = refs[6 : 6 + n_band], refs[6 + n_band :]
    product_ref, list_ref, near_ref, send_ref = refs[:4]
    band_refs, (load_sems, meta_sems, send_sems) = refs[4 : 4 + n_band], refs[4 + n_band :]
    list_in = list_in.at[:, :, pl.ds(0, LANES)]
    near_in = near_rows(near_in, near_ref)
    metadata = copies_of(((list_in, list_ref), (near_in, near_ref)), meta_sems)
    places = [pl.ds(tile * rows, rows) for tile in range(n_tiles)]
    loads = [(product_in.at[place], product_ref.at[0, place]) for place in places]
    loads = copies_of(loads, load_sems)
    values = mirror_ref[...].reshape(rows * n_rhs, -1)
    table_products(values, tile_ref, product_ref.at[1])
    finish(metadata)
    finish(loads)
    copies = []
    pack_bands(sizes, width_k, product_ref.at[0], near_ref, band_refs)
    half = n_rows // 2
    for n, (ref, out) in enumerate(zip(band_refs, band_out)):
        copies += started([pltpu.make_async_copy(ref, out, send_sems.at[half + n])])
    for device in range(half):
        for slot in range(2 * cap):
            side, rank = slot // cap, slot % cap
            code = list_ref[device, 0, side * (LANES // 2) + rank]
            send_ref[device, slot] = product_ref[side, below(code, rows * n_tiles)]
        copy = pltpu.make_async_copy(send_ref.at[device], send_out.at[device], send_sems.at[device])
        copies += started([copy])
    finish(copies)


def place(place_ref, values, n_rhs, n_parts):
    per_tile = LANES // n_rhs
    length = place_ref.shape[0] // per_tile
    parts, rest = [], values
    for _ in range(n_parts):
        part = rest.astype(jnp.bfloat16)
        rest = rest - part.astype(jnp.float32)
        parts.append(part)
    parts = jnp.concatenate(parts, axis=1)
    lane = lax.broadcasted_iota(jnp.int32, (length, LANES), 1)
    result = jnp.zeros((length, LANES), jnp.float32)
    for spot in range(per_tile):
        chosen = jnp.dot(
            place_ref[spot * length : (spot + 1) * length, :],
            parts,
            preferred_element_type=jnp.float32,
        )
        chosen = sum(chosen[:, n * LANES : (n + 1) * LANES] for n in range(n_parts))
        result = jnp.where((lane >= spot * n_rhs) & (lane < (spot + 1) * n_rhs), chosen, result)
    return result


def one_hot(ids, row):
    return jnp.where(ids == row, 1.0, 0.0).astype(jnp.bfloat16)


def count_kernel(sizes, width_k, n_func, *refs):
    rows, n_rows, cap, n_tiles, n_rhs = sizes
    field_ref, list_ref, mirror_list_ref, tile_ref, table_ref, inverse_ref = refs[:6]
    count_out, functional_out, placing_out, scale_ref = refs[6:10]
    count_ref, functional_ref, placing_ref, sems = refs[10:]
    n_groups, n_blocks = count_ref.shape[1:]
    slots, band_rows = n_rows * cap, n_rows * rows
    copies = []

    def send(source, target):
        copies.extend(started([pltpu.make_async_copy(source, target, sems.at[len(copies)])]))

    sums = jnp.sum(tile_ref[...], axis=1)
    line = lax.broadcasted_iota(jnp.int32, (n_func, sums.shape[1]), 0)
    sums = jnp.concatenate([sums, jnp.zeros((n_func - n_tiles, sums.shape[1]), jnp.float32)], axis=0)
    n_diag = inverse_ref.shape[0]
    totals = []
    for d in range(n_diag):
        minus = -jnp.sum(table_ref[d], axis=0, keepdims=True)
        totals.append(-jnp.sum(minus, axis=1, keepdims=True))
        wanted = jnp.where(line == n_tiles, minus, sums)
        high, low = halves(inverse_ref[d])
        right = jnp.concatenate([high, high, low], axis=0)
        solved = jnp.dot(left_operand(wanted), right, preferred_element_type=jnp.float32)
        solved = jnp.where(line == n_tiles + 1, 1.0, solved)
        functional_ref[d * n_func : (d + 1) * n_func, :] = left_operand(solved)
    send(functional_ref, functional_out)

    half = n_rows // 2
    upper = lax.axis_index("rows") >= half
    asked = []
    for ref, first, lanes in (
        (list_ref, jnp.where(upper, half, 0), 0),
        (mirror_list_ref, jnp.where(upper, 0, half), LANES // 2),
    ):
        lists = ref[...]
        asker = first + lax.broadcasted_iota(jnp.int32, lists.shape, 0)
        codes = asker * rows + below(over(lists, rows * n_tiles), rows)
        codes = jnp.where(lists > 0, codes, -1).astype(jnp.float32)
        spread = lax.broadcasted_iota(jnp.int32, (slots // 2, half), 0)
        spread = lax.div(spread, cap) == lax.broadcasted_iota(jnp.int32, (slots // 2, half), 1)
        codes = jnp.dot(
            jnp.where(spread, 1.0, 0.0), codes, precision=HIGH, preferred_element_type=jnp.float32
        )
        rank = lax.rem(lax.broadcasted_iota(jnp.int32, codes.shape, 0), cap)
        lane = lax.broadcasted_iota(jnp.int32, codes.shape, 1)
        codes = jnp.sum(jnp.where(rank + lanes == lane, codes, 0.0), axis=1, keepdims=True)
        asked.append(jnp.where(codes < 0.0, codes - 0.5, codes + 0.5).astype(jnp.int32))
    asked = jnp.concatenate(asked, axis=0)
    own = lax.axis_index("rows") * rows + lax.broadcasted_iota(jnp.int32, (rows, 1), 0)
    band = lax.axis_index("band")

    def field(n, side):
        return field_ref[n, side : side + 1, :]

    row_ids = lax.broadcasted_iota(jnp.int32, (1, band_rows), 1)
    sides = []
    for side, targets in ((0, jnp.concatenate([asked, own], axis=0)), (1, own)):
        first = band == side
        across = jnp.where(first, field(2 + width_k, 1 - side), field(3 + width_k, 1 - side))
        takers = [field(2 + k, side) * n_groups + field(0, side) for k in range(width_k)]
        takers.append(across * n_groups + field(0, 1 - side))
        takers = jnp.concatenate(takers, axis=1)
        origins = [field(4 + width_k + k, side) for k in range(width_k)] + [row_ids]
        hits = one_hot(targets, jnp.concatenate(origins, axis=1))
        sides.append((takers, hits, field(0, side)))
    for t in range(n_tiles):
        found = []
        for takers, hits, _ in sides:
            ids = lax.broadcasted_iota(jnp.int32, (n_groups, takers.shape[1]), 0) + t * n_groups
            found.append(dot_nt(one_hot(ids, takers), hits))
        count_ref[t] = jnp.concatenate(found, axis=1).astype(jnp.bfloat16)
        send(count_ref.at[t], count_out.at[t])
    ids = lax.broadcasted_iota(jnp.int32, (n_groups, band_rows), 0)
    found = [dot_nt(one_hot(ids, groups), hits[:, -band_rows:]) for _, hits, groups in sides]
    found = jnp.concatenate(found, axis=1)
    count_ref[n_tiles] = found.astype(jnp.bfloat16)
    send(count_ref.at[n_tiles], count_out.at[n_tiles])
    block = lax.broadcasted_iota(jnp.int32, found.shape, 1)
    mine = (block >= slots) & (block < slots + rows)
    count_ref[n_tiles + 1] = jnp.where(mine, found, 0.0).astype(jnp.bfloat16)
    send(count_ref.at[n_tiles + 1], count_out.at[n_tiles + 1])

    per_tile = LANES // n_rhs
    depth = rows // per_tile
    length = n_rows * 2 * depth
    order = lax.broadcasted_iota(jnp.int32, (per_tile * length, 1), 0)
    spot, order = lax.div(order, length), lax.rem(order, length)
    device, order = lax.div(order, 2 * depth), lax.rem(order, 2 * depth)
    side, order = lax.div(order, depth), lax.rem(order, depth)
    order = side * band_rows + device * rows + spot * depth + order
    member = [
        one_hot(ids, jnp.where(band == which, field(0, 0), field(0, 1))) for which in range(2)
    ]
    placing = jnp.zeros(placing_ref.shape, jnp.float32)
    for which in range(2):
        placing = placing + dot_nt(one_hot(order, row_ids + which * band_rows), member[which])
    placing_ref[...] = placing.astype(jnp.bfloat16)
    send(placing_ref, placing_out)
    whole = jnp.zeros((n_groups, 1), jnp.float32)
    for side in range(2):
        sums = jnp.zeros((1, band_rows), jnp.float32)
        for d in range(n_diag):
            sums = jnp.where(field(1, side) == d, totals[d], sums)
        weighted = jnp.where(ids == field(0, side), sums, 0.0)
        whole = whole + jnp.sum(weighted, axis=1, keepdims=True)
    scale = place(placing_ref, jnp.broadcast_to(whole, (n_groups, LANES)), n_rhs, 3)
    mine = jnp.zeros(scale_ref.shape, jnp.float32)
    here = lax.axis_index("rows") * 2 + band
    for n in range(2 * n_rows):
        mine = jnp.where(here == n, scale[n * depth : (n + 1) * depth, :], mine)
    scale_ref[...] = mine
    finish(copies)


def gather_solve(
    sizes, slots, diags, arrived_ref, later, terms, inverse_ref, sum_ref, product_ref
):
    rows, n_rows, cap, n_tiles, n_rhs = sizes
    per = n_rows * cap // arrived_ref.shape[0]
    for row in range(rows):
        total = None
        for slot in slots(row):
            start = pl.multiple_of(below(slot, per) * n_rhs, n_rhs)
            block = arrived_ref[over(slot, per), pl.ds(start, n_rhs), :]
            total = block if total is None else total + block
        sum_ref[pl.ds(row * n_rhs, n_rhs), :] = total
    finish(later)
    total = sum_ref[...]
    for term in terms:
        total = total + term[...].reshape(total.shape)
    table_products(total, inverse_ref, product_ref)
    for row in range(rows):
        sum_ref[pl.ds(row * n_rhs, n_rhs), :] = product_ref[diags(row) * rows + row]


def middle_kernel(sizes, width_k, n_band, dense, *refs):
    metadata_in, arrived_ref, inverse_ref, tile_ref = list(refs[:5]), *refs[5:8]
    terms_in, refs = refs[8 : 9 + n_band], refs[9 + n_band :]
    extra, refs = (refs[:3], refs[3:]) if dense else ((), refs)
    send_out, band_out, refs = refs[0], refs[1 : 1 + n_band], refs[1 + n_band :]
    metadata, sum_ref, product_ref, send_ref = refs[:5], *refs[5:8]
    place_ref, index_ref, list_ref, mirror_list_ref, near_ref = metadata
    for n in (2, 3):
        metadata_in[n] = metadata_in[n].at[:, :, pl.ds(0, LANES)]
    metadata_in[4] = near_rows(metadata_in[4], near_ref)
    terms, band_refs, refs = refs[8 : 9 + n_band], refs[9 + n_band : 9 + 2 * n_band], refs[9 + 2 * n_band :]
    term_sems, meta_sems, send_sems, refs = *refs[:3], refs[3:]
    right_ref = terms[0]
    rows, n_rows, cap, n_tiles, n_rhs = sizes
    body, half = cap * n_rhs, n_rows // 2
    metadata = copies_of(zip(metadata_in, metadata), meta_sems)
    later = copies_of(zip(terms_in, terms), term_sems)
    fetched = []
    if dense:
        held, extra_sems, value_ref, spread_ref, result_ref = refs[:3], *refs[3:]
        n_diag = inverse_ref.shape[0]
        fetched = copies_of(zip(extra, held), extra_sems)
    finish(metadata)

    def slots(row):
        return [place_ref[0, 0, k * rows + row] for k in range(width_k)]

    def diags(row):
        return index_ref[0, 0, rows + row]

    gather_solve(sizes, slots, diags, arrived_ref, later, terms, inverse_ref, sum_ref, product_ref)
    table_products(sum_ref[...], tile_ref, product_ref)
    copies = []

    def send(source, target):
        copies.extend(started([pltpu.make_async_copy(source, target, send_sems.at[len(copies)])]))

    pack_bands(sizes, width_k, product_ref, near_ref, band_refs)
    for ref, out in zip(band_refs, band_out):
        send(ref, out)
    upper = lax.axis_index("rows") >= half
    codes, order = [], 0
    for ref, first, lanes in (
        (list_ref, jnp.where(upper, half, 0), 0),
        (mirror_list_ref, jnp.where(upper, 0, half), LANES // 2),
    ):
        for device in range(half):
            for rank in range(cap):
                code = ref[device, 0, lanes + rank]
                codes.append(code)
                block = product_ref[below(code, rows * n_tiles)]
                send_ref[order, rank * n_rhs : (rank + 1) * n_rhs, :] = block
            target = send_out.at[first + device]
            send(send_ref.at[order], target.at[pl.ds(0, body)] if dense else target)
            order += 1
    if dense:
        finish(fetched)
        kinds = [below(over(code, rows * n_tiles * rows), n_diag) for code in codes]
        kinds += [diags(row) for row in range(rows)]
        kinds += [near_ref[0, 0, rows + row] for row in range(rows)]
        result = coarse_parts(
            sizes, kinds, held, right_ref, send_ref, band_refs, value_ref, spread_ref
        )
        result_ref[...] = result.reshape(result_ref.shape)
        send(result_ref, send_out.at[:, pl.ds(body, result_ref.shape[1])])
    finish(copies)


def coarse_parts(sizes, kinds, held, right_ref, send_ref, band_refs, value_ref, spread_ref):
    functional_ref, count_ref, place_ref = held
    rows, n_rows, cap, n_tiles, n_rhs = sizes
    body = cap * n_rhs
    n_func = spread_ref.shape[0] // count_ref.shape[2]
    per_tile = LANES // n_rhs
    functional = functional_ref[...]
    done = 0
    for owner in range(0, n_rows, 2):
        values = [send_ref[owner + more] for more in range(2)]
        values = jnp.concatenate(values, axis=0)
        value_ref[:, done : done + 2 * body] = dot_nt(functional, right_operand(values))
        done += 2 * body
    for ref in (right_ref, *band_refs):
        values = ref[...].reshape(rows * n_rhs, -1)
        value_ref[:, done : done + rows * n_rhs] = dot_nt(functional, right_operand(values))
        done += rows * n_rhs
    lane = lax.broadcasted_iota(jnp.int32, (n_func, LANES), 1)
    for block, kind in enumerate(kinds):
        tile, spot = block // per_tile, block % per_tile
        start = pl.multiple_of(kind * n_func, n_func)
        piece = value_ref[pl.ds(start, n_func), tile * LANES : (tile + 1) * LANES]
        piece = jnp.where((lane >= spot * n_rhs) & (lane < (spot + 1) * n_rhs), piece, 0.0)
        spread_ref[block * n_func : (block + 1) * n_func, :] = piece
    partial = jnp.zeros((count_ref.shape[1], 2 * LANES), jnp.float32)
    for t in range(count_ref.shape[0]):
        values = spread_ref[pl.ds(t, done // n_rhs, stride=n_func), :]
        partial = partial + jnp.dot(
            count_ref[t],
            jnp.concatenate(halves(values), axis=1),
            preferred_element_type=jnp.float32,
        )
    partial = partial[:, :LANES] + partial[:, LANES:]
    source = lax.broadcasted_iota(jnp.int32, (LANES, LANES), 0)
    target = lax.broadcasted_iota(jnp.int32, (LANES, LANES), 1)
    same = jnp.where(lax.rem(source, n_rhs) == lax.rem(target, n_rhs), 1.0, 0.0)
    same = same.astype(jnp.bfloat16)
    same = jnp.concatenate([same, same], axis=0)
    partial = jnp.dot(
        jnp.concatenate(halves(partial), axis=1), same, preferred_element_type=jnp.float32
    )
    return place(place_ref, partial, n_rhs, 2)


def part_kernel(arrived_ref, mine_ref, other_ref):
    depth = mine_ref.shape[0]
    body = arrived_ref.shape[1] - 2 * depth
    total = arrived_ref[0, body:, :]
    for source in range(1, arrived_ref.shape[0]):
        total = total + arrived_ref[source, body:, :]
    upper = lax.axis_index("band") == 0
    mine_ref[...] = jnp.where(upper, total[:depth], total[depth:])
    other_ref[...] = jnp.where(upper, total[depth:], total[:depth])


def last_kernel(sizes, width_k, n_band, *refs):
    metadata_in, arrived_ref, inverse_ref = refs[:2], *refs[2:4]
    terms_in, refs = refs[4 : 5 + n_band], refs[5 + n_band :]
    second_ref, metadata, sum_ref, product_ref = refs[0], refs[1:3], *refs[3:5]
    place_ref, index_ref = metadata
    terms, (term_sems, meta_sems) = refs[5 : 6 + n_band], refs[6 + n_band :]
    rows = sizes[0]
    metadata = copies_of(zip(metadata_in, metadata), meta_sems)
    later = copies_of(zip(terms_in, terms), term_sems)
    finish(metadata)

    def slots(row):
        return [place_ref[0, 0, (width_k + k) * rows + row] for k in range(width_k)]

    def diags(row):
        return index_ref[0, 0, rows + row]

    gather_solve(sizes, slots, diags, arrived_ref, later, terms, inverse_ref, sum_ref, product_ref)
    second_ref[...] = sum_ref[...].reshape(second_ref.shape)


def final_kernel(sizes, mine_ref, other_ref, scale_ref, second_ref, out_ref):
    rows, n_rhs = sizes[0], sizes[4]
    depth = scale_ref.shape[0]
    correction = (mine_ref[...] + other_ref[...]) / scale_ref[...]
    padded = jnp.concatenate([correction, jnp.zeros((8 - depth, LANES), jnp.float32)], axis=0)
    turned = padded.T
    for row in range(rows):
        spot, place = row // depth, row % depth
        column = turned[spot * n_rhs : (spot + 1) * n_rhs, place : place + 1]
        out_ref[row] = second_ref[row] + column


def shifted(value, axis, steps):
    count = lax.axis_size(axis)
    initial, last = (max(0, -steps), min(count, count - steps))
    return lax.ppermute(value, axis, [(source, source + steps) for source in range(initial, last)])


def to_bands(sends):
    if len(sends) == 1:
        return (lax.ppermute(sends[0], "band", [(0, 1), (1, 0)]),)
    return shifted(sends[0], "band", 1), shifted(sends[1], "band", -1)


def on_device(
    start_iterate,
    right_side,
    diag_table,
    inverse_table,
    coupling_tiles,
    diag_index,
    tile_index,
    source_owner,
    source_local,
    aggregate_map,
):
    rows, n_rhs, states = start_iterate.shape
    width_k = source_owner.shape[1]
    n_tiles, n_diag = coupling_tiles.shape[0], inverse_table.shape[0]
    n_rows, n_bands = lax.axis_size("rows"), lax.axis_size("band")
    n_dev = n_rows * n_bands
    cap = max(2, 2 * width_k * rows // n_rows)
    slots = n_rows * cap
    total_groups = AGG_DEV * n_dev
    per_tile = LANES // n_rhs
    depth = rows // per_tile
    n_func = 16
    dense = (
        n_bands == 2
        and n_dev * rows * total_groups <= DENSE_LIMIT
        and depth == 4
        and n_diag * n_func == LANES
        and n_tiles + 2 <= n_func
    )
    sizes = (rows, n_rows, cap, n_tiles, n_rhs)
    f32, i32 = jnp.float32, jnp.int32
    my_band = lax.axis_index("band")
    my_row = lax.axis_index("rows")

    half = n_rows // 2
    wide = -(-(4 + 2 * width_k) * rows // LANES) * LANES
    place_wide = -(-2 * width_k * rows // LANES) * LANES
    index_shapes = [(width_k, rows), (width_k, rows), (width_k + 2, rows), (1, rows), (1, rows)]
    halves_of_rows = [list(range(half)), list(range(half, n_rows))]
    to_mirror = [(i, (i + half) % n_rows) for i in range(n_rows)]
    mirror = lax.ppermute(start_iterate, "rows", to_mirror)
    lists, index, places = call(
        functools.partial(request_kernel, (rows, n_rows, cap, n_tiles, n_diag)),
        (
            jax.ShapeDtypeStruct((half, 1, LANES + wide), i32),
            jax.ShapeDtypeStruct((1, 1, wide), i32),
            jax.ShapeDtypeStruct((1, 1, place_wide), i32),
        ),
        [HBM] * 5,
        [VMEM] * 3,
        [*[pltpu.VMEM(shape, i32) for shape in index_shapes], pltpu.SemaphoreType.DMA((5,))],
    )(source_owner.T, source_local.T, tile_index.T, diag_index[None], aggregate_map.T)
    lists = lax.all_to_all(
        lists, "rows", split_axis=0, concat_axis=0, tiled=True, axis_index_groups=halves_of_rows
    )
    if n_bands == 2:
        near = lax.ppermute(lists, "band", [(0, 1), (1, 0)])
    else:
        ways = [[(b, (b + step) % n_bands) for b in range(n_bands)] for step in (-1, 1)]
        near = jnp.concatenate([lax.ppermute(index, "band", way) for way in ways], axis=0)

    n_ways = 1 if n_bands == 2 else 2
    block = (rows, n_rhs, states)
    band_shapes = [jax.ShapeDtypeStruct(block, f32)] * n_ways
    band_scratch = [pltpu.VMEM(block, f32)] * n_ways
    term_scratch = [pltpu.VMEM(block, f32)] * (1 + n_ways)
    term_sems = pltpu.SemaphoreType.DMA((1 + n_ways,))
    list_scratch = pltpu.SMEM((half, 1, LANES), i32)
    near_scratch = pltpu.SMEM((n_ways, 1, wide), i32)
    row_scratch = [pltpu.SMEM((1, 1, place_wide), i32), pltpu.SMEM((1, 1, wide), i32)]
    flat = rows * n_rhs
    sums = pltpu.VMEM((flat, states), f32)
    products = pltpu.VMEM((max(n_tiles, n_diag) * rows, n_rhs, states), f32)
    work = 6 * flat * states * states
    made_shape = (n_tiles * rows, n_rhs, states)
    table_scratch = [pltpu.VMEM(coupling_tiles.shape, f32)]
    table_sems = pltpu.SemaphoreType.DMA((-(-n_tiles // 2),))
    made = call(
        product_kernel,
        jax.ShapeDtypeStruct(made_shape, f32),
        [HBM, HBM],
        HBM,
        [
            pltpu.VMEM(block, f32),
            *table_scratch,
            pltpu.VMEM(made_shape, f32),
            pltpu.SemaphoreType.DMA((1 + n_tiles,)),
            table_sems,
        ],
        work * n_tiles,
        4 << 20,
    )(start_iterate, coupling_tiles)
    packed, *bands = call(
        functools.partial(first_kernel, sizes, width_k, n_ways),
        (jax.ShapeDtypeStruct((half, 2 * cap, n_rhs, states), f32), *band_shapes),
        [HBM, VMEM, VMEM, ANY, ANY],
        [HBM] * (1 + n_ways),
        [
            pltpu.VMEM((2, *made_shape), f32),
            list_scratch,
            near_scratch,
            pltpu.VMEM((half, 2 * cap, n_rhs, states), f32),
            *band_scratch,
            pltpu.SemaphoreType.DMA((n_tiles,)),
            pltpu.SemaphoreType.DMA((2,)),
            pltpu.SemaphoreType.DMA((half + n_ways,)),
        ],
        work * n_tiles,
        4 << 20,
    )(made, mirror, coupling_tiles, lists, near)
    sends = (packed.reshape(half, 2 * cap * n_rhs, states), *bands)
    halves_of_rows = [list(range(half)), list(range(half, n_rows))]
    def exchange(sends, groups=None):
        arrived = lax.all_to_all(
            sends[0], "rows", split_axis=0, concat_axis=0, tiled=True, axis_index_groups=groups
        )
        return arrived, to_bands(sends[1:])

    arrived_blocks, arrived_bands = exchange(sends, halves_of_rows)

    if not dense:
        mirror_lists = lax.ppermute(lists, "rows", to_mirror)
    extra, extra_scratch, tail = (), [], 0
    if dense:
        near_half = jnp.concatenate([lists, near], axis=1)
        far_half = lax.ppermute(near_half, "rows", to_mirror)
        mirror_lists = far_half[:, :1]
        near_half, far_half = near_half[:, :, LANES:], far_half[:, :, LANES:]
        upper = my_row >= half
        fields = [jnp.where(upper, far_half, near_half), jnp.where(upper, near_half, far_half)]
        fields = jnp.concatenate(fields, axis=0).reshape(n_rows, 2, -1, rows).transpose(2, 1, 0, 3)
        fields = fields.reshape(-1, 2, n_rows * rows)
        n_blocks = slots + 2 * rows
        length = n_dev * depth
        extra_shapes = [
            ((n_diag * n_func, 3 * states), jnp.bfloat16),
            ((n_tiles + 2, total_groups, n_blocks), jnp.bfloat16),
            ((per_tile * length, total_groups), jnp.bfloat16),
        ]
        functional_shape, count_shape, placing_shape = extra_shapes
        counts, functionals, placing, scale = call(
            functools.partial(count_kernel, sizes, width_k, n_func),
            (
                jax.ShapeDtypeStruct(*count_shape),
                jax.ShapeDtypeStruct(*functional_shape),
                jax.ShapeDtypeStruct(*placing_shape),
                jax.ShapeDtypeStruct((depth, LANES), f32),
            ),
            [VMEM] * 6,
            [HBM, HBM, HBM, VMEM],
            [
                pltpu.VMEM(*count_shape),
                pltpu.VMEM(*functional_shape),
                pltpu.VMEM(*placing_shape),
                pltpu.SemaphoreType.DMA((n_tiles + 4,)),
            ],
            4 * total_groups * n_tiles * n_dev * rows * n_blocks,
            4 << 20,
        )(fields, lists[:, 0, :LANES], mirror_lists[:, 0, :LANES], coupling_tiles, diag_table, inverse_table)
        extra = (functionals, counts, placing)
        extra_scratch = [
            *[pltpu.VMEM(*shape) for shape in extra_shapes],
            pltpu.SemaphoreType.DMA((3,)),
            pltpu.VMEM((n_diag * n_func, n_blocks * n_rhs), f32),
            pltpu.VMEM((n_blocks * n_func, LANES), f32),
            pltpu.VMEM((n_rows, n_bands * depth, LANES), f32),
        ]
        tail = n_bands * depth

    send_shape = (n_rows, cap * n_rhs + tail, states)
    sends = call(
        functools.partial(middle_kernel, sizes, width_k, n_ways, dense),
        (jax.ShapeDtypeStruct(send_shape, f32), *band_shapes),
        [ANY] * 5 + [VMEM] * 3 + [HBM] + [ANY] * n_ways + [HBM] * len(extra),
        [HBM] * (1 + n_ways),
        [
            *row_scratch,
            list_scratch,
            list_scratch,
            near_scratch,
            sums,
            products,
            pltpu.VMEM((n_rows, cap * n_rhs, states), f32),
            *term_scratch,
            *band_scratch,
            term_sems,
            pltpu.SemaphoreType.DMA((5,)),
            pltpu.SemaphoreType.DMA((n_rows + n_ways + 1,)),
            *extra_scratch,
        ],
        work * (n_tiles + n_diag),
        4 << 20,
    )(
        places,
        index,
        lists,
        mirror_lists,
        near,
        arrived_blocks,
        inverse_table,
        coupling_tiles,
        right_side,
        *arrived_bands,
        *extra,
    )
    arrived_blocks, arrived_bands = exchange(sends)

    if dense:
        part = jax.ShapeDtypeStruct((depth, LANES), f32)
        mine, other = call(part_kernel, (part, part), [VMEM], [VMEM] * 2)(arrived_blocks)
        other = lax.ppermute(other, "band", [(0, 1), (1, 0)])
    second = call(
        functools.partial(last_kernel, sizes, width_k, n_ways),
        jax.ShapeDtypeStruct(block, f32),
        [ANY] * 2 + [VMEM] * 2 + [HBM] + [ANY] * n_ways,
        VMEM,
        [
            *row_scratch,
            sums,
            products,
            *term_scratch,
            term_sems,
            pltpu.SemaphoreType.DMA((2,)),
        ],
        work * n_diag,
        4 << 20,
    )(places, index, arrived_blocks, inverse_table, right_side, *arrived_bands)
    if dense:
        return call(
            functools.partial(final_kernel, sizes),
            jax.ShapeDtypeStruct(block, f32),
            [VMEM] * 4,
            VMEM,
        )(mine, other, scale, second)

    groups = aggregate_map[:, 0]
    own = jnp.arange(rows, dtype=i32)
    index_all = lax.all_gather(index, ("band", "rows"), axis=0, tiled=True)
    index_all = index_all.reshape(n_bands, n_rows, wide)
    groups_all, diags_all = index_all[:, :, :rows], index_all[:, :, rows : 2 * rows]
    lanes = LANES // 2
    codes = jnp.concatenate([lists[:, 0, :cap], mirror_lists[:, 0, lanes : lanes + cap]], axis=0)
    asker = jnp.arange(n_rows, dtype=i32)
    asker = jnp.where(my_row < half, asker, (asker + half) % n_rows)
    asked = asker[:, None] * rows + codes // (rows * n_tiles) % rows
    asked = jnp.where(codes > 0, asked, -1).reshape(-1)
    table_sums = jnp.sum(diag_table, axis=(1, 2))
    diag_onehot = diags_all.reshape(-1, 1) == jnp.arange(n_diag, dtype=i32)[None]
    block_sums = jnp.sum(jnp.where(diag_onehot, table_sums[None], 0.0), axis=1)
    whole_diag = jnp.sum(
        jnp.where(groups[:, None] == groups_all.reshape(-1)[None], block_sums[None], 0.0), axis=1
    )
    above, below = near[0, 0], near[-1, 0]
    place_of = (2 + width_k) * rows
    band_tiles = jnp.stack([above[place_of : place_of + rows], below[place_of + rows : place_of + 2 * rows]])
    band_groups = jnp.stack([above[:rows], below[:rows]])
    band_valid = jnp.stack([my_band + 1 < n_bands, my_band > 0])
    band_valid = jnp.broadcast_to(band_valid[:, None], (2, rows))
    n_all = n_tiles + n_diag + 1
    code = codes.reshape(-1)
    band_of_mine = lax.dynamic_index_in_dim(groups_all, my_band, 0, keepdims=False).reshape(-1)
    entry_group = jnp.concatenate(
        [jnp.take(band_of_mine, jnp.maximum(asked, 0)), band_groups.reshape(-1), groups, groups]
    )
    entry_func = jnp.concatenate(
        [
            (code % rows) * n_all + (code // rows) % n_tiles,
            (own[None] * n_all + band_tiles).reshape(-1),
            own * n_all + n_tiles + diag_index,
            own * n_all + n_tiles + n_diag,
        ]
    )
    entry_valid = jnp.concatenate([asked >= 0, band_valid.reshape(-1), jnp.ones((2 * rows,), bool)])
    functionals = jnp.concatenate(
        [jnp.sum(coupling_tiles, axis=1), -jnp.sum(diag_table, axis=1)], axis=0
    )
    weights = jnp.einsum("fp,rcp->rfc", functionals, second, precision=HIGH)
    weights = jnp.concatenate([weights, jnp.sum(right_side, axis=2)[:, None]], axis=1)
    chosen = jnp.take(weights.reshape(rows * n_all, n_rhs), entry_func, axis=0)
    chosen = jnp.where(entry_valid[:, None], chosen, 0.0)
    partial = jax.ops.segment_sum(chosen, entry_group, num_segments=total_groups)
    whole = lax.psum(partial, ("band", "rows"))
    correction = jnp.take(whole, groups, axis=0) / whole_diag[:, None]
    return second + correction[:, :, None]


def solution(mesh):
    in_specs = (
        P(("band", "rows"), None, None),
        P(("band", "rows"), None, None),
        P(),
        P(),
        P(),
        P(("band", "rows")),
        P(("band", "rows"), None),
        P(("band", "rows"), None),
        P(("band", "rows"), None),
        P(("band", "rows"), None),
    )
    out_specs = P(("band", "rows"), None, None)
    return jax.shard_map(
        on_device, mesh=mesh, in_specs=in_specs, out_specs=out_specs, check_vma=False
    )
```

```python
import functools

import jax
import jax.numpy as jnp
from jax import lax
from jax.experimental import pallas as pl
from jax.experimental.pallas import tpu as pltpu
from jax.sharding import PartitionSpec as P

AGG_DEV = 8
LANES = 128
DENSE_LIMIT = 1 << 19

VMEM = pl.BlockSpec(memory_space=pltpu.VMEM)
SMEM = pl.BlockSpec(memory_space=pltpu.SMEM)
HBM = pl.BlockSpec(memory_space=pltpu.HBM)
ANY = pl.BlockSpec(memory_space=pl.ANY)
HIGH = lax.Precision.HIGHEST


def params():
    return pltpu.CompilerParams(vmem_limit_bytes=24 * 1024 * 1024)


def call(kernel, out_shape, in_specs, out_specs, scratch=(), flops=0, moved=0):
    def shaped(shape, spec):
        return pltpu.HBM(shape.shape, shape.dtype) if spec is HBM else shape

    if isinstance(out_shape, (tuple, list)):
        out_shape = [shaped(*pair) for pair in zip(out_shape, out_specs)]
    else:
        out_shape = shaped(out_shape, out_specs)
    run = pl.pallas_call(
        kernel,
        out_shape=out_shape,
        in_specs=in_specs,
        out_specs=out_specs,
        scratch_shapes=list(scratch),
        compiler_params=params(),
        cost_estimate=pl.CostEstimate(flops=flops, bytes_accessed=moved, transcendentals=0),
    )

    def apply(*args):
        pinned = [
            pltpu.with_memory_space_constraint(arg, pltpu.HBM) if spec is HBM else arg
            for arg, spec in zip(args, in_specs)
        ]
        return run(*pinned)

    return apply


def below(value, bound):
    return value & (bound - 1) if bound & (bound - 1) == 0 else lax.rem(value, bound)


def over(value, bound):
    if bound & (bound - 1) == 0:
        return lax.shift_right_logical(value, bound.bit_length() - 1)
    return lax.div(value, bound)


def halves(value):
    high = value.astype(jnp.bfloat16)
    low = (value - high.astype(jnp.float32)).astype(jnp.bfloat16)
    return high, low


def left_operand(value):
    high, low = halves(value)
    return jnp.concatenate([high, low, high], axis=1)


def right_operand(value):
    high, low = halves(value)
    return jnp.concatenate([high, high, low], axis=1)


def dot_nt(left, right):
    return lax.dot_general(
        left, right, (((1,), (1,)), ((), ())), preferred_element_type=jnp.float32
    )


def table_products(value, table_ref, out_ref, done=None, loads=None):
    left = left_operand(value)
    count, width = table_ref.shape[0], table_ref.shape[1]
    n_rhs = out_ref.shape[1]
    rows = left.shape[0] // n_rhs
    for first in range(0, count, 2):
        last = min(first + 2, count)
        if loads is not None:
            loads[first // 2].wait()
        right = right_operand(table_ref[first:last].reshape((last - first) * width, -1))
        product = dot_nt(left, right)
        for t in range(first, last):
            part = product[:, (t - first) * width : (t - first + 1) * width]
            out_ref[t * rows : (t + 1) * rows] = part.reshape(rows, n_rhs, width)
        if done is not None:
            done(first * rows, (last - first) * rows)


def started(copies):
    for copy in copies:
        copy.start()
    return copies


def finish(copies):
    for copy in copies:
        copy.wait()


def request_kernel(sizes, *refs):
    rows, n_rows, cap, n_tiles, n_diag = sizes
    inputs, (list_ref, index_ref, place_ref), held, sems = refs[:5], refs[5:8], refs[8:13], refs[13]
    finish(
        started([pltpu.make_async_copy(i, h, sems.at[n]) for n, (i, h) in enumerate(zip(inputs, held))])
    )
    owner_ref, local_ref, tile_ref, diag_ref, group_ref = held
    width_k = owner_ref.shape[0]
    half = n_rows // 2
    row_of = lax.broadcasted_iota(jnp.int32, (rows, rows), 0)
    col_of = lax.broadcasted_iota(jnp.int32, (rows, rows), 1)
    lane = lax.broadcasted_iota(jnp.int32, (rows, LANES), 1)
    owners = lax.broadcasted_iota(jnp.int32, (n_rows, rows), 0)

    def column(row):
        return jnp.sum(jnp.where(row_of == col_of, row, 0), axis=1, keepdims=True)

    def owner_row(k):
        return owner_ref[k : k + 1, :]

    row_ids = lax.broadcasted_iota(jnp.int32, (1, rows), 1)
    owner_columns = [column(owner_row(k)) for k in range(width_k)]
    lists = jnp.zeros((n_rows, LANES), jnp.float32)
    places, half_places = [], []
    for k in range(width_k):
        rank = jnp.zeros((1, rows), jnp.int32)
        for other in range(k + 1):
            match = owner_columns[other] == owner_row(k)
            if other == k:
                match = match & (row_of < col_of)
            rank = rank + jnp.sum(jnp.where(match, 1, 0), axis=0, keepdims=True)
        places.append(owner_row(k) * cap + rank)
        same = (owner_row(k) >= half) == (lax.axis_index("rows") >= half)
        holder = jnp.where(owner_row(k) >= half, owner_row(k) - half, owner_row(k))
        half_places.append(holder * (2 * cap) + rank + jnp.where(same, 0, cap))
        taker = row_ids + rows * (diag_ref[...] + n_diag)
        code = local_ref[k : k + 1, :] + rows * (tile_ref[k : k + 1, :] + n_tiles * taker)
        code, rank = column(code), column(rank)
        mirror = jnp.where(owner_row(k) >= half, owner_row(k) - half, owner_row(k) + half)
        for owner, base in ((owner_row(k), 0), (mirror, LANES // 2)):
            by_rank = jnp.where(lane == rank + base, code, 0).astype(jnp.float32)
            mine = jnp.where(owners == owner, 1.0, 0.0)
            lists = lists + jnp.dot(
                mine, by_rank, precision=HIGH, preferred_element_type=jnp.float32
            )
    lists = (lists + 0.5).astype(jnp.int32)

    def joined(parts, wide):
        spare = wide - len(parts) * rows
        if spare:
            parts = [*parts, jnp.zeros((1, spare), jnp.int32)]
        return jnp.concatenate(parts, axis=1)

    index = [group_ref[...], diag_ref[...]]
    index += [tile_ref[k : k + 1, :] for k in range(width_k + 2)]
    index += [owner_row(k) * rows + local_ref[k : k + 1, :] for k in range(width_k)]
    index = joined(index, index_ref.shape[2])
    index_ref[0] = index
    place_ref[0] = joined(half_places + places, place_ref.shape[2])
    for device in range(n_rows):
        list_ref[device] = jnp.concatenate([lists[device : device + 1, :], index], axis=1)


def copies_of(pairs, sems):
    return started([pltpu.make_async_copy(i, h, sems.at[n]) for n, (i, h) in enumerate(pairs)])


def band_field(rows, width_k, way, n_ways):
    field = (2 + width_k) * rows
    if n_ways == 1:
        return field + jnp.where(lax.axis_index("band") == 0, 0, rows)
    return field + way * rows


def pack_bands(sizes, width_k, product_ref, near_ref, band_refs):
    rows = sizes[0]
    for way, band_ref in enumerate(band_refs):
        field = band_field(rows, width_k, way, len(band_refs))
        for row in range(rows):
            band_ref[row] = product_ref[near_ref[way, 0, field + row] * rows + row]


def table_loads(table_in, table_ref, sems):
    copies = []
    for first in range(0, table_in.shape[0], 2):
        place = pl.ds(first, min(2, table_in.shape[0] - first))
        source, target = table_in.at[place], table_ref.at[place]
        copies.append(pltpu.make_async_copy(source, target, sems.at[first // 2]))
    return started(copies)


def product_kernel(start_in, tile_in, product_out, start_ref, tile_ref, product_ref, sems, tile_sems):
    start = pltpu.make_async_copy(start_in, start_ref, sems.at[0])
    start.start()
    loads = table_loads(tile_in, tile_ref, tile_sems)
    start.wait()
    copies = []

    def done(first, count):
        place = pl.ds(first, count)
        source, target = product_ref.at[place], product_out.at[place]
        copies.extend(started([pltpu.make_async_copy(source, target, sems.at[1 + len(copies)])]))

    rows, n_rhs, states = start_ref.shape
    values = start_ref[...].reshape(rows * n_rhs, states)
    table_products(values, tile_ref, product_ref, done, loads)
    finish(copies)


def first_kernel(sizes, width_k, n_band, *refs):
    rows, n_rows, cap, n_tiles, n_rhs = sizes
    product_in, mirror_ref, tile_ref, list_in, near_in, send_out = refs[:6]
    band_out, refs = refs[6 : 6 + n_band], refs[6 + n_band :]
    product_ref, list_ref, near_ref, send_ref = refs[:4]
    band_refs, (load_sems, meta_sems, send_sems) = refs[4 : 4 + n_band], refs[4 + n_band :]
    half = n_rows // 2
    base = jnp.where(lax.axis_index("rows") >= half, half, 0)
    list_in = list_in.at[pl.ds(base, half), :, pl.ds(0, LANES)]
    metadata = copies_of(((list_in, list_ref), (near_in, near_ref)), meta_sems)
    places = [pl.ds(tile * rows, rows) for tile in range(n_tiles)]
    loads = [(product_in.at[place], product_ref.at[0, place]) for place in places]
    loads = copies_of(loads, load_sems)
    values = mirror_ref[...].reshape(rows * n_rhs, -1)
    table_products(values, tile_ref, product_ref.at[1])
    finish(metadata)
    finish(loads)
    copies = []
    pack_bands(sizes, width_k, product_ref.at[0], near_ref, band_refs)
    for n, (ref, out) in enumerate(zip(band_refs, band_out)):
        copies += started([pltpu.make_async_copy(ref, out, send_sems.at[half + n])])
    for device in range(half):
        for slot in range(2 * cap):
            side, rank = slot // cap, slot % cap
            code = list_ref[device, 0, side * (LANES // 2) + rank]
            send_ref[device, slot] = product_ref[side, below(code, rows * n_tiles)]
        copy = pltpu.make_async_copy(send_ref.at[device], send_out.at[device], send_sems.at[device])
        copies += started([copy])
    finish(copies)


def place(place_ref, values, n_rhs, n_parts):
    per_tile = LANES // n_rhs
    length = place_ref.shape[0] // per_tile
    parts, rest = [], values
    for _ in range(n_parts):
        part = rest.astype(jnp.bfloat16)
        rest = rest - part.astype(jnp.float32)
        parts.append(part)
    parts = jnp.concatenate(parts, axis=1)
    lane = lax.broadcasted_iota(jnp.int32, (length, LANES), 1)
    result = jnp.zeros((length, LANES), jnp.float32)
    for spot in range(per_tile):
        chosen = jnp.dot(
            place_ref[spot * length : (spot + 1) * length, :],
            parts,
            preferred_element_type=jnp.float32,
        )
        chosen = sum(chosen[:, n * LANES : (n + 1) * LANES] for n in range(n_parts))
        result = jnp.where((lane >= spot * n_rhs) & (lane < (spot + 1) * n_rhs), chosen, result)
    return result


def one_hot(ids, row):
    return jnp.where(ids == row, 1.0, 0.0).astype(jnp.bfloat16)


def count_kernel(sizes, width_k, n_func, *refs):
    rows, n_rows, cap, n_tiles, n_rhs = sizes
    field_ref, list_ref, tile_ref, table_ref, inverse_ref = refs[:5]
    count_out, functional_out, placing_out, scale_ref = refs[5:9]
    count_ref, functional_ref, placing_ref, sems = refs[9:]
    n_groups, n_blocks = count_ref.shape[1:]
    slots, band_rows = n_rows * cap, n_rows * rows
    copies = []

    def send(source, target):
        copies.extend(started([pltpu.make_async_copy(source, target, sems.at[len(copies)])]))

    sums = jnp.sum(tile_ref[...], axis=1)
    line = lax.broadcasted_iota(jnp.int32, (n_func, sums.shape[1]), 0)
    sums = jnp.concatenate([sums, jnp.zeros((n_func - n_tiles, sums.shape[1]), jnp.float32)], axis=0)
    n_diag = inverse_ref.shape[0]
    totals = []
    for d in range(n_diag):
        minus = -jnp.sum(table_ref[d], axis=0, keepdims=True)
        totals.append(-jnp.sum(minus, axis=1, keepdims=True))
        wanted = jnp.where(line == n_tiles, minus, sums)
        high, low = halves(inverse_ref[d])
        right = jnp.concatenate([high, high, low], axis=0)
        solved = jnp.dot(left_operand(wanted), right, preferred_element_type=jnp.float32)
        solved = jnp.where(line == n_tiles + 1, 1.0, solved)
        functional_ref[d * n_func : (d + 1) * n_func, :] = left_operand(solved)
    send(functional_ref, functional_out)

    lists = list_ref[...]
    asker = lax.broadcasted_iota(jnp.int32, lists.shape, 0)
    codes = asker * rows + below(over(lists, rows * n_tiles), rows)
    codes = jnp.where(lists > 0, codes, -1).astype(jnp.float32)
    spread = lax.broadcasted_iota(jnp.int32, (slots, n_rows), 0)
    spread = lax.div(spread, cap) == lax.broadcasted_iota(jnp.int32, (slots, n_rows), 1)
    codes = jnp.dot(
        jnp.where(spread, 1.0, 0.0), codes, precision=HIGH, preferred_element_type=jnp.float32
    )
    rank = lax.rem(lax.broadcasted_iota(jnp.int32, codes.shape, 0), cap)
    lane = lax.broadcasted_iota(jnp.int32, codes.shape, 1)
    asked = jnp.sum(jnp.where(rank == lane, codes, 0.0), axis=1, keepdims=True)
    asked = jnp.where(asked < 0.0, asked - 0.5, asked + 0.5).astype(jnp.int32)
    own = lax.axis_index("rows") * rows + lax.broadcasted_iota(jnp.int32, (rows, 1), 0)
    band = lax.axis_index("band")

    def field(n, side):
        return field_ref[n, side : side + 1, :]

    row_ids = lax.broadcasted_iota(jnp.int32, (1, band_rows), 1)
    sides = []
    for side, targets in ((0, jnp.concatenate([asked, own], axis=0)), (1, own)):
        first = band == side
        across = jnp.where(first, field(2 + width_k, 1 - side), field(3 + width_k, 1 - side))
        takers = [field(2 + k, side) * n_groups + field(0, side) for k in range(width_k)]
        takers.append(across * n_groups + field(0, 1 - side))
        takers = jnp.concatenate(takers, axis=1)
        origins = [field(4 + width_k + k, side) for k in range(width_k)] + [row_ids]
        hits = one_hot(targets, jnp.concatenate(origins, axis=1))
        sides.append((takers, hits, field(0, side)))
    for t in range(n_tiles):
        found = []
        for takers, hits, _ in sides:
            ids = lax.broadcasted_iota(jnp.int32, (n_groups, takers.shape[1]), 0) + t * n_groups
            found.append(dot_nt(one_hot(ids, takers), hits))
        count_ref[t] = jnp.concatenate(found, axis=1).astype(jnp.bfloat16)
        send(count_ref.at[t], count_out.at[t])
    ids = lax.broadcasted_iota(jnp.int32, (n_groups, band_rows), 0)
    found = [dot_nt(one_hot(ids, groups), hits[:, -band_rows:]) for _, hits, groups in sides]
    found = jnp.concatenate(found, axis=1)
    count_ref[n_tiles] = found.astype(jnp.bfloat16)
    send(count_ref.at[n_tiles], count_out.at[n_tiles])
    block = lax.broadcasted_iota(jnp.int32, found.shape, 1)
    mine = (block >= slots) & (block < slots + rows)
    count_ref[n_tiles + 1] = jnp.where(mine, found, 0.0).astype(jnp.bfloat16)
    send(count_ref.at[n_tiles + 1], count_out.at[n_tiles + 1])

    per_tile = LANES // n_rhs
    depth = rows // per_tile
    length = n_rows * 2 * depth
    order = lax.broadcasted_iota(jnp.int32, (per_tile * length, 1), 0)
    spot, order = lax.div(order, length), lax.rem(order, length)
    device, order = lax.div(order, 2 * depth), lax.rem(order, 2 * depth)
    side, order = lax.div(order, depth), lax.rem(order, depth)
    order = side * band_rows + device * rows + spot * depth + order
    member = [
        one_hot(ids, jnp.where(band == which, field(0, 0), field(0, 1))) for which in range(2)
    ]
    placing = jnp.zeros(placing_ref.shape, jnp.float32)
    for which in range(2):
        placing = placing + dot_nt(one_hot(order, row_ids + which * band_rows), member[which])
    placing_ref[...] = placing.astype(jnp.bfloat16)
    send(placing_ref, placing_out)
    whole = jnp.zeros((n_groups, 1), jnp.float32)
    for side in range(2):
        sums = jnp.zeros((1, band_rows), jnp.float32)
        for d in range(n_diag):
            sums = jnp.where(field(1, side) == d, totals[d], sums)
        weighted = jnp.where(ids == field(0, side), sums, 0.0)
        whole = whole + jnp.sum(weighted, axis=1, keepdims=True)
    scale = place(placing_ref, jnp.broadcast_to(whole, (n_groups, LANES)), n_rhs, 3)
    mine = jnp.zeros(scale_ref.shape, jnp.float32)
    here = lax.axis_index("rows") * 2 + band
    for n in range(2 * n_rows):
        mine = jnp.where(here == n, scale[n * depth : (n + 1) * depth, :], mine)
    scale_ref[...] = mine
    finish(copies)


def gather_solve(
    sizes, slots, diags, arrived_ref, later, terms, inverse_ref, sum_ref, product_ref
):
    rows, n_rows, cap, n_tiles, n_rhs = sizes
    per = n_rows * cap // arrived_ref.shape[0]
    for row in range(rows):
        total = None
        for slot in slots(row):
            start = pl.multiple_of(below(slot, per) * n_rhs, n_rhs)
            block = arrived_ref[over(slot, per), pl.ds(start, n_rhs), :]
            total = block if total is None else total + block
        sum_ref[pl.ds(row * n_rhs, n_rhs), :] = total
    finish(later)
    total = sum_ref[...]
    for term in terms:
        total = total + term[...].reshape(total.shape)
    table_products(total, inverse_ref, product_ref)
    for row in range(rows):
        sum_ref[pl.ds(row * n_rhs, n_rhs), :] = product_ref[diags(row) * rows + row]


def middle_kernel(sizes, width_k, n_band, dense, *refs):
    metadata_in, arrived_ref, inverse_ref, tile_ref = list(refs[:4]), *refs[4:7]
    metadata_in[2] = metadata_in[2].at[:, :, pl.ds(0, LANES)]
    terms_in, refs = refs[7 : 8 + n_band], refs[8 + n_band :]
    extra, refs = (refs[:3], refs[3:]) if dense else ((), refs)
    send_out, band_out, refs = refs[0], refs[1 : 1 + n_band], refs[1 + n_band :]
    metadata, sum_ref, product_ref, send_ref = refs[:4], *refs[4:7]
    place_ref, index_ref, list_ref, near_ref = metadata
    terms, band_refs, refs = refs[7 : 8 + n_band], refs[8 + n_band : 8 + 2 * n_band], refs[8 + 2 * n_band :]
    term_sems, meta_sems, send_sems, refs = *refs[:3], refs[3:]
    right_ref = terms[0]
    rows, n_rows, cap, n_tiles, n_rhs = sizes
    body = cap * n_rhs
    metadata = copies_of(zip(metadata_in, metadata), meta_sems)
    later = copies_of(zip(terms_in, terms), term_sems)
    fetched = []
    if dense:
        held, extra_sems, value_ref, spread_ref, result_ref = refs[:3], *refs[3:]
        n_diag = inverse_ref.shape[0]
        fetched = copies_of(zip(extra, held), extra_sems)
    finish(metadata)

    def slots(row):
        return [place_ref[0, 0, k * rows + row] for k in range(width_k)]

    def diags(row):
        return index_ref[0, 0, rows + row]

    gather_solve(sizes, slots, diags, arrived_ref, later, terms, inverse_ref, sum_ref, product_ref)
    table_products(sum_ref[...], tile_ref, product_ref)
    copies = []

    def send(source, target):
        copies.extend(started([pltpu.make_async_copy(source, target, send_sems.at[len(copies)])]))

    pack_bands(sizes, width_k, product_ref, near_ref, band_refs)
    for ref, out in zip(band_refs, band_out):
        send(ref, out)
    codes = []
    for owner in range(n_rows):
        for rank in range(cap):
            code = list_ref[owner, 0, rank]
            codes.append(code)
            block = product_ref[below(code, rows * n_tiles)]
            send_ref[owner, rank * n_rhs : (rank + 1) * n_rhs, :] = block
        target = send_out.at[owner]
        send(send_ref.at[owner], target.at[pl.ds(0, body)] if dense else target)
    if dense:
        finish(fetched)
        kinds = [below(over(code, rows * n_tiles * rows), n_diag) for code in codes]
        kinds += [diags(row) for row in range(rows)]
        kinds += [near_ref[0, 0, rows + row] for row in range(rows)]
        result = coarse_parts(
            sizes, kinds, held, right_ref, send_ref, band_refs, value_ref, spread_ref
        )
        result_ref[...] = result.reshape(result_ref.shape)
        send(result_ref, send_out.at[:, pl.ds(body, result_ref.shape[1])])
    finish(copies)


def coarse_parts(sizes, kinds, held, right_ref, send_ref, band_refs, value_ref, spread_ref):
    functional_ref, count_ref, place_ref = held
    rows, n_rows, cap, n_tiles, n_rhs = sizes
    body = cap * n_rhs
    n_func = spread_ref.shape[0] // count_ref.shape[2]
    per_tile = LANES // n_rhs
    functional = functional_ref[...]
    done = 0
    for owner in range(0, n_rows, 2):
        values = [send_ref[owner + more] for more in range(2)]
        values = jnp.concatenate(values, axis=0)
        value_ref[:, done : done + 2 * body] = dot_nt(functional, right_operand(values))
        done += 2 * body
    for ref in (right_ref, *band_refs):
        values = ref[...].reshape(rows * n_rhs, -1)
        value_ref[:, done : done + rows * n_rhs] = dot_nt(functional, right_operand(values))
        done += rows * n_rhs
    lane = lax.broadcasted_iota(jnp.int32, (n_func, LANES), 1)
    for block, kind in enumerate(kinds):
        tile, spot = block // per_tile, block % per_tile
        start = pl.multiple_of(kind * n_func, n_func)
        piece = value_ref[pl.ds(start, n_func), tile * LANES : (tile + 1) * LANES]
        piece = jnp.where((lane >= spot * n_rhs) & (lane < (spot + 1) * n_rhs), piece, 0.0)
        spread_ref[block * n_func : (block + 1) * n_func, :] = piece
    partial = jnp.zeros((count_ref.shape[1], 2 * LANES), jnp.float32)
    for t in range(count_ref.shape[0]):
        values = spread_ref[pl.ds(t, done // n_rhs, stride=n_func), :]
        partial = partial + jnp.dot(
            count_ref[t],
            jnp.concatenate(halves(values), axis=1),
            preferred_element_type=jnp.float32,
        )
    partial = partial[:, :LANES] + partial[:, LANES:]
    source = lax.broadcasted_iota(jnp.int32, (LANES, LANES), 0)
    target = lax.broadcasted_iota(jnp.int32, (LANES, LANES), 1)
    same = jnp.where(lax.rem(source, n_rhs) == lax.rem(target, n_rhs), 1.0, 0.0)
    same = same.astype(jnp.bfloat16)
    same = jnp.concatenate([same, same], axis=0)
    partial = jnp.dot(
        jnp.concatenate(halves(partial), axis=1), same, preferred_element_type=jnp.float32
    )
    return place(place_ref, partial, n_rhs, 2)


def part_kernel(arrived_ref, mine_ref, other_ref):
    depth = mine_ref.shape[0]
    body = arrived_ref.shape[1] - 2 * depth
    total = arrived_ref[0, body:, :]
    for source in range(1, arrived_ref.shape[0]):
        total = total + arrived_ref[source, body:, :]
    upper = lax.axis_index("band") == 0
    mine_ref[...] = jnp.where(upper, total[:depth], total[depth:])
    other_ref[...] = jnp.where(upper, total[depth:], total[:depth])


def last_kernel(sizes, width_k, n_band, *refs):
    metadata_in, arrived_ref, inverse_ref = refs[:2], *refs[2:4]
    terms_in, refs = refs[4 : 5 + n_band], refs[5 + n_band :]
    second_ref, metadata, sum_ref, product_ref = refs[0], refs[1:3], *refs[3:5]
    place_ref, index_ref = metadata
    terms, (term_sems, meta_sems) = refs[5 : 6 + n_band], refs[6 + n_band :]
    rows = sizes[0]
    metadata = copies_of(zip(metadata_in, metadata), meta_sems)
    later = copies_of(zip(terms_in, terms), term_sems)
    finish(metadata)

    def slots(row):
        return [place_ref[0, 0, (width_k + k) * rows + row] for k in range(width_k)]

    def diags(row):
        return index_ref[0, 0, rows + row]

    gather_solve(sizes, slots, diags, arrived_ref, later, terms, inverse_ref, sum_ref, product_ref)
    second_ref[...] = sum_ref[...].reshape(second_ref.shape)


def final_kernel(sizes, mine_ref, other_ref, scale_ref, second_ref, out_ref):
    rows, n_rhs = sizes[0], sizes[4]
    depth = scale_ref.shape[0]
    correction = (mine_ref[...] + other_ref[...]) / scale_ref[...]
    padded = jnp.concatenate([correction, jnp.zeros((8 - depth, LANES), jnp.float32)], axis=0)
    turned = padded.T
    for row in range(rows):
        spot, place = row // depth, row % depth
        column = turned[spot * n_rhs : (spot + 1) * n_rhs, place : place + 1]
        out_ref[row] = second_ref[row] + column


def shifted(value, axis, steps):
    count = lax.axis_size(axis)
    initial, last = (max(0, -steps), min(count, count - steps))
    return lax.ppermute(value, axis, [(source, source + steps) for source in range(initial, last)])


def to_bands(sends):
    if len(sends) == 1:
        return (lax.ppermute(sends[0], "band", [(0, 1), (1, 0)]),)
    return shifted(sends[0], "band", 1), shifted(sends[1], "band", -1)


def on_device(
    start_iterate,
    right_side,
    diag_table,
    inverse_table,
    coupling_tiles,
    diag_index,
    tile_index,
    source_owner,
    source_local,
    aggregate_map,
):
    rows, n_rhs, states = start_iterate.shape
    width_k = source_owner.shape[1]
    n_tiles, n_diag = coupling_tiles.shape[0], inverse_table.shape[0]
    n_rows, n_bands = lax.axis_size("rows"), lax.axis_size("band")
    n_dev = n_rows * n_bands
    cap = max(2, 2 * width_k * rows // n_rows)
    slots = n_rows * cap
    total_groups = AGG_DEV * n_dev
    per_tile = LANES // n_rhs
    depth = rows // per_tile
    n_func = 16
    dense = (
        n_bands == 2
        and n_dev * rows * total_groups <= DENSE_LIMIT
        and depth == 4
        and n_diag * n_func == LANES
        and n_tiles + 2 <= n_func
    )
    sizes = (rows, n_rows, cap, n_tiles, n_rhs)
    f32, i32 = jnp.float32, jnp.int32
    my_band = lax.axis_index("band")
    my_row = lax.axis_index("rows")

    half = n_rows // 2
    wide = -(-(4 + 2 * width_k) * rows // LANES) * LANES
    place_wide = -(-2 * width_k * rows // LANES) * LANES
    index_shapes = [(width_k, rows), (width_k, rows), (width_k + 2, rows), (1, rows), (1, rows)]
    halves_of_rows = [list(range(half)), list(range(half, n_rows))]
    to_mirror = [(i, (i + half) % n_rows) for i in range(n_rows)]
    mirror = lax.ppermute(start_iterate, "rows", to_mirror)
    lists, index, places = call(
        functools.partial(request_kernel, (rows, n_rows, cap, n_tiles, n_diag)),
        (
            jax.ShapeDtypeStruct((n_rows, 1, LANES + wide), i32),
            jax.ShapeDtypeStruct((1, 1, wide), i32),
            jax.ShapeDtypeStruct((1, 1, place_wide), i32),
        ),
        [HBM] * 5,
        [VMEM] * 3,
        [*[pltpu.VMEM(shape, i32) for shape in index_shapes], pltpu.SemaphoreType.DMA((5,))],
    )(source_owner.T, source_local.T, tile_index.T, diag_index[None], aggregate_map.T)
    lists = lax.all_to_all(lists, "rows", split_axis=0, concat_axis=0, tiled=True)
    if n_bands == 2:
        near = lax.ppermute(index, "band", [(0, 1), (1, 0)])
    else:
        ways = [[(b, (b + step) % n_bands) for b in range(n_bands)] for step in (-1, 1)]
        near = jnp.concatenate([lax.ppermute(index, "band", way) for way in ways], axis=0)

    n_ways = 1 if n_bands == 2 else 2
    block = (rows, n_rhs, states)
    band_shapes = [jax.ShapeDtypeStruct(block, f32)] * n_ways
    band_scratch = [pltpu.VMEM(block, f32)] * n_ways
    term_scratch = [pltpu.VMEM(block, f32)] * (1 + n_ways)
    term_sems = pltpu.SemaphoreType.DMA((1 + n_ways,))
    list_scratch = pltpu.SMEM((half, 1, LANES), i32)
    near_scratch = pltpu.SMEM((n_ways, 1, wide), i32)
    row_scratch = [pltpu.SMEM((1, 1, place_wide), i32), pltpu.SMEM((1, 1, wide), i32)]
    flat = rows * n_rhs
    sums = pltpu.VMEM((flat, states), f32)
    products = pltpu.VMEM((max(n_tiles, n_diag) * rows, n_rhs, states), f32)
    work = 6 * flat * states * states
    made_shape = (n_tiles * rows, n_rhs, states)
    table_scratch = [pltpu.VMEM(coupling_tiles.shape, f32)]
    table_sems = pltpu.SemaphoreType.DMA((-(-n_tiles // 2),))
    made = call(
        product_kernel,
        jax.ShapeDtypeStruct(made_shape, f32),
        [HBM, HBM],
        HBM,
        [
            pltpu.VMEM(block, f32),
            *table_scratch,
            pltpu.VMEM(made_shape, f32),
            pltpu.SemaphoreType.DMA((1 + n_tiles,)),
            table_sems,
        ],
        work * n_tiles,
        4 << 20,
    )(start_iterate, coupling_tiles)
    packed, *bands = call(
        functools.partial(first_kernel, sizes, width_k, n_ways),
        (jax.ShapeDtypeStruct((half, 2 * cap, n_rhs, states), f32), *band_shapes),
        [HBM, VMEM, VMEM, ANY, ANY],
        [HBM] * (1 + n_ways),
        [
            pltpu.VMEM((2, *made_shape), f32),
            list_scratch,
            near_scratch,
            pltpu.VMEM((half, 2 * cap, n_rhs, states), f32),
            *band_scratch,
            pltpu.SemaphoreType.DMA((n_tiles,)),
            pltpu.SemaphoreType.DMA((2,)),
            pltpu.SemaphoreType.DMA((half + n_ways,)),
        ],
        work * n_tiles,
        4 << 20,
    )(made, mirror, coupling_tiles, lists, near)
    packed, late = lax.optimization_barrier((packed, lists))
    if dense:
        across = lax.ppermute(late, "band", [(0, 1), (1, 0)])
        across, *bands = lax.optimization_barrier((across, *bands))
    sends = (packed.reshape(half, 2 * cap * n_rhs, states), *bands)
    halves_of_rows = [list(range(half)), list(range(half, n_rows))]
    def exchange(sends, groups=None):
        arrived = lax.all_to_all(
            sends[0], "rows", split_axis=0, concat_axis=0, tiled=True, axis_index_groups=groups
        )
        return arrived, to_bands(sends[1:])

    arrived_blocks, arrived_bands = exchange(sends, halves_of_rows)

    extra, extra_scratch, tail = (), [], 0
    if dense:
        fields = jnp.stack([late, across])[:, :, 0, LANES:]
        fields = fields.reshape(2, n_rows, -1, rows).transpose(2, 0, 1, 3)
        fields = fields.reshape(-1, 2, n_rows * rows)
        n_blocks = slots + 2 * rows
        length = n_dev * depth
        extra_shapes = [
            ((n_diag * n_func, 3 * states), jnp.bfloat16),
            ((n_tiles + 2, total_groups, n_blocks), jnp.bfloat16),
            ((per_tile * length, total_groups), jnp.bfloat16),
        ]
        functional_shape, count_shape, placing_shape = extra_shapes
        counts, functionals, placing, scale = call(
            functools.partial(count_kernel, sizes, width_k, n_func),
            (
                jax.ShapeDtypeStruct(*count_shape),
                jax.ShapeDtypeStruct(*functional_shape),
                jax.ShapeDtypeStruct(*placing_shape),
                jax.ShapeDtypeStruct((depth, LANES), f32),
            ),
            [VMEM] * 5,
            [HBM, HBM, HBM, VMEM],
            [
                pltpu.VMEM(*count_shape),
                pltpu.VMEM(*functional_shape),
                pltpu.VMEM(*placing_shape),
                pltpu.SemaphoreType.DMA((n_tiles + 4,)),
            ],
            4 * total_groups * n_tiles * n_dev * rows * n_blocks,
            4 << 20,
        )(fields, late[:, 0, :LANES], coupling_tiles, diag_table, inverse_table)
        extra = (functionals, counts, placing)
        extra_scratch = [
            *[pltpu.VMEM(*shape) for shape in extra_shapes],
            pltpu.SemaphoreType.DMA((3,)),
            pltpu.VMEM((n_diag * n_func, n_blocks * n_rhs), f32),
            pltpu.VMEM((n_blocks * n_func, LANES), f32),
            pltpu.VMEM((n_rows, n_bands * depth, LANES), f32),
        ]
        tail = n_bands * depth

    send_shape = (n_rows, cap * n_rhs + tail, states)
    sends = call(
        functools.partial(middle_kernel, sizes, width_k, n_ways, dense),
        (jax.ShapeDtypeStruct(send_shape, f32), *band_shapes),
        [ANY] * 4 + [VMEM] * 3 + [HBM] + [ANY] * n_ways + [HBM] * len(extra),
        [HBM] * (1 + n_ways),
        [
            *row_scratch,
            pltpu.SMEM((n_rows, 1, LANES), i32),
            near_scratch,
            sums,
            products,
            pltpu.VMEM((n_rows, cap * n_rhs, states), f32),
            *term_scratch,
            *band_scratch,
            term_sems,
            pltpu.SemaphoreType.DMA((4,)),
            pltpu.SemaphoreType.DMA((n_rows + n_ways + 1,)),
            *extra_scratch,
        ],
        work * (n_tiles + n_diag),
        4 << 20,
    )(
        places,
        index,
        lists,
        near,
        arrived_blocks,
        inverse_table,
        coupling_tiles,
        right_side,
        *arrived_bands,
        *extra,
    )
    arrived_blocks, arrived_bands = exchange(sends)

    if dense:
        part = jax.ShapeDtypeStruct((depth, LANES), f32)
        mine, other = call(part_kernel, (part, part), [VMEM], [VMEM] * 2)(arrived_blocks)
        other = lax.ppermute(other, "band", [(0, 1), (1, 0)])
    second = call(
        functools.partial(last_kernel, sizes, width_k, n_ways),
        jax.ShapeDtypeStruct(block, f32),
        [ANY] * 2 + [VMEM] * 2 + [HBM] + [ANY] * n_ways,
        VMEM,
        [
            *row_scratch,
            sums,
            products,
            *term_scratch,
            term_sems,
            pltpu.SemaphoreType.DMA((2,)),
        ],
        work * n_diag,
        4 << 20,
    )(places, index, arrived_blocks, inverse_table, right_side, *arrived_bands)
    if dense:
        return call(
            functools.partial(final_kernel, sizes),
            jax.ShapeDtypeStruct(block, f32),
            [VMEM] * 4,
            VMEM,
        )(mine, other, scale, second)

    groups = aggregate_map[:, 0]
    own = jnp.arange(rows, dtype=i32)
    index_all = lax.all_gather(index, ("band", "rows"), axis=0, tiled=True)
    index_all = index_all.reshape(n_bands, n_rows, wide)
    groups_all, diags_all = index_all[:, :, :rows], index_all[:, :, rows : 2 * rows]
    codes = lists[:, 0, :cap]
    asked = jnp.arange(n_rows, dtype=i32)[:, None] * rows + codes // (rows * n_tiles) % rows
    asked = jnp.where(codes > 0, asked, -1).reshape(-1)
    table_sums = jnp.sum(diag_table, axis=(1, 2))
    diag_onehot = diags_all.reshape(-1, 1) == jnp.arange(n_diag, dtype=i32)[None]
    block_sums = jnp.sum(jnp.where(diag_onehot, table_sums[None], 0.0), axis=1)
    whole_diag = jnp.sum(
        jnp.where(groups[:, None] == groups_all.reshape(-1)[None], block_sums[None], 0.0), axis=1
    )
    above, below = near[0, 0], near[-1, 0]
    place_of = (2 + width_k) * rows
    band_tiles = jnp.stack([above[place_of : place_of + rows], below[place_of + rows : place_of + 2 * rows]])
    band_groups = jnp.stack([above[:rows], below[:rows]])
    band_valid = jnp.stack([my_band + 1 < n_bands, my_band > 0])
    band_valid = jnp.broadcast_to(band_valid[:, None], (2, rows))
    n_all = n_tiles + n_diag + 1
    code = codes.reshape(-1)
    band_of_mine = lax.dynamic_index_in_dim(groups_all, my_band, 0, keepdims=False).reshape(-1)
    entry_group = jnp.concatenate(
        [jnp.take(band_of_mine, jnp.maximum(asked, 0)), band_groups.reshape(-1), groups, groups]
    )
    entry_func = jnp.concatenate(
        [
            (code % rows) * n_all + (code // rows) % n_tiles,
            (own[None] * n_all + band_tiles).reshape(-1),
            own * n_all + n_tiles + diag_index,
            own * n_all + n_tiles + n_diag,
        ]
    )
    entry_valid = jnp.concatenate([asked >= 0, band_valid.reshape(-1), jnp.ones((2 * rows,), bool)])
    functionals = jnp.concatenate(
        [jnp.sum(coupling_tiles, axis=1), -jnp.sum(diag_table, axis=1)], axis=0
    )
    weights = jnp.einsum("fp,rcp->rfc", functionals, second, precision=HIGH)
    weights = jnp.concatenate([weights, jnp.sum(right_side, axis=2)[:, None]], axis=1)
    chosen = jnp.take(weights.reshape(rows * n_all, n_rhs), entry_func, axis=0)
    chosen = jnp.where(entry_valid[:, None], chosen, 0.0)
    partial = jax.ops.segment_sum(chosen, entry_group, num_segments=total_groups)
    whole = lax.psum(partial, ("band", "rows"))
    correction = jnp.take(whole, groups, axis=0) / whole_diag[:, None]
    return second + correction[:, :, None]


def solution(mesh):
    in_specs = (
        P(("band", "rows"), None, None),
        P(("band", "rows"), None, None),
        P(),
        P(),
        P(),
        P(("band", "rows")),
        P(("band", "rows"), None),
        P(("band", "rows"), None),
        P(("band", "rows"), None),
        P(("band", "rows"), None),
    )
    out_specs = P(("band", "rows"), None, None)
    return jax.shard_map(
        on_device, mesh=mesh, in_specs=in_specs, out_specs=out_specs, check_vma=False
    )
```

```python
import functools

import jax
import jax.numpy as jnp
from jax import lax
from jax.experimental import pallas as pl
from jax.experimental.pallas import tpu as pltpu
from jax.sharding import PartitionSpec as P

AGG_DEV = 8
LANES = 128
DENSE_LIMIT = 1 << 19
BEHIND_SWAP = 100

VMEM = pl.BlockSpec(memory_space=pltpu.VMEM)
SMEM = pl.BlockSpec(memory_space=pltpu.SMEM)
HBM = pl.BlockSpec(memory_space=pltpu.HBM)
ANY = pl.BlockSpec(memory_space=pl.ANY)
HIGH = lax.Precision.HIGHEST


def params():
    return pltpu.CompilerParams(vmem_limit_bytes=24 * 1024 * 1024)


def call(kernel, out_shape, in_specs, out_specs, scratch=(), flops=0, moved=0):
    def shaped(shape, spec):
        return pltpu.HBM(shape.shape, shape.dtype) if spec is HBM else shape

    if isinstance(out_shape, (tuple, list)):
        out_shape = [shaped(*pair) for pair in zip(out_shape, out_specs)]
    else:
        out_shape = shaped(out_shape, out_specs)
    run = pl.pallas_call(
        kernel,
        out_shape=out_shape,
        in_specs=in_specs,
        out_specs=out_specs,
        scratch_shapes=list(scratch),
        compiler_params=params(),
        cost_estimate=pl.CostEstimate(flops=flops, bytes_accessed=moved, transcendentals=0),
    )

    def apply(*args):
        pinned = [
            pltpu.with_memory_space_constraint(arg, pltpu.HBM) if spec is HBM else arg
            for arg, spec in zip(args, in_specs)
        ]
        return run(*pinned)

    return apply


def below(value, bound):
    return value & (bound - 1) if bound & (bound - 1) == 0 else lax.rem(value, bound)


def over(value, bound):
    if bound & (bound - 1) == 0:
        return lax.shift_right_logical(value, bound.bit_length() - 1)
    return lax.div(value, bound)


def halves(value):
    high = value.astype(jnp.bfloat16)
    low = (value - high.astype(jnp.float32)).astype(jnp.bfloat16)
    return high, low


def left_operand(value):
    high, low = halves(value)
    return jnp.concatenate([high, low, high], axis=1)


def right_operand(value):
    high, low = halves(value)
    return jnp.concatenate([high, high, low], axis=1)


def dot_nt(left, right):
    return lax.dot_general(
        left, right, (((1,), (1,)), ((), ())), preferred_element_type=jnp.float32
    )


def table_products(value, table_ref, out_ref, done=None, loads=None):
    left = left_operand(value)
    count, width = table_ref.shape[0], table_ref.shape[1]
    n_rhs = out_ref.shape[1]
    rows = left.shape[0] // n_rhs
    for first in range(0, count, 2):
        last = min(first + 2, count)
        if loads is not None:
            loads[first // 2].wait()
        right = right_operand(table_ref[first:last].reshape((last - first) * width, -1))
        product = dot_nt(left, right)
        for t in range(first, last):
            part = product[:, (t - first) * width : (t - first + 1) * width]
            out_ref[t * rows : (t + 1) * rows] = part.reshape(rows, n_rhs, width)
        if done is not None:
            done(first * rows, (last - first) * rows)


def started(copies):
    for copy in copies:
        copy.start()
    return copies


def finish(copies):
    for copy in copies:
        copy.wait()


def request_kernel(sizes, *refs):
    rows, n_rows, cap, n_tiles, n_diag = sizes
    inputs, (list_ref, index_ref, place_ref), held, sems = refs[:5], refs[5:8], refs[8:13], refs[13]
    finish(
        started([pltpu.make_async_copy(i, h, sems.at[n]) for n, (i, h) in enumerate(zip(inputs, held))])
    )
    owner_ref, local_ref, tile_ref, diag_ref, group_ref = held
    width_k = owner_ref.shape[0]
    half = n_rows // 2
    row_of = lax.broadcasted_iota(jnp.int32, (rows, rows), 0)
    col_of = lax.broadcasted_iota(jnp.int32, (rows, rows), 1)
    lane = lax.broadcasted_iota(jnp.int32, (rows, LANES), 1)
    owners = lax.broadcasted_iota(jnp.int32, (n_rows, rows), 0)

    def column(row):
        return jnp.sum(jnp.where(row_of == col_of, row, 0), axis=1, keepdims=True)

    def owner_row(k):
        return owner_ref[k : k + 1, :]

    row_ids = lax.broadcasted_iota(jnp.int32, (1, rows), 1)
    owner_columns = [column(owner_row(k)) for k in range(width_k)]
    lists = jnp.zeros((n_rows, LANES), jnp.float32)
    places, half_places = [], []
    for k in range(width_k):
        rank = jnp.zeros((1, rows), jnp.int32)
        for other in range(k + 1):
            match = owner_columns[other] == owner_row(k)
            if other == k:
                match = match & (row_of < col_of)
            rank = rank + jnp.sum(jnp.where(match, 1, 0), axis=0, keepdims=True)
        places.append(owner_row(k) * cap + rank)
        same = (owner_row(k) >= half) == (lax.axis_index("rows") >= half)
        holder = jnp.where(owner_row(k) >= half, owner_row(k) - half, owner_row(k))
        half_places.append(holder * (2 * cap) + rank + jnp.where(same, 0, cap))
        taker = row_ids + rows * (diag_ref[...] + n_diag)
        code = local_ref[k : k + 1, :] + rows * (tile_ref[k : k + 1, :] + n_tiles * taker)
        code, rank = column(code), column(rank)
        mirror = jnp.where(owner_row(k) >= half, owner_row(k) - half, owner_row(k) + half)
        for owner, base in ((owner_row(k), 0), (mirror, LANES // 2)):
            by_rank = jnp.where(lane == rank + base, code, 0).astype(jnp.float32)
            mine = jnp.where(owners == owner, 1.0, 0.0)
            lists = lists + jnp.dot(
                mine, by_rank, precision=HIGH, preferred_element_type=jnp.float32
            )
    lists = (lists + 0.5).astype(jnp.int32)

    def joined(parts, wide):
        spare = wide - len(parts) * rows
        if spare:
            parts = [*parts, jnp.zeros((1, spare), jnp.int32)]
        return jnp.concatenate(parts, axis=1)

    index = [group_ref[...], diag_ref[...]]
    index += [tile_ref[k : k + 1, :] for k in range(width_k + 2)]
    index += [owner_row(k) * rows + local_ref[k : k + 1, :] for k in range(width_k)]
    index = joined(index, index_ref.shape[2])
    index_ref[0] = index
    place_ref[0] = joined(half_places + places, place_ref.shape[2])
    for device in range(n_rows):
        list_ref[device] = jnp.concatenate([lists[device : device + 1, :], index], axis=1)


def copies_of(pairs, sems):
    return started([pltpu.make_async_copy(i, h, sems.at[n]) for n, (i, h) in enumerate(pairs)])


def band_field(rows, width_k, way, n_ways):
    field = (2 + width_k) * rows
    if n_ways == 1:
        return field + jnp.where(lax.axis_index("band") == 0, 0, rows)
    return field + way * rows


def pack_bands(sizes, width_k, product_ref, near_ref, band_refs):
    rows = sizes[0]
    for way, band_ref in enumerate(band_refs):
        field = band_field(rows, width_k, way, len(band_refs))
        for row in range(rows):
            band_ref[row] = product_ref[near_ref[way, 0, field + row] * rows + row]


def table_loads(table_in, table_ref, sems):
    copies = []
    for first in range(0, table_in.shape[0], 2):
        place = pl.ds(first, min(2, table_in.shape[0] - first))
        source, target = table_in.at[place], table_ref.at[place]
        copies.append(pltpu.make_async_copy(source, target, sems.at[first // 2]))
    return started(copies)


def product_kernel(start_in, tile_in, product_out, start_ref, tile_ref, product_ref, sems, tile_sems):
    start = pltpu.make_async_copy(start_in, start_ref, sems.at[0])
    start.start()
    loads = table_loads(tile_in, tile_ref, tile_sems)
    start.wait()
    copies = []

    def done(first, count):
        place = pl.ds(first, count)
        source, target = product_ref.at[place], product_out.at[place]
        copies.extend(started([pltpu.make_async_copy(source, target, sems.at[1 + len(copies)])]))

    rows, n_rhs, states = start_ref.shape
    values = start_ref[...].reshape(rows * n_rhs, states)
    table_products(values, tile_ref, product_ref, done, loads)
    finish(copies)


def first_kernel(sizes, width_k, n_band, *refs):
    rows, n_rows, cap, n_tiles, n_rhs = sizes
    product_in, mirror_ref, tile_ref, list_in, near_in, send_out = refs[:6]
    band_out, refs = refs[6 : 6 + n_band], refs[6 + n_band :]
    product_ref, list_ref, near_ref, send_ref = refs[:4]
    band_refs, (load_sems, meta_sems, send_sems) = refs[4 : 4 + n_band], refs[4 + n_band :]
    half = n_rows // 2
    base = jnp.where(lax.axis_index("rows") >= half, half, 0)
    list_in = list_in.at[pl.ds(base, half), :, pl.ds(0, LANES)]
    metadata = copies_of(((list_in, list_ref), (near_in, near_ref)), meta_sems)
    places = [pl.ds(tile * rows, rows) for tile in range(n_tiles)]
    loads = [(product_in.at[place], product_ref.at[0, place]) for place in places]
    loads = copies_of(loads, load_sems)
    values = mirror_ref[...].reshape(rows * n_rhs, -1)
    table_products(values, tile_ref, product_ref.at[1])
    finish(metadata)
    finish(loads)
    copies = []
    pack_bands(sizes, width_k, product_ref.at[0], near_ref, band_refs)
    for n, (ref, out) in enumerate(zip(band_refs, band_out)):
        copies += started([pltpu.make_async_copy(ref, out, send_sems.at[half + n])])
    for device in range(half):
        for slot in range(2 * cap):
            side, rank = slot // cap, slot % cap
            code = list_ref[device, 0, side * (LANES // 2) + rank]
            send_ref[device, slot] = product_ref[side, below(code, rows * n_tiles)]
        copy = pltpu.make_async_copy(send_ref.at[device], send_out.at[device], send_sems.at[device])
        copies += started([copy])
    finish(copies)


def place(place_ref, values, n_rhs, n_parts):
    per_tile = LANES // n_rhs
    length = place_ref.shape[0] // per_tile
    parts, rest = [], values
    for _ in range(n_parts):
        part = rest.astype(jnp.bfloat16)
        rest = rest - part.astype(jnp.float32)
        parts.append(part)
    parts = jnp.concatenate(parts, axis=1)
    lane = lax.broadcasted_iota(jnp.int32, (length, LANES), 1)
    result = jnp.zeros((length, LANES), jnp.float32)
    placed = jnp.dot(place_ref[...], parts, preferred_element_type=jnp.float32)
    for spot in range(per_tile):
        chosen = placed[spot * length : (spot + 1) * length]
        chosen = sum(chosen[:, n * LANES : (n + 1) * LANES] for n in range(n_parts))
        result = jnp.where((lane >= spot * n_rhs) & (lane < (spot + 1) * n_rhs), chosen, result)
    return result


def one_hot(ids, row):
    return jnp.where(ids == row, 1.0, 0.0).astype(jnp.bfloat16)


def count_kernel(sizes, width_k, n_func, *refs):
    rows, n_rows, cap, n_tiles, n_rhs = sizes
    field_ref, list_ref, tile_ref, table_ref, inverse_ref = refs[:5]
    count_out, functional_out, placing_out, scale_ref = refs[5:9]
    count_ref, functional_ref, placing_ref, sems = refs[9:]
    n_groups, n_blocks = count_ref.shape[0], count_ref.shape[1] // (n_tiles + 2)
    slots, band_rows = n_rows * cap, n_rows * rows
    copies = []

    def send(source, target):
        copies.extend(started([pltpu.make_async_copy(source, target, sems.at[len(copies)])]))

    sums = jnp.sum(tile_ref[...], axis=1)
    line = lax.broadcasted_iota(jnp.int32, (n_func, sums.shape[1]), 0)
    sums = jnp.concatenate([sums, jnp.zeros((n_func - n_tiles, sums.shape[1]), jnp.float32)], axis=0)
    n_diag = inverse_ref.shape[0]
    totals = []
    for d in range(n_diag):
        minus = -jnp.sum(table_ref[d], axis=0, keepdims=True)
        totals.append(-jnp.sum(minus, axis=1, keepdims=True))
        wanted = jnp.where(line == n_tiles, minus, sums)
        high, low = halves(inverse_ref[d])
        right = jnp.concatenate([high, high, low], axis=0)
        solved = jnp.dot(left_operand(wanted), right, preferred_element_type=jnp.float32)
        solved = jnp.where(line == n_tiles + 1, 1.0, solved)
        functional_ref[d * n_func : (d + 1) * n_func, :] = left_operand(solved)
    send(functional_ref, functional_out)

    lists = list_ref[...]
    asker = lax.broadcasted_iota(jnp.int32, lists.shape, 0)
    codes = asker * rows + below(over(lists, rows * n_tiles), rows)
    codes = jnp.where(lists > 0, codes, -1).astype(jnp.float32)
    spread = lax.broadcasted_iota(jnp.int32, (slots, n_rows), 0)
    spread = lax.div(spread, cap) == lax.broadcasted_iota(jnp.int32, (slots, n_rows), 1)
    codes = jnp.dot(
        jnp.where(spread, 1.0, 0.0), codes, precision=HIGH, preferred_element_type=jnp.float32
    )
    rank = lax.rem(lax.broadcasted_iota(jnp.int32, codes.shape, 0), cap)
    lane = lax.broadcasted_iota(jnp.int32, codes.shape, 1)
    asked = jnp.sum(jnp.where(rank == lane, codes, 0.0), axis=1, keepdims=True)
    asked = jnp.where(asked < 0.0, asked - 0.5, asked + 0.5).astype(jnp.int32)
    own = lax.axis_index("rows") * rows + lax.broadcasted_iota(jnp.int32, (rows, 1), 0)
    band = lax.axis_index("band")

    def field(n, side):
        return field_ref[n, side : side + 1, :]

    row_ids = lax.broadcasted_iota(jnp.int32, (1, band_rows), 1)
    sides = []
    for side, targets in ((0, jnp.concatenate([asked, own], axis=0)), (1, own)):
        first = band == side
        across = jnp.where(first, field(2 + width_k, 1 - side), field(3 + width_k, 1 - side))
        takers = [field(2 + k, side) * n_groups + field(0, side) for k in range(width_k)]
        takers.append(across * n_groups + field(0, 1 - side))
        takers = jnp.concatenate(takers, axis=1)
        origins = [field(4 + width_k + k, side) for k in range(width_k)] + [row_ids]
        hits = one_hot(targets, jnp.concatenate(origins, axis=1))
        sides.append((takers, hits, field(0, side)))
    pieces = []
    for t in range(n_tiles):
        found = []
        for takers, hits, _ in sides:
            ids = lax.broadcasted_iota(jnp.int32, (n_groups, takers.shape[1]), 0) + t * n_groups
            found.append(dot_nt(one_hot(ids, takers), hits))
        pieces += found
    ids = lax.broadcasted_iota(jnp.int32, (n_groups, band_rows), 0)
    found = [dot_nt(one_hot(ids, groups), hits[:, -band_rows:]) for _, hits, groups in sides]
    found = jnp.concatenate(found, axis=1)
    block = lax.broadcasted_iota(jnp.int32, found.shape, 1)
    mine = (block >= slots) & (block < slots + rows)
    pieces += [found, jnp.where(mine, found, 0.0)]
    count_ref[...] = jnp.concatenate(pieces, axis=1).astype(jnp.bfloat16)
    send(count_ref, count_out)

    per_tile = LANES // n_rhs
    depth = rows // per_tile
    length = n_rows * 2 * depth
    order = lax.broadcasted_iota(jnp.int32, (per_tile * length, 1), 0)
    spot, order = lax.div(order, length), lax.rem(order, length)
    device, order = lax.div(order, 2 * depth), lax.rem(order, 2 * depth)
    side, order = lax.div(order, depth), lax.rem(order, depth)
    order = side * band_rows + device * rows + spot * depth + order
    member = [
        one_hot(ids, jnp.where(band == which, field(0, 0), field(0, 1))) for which in range(2)
    ]
    placing = jnp.zeros(placing_ref.shape, jnp.float32)
    for which in range(2):
        placing = placing + dot_nt(one_hot(order, row_ids + which * band_rows), member[which])
    placing_ref[...] = placing.astype(jnp.bfloat16)
    send(placing_ref, placing_out)
    whole = jnp.zeros((n_groups, 1), jnp.float32)
    for side in range(2):
        sums = jnp.zeros((1, band_rows), jnp.float32)
        for d in range(n_diag):
            sums = jnp.where(field(1, side) == d, totals[d], sums)
        weighted = jnp.where(ids == field(0, side), sums, 0.0)
        whole = whole + jnp.sum(weighted, axis=1, keepdims=True)
    scale = place(placing_ref, jnp.broadcast_to(whole, (n_groups, LANES)), n_rhs, 3)
    mine = jnp.zeros(scale_ref.shape, jnp.float32)
    here = lax.axis_index("rows") * 2 + band
    for n in range(2 * n_rows):
        mine = jnp.where(here == n, scale[n * depth : (n + 1) * depth, :], mine)
    scale_ref[...] = mine
    finish(copies)


def gather_solve(sizes, fetch, diags, later, terms, inverse_ref, sum_ref, product_ref):
    rows, n_rows, cap, n_tiles, n_rhs = sizes
    for row in range(rows):
        sum_ref[pl.ds(row * n_rhs, n_rhs), :] = fetch(row)
    finish(later)
    total = sum_ref[...]
    for term in terms:
        total = total + term[...].reshape(total.shape)
    table_products(total, inverse_ref, product_ref)
    for row in range(rows):
        sum_ref[pl.ds(row * n_rhs, n_rhs), :] = product_ref[diags(row) * rows + row]


def arrived_blocks_of(sizes, width_k, place_ref, field, arrived_ref):
    rows, n_rows, cap, n_tiles, n_rhs = sizes
    per = n_rows * cap // arrived_ref.shape[0]

    def fetch(row):
        total = None
        for k in range(width_k):
            slot = place_ref[0, 0, (field + k) * rows + row]
            start = pl.multiple_of(below(slot, per) * n_rhs, n_rhs)
            block = arrived_ref[over(slot, per), pl.ds(start, n_rhs), :]
            total = block if total is None else total + block
        return total

    return fetch


def solve_kernel(sizes, width_k, n_band, field, *refs):
    metadata_in, arrived_ref, inverse_ref = refs[:2], *refs[2:4]
    terms_in, refs = refs[4 : 5 + n_band], refs[5 + n_band :]
    out_ref, metadata, sum_ref, product_ref = refs[0], refs[1:3], *refs[3:5]
    place_ref, index_ref = metadata
    terms, (term_sems, meta_sems) = refs[5 : 6 + n_band], refs[6 + n_band :]
    rows = sizes[0]
    metadata = copies_of(zip(metadata_in, metadata), meta_sems)
    later = copies_of(zip(terms_in, terms), term_sems)
    finish(metadata)
    fetch = arrived_blocks_of(sizes, width_k, place_ref, field, arrived_ref)

    def diags(row):
        return index_ref[0, 0, rows + row]

    gather_solve(sizes, fetch, diags, later, terms, inverse_ref, sum_ref, product_ref)
    out_ref[...] = sum_ref[...].reshape(out_ref.shape)


def pack_kernel(sizes, width_k, n_band, *refs):
    rows, n_rows, cap, n_tiles, n_rhs = sizes
    list_in, near_in, first_ref, tile_ref, send_out = refs[:5]
    band_out, refs = refs[5 : 5 + n_band], refs[5 + n_band :]
    list_ref, near_ref, product_ref, send_ref = refs[:4]
    band_refs, (meta_sems, send_sems) = refs[4 : 4 + n_band], refs[4 + n_band :]
    list_in = list_in.at[:, :, pl.ds(0, LANES)]
    metadata = copies_of(((list_in, list_ref), (near_in, near_ref)), meta_sems)
    table_products(first_ref[...].reshape(rows * n_rhs, -1), tile_ref, product_ref)
    finish(metadata)
    pack_bands(sizes, width_k, product_ref, near_ref, band_refs)
    for owner in range(n_rows):
        for rank in range(cap):
            block = product_ref[below(list_ref[owner, 0, rank], rows * n_tiles)]
            send_ref[owner, rank * n_rhs : (rank + 1) * n_rhs, :] = block
    finish(copies_of(zip((send_ref, *band_refs), (send_out, *band_out)), send_sems))


def own_kernel(sizes, width_k, *refs):
    rows, n_rows, cap, n_tiles, n_rhs = sizes
    metadata_in, first_ref, tile_ref, right_in, extra = list(refs[:3]), *refs[3:6], refs[6:9]
    send_out, band_out, metadata, product_ref, send_ref, right_ref, band_ref = refs[9], refs[10], refs[11:14], *refs[14:18]
    held, value_ref, spread_ref, result_ref, meta_sems, load_sems, send_sems = refs[18:21], *refs[21:]
    index_ref, list_ref, near_ref = metadata
    metadata_in[1] = metadata_in[1].at[:, :, pl.ds(0, LANES)]
    metadata = copies_of(zip(metadata_in, metadata), meta_sems)
    fetched = copies_of(zip((right_in, *extra), (right_ref, *held)), load_sems)
    table_products(first_ref[...].reshape(rows * n_rhs, -1), tile_ref, product_ref)
    finish(metadata)
    copies = []

    def send(source, target):
        copies.extend(started([pltpu.make_async_copy(source, target, send_sems.at[len(copies)])]))

    pack_bands(sizes, width_k, product_ref, near_ref, (band_ref,))
    send(band_ref, band_out)
    body, half = cap * n_rhs, n_rows // 2
    upper = lax.axis_index("rows") >= half
    mine, others = jnp.where(upper, half, 0), jnp.where(upper, 0, half)
    for first in (mine, others):
        for device in range(half):
            owner = first + device
            for rank in range(cap):
                block = product_ref[below(list_ref[owner, 0, rank], rows * n_tiles)]
                send_ref[owner, rank * n_rhs : (rank + 1) * n_rhs, :] = block
            if first is mine:
                send(send_ref.at[owner], send_out.at[device, pl.ds(0, body)])
    finish(fetched)
    functional_ref, count_ref, place_ref = held
    n_blocks = n_rows * cap + 2 * rows
    n_func = spread_ref.shape[0] // n_blocks
    n_diag = functional_ref.shape[0] // n_func
    functional = functional_ref[...]
    per_tile = LANES // n_rhs
    lane = lax.broadcasted_iota(jnp.int32, (n_func, LANES), 1)

    def spread(first, values, kinds):
        wide = values.shape[0]
        value_ref[:, first * n_rhs : first * n_rhs + wide] = dot_nt(functional, right_operand(values))
        for block, kind in enumerate(kinds, first):
            tile, spot = block // per_tile, block % per_tile
            start = pl.multiple_of(kind * n_func, n_func)
            piece = value_ref[pl.ds(start, n_func), tile * LANES : (tile + 1) * LANES]
            piece = jnp.where((lane >= spot * n_rhs) & (lane < (spot + 1) * n_rhs), piece, 0.0)
            spread_ref[block * n_func : (block + 1) * n_func, :] = piece

    for owner in range(0, n_rows, 2):
        kinds = []
        for more in range(2):
            for rank in range(cap):
                code = list_ref[owner + more, 0, rank]
                kinds.append(below(over(code, rows * n_tiles * rows), n_diag))
        values = jnp.concatenate([send_ref[owner], send_ref[owner + 1]], axis=0)
        spread(owner * cap, values, kinds)
    done = n_rows * cap
    kinds = [index_ref[0, 0, rows + row] for row in range(rows)]
    spread(done, right_ref[...].reshape(rows * n_rhs, -1), kinds)
    kinds = [near_ref[0, 0, rows + row] for row in range(rows)]
    spread(done + rows, band_ref[...].reshape(rows * n_rhs, -1), kinds)
    result = coarse_parts(n_rhs, n_blocks, count_ref, place_ref, spread_ref)
    result_ref[...] = result.reshape(result_ref.shape)
    depth = result_ref.shape[1]
    for n, first in enumerate((mine, others)):
        target = send_out.at[:, pl.ds(body + n * depth, depth)]
        send(result_ref.at[pl.ds(first, half)], target)
    finish(copies)


def mirror_kernel(sizes, list_in, mirror_ref, tile_ref, send_out, list_ref, product_ref, send_ref, sems):
    rows, n_rows, cap, n_tiles, n_rhs = sizes
    half = n_rows // 2
    base = jnp.where(lax.axis_index("rows") >= half, half, 0)
    list_in = list_in.at[pl.ds(base, half), :, pl.ds(0, LANES)]
    metadata = started([pltpu.make_async_copy(list_in, list_ref, sems.at[half])])
    table_products(mirror_ref[...].reshape(rows * n_rhs, -1), tile_ref, product_ref)
    finish(metadata)
    copies = []
    for device in range(half):
        for rank in range(cap):
            code = list_ref[device, 0, LANES // 2 + rank]
            block = product_ref[below(code, rows * n_tiles)]
            send_ref[device, rank * n_rhs : (rank + 1) * n_rhs, :] = block
        copy = pltpu.make_async_copy(send_ref.at[device], send_out.at[device], sems.at[device])
        copies += started([copy])
    finish(copies)


def coarse_parts(n_rhs, n_blocks, count_ref, place_ref, spread_ref):
    n_func = spread_ref.shape[0] // n_blocks
    values = [
        spread_ref[pl.ds(t, n_blocks, stride=n_func), :] for t in range(count_ref.shape[1] // n_blocks)
    ]
    values = jnp.concatenate(values, axis=0)
    partial = jnp.dot(
        count_ref[...], jnp.concatenate(halves(values), axis=1), preferred_element_type=jnp.float32
    )
    partial = partial[:, :LANES] + partial[:, LANES:]
    shift = LANES // 2
    while shift >= n_rhs:
        partial = partial + pltpu.roll(partial, shift, axis=1)
        shift //= 2
    return place(place_ref, partial, n_rhs, 2)


def part_kernel(arrived_ref, keep_ref, give_ref):
    depth = keep_ref.shape[0] // 2
    body = arrived_ref.shape[1] - 4 * depth
    total = arrived_ref[0, body:, :]
    for source in range(1, arrived_ref.shape[0]):
        total = total + arrived_ref[source, body:, :]
    lower = lax.axis_index("band") == 0
    for n in range(2):
        zero, one = (total[(2 * n + m) * depth : (2 * n + m + 1) * depth] for m in range(2))
        keep_ref[n * depth : (n + 1) * depth] = jnp.where(lower, zero, one)
        give_ref[n * depth : (n + 1) * depth] = jnp.where(lower, one, zero)


def final_kernel(sizes, width_k, *refs):
    rows, n_rows, cap, n_tiles, n_rhs = sizes
    metadata_in, own_ref, mirror_ref, inverse_ref, terms_in = refs[:2], *refs[2:5], refs[5:7]
    near_ref, far_ref, scale_ref, out_ref = refs[7:11]
    metadata, sum_ref, product_ref, terms, term_sems, meta_sems = refs[11:13], *refs[13:15], refs[15:17], *refs[17:]
    place_ref, index_ref = metadata
    metadata = copies_of(zip(metadata_in, metadata), meta_sems)
    later = copies_of(zip(terms_in, terms), term_sems)
    finish(metadata)

    def fetch(row):
        total = None
        for k in range(width_k):
            slot = place_ref[0, 0, k * rows + row]
            holder, slot = over(slot, 2 * cap), below(slot, 2 * cap)
            start = pl.ds(pl.multiple_of(below(slot, cap) * n_rhs, n_rhs), n_rhs)
            block = jnp.where(slot < cap, own_ref[holder, start, :], mirror_ref[holder, start, :])
            total = block if total is None else total + block
        return total

    def diags(row):
        return index_ref[0, 0, rows + row]

    depth = scale_ref.shape[0]
    correction = (near_ref[...] + far_ref[...]) / scale_ref[...]
    padded = jnp.concatenate([correction, jnp.zeros((8 - depth, LANES), jnp.float32)], axis=0)
    turned = padded.T
    gather_solve(sizes, fetch, diags, later, terms, inverse_ref, sum_ref, product_ref)
    for row in range(rows):
        spot, place = row // depth, row % depth
        column = turned[spot * n_rhs : (spot + 1) * n_rhs, place : place + 1]
        out_ref[row] = sum_ref[pl.ds(row * n_rhs, n_rhs), :] + column


def shifted(value, axis, steps):
    count = lax.axis_size(axis)
    initial, last = (max(0, -steps), min(count, count - steps))
    return lax.ppermute(value, axis, [(source, source + steps) for source in range(initial, last)])


def to_bands(sends):
    if len(sends) == 1:
        return (lax.ppermute(sends[0], "band", [(0, 1), (1, 0)]),)
    return shifted(sends[0], "band", 1), shifted(sends[1], "band", -1)


def on_device(
    start_iterate,
    right_side,
    diag_table,
    inverse_table,
    coupling_tiles,
    diag_index,
    tile_index,
    source_owner,
    source_local,
    aggregate_map,
):
    rows, n_rhs, states = start_iterate.shape
    width_k = source_owner.shape[1]
    n_tiles, n_diag = coupling_tiles.shape[0], inverse_table.shape[0]
    n_rows, n_bands = lax.axis_size("rows"), lax.axis_size("band")
    n_dev = n_rows * n_bands
    cap = max(2, 2 * width_k * rows // n_rows)
    slots = n_rows * cap
    total_groups = AGG_DEV * n_dev
    per_tile = LANES // n_rhs
    depth = rows // per_tile
    n_func = 16
    dense = (
        n_bands == 2
        and n_dev * rows * total_groups <= DENSE_LIMIT
        and depth == 4
        and n_diag * n_func == LANES
        and n_tiles + 2 <= n_func
    )
    sizes = (rows, n_rows, cap, n_tiles, n_rhs)
    f32, i32 = jnp.float32, jnp.int32
    my_band = lax.axis_index("band")
    my_row = lax.axis_index("rows")

    half = n_rows // 2
    wide = -(-(4 + 2 * width_k) * rows // LANES) * LANES
    place_wide = -(-2 * width_k * rows // LANES) * LANES
    index_shapes = [(width_k, rows), (width_k, rows), (width_k + 2, rows), (1, rows), (1, rows)]
    halves_of_rows = [list(range(half)), list(range(half, n_rows))]
    to_mirror = [(i, (i + half) % n_rows) for i in range(n_rows)]
    mirror = lax.ppermute(start_iterate, "rows", to_mirror)
    lists, index, places = call(
        functools.partial(request_kernel, (rows, n_rows, cap, n_tiles, n_diag)),
        (
            jax.ShapeDtypeStruct((n_rows, 1, LANES + wide), i32),
            jax.ShapeDtypeStruct((1, 1, wide), i32),
            jax.ShapeDtypeStruct((1, 1, place_wide), i32),
        ),
        [HBM] * 5,
        [VMEM] * 3,
        [*[pltpu.VMEM(shape, i32) for shape in index_shapes], pltpu.SemaphoreType.DMA((5,))],
    )(source_owner.T, source_local.T, tile_index.T, diag_index[None], aggregate_map.T)
    lists = lax.all_to_all(lists, "rows", split_axis=0, concat_axis=0, tiled=True)
    if n_bands == 2:
        near = lax.ppermute(index, "band", [(0, 1), (1, 0)])
    else:
        ways = [[(b, (b + step) % n_bands) for b in range(n_bands)] for step in (-1, 1)]
        near = jnp.concatenate([lax.ppermute(index, "band", way) for way in ways], axis=0)

    n_ways = 1 if n_bands == 2 else 2
    block = (rows, n_rhs, states)
    band_shapes = [jax.ShapeDtypeStruct(block, f32)] * n_ways
    band_scratch = [pltpu.VMEM(block, f32)] * n_ways
    term_scratch = [pltpu.VMEM(block, f32)] * (1 + n_ways)
    term_sems = pltpu.SemaphoreType.DMA((1 + n_ways,))
    list_scratch = pltpu.SMEM((half, 1, LANES), i32)
    near_scratch = pltpu.SMEM((n_ways, 1, wide), i32)
    row_scratch = [pltpu.SMEM((1, 1, place_wide), i32), pltpu.SMEM((1, 1, wide), i32)]
    flat = rows * n_rhs
    sums = pltpu.VMEM((flat, states), f32)
    products = pltpu.VMEM((max(n_tiles, n_diag) * rows, n_rhs, states), f32)
    work = 6 * flat * states * states
    made_shape = (n_tiles * rows, n_rhs, states)
    table_scratch = [pltpu.VMEM(coupling_tiles.shape, f32)]
    table_sems = pltpu.SemaphoreType.DMA((-(-n_tiles // 2),))
    made = call(
        product_kernel,
        jax.ShapeDtypeStruct(made_shape, f32),
        [HBM, HBM],
        HBM,
        [
            pltpu.VMEM(block, f32),
            *table_scratch,
            pltpu.VMEM(made_shape, f32),
            pltpu.SemaphoreType.DMA((1 + n_tiles,)),
            table_sems,
        ],
        work * n_tiles,
        4 << 20,
    )(start_iterate, coupling_tiles)
    packed, *bands = call(
        functools.partial(first_kernel, sizes, width_k, n_ways),
        (jax.ShapeDtypeStruct((half, 2 * cap, n_rhs, states), f32), *band_shapes),
        [HBM, VMEM, VMEM, ANY, ANY],
        [HBM] * (1 + n_ways),
        [
            pltpu.VMEM((2, *made_shape), f32),
            list_scratch,
            near_scratch,
            pltpu.VMEM((half, 2 * cap, n_rhs, states), f32),
            *band_scratch,
            pltpu.SemaphoreType.DMA((n_tiles,)),
            pltpu.SemaphoreType.DMA((2,)),
            pltpu.SemaphoreType.DMA((half + n_ways,)),
        ],
        work * n_tiles,
        4 << 20,
    )(made, mirror, coupling_tiles, lists, near)
    packed, late = lax.optimization_barrier((packed, lists))
    if dense:
        across = lax.ppermute(late, "band", [(0, 1), (1, 0)])
        across, *bands = lax.optimization_barrier((across, *bands))
    sends = (packed.reshape(half, 2 * cap * n_rhs, states), *bands)
    halves_of_rows = [list(range(half)), list(range(half, n_rows))]
    def exchange(sends, groups=None):
        arrived = lax.all_to_all(
            sends[0], "rows", split_axis=0, concat_axis=0, tiled=True, axis_index_groups=groups
        )
        return arrived, to_bands(sends[1:])

    arrived_blocks, arrived_bands = exchange(sends, halves_of_rows)

    if dense:
        fields = jnp.stack([late, across])[:, :, 0, LANES:]
        fields = fields.reshape(2, n_rows, -1, rows).transpose(2, 0, 1, 3)
        fields = fields.reshape(-1, 2, n_rows * rows)
        n_blocks = slots + 2 * rows
        length = n_dev * depth
        extra_shapes = [
            ((n_diag * n_func, 3 * states), jnp.bfloat16),
            ((total_groups, (n_tiles + 2) * n_blocks), jnp.bfloat16),
            ((per_tile * length, total_groups), jnp.bfloat16),
        ]
        functional_shape, count_shape, placing_shape = extra_shapes
        counts, functionals, placing, scale = call(
            functools.partial(count_kernel, sizes, width_k, n_func),
            (
                jax.ShapeDtypeStruct(*count_shape),
                jax.ShapeDtypeStruct(*functional_shape),
                jax.ShapeDtypeStruct(*placing_shape),
                jax.ShapeDtypeStruct((depth, LANES), f32),
            ),
            [VMEM] * 5,
            [HBM, HBM, HBM, VMEM],
            [
                pltpu.VMEM(*count_shape),
                pltpu.VMEM(*functional_shape),
                pltpu.VMEM(*placing_shape),
                pltpu.SemaphoreType.DMA((3,)),
            ],
            4 * total_groups * n_tiles * n_dev * rows * n_blocks,
            4 << 20,
        )(fields, late[:, 0, :LANES], coupling_tiles, diag_table, inverse_table)
        extra_scratch = [
            *[pltpu.VMEM(*shape) for shape in extra_shapes],
            pltpu.VMEM((n_diag * n_func, n_blocks * n_rhs), f32),
            pltpu.VMEM((n_blocks * n_func, LANES), f32),
            pltpu.VMEM((n_rows, n_bands * depth, LANES), f32),
        ]

        made = (arrived_blocks, functionals, counts, placing, scale)
        arrived_blocks, functionals, counts, placing, scale = lax.optimization_barrier(made)

    def solve(field, arrived, bands):
        return call(
            functools.partial(solve_kernel, sizes, width_k, n_ways, field),
            jax.ShapeDtypeStruct(block, f32),
            [ANY] * 2 + [VMEM] * 2 + [HBM] + [ANY] * n_ways,
            VMEM,
            [
                *row_scratch,
                sums,
                products,
                *term_scratch,
                term_sems,
                pltpu.SemaphoreType.DMA((2,)),
            ],
            work * n_diag,
            4 << 20,
        )(places, index, arrived, inverse_table, right_side, *bands)

    first = solve(0, arrived_blocks, arrived_bands)
    body = cap * n_rhs
    full_list = pltpu.SMEM((n_rows, 1, LANES), i32)
    if dense:
        mirror = lax.ppermute(first, "rows", to_mirror)
        own, band = call(
            functools.partial(own_kernel, sizes, width_k),
            (
                jax.ShapeDtypeStruct((half, body + 2 * n_bands * depth, states), f32),
                jax.ShapeDtypeStruct(block, f32),
            ),
            [ANY] * 3 + [VMEM] * 2 + [HBM] * 4,
            [HBM] * 2,
            [
                row_scratch[1],
                full_list,
                near_scratch,
                products,
                pltpu.VMEM((n_rows, body, states), f32),
                pltpu.VMEM(block, f32),
                pltpu.VMEM(block, f32),
                *extra_scratch,
                pltpu.SemaphoreType.DMA((3,)),
                pltpu.SemaphoreType.DMA((4,)),
                pltpu.SemaphoreType.DMA((half + 3,)),
            ],
            2 * work * n_tiles,
            4 << 20,
        )(index, lists, near, first, coupling_tiles, right_side, functionals, counts, placing)
        own, (band,) = exchange((own, band), halves_of_rows)
        packed = call(
            functools.partial(mirror_kernel, sizes),
            jax.ShapeDtypeStruct((half, body, states), f32),
            [ANY] + [VMEM] * 2,
            HBM,
            [
                list_scratch,
                products,
                pltpu.VMEM((half, body, states), f32),
                pltpu.SemaphoreType.DMA((half + 1,)),
            ],
            BEHIND_SWAP * work * n_tiles,
            4 << 20,
        )(lists, mirror, coupling_tiles)
        packed, band = lax.optimization_barrier((packed, band))
        swapped = lax.all_to_all(
            packed, "rows", split_axis=0, concat_axis=0, tiled=True, axis_index_groups=halves_of_rows
        )
        part = jax.ShapeDtypeStruct((2 * depth, LANES), f32)
        keep, give = call(part_kernel, (part, part), [VMEM], [VMEM] * 2)(own)
        keep = keep + lax.ppermute(give, "band", [(0, 1), (1, 0)])
        far = lax.ppermute(keep[depth:], "rows", to_mirror)
        return call(
            functools.partial(final_kernel, sizes, width_k),
            jax.ShapeDtypeStruct(block, f32),
            [ANY] * 2 + [VMEM] * 3 + [HBM, ANY] + [VMEM] * 3,
            VMEM,
            [
                *row_scratch,
                sums,
                products,
                *term_scratch,
                term_sems,
                pltpu.SemaphoreType.DMA((2,)),
            ],
            work * n_diag,
            4 << 20,
        )(places, index, own, swapped, inverse_table, right_side, band, keep[:depth], far, scale)

    sends = call(
        functools.partial(pack_kernel, sizes, width_k, n_ways),
        (jax.ShapeDtypeStruct((n_rows, body, states), f32), *band_shapes),
        [ANY] * 2 + [VMEM] * 2,
        [HBM] * (1 + n_ways),
        [
            full_list,
            near_scratch,
            products,
            pltpu.VMEM((n_rows, body, states), f32),
            *band_scratch,
            pltpu.SemaphoreType.DMA((2,)),
            pltpu.SemaphoreType.DMA((1 + n_ways,)),
        ],
        work * n_tiles,
        4 << 20,
    )(lists, near, first, coupling_tiles)
    arrived_blocks, arrived_bands = exchange(sends)
    second = solve(width_k, arrived_blocks, arrived_bands)

    groups = aggregate_map[:, 0]
    own = jnp.arange(rows, dtype=i32)
    index_all = lax.all_gather(index, ("band", "rows"), axis=0, tiled=True)
    index_all = index_all.reshape(n_bands, n_rows, wide)
    groups_all, diags_all = index_all[:, :, :rows], index_all[:, :, rows : 2 * rows]
    codes = lists[:, 0, :cap]
    asked = jnp.arange(n_rows, dtype=i32)[:, None] * rows + codes // (rows * n_tiles) % rows
    asked = jnp.where(codes > 0, asked, -1).reshape(-1)
    table_sums = jnp.sum(diag_table, axis=(1, 2))
    diag_onehot = diags_all.reshape(-1, 1) == jnp.arange(n_diag, dtype=i32)[None]
    block_sums = jnp.sum(jnp.where(diag_onehot, table_sums[None], 0.0), axis=1)
    whole_diag = jnp.sum(
        jnp.where(groups[:, None] == groups_all.reshape(-1)[None], block_sums[None], 0.0), axis=1
    )
    above, below = near[0, 0], near[-1, 0]
    place_of = (2 + width_k) * rows
    band_tiles = jnp.stack([above[place_of : place_of + rows], below[place_of + rows : place_of + 2 * rows]])
    band_groups = jnp.stack([above[:rows], below[:rows]])
    band_valid = jnp.stack([my_band + 1 < n_bands, my_band > 0])
    band_valid = jnp.broadcast_to(band_valid[:, None], (2, rows))
    n_all = n_tiles + n_diag + 1
    code = codes.reshape(-1)
    band_of_mine = lax.dynamic_index_in_dim(groups_all, my_band, 0, keepdims=False).reshape(-1)
    entry_group = jnp.concatenate(
        [jnp.take(band_of_mine, jnp.maximum(asked, 0)), band_groups.reshape(-1), groups, groups]
    )
    entry_func = jnp.concatenate(
        [
            (code % rows) * n_all + (code // rows) % n_tiles,
            (own[None] * n_all + band_tiles).reshape(-1),
            own * n_all + n_tiles + diag_index,
            own * n_all + n_tiles + n_diag,
        ]
    )
    entry_valid = jnp.concatenate([asked >= 0, band_valid.reshape(-1), jnp.ones((2 * rows,), bool)])
    functionals = jnp.concatenate(
        [jnp.sum(coupling_tiles, axis=1), -jnp.sum(diag_table, axis=1)], axis=0
    )
    weights = jnp.einsum("fp,rcp->rfc", functionals, second, precision=HIGH)
    weights = jnp.concatenate([weights, jnp.sum(right_side, axis=2)[:, None]], axis=1)
    chosen = jnp.take(weights.reshape(rows * n_all, n_rhs), entry_func, axis=0)
    chosen = jnp.where(entry_valid[:, None], chosen, 0.0)
    partial = jax.ops.segment_sum(chosen, entry_group, num_segments=total_groups)
    whole = lax.psum(partial, ("band", "rows"))
    correction = jnp.take(whole, groups, axis=0) / whole_diag[:, None]
    return second + correction[:, :, None]


def solution(mesh):
    in_specs = (
        P(("band", "rows"), None, None),
        P(("band", "rows"), None, None),
        P(),
        P(),
        P(),
        P(("band", "rows")),
        P(("band", "rows"), None),
        P(("band", "rows"), None),
        P(("band", "rows"), None),
        P(("band", "rows"), None),
    )
    out_specs = P(("band", "rows"), None, None)
    return jax.shard_map(
        on_device, mesh=mesh, in_specs=in_specs, out_specs=out_specs, check_vma=False
    )
```

```python
import functools

import jax
import jax.numpy as jnp
from jax import lax
from jax.experimental import pallas as pl
from jax.experimental.pallas import tpu as pltpu
from jax.sharding import PartitionSpec as P

AGG_DEV = 8
LANES = 128
DENSE_LIMIT = 1 << 19
BEHIND_SWAP = 100

VMEM = pl.BlockSpec(memory_space=pltpu.VMEM)
SMEM = pl.BlockSpec(memory_space=pltpu.SMEM)
HBM = pl.BlockSpec(memory_space=pltpu.HBM)
ANY = pl.BlockSpec(memory_space=pl.ANY)
HIGH = lax.Precision.HIGHEST


def params():
    return pltpu.CompilerParams(vmem_limit_bytes=24 * 1024 * 1024)


def call(kernel, out_shape, in_specs, out_specs, scratch=(), flops=0, moved=0):
    def shaped(shape, spec):
        return pltpu.HBM(shape.shape, shape.dtype) if spec is HBM else shape

    if isinstance(out_shape, (tuple, list)):
        out_shape = [shaped(*pair) for pair in zip(out_shape, out_specs)]
    else:
        out_shape = shaped(out_shape, out_specs)
    run = pl.pallas_call(
        kernel,
        out_shape=out_shape,
        in_specs=in_specs,
        out_specs=out_specs,
        scratch_shapes=list(scratch),
        compiler_params=params(),
        cost_estimate=pl.CostEstimate(flops=flops, bytes_accessed=moved, transcendentals=0),
    )

    def apply(*args):
        pinned = [
            pltpu.with_memory_space_constraint(arg, pltpu.HBM) if spec is HBM else arg
            for arg, spec in zip(args, in_specs)
        ]
        return run(*pinned)

    return apply


def below(value, bound):
    return value & (bound - 1) if bound & (bound - 1) == 0 else lax.rem(value, bound)


def over(value, bound):
    if bound & (bound - 1) == 0:
        return lax.shift_right_logical(value, bound.bit_length() - 1)
    return lax.div(value, bound)


def halves(value):
    high = value.astype(jnp.bfloat16)
    low = (value - high.astype(jnp.float32)).astype(jnp.bfloat16)
    return high, low


def left_operand(value):
    high, low = halves(value)
    return jnp.concatenate([high, low, high], axis=1)


def right_operand(value):
    high, low = halves(value)
    return jnp.concatenate([high, high, low], axis=1)


def dot_nt(left, right):
    return lax.dot_general(
        left, right, (((1,), (1,)), ((), ())), preferred_element_type=jnp.float32
    )


def table_products(value, table_ref, out_ref, done=None, loads=None):
    left = left_operand(value)
    count, width = table_ref.shape[0], table_ref.shape[1]
    n_rhs = out_ref.shape[1]
    rows = left.shape[0] // n_rhs
    for first in range(0, count, 2):
        last = min(first + 2, count)
        if loads is not None:
            loads[first // 2].wait()
        right = right_operand(table_ref[first:last].reshape((last - first) * width, -1))
        product = dot_nt(left, right)
        for t in range(first, last):
            part = product[:, (t - first) * width : (t - first + 1) * width]
            out_ref[t * rows : (t + 1) * rows] = part.reshape(rows, n_rhs, width)
        if done is not None:
            done(first * rows, (last - first) * rows)


def started(copies):
    for copy in copies:
        copy.start()
    return copies


def finish(copies):
    for copy in copies:
        copy.wait()


def request_kernel(sizes, *refs):
    rows, n_rows, cap, n_tiles, n_diag = sizes
    inputs, (list_ref, index_ref, place_ref), held, sems = refs[:5], refs[5:8], refs[8:13], refs[13]
    finish(
        started([pltpu.make_async_copy(i, h, sems.at[n]) for n, (i, h) in enumerate(zip(inputs, held))])
    )
    owner_ref, local_ref, tile_ref, diag_ref, group_ref = held
    width_k = owner_ref.shape[0]
    half = n_rows // 2
    row_of = lax.broadcasted_iota(jnp.int32, (rows, rows), 0)
    col_of = lax.broadcasted_iota(jnp.int32, (rows, rows), 1)
    lane = lax.broadcasted_iota(jnp.int32, (rows, LANES), 1)
    owners = lax.broadcasted_iota(jnp.int32, (n_rows, rows), 0)

    def column(row):
        return jnp.sum(jnp.where(row_of == col_of, row, 0), axis=1, keepdims=True)

    def owner_row(k):
        return owner_ref[k : k + 1, :]

    row_ids = lax.broadcasted_iota(jnp.int32, (1, rows), 1)
    owner_columns = [column(owner_row(k)) for k in range(width_k)]
    lists = jnp.zeros((n_rows, LANES), jnp.float32)
    places, half_places = [], []
    for k in range(width_k):
        rank = jnp.zeros((1, rows), jnp.int32)
        for other in range(k + 1):
            match = owner_columns[other] == owner_row(k)
            if other == k:
                match = match & (row_of < col_of)
            rank = rank + jnp.sum(jnp.where(match, 1, 0), axis=0, keepdims=True)
        places.append(owner_row(k) * cap + rank)
        same = (owner_row(k) >= half) == (lax.axis_index("rows") >= half)
        holder = jnp.where(owner_row(k) >= half, owner_row(k) - half, owner_row(k))
        half_places.append(holder * (2 * cap) + rank + jnp.where(same, 0, cap))
        taker = row_ids + rows * (diag_ref[...] + n_diag)
        code = local_ref[k : k + 1, :] + rows * (tile_ref[k : k + 1, :] + n_tiles * taker)
        code, rank = column(code), column(rank)
        mirror = jnp.where(owner_row(k) >= half, owner_row(k) - half, owner_row(k) + half)
        for owner, base in ((owner_row(k), 0), (mirror, LANES // 2)):
            by_rank = jnp.where(lane == rank + base, code, 0).astype(jnp.float32)
            mine = jnp.where(owners == owner, 1.0, 0.0)
            lists = lists + jnp.dot(
                mine, by_rank, precision=HIGH, preferred_element_type=jnp.float32
            )
    lists = (lists + 0.5).astype(jnp.int32)

    def joined(parts, wide):
        spare = wide - len(parts) * rows
        if spare:
            parts = [*parts, jnp.zeros((1, spare), jnp.int32)]
        return jnp.concatenate(parts, axis=1)

    index = [group_ref[...], diag_ref[...]]
    index += [tile_ref[k : k + 1, :] for k in range(width_k + 2)]
    index += [owner_row(k) * rows + local_ref[k : k + 1, :] for k in range(width_k)]
    index = joined(index, index_ref.shape[2])
    index_ref[0] = index
    place_ref[0] = joined(half_places + places, place_ref.shape[2])
    for device in range(n_rows):
        list_ref[device] = jnp.concatenate([lists[device : device + 1, :], index], axis=1)


def copies_of(pairs, sems):
    return started([pltpu.make_async_copy(i, h, sems.at[n]) for n, (i, h) in enumerate(pairs)])


def band_field(rows, width_k, way, n_ways):
    field = (2 + width_k) * rows
    if n_ways == 1:
        return field + jnp.where(lax.axis_index("band") == 0, 0, rows)
    return field + way * rows


def pack_bands(sizes, width_k, product_ref, near_ref, band_refs):
    rows = sizes[0]
    for way, band_ref in enumerate(band_refs):
        field = band_field(rows, width_k, way, len(band_refs))
        for row in range(rows):
            band_ref[row] = product_ref[near_ref[way, 0, field + row] * rows + row]


def table_loads(table_in, table_ref, sems):
    copies = []
    for first in range(0, table_in.shape[0], 2):
        place = pl.ds(first, min(2, table_in.shape[0] - first))
        source, target = table_in.at[place], table_ref.at[place]
        copies.append(pltpu.make_async_copy(source, target, sems.at[first // 2]))
    return started(copies)


def product_kernel(start_in, tile_in, product_out, start_ref, tile_ref, product_ref, sems, tile_sems):
    start = pltpu.make_async_copy(start_in, start_ref, sems.at[0])
    start.start()
    loads = table_loads(tile_in, tile_ref, tile_sems)
    start.wait()
    copies = []

    def done(first, count):
        place = pl.ds(first, count)
        source, target = product_ref.at[place], product_out.at[place]
        copies.extend(started([pltpu.make_async_copy(source, target, sems.at[1 + len(copies)])]))

    rows, n_rhs, states = start_ref.shape
    values = start_ref[...].reshape(rows * n_rhs, states)
    table_products(values, tile_ref, product_ref, done, loads)
    finish(copies)


def first_kernel(sizes, width_k, n_band, *refs):
    rows, n_rows, cap, n_tiles, n_rhs = sizes
    product_in, mirror_ref, tile_ref, list_in, near_in, send_out = refs[:6]
    band_out, refs = refs[6 : 6 + n_band], refs[6 + n_band :]
    product_ref, list_ref, near_ref, send_ref = refs[:4]
    band_refs, (load_sems, meta_sems, send_sems) = refs[4 : 4 + n_band], refs[4 + n_band :]
    half = n_rows // 2
    base = jnp.where(lax.axis_index("rows") >= half, half, 0)
    list_in = list_in.at[pl.ds(base, half), :, pl.ds(0, LANES)]
    metadata = copies_of(((list_in, list_ref), (near_in, near_ref)), meta_sems)
    places = [pl.ds(tile * rows, rows) for tile in range(n_tiles)]
    loads = [(product_in.at[place], product_ref.at[0, place]) for place in places]
    loads = copies_of(loads, load_sems)
    values = mirror_ref[...].reshape(rows * n_rhs, -1)
    table_products(values, tile_ref, product_ref.at[1])
    finish(metadata)
    finish(loads)
    copies = []
    pack_bands(sizes, width_k, product_ref.at[0], near_ref, band_refs)
    for n, (ref, out) in enumerate(zip(band_refs, band_out)):
        copies += started([pltpu.make_async_copy(ref, out, send_sems.at[half + n])])
    for device in range(half):
        for slot in range(2 * cap):
            side, rank = slot // cap, slot % cap
            code = list_ref[device, 0, side * (LANES // 2) + rank]
            send_ref[device, slot] = product_ref[side, below(code, rows * n_tiles)]
        copy = pltpu.make_async_copy(send_ref.at[device], send_out.at[device], send_sems.at[device])
        copies += started([copy])
    finish(copies)


def place(place_ref, values, n_rhs, n_parts):
    per_tile = LANES // n_rhs
    length = place_ref.shape[0] // per_tile
    parts, rest = [], values
    for _ in range(n_parts):
        part = rest.astype(jnp.bfloat16)
        rest = rest - part.astype(jnp.float32)
        parts.append(part)
    parts = jnp.concatenate(parts, axis=1)
    lane = lax.broadcasted_iota(jnp.int32, (length, LANES), 1)
    result = jnp.zeros((length, LANES), jnp.float32)
    placed = jnp.dot(place_ref[...], parts, preferred_element_type=jnp.float32)
    for spot in range(per_tile):
        chosen = placed[spot * length : (spot + 1) * length]
        chosen = sum(chosen[:, n * LANES : (n + 1) * LANES] for n in range(n_parts))
        result = jnp.where((lane >= spot * n_rhs) & (lane < (spot + 1) * n_rhs), chosen, result)
    return result


def one_hot(ids, row):
    return jnp.where(ids == row, 1.0, 0.0).astype(jnp.bfloat16)


def count_kernel(sizes, width_k, n_func, *refs):
    rows, n_rows, cap, n_tiles, n_rhs = sizes
    field_ref, list_ref, tile_ref, table_ref, inverse_ref = refs[:5]
    count_out, functional_out, through_out, placing_out, scale_ref = refs[5:10]
    count_ref, functional_ref, through_ref, placing_ref, sems = refs[10:]
    n_groups, n_blocks = count_ref.shape[0], count_ref.shape[1] // (n_tiles + 2)
    slots, band_rows = n_rows * cap, n_rows * rows
    copies = []

    def send(source, target):
        copies.extend(started([pltpu.make_async_copy(source, target, sems.at[len(copies)])]))

    sums = jnp.sum(tile_ref[...], axis=1)
    line = lax.broadcasted_iota(jnp.int32, (n_func, sums.shape[1]), 0)
    sums = jnp.concatenate([sums, jnp.zeros((n_func - n_tiles, sums.shape[1]), jnp.float32)], axis=0)
    n_diag = inverse_ref.shape[0]
    totals, functionals = [], []
    for d in range(n_diag):
        minus = -jnp.sum(table_ref[d], axis=0, keepdims=True)
        totals.append(-jnp.sum(minus, axis=1, keepdims=True))
        wanted = jnp.where(line == n_tiles, minus, sums)
        high, low = halves(inverse_ref[d])
        right = jnp.concatenate([high, high, low], axis=0)
        solved = jnp.dot(left_operand(wanted), right, preferred_element_type=jnp.float32)
        solved = jnp.where(line == n_tiles + 1, 1.0, solved)
        functionals.append(solved)
    functionals = left_operand(jnp.concatenate(functionals, axis=0))
    functional_ref[...] = functionals
    send(functional_ref, functional_out)
    for t in range(n_tiles):
        high, low = halves(tile_ref[t])
        right = jnp.concatenate([high, high, low], axis=0)
        through = jnp.dot(functionals, right, preferred_element_type=jnp.float32)
        place_of = pl.ds(t * n_diag * n_func, n_diag * n_func)
        through_ref[place_of, :] = left_operand(through)
    send(through_ref, through_out)

    lists = list_ref[...]
    asker = lax.broadcasted_iota(jnp.int32, lists.shape, 0)
    codes = asker * rows + below(over(lists, rows * n_tiles), rows)
    codes = jnp.where(lists > 0, codes, -1).astype(jnp.float32)
    spread = lax.broadcasted_iota(jnp.int32, (slots, n_rows), 0)
    spread = lax.div(spread, cap) == lax.broadcasted_iota(jnp.int32, (slots, n_rows), 1)
    codes = jnp.dot(
        jnp.where(spread, 1.0, 0.0), codes, precision=HIGH, preferred_element_type=jnp.float32
    )
    rank = lax.rem(lax.broadcasted_iota(jnp.int32, codes.shape, 0), cap)
    lane = lax.broadcasted_iota(jnp.int32, codes.shape, 1)
    asked = jnp.sum(jnp.where(rank == lane, codes, 0.0), axis=1, keepdims=True)
    asked = jnp.where(asked < 0.0, asked - 0.5, asked + 0.5).astype(jnp.int32)
    own = lax.axis_index("rows") * rows + lax.broadcasted_iota(jnp.int32, (rows, 1), 0)
    band = lax.axis_index("band")

    def field(n, side):
        return field_ref[n, side : side + 1, :]

    row_ids = lax.broadcasted_iota(jnp.int32, (1, band_rows), 1)
    sides = []
    for side, targets in ((0, jnp.concatenate([asked, own], axis=0)), (1, own)):
        first = band == side
        across = jnp.where(first, field(2 + width_k, 1 - side), field(3 + width_k, 1 - side))
        takers = [field(2 + k, side) * n_groups + field(0, side) for k in range(width_k)]
        takers.append(across * n_groups + field(0, 1 - side))
        takers = jnp.concatenate(takers, axis=1)
        origins = [field(4 + width_k + k, side) for k in range(width_k)] + [row_ids]
        hits = one_hot(targets, jnp.concatenate(origins, axis=1))
        sides.append((takers, hits, field(0, side)))
    pieces = []
    for t in range(n_tiles):
        found = []
        for takers, hits, _ in sides:
            ids = lax.broadcasted_iota(jnp.int32, (n_groups, takers.shape[1]), 0) + t * n_groups
            found.append(dot_nt(one_hot(ids, takers), hits))
        pieces += found
    ids = lax.broadcasted_iota(jnp.int32, (n_groups, band_rows), 0)
    found = [dot_nt(one_hot(ids, groups), hits[:, -band_rows:]) for _, hits, groups in sides]
    found = jnp.concatenate(found, axis=1)
    block = lax.broadcasted_iota(jnp.int32, found.shape, 1)
    mine = (block >= slots) & (block < slots + rows)
    pieces += [found, jnp.where(mine, found, 0.0)]
    count_ref[...] = jnp.concatenate(pieces, axis=1).astype(jnp.bfloat16)
    send(count_ref, count_out)

    per_tile = LANES // n_rhs
    depth = rows // per_tile
    length = n_rows * 2 * depth
    order = lax.broadcasted_iota(jnp.int32, (per_tile * length, 1), 0)
    spot, order = lax.div(order, length), lax.rem(order, length)
    device, order = lax.div(order, 2 * depth), lax.rem(order, 2 * depth)
    side, order = lax.div(order, depth), lax.rem(order, depth)
    order = side * band_rows + device * rows + spot * depth + order
    member = [
        one_hot(ids, jnp.where(band == which, field(0, 0), field(0, 1))) for which in range(2)
    ]
    placing = jnp.zeros(placing_ref.shape, jnp.float32)
    for which in range(2):
        placing = placing + dot_nt(one_hot(order, row_ids + which * band_rows), member[which])
    placing_ref[...] = placing.astype(jnp.bfloat16)
    send(placing_ref, placing_out)
    whole = jnp.zeros((n_groups, 1), jnp.float32)
    for side in range(2):
        sums = jnp.zeros((1, band_rows), jnp.float32)
        for d in range(n_diag):
            sums = jnp.where(field(1, side) == d, totals[d], sums)
        weighted = jnp.where(ids == field(0, side), sums, 0.0)
        whole = whole + jnp.sum(weighted, axis=1, keepdims=True)
    scale = place(placing_ref, jnp.broadcast_to(whole, (n_groups, LANES)), n_rhs, 3)
    mine = jnp.zeros(scale_ref.shape, jnp.float32)
    here = lax.axis_index("rows") * 2 + band
    for n in range(2 * n_rows):
        mine = jnp.where(here == n, scale[n * depth : (n + 1) * depth, :], mine)
    scale_ref[...] = mine
    finish(copies)


def gather_solve(sizes, fetch, diags, later, terms, inverse_ref, sum_ref, product_ref):
    rows, n_rows, cap, n_tiles, n_rhs = sizes
    for row in range(rows):
        sum_ref[pl.ds(row * n_rhs, n_rhs), :] = fetch(row)
    finish(later)
    total = sum_ref[...]
    for term in terms:
        total = total + term[...].reshape(total.shape)
    table_products(total, inverse_ref, product_ref)
    for row in range(rows):
        sum_ref[pl.ds(row * n_rhs, n_rhs), :] = product_ref[diags(row) * rows + row]


def arrived_blocks_of(sizes, width_k, place_ref, field, arrived_ref):
    rows, n_rows, cap, n_tiles, n_rhs = sizes
    per = n_rows * cap // arrived_ref.shape[0]

    def fetch(row):
        total = None
        for k in range(width_k):
            slot = place_ref[0, 0, (field + k) * rows + row]
            start = pl.multiple_of(below(slot, per) * n_rhs, n_rhs)
            block = arrived_ref[over(slot, per), pl.ds(start, n_rhs), :]
            total = block if total is None else total + block
        return total

    return fetch


def solve_kernel(sizes, width_k, n_band, field, *refs):
    metadata_in, arrived_ref, inverse_ref = refs[:2], *refs[2:4]
    terms_in, refs = refs[4 : 5 + n_band], refs[5 + n_band :]
    out_ref, metadata, sum_ref, product_ref = refs[0], refs[1:3], *refs[3:5]
    place_ref, index_ref = metadata
    terms, (term_sems, meta_sems) = refs[5 : 6 + n_band], refs[6 + n_band :]
    rows = sizes[0]
    metadata = copies_of(zip(metadata_in, metadata), meta_sems)
    later = copies_of(zip(terms_in, terms), term_sems)
    finish(metadata)
    fetch = arrived_blocks_of(sizes, width_k, place_ref, field, arrived_ref)

    def diags(row):
        return index_ref[0, 0, rows + row]

    gather_solve(sizes, fetch, diags, later, terms, inverse_ref, sum_ref, product_ref)
    out_ref[...] = sum_ref[...].reshape(out_ref.shape)


def pack_kernel(sizes, width_k, n_band, *refs):
    rows, n_rows, cap, n_tiles, n_rhs = sizes
    list_in, near_in, first_ref, tile_ref, send_out = refs[:5]
    band_out, refs = refs[5 : 5 + n_band], refs[5 + n_band :]
    list_ref, near_ref, product_ref, send_ref = refs[:4]
    band_refs, (meta_sems, send_sems) = refs[4 : 4 + n_band], refs[4 + n_band :]
    list_in = list_in.at[:, :, pl.ds(0, LANES)]
    metadata = copies_of(((list_in, list_ref), (near_in, near_ref)), meta_sems)
    table_products(first_ref[...].reshape(rows * n_rhs, -1), tile_ref, product_ref)
    finish(metadata)
    pack_bands(sizes, width_k, product_ref, near_ref, band_refs)
    for owner in range(n_rows):
        for rank in range(cap):
            block = product_ref[below(list_ref[owner, 0, rank], rows * n_tiles)]
            send_ref[owner, rank * n_rhs : (rank + 1) * n_rhs, :] = block
    finish(copies_of(zip((send_ref, *band_refs), (send_out, *band_out)), send_sems))


def own_kernel(sizes, width_k, *refs):
    rows, n_rows, cap, n_tiles, n_rhs = sizes
    metadata_in, first_ref, tile_ref, right_in, extra = list(refs[:3]), *refs[3:6], refs[6:10]
    send_out, band_out, metadata, product_ref, send_ref, right_ref, band_ref = refs[10], refs[11], refs[12:15], *refs[15:19]
    held, value_ref, through_ref, spread_ref, result_ref = refs[19:23], *refs[23:27]
    meta_sems, load_sems, send_sems = refs[27:]
    index_ref, list_ref, near_ref = metadata
    metadata_in[1] = metadata_in[1].at[:, :, pl.ds(0, LANES)]
    metadata = copies_of(zip(metadata_in, metadata), meta_sems)
    fetched = copies_of(zip((right_in, *extra), (right_ref, *held)), load_sems)
    table_products(first_ref[...].reshape(rows * n_rhs, -1), tile_ref, product_ref)
    finish(metadata)
    copies = []

    def send(source, target):
        copies.extend(started([pltpu.make_async_copy(source, target, send_sems.at[len(copies)])]))

    pack_bands(sizes, width_k, product_ref, near_ref, (band_ref,))
    send(band_ref, band_out)
    body, half = cap * n_rhs, n_rows // 2
    upper = lax.axis_index("rows") >= half
    mine, others = jnp.where(upper, half, 0), jnp.where(upper, 0, half)
    for device in range(half):
        for rank in range(cap):
            block = product_ref[below(list_ref[mine + device, 0, rank], rows * n_tiles)]
            send_ref[device, rank * n_rhs : (rank + 1) * n_rhs, :] = block
        send(send_ref.at[device], send_out.at[device, pl.ds(0, body)])
    finish(fetched)
    functional_ref, through_in, count_ref, place_ref = held
    n_blocks = n_rows * cap + 2 * rows
    n_func = spread_ref.shape[0] // n_blocks
    n_diag = functional_ref.shape[0] // n_func
    per_tile = LANES // n_rhs
    values = right_operand(first_ref[...].reshape(rows * n_rhs, -1))
    step = 2 * n_diag * n_func
    for done in range(0, through_in.shape[0], step):
        through_ref[done : done + step, :] = dot_nt(through_in[done : done + step, :], values)
    value_ref[...] = dot_nt(
        functional_ref[...], right_operand(right_ref[...].reshape(rows * n_rhs, -1))
    )
    lane = lax.broadcasted_iota(jnp.int32, (n_func, LANES), 1)

    def spread(block, ref, kind, row):
        start = pl.multiple_of(kind * n_func, n_func)
        tile = pl.multiple_of(over(row, per_tile) * LANES, LANES)
        piece = ref[pl.ds(start, n_func), pl.ds(tile, LANES)]
        low = below(row, per_tile) * n_rhs
        piece = jnp.where((lane >= low) & (lane < low + n_rhs), piece, 0.0)
        spread_ref[block * n_func : (block + 1) * n_func, :] = piece

    for owner in range(n_rows):
        for rank in range(cap):
            code = list_ref[owner, 0, rank]
            tile = below(over(code, rows), n_tiles)
            kind = below(over(code, rows * n_tiles * rows), n_diag)
            spread(owner * cap + rank, through_ref, tile * n_diag + kind, below(code, rows))
    field = band_field(rows, width_k, 0, 1)
    for row in range(rows):
        done = n_rows * cap + row
        place_of = jnp.int32(row)
        spread(done, value_ref, index_ref[0, 0, rows + row], place_of)
        kind = near_ref[0, 0, field + row] * n_diag + near_ref[0, 0, rows + row]
        spread(done + rows, through_ref, kind, place_of)
    result = coarse_parts(n_rhs, n_blocks, count_ref, place_ref, spread_ref)
    result_ref[...] = result.reshape(result_ref.shape)
    depth = result_ref.shape[1]
    for n, first in enumerate((mine, others)):
        target = send_out.at[:, pl.ds(body + n * depth, depth)]
        send(result_ref.at[pl.ds(first, half)], target)
    finish(copies)


def mirror_kernel(sizes, list_in, mirror_ref, tile_ref, send_out, list_ref, product_ref, send_ref, sems):
    rows, n_rows, cap, n_tiles, n_rhs = sizes
    half = n_rows // 2
    base = jnp.where(lax.axis_index("rows") >= half, half, 0)
    list_in = list_in.at[pl.ds(base, half), :, pl.ds(0, LANES)]
    metadata = started([pltpu.make_async_copy(list_in, list_ref, sems.at[half])])
    table_products(mirror_ref[...].reshape(rows * n_rhs, -1), tile_ref, product_ref)
    finish(metadata)
    copies = []
    for device in range(half):
        for rank in range(cap):
            code = list_ref[device, 0, LANES // 2 + rank]
            block = product_ref[below(code, rows * n_tiles)]
            send_ref[device, rank * n_rhs : (rank + 1) * n_rhs, :] = block
        copy = pltpu.make_async_copy(send_ref.at[device], send_out.at[device], sems.at[device])
        copies += started([copy])
    finish(copies)


def coarse_parts(n_rhs, n_blocks, count_ref, place_ref, spread_ref):
    n_func = spread_ref.shape[0] // n_blocks
    values = [
        spread_ref[pl.ds(t, n_blocks, stride=n_func), :] for t in range(count_ref.shape[1] // n_blocks)
    ]
    values = jnp.concatenate(values, axis=0)
    partial = jnp.dot(
        count_ref[...], jnp.concatenate(halves(values), axis=1), preferred_element_type=jnp.float32
    )
    partial = partial[:, :LANES] + partial[:, LANES:]
    shift = LANES // 2
    while shift >= n_rhs:
        partial = partial + pltpu.roll(partial, shift, axis=1)
        shift //= 2
    return place(place_ref, partial, n_rhs, 2)


def part_kernel(arrived_ref, keep_ref, give_ref):
    depth = keep_ref.shape[0] // 2
    body = arrived_ref.shape[1] - 4 * depth
    total = arrived_ref[0, body:, :]
    for source in range(1, arrived_ref.shape[0]):
        total = total + arrived_ref[source, body:, :]
    lower = lax.axis_index("band") == 0
    for n in range(2):
        zero, one = (total[(2 * n + m) * depth : (2 * n + m + 1) * depth] for m in range(2))
        keep_ref[n * depth : (n + 1) * depth] = jnp.where(lower, zero, one)
        give_ref[n * depth : (n + 1) * depth] = jnp.where(lower, one, zero)


def final_kernel(sizes, width_k, *refs):
    rows, n_rows, cap, n_tiles, n_rhs = sizes
    metadata_in, own_ref, mirror_ref, inverse_ref, terms_in = refs[:2], *refs[2:5], refs[5:7]
    near_ref, far_ref, scale_ref, out_ref = refs[7:11]
    metadata, sum_ref, product_ref, terms, term_sems, meta_sems = refs[11:13], *refs[13:15], refs[15:17], *refs[17:]
    place_ref, index_ref = metadata
    metadata = copies_of(zip(metadata_in, metadata), meta_sems)
    later = copies_of(zip(terms_in, terms), term_sems)
    finish(metadata)

    def fetch(row):
        total = None
        for k in range(width_k):
            slot = place_ref[0, 0, k * rows + row]
            holder, slot = over(slot, 2 * cap), below(slot, 2 * cap)
            start = pl.ds(pl.multiple_of(below(slot, cap) * n_rhs, n_rhs), n_rhs)
            block = jnp.where(slot < cap, own_ref[holder, start, :], mirror_ref[holder, start, :])
            total = block if total is None else total + block
        return total

    def diags(row):
        return index_ref[0, 0, rows + row]

    depth = scale_ref.shape[0]
    correction = (near_ref[...] + far_ref[...]) / scale_ref[...]
    padded = jnp.concatenate([correction, jnp.zeros((8 - depth, LANES), jnp.float32)], axis=0)
    turned = padded.T
    gather_solve(sizes, fetch, diags, later, terms, inverse_ref, sum_ref, product_ref)
    for row in range(rows):
        spot, place = row // depth, row % depth
        column = turned[spot * n_rhs : (spot + 1) * n_rhs, place : place + 1]
        out_ref[row] = sum_ref[pl.ds(row * n_rhs, n_rhs), :] + column


def shifted(value, axis, steps):
    count = lax.axis_size(axis)
    initial, last = (max(0, -steps), min(count, count - steps))
    return lax.ppermute(value, axis, [(source, source + steps) for source in range(initial, last)])


def to_bands(sends):
    if len(sends) == 1:
        return (lax.ppermute(sends[0], "band", [(0, 1), (1, 0)]),)
    return shifted(sends[0], "band", 1), shifted(sends[1], "band", -1)


def on_device(
    start_iterate,
    right_side,
    diag_table,
    inverse_table,
    coupling_tiles,
    diag_index,
    tile_index,
    source_owner,
    source_local,
    aggregate_map,
):
    rows, n_rhs, states = start_iterate.shape
    width_k = source_owner.shape[1]
    n_tiles, n_diag = coupling_tiles.shape[0], inverse_table.shape[0]
    n_rows, n_bands = lax.axis_size("rows"), lax.axis_size("band")
    n_dev = n_rows * n_bands
    cap = max(2, 2 * width_k * rows // n_rows)
    slots = n_rows * cap
    total_groups = AGG_DEV * n_dev
    per_tile = LANES // n_rhs
    depth = rows // per_tile
    n_func = 16
    dense = (
        n_bands == 2
        and n_dev * rows * total_groups <= DENSE_LIMIT
        and depth == 4
        and n_diag * n_func == LANES
        and n_tiles + 2 <= n_func
    )
    sizes = (rows, n_rows, cap, n_tiles, n_rhs)
    f32, i32 = jnp.float32, jnp.int32
    my_band = lax.axis_index("band")
    my_row = lax.axis_index("rows")

    half = n_rows // 2
    wide = -(-(4 + 2 * width_k) * rows // LANES) * LANES
    place_wide = -(-2 * width_k * rows // LANES) * LANES
    index_shapes = [(width_k, rows), (width_k, rows), (width_k + 2, rows), (1, rows), (1, rows)]
    halves_of_rows = [list(range(half)), list(range(half, n_rows))]
    to_mirror = [(i, (i + half) % n_rows) for i in range(n_rows)]
    mirror = lax.ppermute(start_iterate, "rows", to_mirror)
    lists, index, places = call(
        functools.partial(request_kernel, (rows, n_rows, cap, n_tiles, n_diag)),
        (
            jax.ShapeDtypeStruct((n_rows, 1, LANES + wide), i32),
            jax.ShapeDtypeStruct((1, 1, wide), i32),
            jax.ShapeDtypeStruct((1, 1, place_wide), i32),
        ),
        [HBM] * 5,
        [VMEM] * 3,
        [*[pltpu.VMEM(shape, i32) for shape in index_shapes], pltpu.SemaphoreType.DMA((5,))],
    )(source_owner.T, source_local.T, tile_index.T, diag_index[None], aggregate_map.T)
    lists = lax.all_to_all(lists, "rows", split_axis=0, concat_axis=0, tiled=True)
    if n_bands == 2:
        near = lax.ppermute(index, "band", [(0, 1), (1, 0)])
    else:
        ways = [[(b, (b + step) % n_bands) for b in range(n_bands)] for step in (-1, 1)]
        near = jnp.concatenate([lax.ppermute(index, "band", way) for way in ways], axis=0)

    n_ways = 1 if n_bands == 2 else 2
    block = (rows, n_rhs, states)
    band_shapes = [jax.ShapeDtypeStruct(block, f32)] * n_ways
    band_scratch = [pltpu.VMEM(block, f32)] * n_ways
    term_scratch = [pltpu.VMEM(block, f32)] * (1 + n_ways)
    term_sems = pltpu.SemaphoreType.DMA((1 + n_ways,))
    list_scratch = pltpu.SMEM((half, 1, LANES), i32)
    near_scratch = pltpu.SMEM((n_ways, 1, wide), i32)
    row_scratch = [pltpu.SMEM((1, 1, place_wide), i32), pltpu.SMEM((1, 1, wide), i32)]
    flat = rows * n_rhs
    sums = pltpu.VMEM((flat, states), f32)
    products = pltpu.VMEM((max(n_tiles, n_diag) * rows, n_rhs, states), f32)
    work = 6 * flat * states * states
    made_shape = (n_tiles * rows, n_rhs, states)
    table_scratch = [pltpu.VMEM(coupling_tiles.shape, f32)]
    table_sems = pltpu.SemaphoreType.DMA((-(-n_tiles // 2),))
    made = call(
        product_kernel,
        jax.ShapeDtypeStruct(made_shape, f32),
        [HBM, HBM],
        HBM,
        [
            pltpu.VMEM(block, f32),
            *table_scratch,
            pltpu.VMEM(made_shape, f32),
            pltpu.SemaphoreType.DMA((1 + n_tiles,)),
            table_sems,
        ],
        work * n_tiles,
        4 << 20,
    )(start_iterate, coupling_tiles)
    packed, *bands = call(
        functools.partial(first_kernel, sizes, width_k, n_ways),
        (jax.ShapeDtypeStruct((half, 2 * cap, n_rhs, states), f32), *band_shapes),
        [HBM, VMEM, VMEM, ANY, ANY],
        [HBM] * (1 + n_ways),
        [
            pltpu.VMEM((2, *made_shape), f32),
            list_scratch,
            near_scratch,
            pltpu.VMEM((half, 2 * cap, n_rhs, states), f32),
            *band_scratch,
            pltpu.SemaphoreType.DMA((n_tiles,)),
            pltpu.SemaphoreType.DMA((2,)),
            pltpu.SemaphoreType.DMA((half + n_ways,)),
        ],
        work * n_tiles,
        4 << 20,
    )(made, mirror, coupling_tiles, lists, near)
    packed, late = lax.optimization_barrier((packed, lists))
    if dense:
        across = lax.ppermute(late, "band", [(0, 1), (1, 0)])
        across, *bands = lax.optimization_barrier((across, *bands))
    sends = (packed.reshape(half, 2 * cap * n_rhs, states), *bands)
    halves_of_rows = [list(range(half)), list(range(half, n_rows))]
    def exchange(sends, groups=None):
        arrived = lax.all_to_all(
            sends[0], "rows", split_axis=0, concat_axis=0, tiled=True, axis_index_groups=groups
        )
        return arrived, to_bands(sends[1:])

    arrived_blocks, arrived_bands = exchange(sends, halves_of_rows)

    if dense:
        fields = jnp.stack([late, across])[:, :, 0, LANES:]
        fields = fields.reshape(2, n_rows, -1, rows).transpose(2, 0, 1, 3)
        fields = fields.reshape(-1, 2, n_rows * rows)
        n_blocks = slots + 2 * rows
        length = n_dev * depth
        extra_shapes = [
            ((n_diag * n_func, 3 * states), jnp.bfloat16),
            ((n_tiles * n_diag * n_func, 3 * states), jnp.bfloat16),
            ((total_groups, (n_tiles + 2) * n_blocks), jnp.bfloat16),
            ((per_tile * length, total_groups), jnp.bfloat16),
        ]
        functional_shape, through_shape, count_shape, placing_shape = extra_shapes
        counts, functionals, through, placing, scale = call(
            functools.partial(count_kernel, sizes, width_k, n_func),
            (
                jax.ShapeDtypeStruct(*count_shape),
                jax.ShapeDtypeStruct(*functional_shape),
                jax.ShapeDtypeStruct(*through_shape),
                jax.ShapeDtypeStruct(*placing_shape),
                jax.ShapeDtypeStruct((depth, LANES), f32),
            ),
            [VMEM] * 5,
            [HBM] * 4 + [VMEM],
            [
                pltpu.VMEM(*count_shape),
                pltpu.VMEM(*functional_shape),
                pltpu.VMEM(*through_shape),
                pltpu.VMEM(*placing_shape),
                pltpu.SemaphoreType.DMA((4,)),
            ],
            4 * total_groups * n_tiles * n_dev * rows * n_blocks,
            4 << 20,
        )(fields, late[:, 0, :LANES], coupling_tiles, diag_table, inverse_table)
        extra_scratch = [
            *[pltpu.VMEM(*shape) for shape in extra_shapes],
            pltpu.VMEM((n_diag * n_func, flat), f32),
            pltpu.VMEM((n_tiles * n_diag * n_func, flat), f32),
            pltpu.VMEM((n_blocks * n_func, LANES), f32),
            pltpu.VMEM((n_rows, n_bands * depth, LANES), f32),
        ]

        made = (arrived_blocks, functionals, through, counts, placing, scale)
        made = lax.optimization_barrier(made)
        arrived_blocks, functionals, through, counts, placing, scale = made

    def solve(field, arrived, bands):
        return call(
            functools.partial(solve_kernel, sizes, width_k, n_ways, field),
            jax.ShapeDtypeStruct(block, f32),
            [ANY] * 2 + [VMEM] * 2 + [HBM] + [ANY] * n_ways,
            VMEM,
            [
                *row_scratch,
                sums,
                products,
                *term_scratch,
                term_sems,
                pltpu.SemaphoreType.DMA((2,)),
            ],
            work * n_diag,
            4 << 20,
        )(places, index, arrived, inverse_table, right_side, *bands)

    first = solve(0, arrived_blocks, arrived_bands)
    body = cap * n_rhs
    full_list = pltpu.SMEM((n_rows, 1, LANES), i32)
    if dense:
        mirror = lax.ppermute(first, "rows", to_mirror)
        own, band = call(
            functools.partial(own_kernel, sizes, width_k),
            (
                jax.ShapeDtypeStruct((half, body + 2 * n_bands * depth, states), f32),
                jax.ShapeDtypeStruct(block, f32),
            ),
            [ANY] * 3 + [VMEM] * 2 + [HBM] * 5,
            [HBM] * 2,
            [
                row_scratch[1],
                full_list,
                near_scratch,
                products,
                pltpu.VMEM((half, body, states), f32),
                pltpu.VMEM(block, f32),
                pltpu.VMEM(block, f32),
                *extra_scratch,
                pltpu.SemaphoreType.DMA((3,)),
                pltpu.SemaphoreType.DMA((5,)),
                pltpu.SemaphoreType.DMA((half + 3,)),
            ],
            2 * work * n_tiles,
            4 << 20,
        )(
            index,
            lists,
            near,
            first,
            coupling_tiles,
            right_side,
            functionals,
            through,
            counts,
            placing,
        )
        own, (band,) = exchange((own, band), halves_of_rows)
        packed = call(
            functools.partial(mirror_kernel, sizes),
            jax.ShapeDtypeStruct((half, body, states), f32),
            [ANY] + [VMEM] * 2,
            HBM,
            [
                list_scratch,
                products,
                pltpu.VMEM((half, body, states), f32),
                pltpu.SemaphoreType.DMA((half + 1,)),
            ],
            BEHIND_SWAP * work * n_tiles,
            4 << 20,
        )(lists, mirror, coupling_tiles)
        packed, band = lax.optimization_barrier((packed, band))
        swapped = lax.all_to_all(
            packed, "rows", split_axis=0, concat_axis=0, tiled=True, axis_index_groups=halves_of_rows
        )
        part = jax.ShapeDtypeStruct((2 * depth, LANES), f32)
        keep, give = call(part_kernel, (part, part), [VMEM], [VMEM] * 2)(own)
        keep = keep + lax.ppermute(give, "band", [(0, 1), (1, 0)])
        far = lax.ppermute(keep[depth:], "rows", to_mirror)
        return call(
            functools.partial(final_kernel, sizes, width_k),
            jax.ShapeDtypeStruct(block, f32),
            [ANY] * 2 + [VMEM] * 3 + [HBM, ANY] + [VMEM] * 3,
            VMEM,
            [
                *row_scratch,
                sums,
                products,
                *term_scratch,
                term_sems,
                pltpu.SemaphoreType.DMA((2,)),
            ],
            work * n_diag,
            4 << 20,
        )(places, index, own, swapped, inverse_table, right_side, band, keep[:depth], far, scale)

    sends = call(
        functools.partial(pack_kernel, sizes, width_k, n_ways),
        (jax.ShapeDtypeStruct((n_rows, body, states), f32), *band_shapes),
        [ANY] * 2 + [VMEM] * 2,
        [HBM] * (1 + n_ways),
        [
            full_list,
            near_scratch,
            products,
            pltpu.VMEM((n_rows, body, states), f32),
            *band_scratch,
            pltpu.SemaphoreType.DMA((2,)),
            pltpu.SemaphoreType.DMA((1 + n_ways,)),
        ],
        work * n_tiles,
        4 << 20,
    )(lists, near, first, coupling_tiles)
    arrived_blocks, arrived_bands = exchange(sends)
    second = solve(width_k, arrived_blocks, arrived_bands)

    groups = aggregate_map[:, 0]
    own = jnp.arange(rows, dtype=i32)
    index_all = lax.all_gather(index, ("band", "rows"), axis=0, tiled=True)
    index_all = index_all.reshape(n_bands, n_rows, wide)
    groups_all, diags_all = index_all[:, :, :rows], index_all[:, :, rows : 2 * rows]
    codes = lists[:, 0, :cap]
    asked = jnp.arange(n_rows, dtype=i32)[:, None] * rows + codes // (rows * n_tiles) % rows
    asked = jnp.where(codes > 0, asked, -1).reshape(-1)
    table_sums = jnp.sum(diag_table, axis=(1, 2))
    diag_onehot = diags_all.reshape(-1, 1) == jnp.arange(n_diag, dtype=i32)[None]
    block_sums = jnp.sum(jnp.where(diag_onehot, table_sums[None], 0.0), axis=1)
    whole_diag = jnp.sum(
        jnp.where(groups[:, None] == groups_all.reshape(-1)[None], block_sums[None], 0.0), axis=1
    )
    above, below = near[0, 0], near[-1, 0]
    place_of = (2 + width_k) * rows
    band_tiles = jnp.stack([above[place_of : place_of + rows], below[place_of + rows : place_of + 2 * rows]])
    band_groups = jnp.stack([above[:rows], below[:rows]])
    band_valid = jnp.stack([my_band + 1 < n_bands, my_band > 0])
    band_valid = jnp.broadcast_to(band_valid[:, None], (2, rows))
    n_all = n_tiles + n_diag + 1
    code = codes.reshape(-1)
    band_of_mine = lax.dynamic_index_in_dim(groups_all, my_band, 0, keepdims=False).reshape(-1)
    entry_group = jnp.concatenate(
        [jnp.take(band_of_mine, jnp.maximum(asked, 0)), band_groups.reshape(-1), groups, groups]
    )
    entry_func = jnp.concatenate(
        [
            (code % rows) * n_all + (code // rows) % n_tiles,
            (own[None] * n_all + band_tiles).reshape(-1),
            own * n_all + n_tiles + diag_index,
            own * n_all + n_tiles + n_diag,
        ]
    )
    entry_valid = jnp.concatenate([asked >= 0, band_valid.reshape(-1), jnp.ones((2 * rows,), bool)])
    functionals = jnp.concatenate(
        [jnp.sum(coupling_tiles, axis=1), -jnp.sum(diag_table, axis=1)], axis=0
    )
    weights = jnp.einsum("fp,rcp->rfc", functionals, second, precision=HIGH)
    weights = jnp.concatenate([weights, jnp.sum(right_side, axis=2)[:, None]], axis=1)
    chosen = jnp.take(weights.reshape(rows * n_all, n_rhs), entry_func, axis=0)
    chosen = jnp.where(entry_valid[:, None], chosen, 0.0)
    partial = jax.ops.segment_sum(chosen, entry_group, num_segments=total_groups)
    whole = lax.psum(partial, ("band", "rows"))
    correction = jnp.take(whole, groups, axis=0) / whole_diag[:, None]
    return second + correction[:, :, None]


def solution(mesh):
    in_specs = (
        P(("band", "rows"), None, None),
        P(("band", "rows"), None, None),
        P(),
        P(),
        P(),
        P(("band", "rows")),
        P(("band", "rows"), None),
        P(("band", "rows"), None),
        P(("band", "rows"), None),
        P(("band", "rows"), None),
    )
    out_specs = P(("band", "rows"), None, None)
    return jax.shard_map(
        on_device, mesh=mesh, in_specs=in_specs, out_specs=out_specs, check_vma=False
    )
```

```python
import functools

import jax
import jax.numpy as jnp
from jax import lax
from jax.experimental import pallas as pl
from jax.experimental.pallas import tpu as pltpu
from jax.sharding import PartitionSpec as P

AGG_DEV = 8
LANES = 128
DENSE_LIMIT = 1 << 19
BEHIND_SWAP = 100

VMEM = pl.BlockSpec(memory_space=pltpu.VMEM)
SMEM = pl.BlockSpec(memory_space=pltpu.SMEM)
HBM = pl.BlockSpec(memory_space=pltpu.HBM)
ANY = pl.BlockSpec(memory_space=pl.ANY)
HIGH = lax.Precision.HIGHEST


def params():
    return pltpu.CompilerParams(vmem_limit_bytes=24 * 1024 * 1024)


def call(kernel, out_shape, in_specs, out_specs, scratch=(), flops=0, moved=0):
    def shaped(shape, spec):
        return pltpu.HBM(shape.shape, shape.dtype) if spec is HBM else shape

    if isinstance(out_shape, (tuple, list)):
        out_shape = [shaped(*pair) for pair in zip(out_shape, out_specs)]
    else:
        out_shape = shaped(out_shape, out_specs)
    run = pl.pallas_call(
        kernel,
        out_shape=out_shape,
        in_specs=in_specs,
        out_specs=out_specs,
        scratch_shapes=list(scratch),
        compiler_params=params(),
        cost_estimate=pl.CostEstimate(flops=flops, bytes_accessed=moved, transcendentals=0),
    )

    def apply(*args):
        pinned = [
            pltpu.with_memory_space_constraint(arg, pltpu.HBM) if spec is HBM else arg
            for arg, spec in zip(args, in_specs)
        ]
        return run(*pinned)

    return apply


def below(value, bound):
    return value & (bound - 1) if bound & (bound - 1) == 0 else lax.rem(value, bound)


def over(value, bound):
    if bound & (bound - 1) == 0:
        return lax.shift_right_logical(value, bound.bit_length() - 1)
    return lax.div(value, bound)


def halves(value):
    high = value.astype(jnp.bfloat16)
    low = (value - high.astype(jnp.float32)).astype(jnp.bfloat16)
    return high, low


def left_operand(value):
    high, low = halves(value)
    return jnp.concatenate([high, low, high], axis=1)


def right_operand(value):
    high, low = halves(value)
    return jnp.concatenate([high, high, low], axis=1)


def dot_nt(left, right):
    return lax.dot_general(
        left, right, (((1,), (1,)), ((), ())), preferred_element_type=jnp.float32
    )


def table_products(value, table_ref, out_ref, done=None, loads=None):
    left = left_operand(value)
    count, width = table_ref.shape[0], table_ref.shape[1]
    n_rhs = out_ref.shape[1]
    rows = left.shape[0] // n_rhs
    for first in range(0, count, 2):
        last = min(first + 2, count)
        if loads is not None:
            loads[first // 2].wait()
        right = right_operand(table_ref[first:last].reshape((last - first) * width, -1))
        product = dot_nt(left, right)
        for t in range(first, last):
            part = product[:, (t - first) * width : (t - first + 1) * width]
            out_ref[t * rows : (t + 1) * rows] = part.reshape(rows, n_rhs, width)
        if done is not None:
            done(first * rows, (last - first) * rows)


def started(copies):
    for copy in copies:
        copy.start()
    return copies


def finish(copies):
    for copy in copies:
        copy.wait()


def request_kernel(sizes, *refs):
    rows, n_rows, cap, n_tiles, n_diag = sizes
    inputs, (list_ref, index_ref, place_ref), held, sems = refs[:5], refs[5:8], refs[8:13], refs[13]
    finish(
        started([pltpu.make_async_copy(i, h, sems.at[n]) for n, (i, h) in enumerate(zip(inputs, held))])
    )
    owner_ref, local_ref, tile_ref, diag_ref, group_ref = held
    width_k = owner_ref.shape[0]
    half = n_rows // 2
    row_of = lax.broadcasted_iota(jnp.int32, (rows, rows), 0)
    col_of = lax.broadcasted_iota(jnp.int32, (rows, rows), 1)
    lane = lax.broadcasted_iota(jnp.int32, (rows, LANES), 1)
    owners = lax.broadcasted_iota(jnp.int32, (n_rows, rows), 0)

    def column(row):
        return jnp.sum(jnp.where(row_of == col_of, row, 0), axis=1, keepdims=True)

    def owner_row(k):
        return owner_ref[k : k + 1, :]

    row_ids = lax.broadcasted_iota(jnp.int32, (1, rows), 1)
    owner_columns = [column(owner_row(k)) for k in range(width_k)]
    lists = jnp.zeros((n_rows, LANES), jnp.float32)
    places, half_places = [], []
    for k in range(width_k):
        rank = jnp.zeros((1, rows), jnp.int32)
        for other in range(k + 1):
            match = owner_columns[other] == owner_row(k)
            if other == k:
                match = match & (row_of < col_of)
            rank = rank + jnp.sum(jnp.where(match, 1, 0), axis=0, keepdims=True)
        places.append(owner_row(k) * cap + rank)
        same = (owner_row(k) >= half) == (lax.axis_index("rows") >= half)
        holder = jnp.where(owner_row(k) >= half, owner_row(k) - half, owner_row(k))
        half_places.append(holder * (2 * cap) + rank + jnp.where(same, 0, cap))
        taker = row_ids + rows * (diag_ref[...] + n_diag)
        code = local_ref[k : k + 1, :] + rows * (tile_ref[k : k + 1, :] + n_tiles * taker)
        code, rank = column(code), column(rank)
        mirror = jnp.where(owner_row(k) >= half, owner_row(k) - half, owner_row(k) + half)
        for owner, base in ((owner_row(k), 0), (mirror, LANES // 2)):
            by_rank = jnp.where(lane == rank + base, code, 0).astype(jnp.float32)
            mine = jnp.where(owners == owner, 1.0, 0.0)
            lists = lists + jnp.dot(
                mine, by_rank, precision=HIGH, preferred_element_type=jnp.float32
            )
    lists = (lists + 0.5).astype(jnp.int32)

    def joined(parts, wide):
        spare = wide - len(parts) * rows
        if spare:
            parts = [*parts, jnp.zeros((1, spare), jnp.int32)]
        return jnp.concatenate(parts, axis=1)

    index = [group_ref[...], diag_ref[...]]
    index += [tile_ref[k : k + 1, :] for k in range(width_k + 2)]
    index += [owner_row(k) * rows + local_ref[k : k + 1, :] for k in range(width_k)]
    index = joined(index, index_ref.shape[2])
    index_ref[0] = index
    place_ref[0] = joined(half_places + places, place_ref.shape[2])
    for device in range(n_rows):
        list_ref[device] = jnp.concatenate([lists[device : device + 1, :], index], axis=1)


def copies_of(pairs, sems):
    return started([pltpu.make_async_copy(i, h, sems.at[n]) for n, (i, h) in enumerate(pairs)])


def band_field(rows, width_k, way, n_ways):
    field = (2 + width_k) * rows
    if n_ways == 1:
        return field + jnp.where(lax.axis_index("band") == 0, 0, rows)
    return field + way * rows


def pack_bands(sizes, width_k, product_ref, near_ref, band_refs):
    rows = sizes[0]
    for way, band_ref in enumerate(band_refs):
        field = band_field(rows, width_k, way, len(band_refs))
        for row in range(rows):
            band_ref[row] = product_ref[near_ref[way, 0, field + row] * rows + row]


def table_loads(table_in, table_ref, sems):
    copies = []
    for first in range(0, table_in.shape[0], 2):
        place = pl.ds(first, min(2, table_in.shape[0] - first))
        source, target = table_in.at[place], table_ref.at[place]
        copies.append(pltpu.make_async_copy(source, target, sems.at[first // 2]))
    return started(copies)


def product_kernel(start_in, tile_in, product_out, start_ref, tile_ref, product_ref, sems, tile_sems):
    start = pltpu.make_async_copy(start_in, start_ref, sems.at[0])
    start.start()
    loads = table_loads(tile_in, tile_ref, tile_sems)
    start.wait()
    copies = []

    def done(first, count):
        place = pl.ds(first, count)
        source, target = product_ref.at[place], product_out.at[place]
        copies.extend(started([pltpu.make_async_copy(source, target, sems.at[1 + len(copies)])]))

    rows, n_rhs, states = start_ref.shape
    values = start_ref[...].reshape(rows * n_rhs, states)
    table_products(values, tile_ref, product_ref, done, loads)
    finish(copies)


def first_kernel(sizes, width_k, n_band, *refs):
    rows, n_rows, cap, n_tiles, n_rhs = sizes
    product_in, mirror_ref, tile_ref, list_in, near_in, send_out = refs[:6]
    band_out, refs = refs[6 : 6 + n_band], refs[6 + n_band :]
    product_ref, list_ref, near_ref, send_ref = refs[:4]
    band_refs, (load_sems, meta_sems, send_sems) = refs[4 : 4 + n_band], refs[4 + n_band :]
    half = n_rows // 2
    base = jnp.where(lax.axis_index("rows") >= half, half, 0)
    list_in = list_in.at[pl.ds(base, half), :, pl.ds(0, LANES)]
    metadata = copies_of(((list_in, list_ref), (near_in, near_ref)), meta_sems)
    places = [pl.ds(tile * rows, rows) for tile in range(n_tiles)]
    loads = [(product_in.at[place], product_ref.at[0, place]) for place in places]
    loads = copies_of(loads, load_sems)
    values = mirror_ref[...].reshape(rows * n_rhs, -1)
    table_products(values, tile_ref, product_ref.at[1])
    finish(metadata)
    finish(loads)
    copies = []
    pack_bands(sizes, width_k, product_ref.at[0], near_ref, band_refs)
    for n, (ref, out) in enumerate(zip(band_refs, band_out)):
        copies += started([pltpu.make_async_copy(ref, out, send_sems.at[half + n])])
    for device in range(half):
        for slot in range(2 * cap):
            side, rank = slot // cap, slot % cap
            code = list_ref[device, 0, side * (LANES // 2) + rank]
            send_ref[device, slot] = product_ref[side, below(code, rows * n_tiles)]
        copy = pltpu.make_async_copy(send_ref.at[device], send_out.at[device], send_sems.at[device])
        copies += started([copy])
    finish(copies)


def place(place_ref, values, n_rhs, n_parts):
    per_tile = LANES // n_rhs
    length = place_ref.shape[0] // per_tile
    parts, rest = [], values
    for _ in range(n_parts):
        part = rest.astype(jnp.bfloat16)
        rest = rest - part.astype(jnp.float32)
        parts.append(part)
    parts = jnp.concatenate(parts, axis=1)
    lane = lax.broadcasted_iota(jnp.int32, (length, LANES), 1)
    result = jnp.zeros((length, LANES), jnp.float32)
    placed = jnp.dot(place_ref[...], parts, preferred_element_type=jnp.float32)
    for spot in range(per_tile):
        chosen = placed[spot * length : (spot + 1) * length]
        chosen = sum(chosen[:, n * LANES : (n + 1) * LANES] for n in range(n_parts))
        result = jnp.where((lane >= spot * n_rhs) & (lane < (spot + 1) * n_rhs), chosen, result)
    return result


def spread_values(n_rhs, n_func, functional_ref, blocks, kinds, value_ref, spread_ref, done):
    per_tile = LANES // n_rhs
    lane = lax.broadcasted_iota(jnp.int32, (n_func, LANES), 1)
    columns = slice(done * n_rhs, done * n_rhs + blocks.shape[0])
    value_ref[:, columns] = dot_nt(functional_ref[...], right_operand(blocks))
    for block, kind in enumerate(kinds, done):
        tile, spot = block // per_tile, block % per_tile
        start = pl.multiple_of(kind * n_func, n_func)
        piece = value_ref[pl.ds(start, n_func), tile * LANES : (tile + 1) * LANES]
        piece = jnp.where((lane >= spot * n_rhs) & (lane < (spot + 1) * n_rhs), piece, 0.0)
        spread_ref[block * n_func : (block + 1) * n_func, :] = piece


def one_hot(ids, row):
    return jnp.where(ids == row, 1.0, 0.0).astype(jnp.bfloat16)


def count_kernel(sizes, width_k, n_func, *refs):
    rows, n_rows, cap, n_tiles, n_rhs = sizes
    index_in, right_in, field_ref, list_ref, tile_ref, table_ref, inverse_ref = refs[:7]
    count_out, functional_out, placing_out, partial_out, scale_ref = refs[7:12]
    count_ref, functional_ref, placing_ref, partial_ref = refs[12:16]
    index_ref, right_ref, value_ref, spread_ref, load_sems, sems = refs[16:]
    loads = copies_of(((index_in, index_ref), (right_in, right_ref)), load_sems)
    n_groups = count_ref.shape[0]
    slots, band_rows = n_rows * cap, n_rows * rows
    copies = []

    def send(source, target):
        copies.extend(started([pltpu.make_async_copy(source, target, sems.at[len(copies)])]))

    sums = jnp.sum(tile_ref[...], axis=1)
    line = lax.broadcasted_iota(jnp.int32, (n_func, sums.shape[1]), 0)
    sums = jnp.concatenate([sums, jnp.zeros((n_func - n_tiles, sums.shape[1]), jnp.float32)], axis=0)
    n_diag = inverse_ref.shape[0]
    totals = []
    for d in range(n_diag):
        minus = -jnp.sum(table_ref[d], axis=0, keepdims=True)
        totals.append(-jnp.sum(minus, axis=1, keepdims=True))
        wanted = jnp.where(line == n_tiles, minus, sums)
        high, low = halves(inverse_ref[d])
        right = jnp.concatenate([high, high, low], axis=0)
        solved = jnp.dot(left_operand(wanted), right, preferred_element_type=jnp.float32)
        solved = jnp.where(line == n_tiles + 1, 1.0, solved)
        functional_ref[d * n_func : (d + 1) * n_func, :] = left_operand(solved)
    send(functional_ref, functional_out)

    lists = list_ref[...]
    asker = lax.broadcasted_iota(jnp.int32, lists.shape, 0)
    codes = asker * rows + below(over(lists, rows * n_tiles), rows)
    codes = jnp.where(lists > 0, codes, -1).astype(jnp.float32)
    spread = lax.broadcasted_iota(jnp.int32, (slots, n_rows), 0)
    spread = lax.div(spread, cap) == lax.broadcasted_iota(jnp.int32, (slots, n_rows), 1)
    codes = jnp.dot(
        jnp.where(spread, 1.0, 0.0), codes, precision=HIGH, preferred_element_type=jnp.float32
    )
    rank = lax.rem(lax.broadcasted_iota(jnp.int32, codes.shape, 0), cap)
    lane = lax.broadcasted_iota(jnp.int32, codes.shape, 1)
    asked = jnp.sum(jnp.where(rank == lane, codes, 0.0), axis=1, keepdims=True)
    asked = jnp.where(asked < 0.0, asked - 0.5, asked + 0.5).astype(jnp.int32)
    low, high = asked[: slots // 2], asked[slots // 2 :]
    upper = lax.axis_index("rows") >= n_rows // 2
    asked = jnp.concatenate([jnp.where(upper, high, low), jnp.where(upper, low, high)], axis=0)
    own = lax.axis_index("rows") * rows + lax.broadcasted_iota(jnp.int32, (rows, 1), 0)
    band = lax.axis_index("band")

    def field(n, side):
        return field_ref[n, side : side + 1, :]

    row_ids = lax.broadcasted_iota(jnp.int32, (1, band_rows), 1)
    sides = []
    for side, targets in ((0, jnp.concatenate([asked, own], axis=0)), (1, own)):
        first = band == side
        across = jnp.where(first, field(2 + width_k, 1 - side), field(3 + width_k, 1 - side))
        takers = [field(2 + k, side) * n_groups + field(0, side) for k in range(width_k)]
        takers.append(across * n_groups + field(0, 1 - side))
        takers = jnp.concatenate(takers, axis=1)
        origins = [field(4 + width_k + k, side) for k in range(width_k)] + [row_ids]
        hits = one_hot(targets, jnp.concatenate(origins, axis=1))
        sides.append((takers, hits, field(0, side)))
    pieces, own_pieces = [], []
    ids = lax.broadcasted_iota(jnp.int32, (n_groups, band_rows), 0)
    for t in range(n_tiles + 1):
        found = []
        for takers, hits, groups in sides:
            if t < n_tiles:
                wide = lax.broadcasted_iota(jnp.int32, (n_groups, takers.shape[1]), 0)
                found.append(dot_nt(one_hot(wide + t * n_groups, takers), hits))
            else:
                found.append(dot_nt(one_hot(ids, groups), hits[:, -band_rows:]))
        pieces += [found[0][:, :slots], found[1]]
        own_pieces.append(found[0][:, slots:])
    count_ref[...] = jnp.concatenate(pieces, axis=1).astype(jnp.bfloat16)
    send(count_ref, count_out)

    own_counts = jnp.concatenate([*own_pieces, own_pieces[-1]], axis=1).astype(jnp.bfloat16)
    finish(loads)
    rights = right_ref[...].reshape(rows * n_rhs, -1)
    kinds = [index_ref[0, 0, rows + row] for row in range(rows)]
    spread_values(n_rhs, n_func, functional_ref, rights, kinds, value_ref, spread_ref, 0)
    values = [spread_ref[pl.ds(t, rows, stride=n_func), :] for t in range(n_tiles + 2)]
    values = jnp.concatenate(halves(jnp.concatenate(values, axis=0)), axis=1)
    partial = jnp.dot(own_counts, values, preferred_element_type=jnp.float32)
    partial_ref[...] = partial[:, :LANES] + partial[:, LANES:]
    send(partial_ref, partial_out)

    per_tile = LANES // n_rhs
    depth = rows // per_tile
    length = n_rows * 2 * depth
    order = lax.broadcasted_iota(jnp.int32, (per_tile * length, 1), 0)
    spot, order = lax.div(order, length), lax.rem(order, length)
    device, order = lax.div(order, 2 * depth), lax.rem(order, 2 * depth)
    side, order = lax.div(order, depth), lax.rem(order, depth)
    order = side * band_rows + device * rows + spot * depth + order
    member = [
        one_hot(ids, jnp.where(band == which, field(0, 0), field(0, 1))) for which in range(2)
    ]
    placing = jnp.zeros(placing_ref.shape, jnp.float32)
    for which in range(2):
        placing = placing + dot_nt(one_hot(order, row_ids + which * band_rows), member[which])
    placing_ref[...] = placing.astype(jnp.bfloat16)
    send(placing_ref, placing_out)
    whole = jnp.zeros((n_groups, 1), jnp.float32)
    for side in range(2):
        sums = jnp.zeros((1, band_rows), jnp.float32)
        for d in range(n_diag):
            sums = jnp.where(field(1, side) == d, totals[d], sums)
        weighted = jnp.where(ids == field(0, side), sums, 0.0)
        whole = whole + jnp.sum(weighted, axis=1, keepdims=True)
    scale = place(placing_ref, jnp.broadcast_to(whole, (n_groups, LANES)), n_rhs, 3)
    mine = jnp.zeros(scale_ref.shape, jnp.float32)
    here = lax.axis_index("rows") * 2 + band
    for n in range(2 * n_rows):
        mine = jnp.where(here == n, scale[n * depth : (n + 1) * depth, :], mine)
    scale_ref[...] = mine
    finish(copies)


def gather_solve(sizes, fetch, diags, later, terms, inverse_ref, sum_ref, product_ref):
    rows, n_rows, cap, n_tiles, n_rhs = sizes
    for row in range(rows):
        sum_ref[pl.ds(row * n_rhs, n_rhs), :] = fetch(row)
    finish(later)
    total = sum_ref[...]
    for term in terms:
        total = total + term[...].reshape(total.shape)
    table_products(total, inverse_ref, product_ref)
    for row in range(rows):
        sum_ref[pl.ds(row * n_rhs, n_rhs), :] = product_ref[diags(row) * rows + row]


def arrived_blocks_of(sizes, width_k, place_ref, field, arrived_ref):
    rows, n_rows, cap, n_tiles, n_rhs = sizes
    per = n_rows * cap // arrived_ref.shape[0]

    def fetch(row):
        total = None
        for k in range(width_k):
            slot = place_ref[0, 0, (field + k) * rows + row]
            start = pl.multiple_of(below(slot, per) * n_rhs, n_rhs)
            block = arrived_ref[over(slot, per), pl.ds(start, n_rhs), :]
            total = block if total is None else total + block
        return total

    return fetch


def solve_kernel(sizes, width_k, n_band, field, *refs):
    metadata_in, arrived_ref, inverse_ref = refs[:2], *refs[2:4]
    terms_in, refs = refs[4 : 5 + n_band], refs[5 + n_band :]
    out_ref, metadata, sum_ref, product_ref = refs[0], refs[1:3], *refs[3:5]
    place_ref, index_ref = metadata
    terms, (term_sems, meta_sems) = refs[5 : 6 + n_band], refs[6 + n_band :]
    rows = sizes[0]
    metadata = copies_of(zip(metadata_in, metadata), meta_sems)
    later = copies_of(zip(terms_in, terms), term_sems)
    finish(metadata)
    fetch = arrived_blocks_of(sizes, width_k, place_ref, field, arrived_ref)

    def diags(row):
        return index_ref[0, 0, rows + row]

    gather_solve(sizes, fetch, diags, later, terms, inverse_ref, sum_ref, product_ref)
    out_ref[...] = sum_ref[...].reshape(out_ref.shape)


def pack_kernel(sizes, width_k, n_band, *refs):
    rows, n_rows, cap, n_tiles, n_rhs = sizes
    list_in, near_in, first_ref, tile_ref, send_out = refs[:5]
    band_out, refs = refs[5 : 5 + n_band], refs[5 + n_band :]
    list_ref, near_ref, product_ref, send_ref = refs[:4]
    band_refs, (meta_sems, send_sems) = refs[4 : 4 + n_band], refs[4 + n_band :]
    list_in = list_in.at[:, :, pl.ds(0, LANES)]
    metadata = copies_of(((list_in, list_ref), (near_in, near_ref)), meta_sems)
    table_products(first_ref[...].reshape(rows * n_rhs, -1), tile_ref, product_ref)
    finish(metadata)
    pack_bands(sizes, width_k, product_ref, near_ref, band_refs)
    for owner in range(n_rows):
        for rank in range(cap):
            block = product_ref[below(list_ref[owner, 0, rank], rows * n_tiles)]
            send_ref[owner, rank * n_rhs : (rank + 1) * n_rhs, :] = block
    finish(copies_of(zip((send_ref, *band_refs), (send_out, *band_out)), send_sems))


def own_kernel(sizes, width_k, *refs):
    rows, n_rows, cap, n_tiles, n_rhs = sizes
    metadata_in, first_ref, tile_ref, extra = list(refs[:2]), *refs[2:4], refs[4:8]
    send_out, band_out, metadata, product_ref, send_ref, band_ref = refs[8], refs[9], refs[10:12], *refs[12:15]
    held, value_ref, spread_ref, result_ref, meta_sems, load_sems, send_sems = refs[15:19], *refs[19:]
    list_ref, near_ref = metadata
    metadata_in[0] = metadata_in[0].at[:, :, pl.ds(0, LANES)]
    metadata = copies_of(zip(metadata_in, metadata), meta_sems)
    fetched = copies_of(zip(extra, held), load_sems)
    table_products(first_ref[...].reshape(rows * n_rhs, -1), tile_ref, product_ref)
    finish(metadata)
    copies = []

    def send(source, target):
        copies.extend(started([pltpu.make_async_copy(source, target, send_sems.at[len(copies)])]))

    pack_bands(sizes, width_k, product_ref, near_ref, (band_ref,))
    send(band_ref, band_out)
    body, half = cap * n_rhs, n_rows // 2
    upper = lax.axis_index("rows") >= half
    mine, others = jnp.where(upper, half, 0), jnp.where(upper, 0, half)
    finish(fetched)
    functional_ref, count_ref, place_ref, partial_ref = held
    n_blocks = n_rows * cap + rows
    n_func = spread_ref.shape[0] // n_blocks
    n_diag = functional_ref.shape[0] // n_func

    def spread(done, blocks, kinds):
        spread_values(n_rhs, n_func, functional_ref, blocks, kinds, value_ref, spread_ref, done)

    kinds = [near_ref[0, 0, rows + row] for row in range(rows)]
    spread(n_rows * cap, band_ref[...].reshape(rows * n_rhs, -1), kinds)
    kinds = []
    for order in range(n_rows):
        owner = order % half + (mine if order < half else others)
        for rank in range(cap):
            code = list_ref[owner, 0, rank]
            kinds.append(below(over(code, rows * n_tiles * rows), n_diag))
            block = product_ref[below(code, rows * n_tiles)]
            send_ref[order, rank * n_rhs : (rank + 1) * n_rhs, :] = block
        if order < half:
            send(send_ref.at[order], send_out.at[order, pl.ds(0, body)])
        if order % 2:
            blocks = jnp.concatenate([send_ref[order - 1], send_ref[order]], axis=0)
            spread((order - 1) * cap, blocks, kinds)
            kinds = []
    result = coarse_parts(n_rhs, n_blocks, count_ref, place_ref, partial_ref, spread_ref)
    result_ref[...] = result.reshape(result_ref.shape)
    depth = result_ref.shape[1]
    for n, first in enumerate((mine, others)):
        target = send_out.at[:, pl.ds(body + n * depth, depth)]
        send(result_ref.at[pl.ds(first, half)], target)
    finish(copies)


def mirror_kernel(sizes, list_in, mirror_ref, tile_ref, send_out, list_ref, product_ref, send_ref, sems):
    rows, n_rows, cap, n_tiles, n_rhs = sizes
    half = n_rows // 2
    base = jnp.where(lax.axis_index("rows") >= half, half, 0)
    list_in = list_in.at[pl.ds(base, half), :, pl.ds(0, LANES)]
    metadata = started([pltpu.make_async_copy(list_in, list_ref, sems.at[half])])
    table_products(mirror_ref[...].reshape(rows * n_rhs, -1), tile_ref, product_ref)
    finish(metadata)
    copies = []
    for device in range(half):
        for rank in range(cap):
            code = list_ref[device, 0, LANES // 2 + rank]
            block = product_ref[below(code, rows * n_tiles)]
            send_ref[device, rank * n_rhs : (rank + 1) * n_rhs, :] = block
        copy = pltpu.make_async_copy(send_ref.at[device], send_out.at[device], sems.at[device])
        copies += started([copy])
    finish(copies)


def coarse_parts(n_rhs, n_blocks, count_ref, place_ref, partial_ref, spread_ref):
    n_func = spread_ref.shape[0] // n_blocks
    values = [
        spread_ref[pl.ds(t, n_blocks, stride=n_func), :] for t in range(count_ref.shape[1] // n_blocks)
    ]
    values = jnp.concatenate(values, axis=0)
    partial = jnp.dot(
        count_ref[...], jnp.concatenate(halves(values), axis=1), preferred_element_type=jnp.float32
    )
    partial = partial[:, :LANES] + partial[:, LANES:] + partial_ref[...]
    shift = LANES // 2
    while shift >= n_rhs:
        partial = partial + pltpu.roll(partial, shift, axis=1)
        shift //= 2
    return place(place_ref, partial, n_rhs, 2)


def part_kernel(arrived_ref, keep_ref, give_ref):
    depth = keep_ref.shape[0] // 2
    body = arrived_ref.shape[1] - 4 * depth
    total = arrived_ref[0, body:, :]
    for source in range(1, arrived_ref.shape[0]):
        total = total + arrived_ref[source, body:, :]
    lower = lax.axis_index("band") == 0
    for n in range(2):
        zero, one = (total[(2 * n + m) * depth : (2 * n + m + 1) * depth] for m in range(2))
        keep_ref[n * depth : (n + 1) * depth] = jnp.where(lower, zero, one)
        give_ref[n * depth : (n + 1) * depth] = jnp.where(lower, one, zero)


def half_blocks_of(sizes, width_k, place_ref, arrived_ref, far):
    rows, n_rows, cap, n_tiles, n_rhs = sizes

    def fetch(row):
        total = None
        for k in range(width_k):
            slot = place_ref[0, 0, k * rows + row]
            holder, slot = over(slot, 2 * cap), below(slot, 2 * cap)
            start = pl.ds(pl.multiple_of(below(slot, cap) * n_rhs, n_rhs), n_rhs)
            mine = slot >= cap if far else slot < cap
            block = jnp.where(mine, arrived_ref[holder, start, :], 0.0)
            total = block if total is None else total + block
        return total

    return fetch


def base_kernel(sizes, width_k, *refs):
    metadata_in, own_ref, inverse_ref, terms_in, out_ref = refs[:2], *refs[2:4], refs[4:6], refs[6]
    metadata, sum_ref, product_ref, terms, term_sems, meta_sems = refs[7:9], *refs[9:11], refs[11:13], *refs[13:]
    place_ref, index_ref = metadata
    rows = sizes[0]
    metadata = copies_of(zip(metadata_in, metadata), meta_sems)
    later = copies_of(zip(terms_in, terms), term_sems)
    finish(metadata)
    fetch = half_blocks_of(sizes, width_k, place_ref, own_ref, False)

    def diags(row):
        return index_ref[0, 0, rows + row]

    gather_solve(sizes, fetch, diags, later, terms, inverse_ref, sum_ref, product_ref)
    out_ref[...] = sum_ref[...].reshape(out_ref.shape)


def final_kernel(sizes, width_k, *refs):
    rows, n_rows, cap, n_tiles, n_rhs = sizes
    metadata_in, mirror_ref, inverse_ref, base_ref, near_ref, far_ref, scale_ref = refs[:2], *refs[2:8]
    out_ref, metadata, sum_ref, product_ref, meta_sems = refs[8], refs[9:11], *refs[11:]
    place_ref, index_ref = metadata
    metadata = copies_of(zip(metadata_in, metadata), meta_sems)
    depth = scale_ref.shape[0]
    correction = (near_ref[...] + far_ref[...]) / scale_ref[...]
    padded = jnp.concatenate([correction, jnp.zeros((8 - depth, LANES), jnp.float32)], axis=0)
    turned = padded.T
    finish(metadata)
    fetch = half_blocks_of(sizes, width_k, place_ref, mirror_ref, True)

    def diags(row):
        return index_ref[0, 0, rows + row]

    gather_solve(sizes, fetch, diags, [], [], inverse_ref, sum_ref, product_ref)
    for row in range(rows):
        spot, place = row // depth, row % depth
        column = turned[spot * n_rhs : (spot + 1) * n_rhs, place : place + 1]
        out_ref[row] = (base_ref[row] + column) + sum_ref[pl.ds(row * n_rhs, n_rhs), :]


def shifted(value, axis, steps):
    count = lax.axis_size(axis)
    initial, last = (max(0, -steps), min(count, count - steps))
    return lax.ppermute(value, axis, [(source, source + steps) for source in range(initial, last)])


def to_bands(sends):
    if len(sends) == 1:
        return (lax.ppermute(sends[0], "band", [(0, 1), (1, 0)]),)
    return shifted(sends[0], "band", 1), shifted(sends[1], "band", -1)


def on_device(
    start_iterate,
    right_side,
    diag_table,
    inverse_table,
    coupling_tiles,
    diag_index,
    tile_index,
    source_owner,
    source_local,
    aggregate_map,
):
    rows, n_rhs, states = start_iterate.shape
    width_k = source_owner.shape[1]
    n_tiles, n_diag = coupling_tiles.shape[0], inverse_table.shape[0]
    n_rows, n_bands = lax.axis_size("rows"), lax.axis_size("band")
    n_dev = n_rows * n_bands
    cap = max(2, 2 * width_k * rows // n_rows)
    slots = n_rows * cap
    total_groups = AGG_DEV * n_dev
    per_tile = LANES // n_rhs
    depth = rows // per_tile
    n_func = 16
    dense = (
        n_bands == 2
        and n_dev * rows * total_groups <= DENSE_LIMIT
        and depth == 4
        and n_diag * n_func == LANES
        and n_tiles + 2 <= n_func
    )
    sizes = (rows, n_rows, cap, n_tiles, n_rhs)
    f32, i32 = jnp.float32, jnp.int32
    my_band = lax.axis_index("band")
    my_row = lax.axis_index("rows")

    half = n_rows // 2
    wide = -(-(4 + 2 * width_k) * rows // LANES) * LANES
    place_wide = -(-2 * width_k * rows // LANES) * LANES
    index_shapes = [(width_k, rows), (width_k, rows), (width_k + 2, rows), (1, rows), (1, rows)]
    halves_of_rows = [list(range(half)), list(range(half, n_rows))]
    to_mirror = [(i, (i + half) % n_rows) for i in range(n_rows)]
    mirror = lax.ppermute(start_iterate, "rows", to_mirror)
    lists, index, places = call(
        functools.partial(request_kernel, (rows, n_rows, cap, n_tiles, n_diag)),
        (
            jax.ShapeDtypeStruct((n_rows, 1, LANES + wide), i32),
            jax.ShapeDtypeStruct((1, 1, wide), i32),
            jax.ShapeDtypeStruct((1, 1, place_wide), i32),
        ),
        [HBM] * 5,
        [VMEM] * 3,
        [*[pltpu.VMEM(shape, i32) for shape in index_shapes], pltpu.SemaphoreType.DMA((5,))],
    )(source_owner.T, source_local.T, tile_index.T, diag_index[None], aggregate_map.T)
    lists = lax.all_to_all(lists, "rows", split_axis=0, concat_axis=0, tiled=True)
    if n_bands == 2:
        near = lax.ppermute(index, "band", [(0, 1), (1, 0)])
    else:
        ways = [[(b, (b + step) % n_bands) for b in range(n_bands)] for step in (-1, 1)]
        near = jnp.concatenate([lax.ppermute(index, "band", way) for way in ways], axis=0)

    n_ways = 1 if n_bands == 2 else 2
    block = (rows, n_rhs, states)
    band_shapes = [jax.ShapeDtypeStruct(block, f32)] * n_ways
    band_scratch = [pltpu.VMEM(block, f32)] * n_ways
    term_scratch = [pltpu.VMEM(block, f32)] * (1 + n_ways)
    term_sems = pltpu.SemaphoreType.DMA((1 + n_ways,))
    list_scratch = pltpu.SMEM((half, 1, LANES), i32)
    near_scratch = pltpu.SMEM((n_ways, 1, wide), i32)
    row_scratch = [pltpu.SMEM((1, 1, place_wide), i32), pltpu.SMEM((1, 1, wide), i32)]
    flat = rows * n_rhs
    sums = pltpu.VMEM((flat, states), f32)
    products = pltpu.VMEM((max(n_tiles, n_diag) * rows, n_rhs, states), f32)
    work = 6 * flat * states * states
    made_shape = (n_tiles * rows, n_rhs, states)
    table_scratch = [pltpu.VMEM(coupling_tiles.shape, f32)]
    table_sems = pltpu.SemaphoreType.DMA((-(-n_tiles // 2),))
    made = call(
        product_kernel,
        jax.ShapeDtypeStruct(made_shape, f32),
        [HBM, HBM],
        HBM,
        [
            pltpu.VMEM(block, f32),
            *table_scratch,
            pltpu.VMEM(made_shape, f32),
            pltpu.SemaphoreType.DMA((1 + n_tiles,)),
            table_sems,
        ],
        work * n_tiles,
        4 << 20,
    )(start_iterate, coupling_tiles)
    packed, *bands = call(
        functools.partial(first_kernel, sizes, width_k, n_ways),
        (jax.ShapeDtypeStruct((half, 2 * cap, n_rhs, states), f32), *band_shapes),
        [HBM, VMEM, VMEM, ANY, ANY],
        [HBM] * (1 + n_ways),
        [
            pltpu.VMEM((2, *made_shape), f32),
            list_scratch,
            near_scratch,
            pltpu.VMEM((half, 2 * cap, n_rhs, states), f32),
            *band_scratch,
            pltpu.SemaphoreType.DMA((n_tiles,)),
            pltpu.SemaphoreType.DMA((2,)),
            pltpu.SemaphoreType.DMA((half + n_ways,)),
        ],
        work * n_tiles,
        4 << 20,
    )(made, mirror, coupling_tiles, lists, near)
    packed, late = lax.optimization_barrier((packed, lists))
    if dense:
        across = lax.ppermute(late, "band", [(0, 1), (1, 0)])
        across, *bands = lax.optimization_barrier((across, *bands))
    sends = (packed.reshape(half, 2 * cap * n_rhs, states), *bands)
    halves_of_rows = [list(range(half)), list(range(half, n_rows))]
    def exchange(sends, groups=None):
        arrived = lax.all_to_all(
            sends[0], "rows", split_axis=0, concat_axis=0, tiled=True, axis_index_groups=groups
        )
        return arrived, to_bands(sends[1:])

    arrived_blocks, arrived_bands = exchange(sends, halves_of_rows)

    if dense:
        fields = jnp.stack([late, across])[:, :, 0, LANES:]
        fields = fields.reshape(2, n_rows, -1, rows).transpose(2, 0, 1, 3)
        fields = fields.reshape(-1, 2, n_rows * rows)
        n_blocks = slots + rows
        length = n_dev * depth
        extra_shapes = [
            ((n_diag * n_func, 3 * states), jnp.bfloat16),
            ((total_groups, (n_tiles + 1) * n_blocks), jnp.bfloat16),
            ((per_tile * length, total_groups), jnp.bfloat16),
            ((total_groups, LANES), f32),
        ]
        functional_shape, count_shape, placing_shape, partial_shape = extra_shapes
        counts, functionals, placing, partial, scale = call(
            functools.partial(count_kernel, sizes, width_k, n_func),
            (
                jax.ShapeDtypeStruct(*count_shape),
                jax.ShapeDtypeStruct(*functional_shape),
                jax.ShapeDtypeStruct(*placing_shape),
                jax.ShapeDtypeStruct(*partial_shape),
                jax.ShapeDtypeStruct((depth, LANES), f32),
            ),
            [ANY, HBM] + [VMEM] * 5,
            [HBM] * 4 + [VMEM],
            [
                pltpu.VMEM(*count_shape),
                pltpu.VMEM(*functional_shape),
                pltpu.VMEM(*placing_shape),
                pltpu.VMEM(*partial_shape),
                row_scratch[1],
                pltpu.VMEM(block, f32),
                pltpu.VMEM((n_diag * n_func, flat), f32),
                pltpu.VMEM((rows * n_func, LANES), f32),
                pltpu.SemaphoreType.DMA((2,)),
                pltpu.SemaphoreType.DMA((4,)),
            ],
            4 * total_groups * n_tiles * n_dev * rows * n_blocks,
            4 << 20,
        )(
            index, right_side, fields, late[:, 0, :LANES], coupling_tiles, diag_table, inverse_table
        )
        extra_scratch = [
            *[pltpu.VMEM(*shape) for shape in extra_shapes],
            pltpu.VMEM((n_diag * n_func, n_blocks * n_rhs), f32),
            pltpu.VMEM((n_blocks * n_func, LANES), f32),
            pltpu.VMEM((n_rows, n_bands * depth, LANES), f32),
        ]

        made = (arrived_blocks, functionals, counts, placing, partial, scale)
        made = lax.optimization_barrier(made)
        arrived_blocks, functionals, counts, placing, partial, scale = made

    def solve(field, arrived, bands):
        return call(
            functools.partial(solve_kernel, sizes, width_k, n_ways, field),
            jax.ShapeDtypeStruct(block, f32),
            [ANY] * 2 + [VMEM] * 2 + [HBM] + [ANY] * n_ways,
            VMEM,
            [
                *row_scratch,
                sums,
                products,
                *term_scratch,
                term_sems,
                pltpu.SemaphoreType.DMA((2,)),
            ],
            work * n_diag,
            4 << 20,
        )(places, index, arrived, inverse_table, right_side, *bands)

    first = solve(0, arrived_blocks, arrived_bands)
    body = cap * n_rhs
    full_list = pltpu.SMEM((n_rows, 1, LANES), i32)
    if dense:
        mirror = lax.ppermute(first, "rows", to_mirror)
        own, band = call(
            functools.partial(own_kernel, sizes, width_k),
            (
                jax.ShapeDtypeStruct((half, body + 2 * n_bands * depth, states), f32),
                jax.ShapeDtypeStruct(block, f32),
            ),
            [ANY] * 2 + [VMEM] * 2 + [HBM] * 4,
            [HBM] * 2,
            [
                full_list,
                near_scratch,
                products,
                pltpu.VMEM((n_rows, body, states), f32),
                pltpu.VMEM(block, f32),
                *extra_scratch,
                pltpu.SemaphoreType.DMA((2,)),
                pltpu.SemaphoreType.DMA((4,)),
                pltpu.SemaphoreType.DMA((half + 3,)),
            ],
            2 * work * n_tiles,
            4 << 20,
        )(lists, near, first, coupling_tiles, functionals, counts, placing, partial)
        own, (band,) = exchange((own, band), halves_of_rows)
        packed = call(
            functools.partial(mirror_kernel, sizes),
            jax.ShapeDtypeStruct((half, body, states), f32),
            [ANY] + [VMEM] * 2,
            HBM,
            [
                list_scratch,
                products,
                pltpu.VMEM((half, body, states), f32),
                pltpu.SemaphoreType.DMA((half + 1,)),
            ],
            BEHIND_SWAP * work * n_tiles,
            4 << 20,
        )(lists, mirror, coupling_tiles)
        packed, band = lax.optimization_barrier((packed, band))
        swapped = lax.all_to_all(
            packed, "rows", split_axis=0, concat_axis=0, tiled=True, axis_index_groups=halves_of_rows
        )
        part = jax.ShapeDtypeStruct((2 * depth, LANES), f32)
        keep, give = call(part_kernel, (part, part), [VMEM], [VMEM] * 2)(own)
        keep = keep + lax.ppermute(give, "band", [(0, 1), (1, 0)])
        far = lax.ppermute(keep[depth:], "rows", to_mirror)
        base = call(
            functools.partial(base_kernel, sizes, width_k),
            jax.ShapeDtypeStruct(block, f32),
            [ANY] * 2 + [VMEM] * 2 + [HBM, ANY],
            VMEM,
            [
                *row_scratch,
                sums,
                products,
                *term_scratch,
                term_sems,
                pltpu.SemaphoreType.DMA((2,)),
            ],
            work * n_diag,
            4 << 20,
        )(places, index, own, inverse_table, right_side, band)
        return call(
            functools.partial(final_kernel, sizes, width_k),
            jax.ShapeDtypeStruct(block, f32),
            [ANY] * 2 + [VMEM] * 6,
            VMEM,
            [*row_scratch, sums, products, pltpu.SemaphoreType.DMA((2,))],
            work * n_diag,
            4 << 20,
        )(places, index, swapped, inverse_table, base, keep[:depth], far, scale)

    sends = call(
        functools.partial(pack_kernel, sizes, width_k, n_ways),
        (jax.ShapeDtypeStruct((n_rows, body, states), f32), *band_shapes),
        [ANY] * 2 + [VMEM] * 2,
        [HBM] * (1 + n_ways),
        [
            full_list,
            near_scratch,
            products,
            pltpu.VMEM((n_rows, body, states), f32),
            *band_scratch,
            pltpu.SemaphoreType.DMA((2,)),
            pltpu.SemaphoreType.DMA((1 + n_ways,)),
        ],
        work * n_tiles,
        4 << 20,
    )(lists, near, first, coupling_tiles)
    arrived_blocks, arrived_bands = exchange(sends)
    second = solve(width_k, arrived_blocks, arrived_bands)

    groups = aggregate_map[:, 0]
    own = jnp.arange(rows, dtype=i32)
    index_all = lax.all_gather(index, ("band", "rows"), axis=0, tiled=True)
    index_all = index_all.reshape(n_bands, n_rows, wide)
    groups_all, diags_all = index_all[:, :, :rows], index_all[:, :, rows : 2 * rows]
    codes = lists[:, 0, :cap]
    asked = jnp.arange(n_rows, dtype=i32)[:, None] * rows + codes // (rows * n_tiles) % rows
    asked = jnp.where(codes > 0, asked, -1).reshape(-1)
    table_sums = jnp.sum(diag_table, axis=(1, 2))
    diag_onehot = diags_all.reshape(-1, 1) == jnp.arange(n_diag, dtype=i32)[None]
    block_sums = jnp.sum(jnp.where(diag_onehot, table_sums[None], 0.0), axis=1)
    whole_diag = jnp.sum(
        jnp.where(groups[:, None] == groups_all.reshape(-1)[None], block_sums[None], 0.0), axis=1
    )
    above, below = near[0, 0], near[-1, 0]
    place_of = (2 + width_k) * rows
    band_tiles = jnp.stack([above[place_of : place_of + rows], below[place_of + rows : place_of + 2 * rows]])
    band_groups = jnp.stack([above[:rows], below[:rows]])
    band_valid = jnp.stack([my_band + 1 < n_bands, my_band > 0])
    band_valid = jnp.broadcast_to(band_valid[:, None], (2, rows))
    n_all = n_tiles + n_diag + 1
    code = codes.reshape(-1)
    band_of_mine = lax.dynamic_index_in_dim(groups_all, my_band, 0, keepdims=False).reshape(-1)
    entry_group = jnp.concatenate(
        [jnp.take(band_of_mine, jnp.maximum(asked, 0)), band_groups.reshape(-1), groups, groups]
    )
    entry_func = jnp.concatenate(
        [
            (code % rows) * n_all + (code // rows) % n_tiles,
            (own[None] * n_all + band_tiles).reshape(-1),
            own * n_all + n_tiles + diag_index,
            own * n_all + n_tiles + n_diag,
        ]
    )
    entry_valid = jnp.concatenate([asked >= 0, band_valid.reshape(-1), jnp.ones((2 * rows,), bool)])
    functionals = jnp.concatenate(
        [jnp.sum(coupling_tiles, axis=1), -jnp.sum(diag_table, axis=1)], axis=0
    )
    weights = jnp.einsum("fp,rcp->rfc", functionals, second, precision=HIGH)
    weights = jnp.concatenate([weights, jnp.sum(right_side, axis=2)[:, None]], axis=1)
    chosen = jnp.take(weights.reshape(rows * n_all, n_rhs), entry_func, axis=0)
    chosen = jnp.where(entry_valid[:, None], chosen, 0.0)
    partial = jax.ops.segment_sum(chosen, entry_group, num_segments=total_groups)
    whole = lax.psum(partial, ("band", "rows"))
    correction = jnp.take(whole, groups, axis=0) / whole_diag[:, None]
    return second + correction[:, :, None]


def solution(mesh):
    in_specs = (
        P(("band", "rows"), None, None),
        P(("band", "rows"), None, None),
        P(),
        P(),
        P(),
        P(("band", "rows")),
        P(("band", "rows"), None),
        P(("band", "rows"), None),
        P(("band", "rows"), None),
        P(("band", "rows"), None),
    )
    out_specs = P(("band", "rows"), None, None)
    return jax.shard_map(
        on_device, mesh=mesh, in_specs=in_specs, out_specs=out_specs, check_vma=False
    )
```

```python
import functools

import jax
import jax.numpy as jnp
from jax import lax
from jax.experimental import pallas as pl
from jax.experimental.pallas import tpu as pltpu
from jax.sharding import PartitionSpec as P

AGG_DEV = 8
LANES = 128
DENSE_LIMIT = 1 << 19
BEHIND_SWAP = 100

VMEM = pl.BlockSpec(memory_space=pltpu.VMEM)
SMEM = pl.BlockSpec(memory_space=pltpu.SMEM)
HBM = pl.BlockSpec(memory_space=pltpu.HBM)
ANY = pl.BlockSpec(memory_space=pl.ANY)
HIGH = lax.Precision.HIGHEST


def params():
    return pltpu.CompilerParams(vmem_limit_bytes=24 * 1024 * 1024)


def call(kernel, out_shape, in_specs, out_specs, scratch=(), flops=0, moved=0):
    def shaped(shape, spec):
        return pltpu.HBM(shape.shape, shape.dtype) if spec is HBM else shape

    if isinstance(out_shape, (tuple, list)):
        out_shape = [shaped(*pair) for pair in zip(out_shape, out_specs)]
    else:
        out_shape = shaped(out_shape, out_specs)
    run = pl.pallas_call(
        kernel,
        out_shape=out_shape,
        in_specs=in_specs,
        out_specs=out_specs,
        scratch_shapes=list(scratch),
        compiler_params=params(),
        cost_estimate=pl.CostEstimate(flops=flops, bytes_accessed=moved, transcendentals=0),
    )

    def apply(*args):
        pinned = [
            pltpu.with_memory_space_constraint(arg, pltpu.HBM) if spec is HBM else arg
            for arg, spec in zip(args, in_specs)
        ]
        return run(*pinned)

    return apply


def below(value, bound):
    return value & (bound - 1) if bound & (bound - 1) == 0 else lax.rem(value, bound)


def over(value, bound):
    if bound & (bound - 1) == 0:
        return lax.shift_right_logical(value, bound.bit_length() - 1)
    return lax.div(value, bound)


def halves(value):
    high = value.astype(jnp.bfloat16)
    low = (value - high.astype(jnp.float32)).astype(jnp.bfloat16)
    return high, low


def left_operand(value):
    high, low = halves(value)
    return jnp.concatenate([high, low, high], axis=1)


def right_operand(value):
    high, low = halves(value)
    return jnp.concatenate([high, high, low], axis=1)


def dot_nt(left, right):
    return lax.dot_general(
        left, right, (((1,), (1,)), ((), ())), preferred_element_type=jnp.float32
    )


def table_products(value, table_ref, out_ref, done=None, loads=None):
    left = left_operand(value)
    count, width = table_ref.shape[0], table_ref.shape[1]
    n_rhs = out_ref.shape[1]
    rows = left.shape[0] // n_rhs
    for first in range(0, count, 2):
        last = min(first + 2, count)
        if loads is not None:
            loads[first // 2].wait()
        right = right_operand(table_ref[first:last].reshape((last - first) * width, -1))
        product = dot_nt(left, right)
        for t in range(first, last):
            part = product[:, (t - first) * width : (t - first + 1) * width]
            out_ref[t * rows : (t + 1) * rows] = part.reshape(rows, n_rhs, width)
        if done is not None:
            done(first * rows, (last - first) * rows)


def started(copies):
    for copy in copies:
        copy.start()
    return copies


def finish(copies):
    for copy in copies:
        copy.wait()


def request_kernel(sizes, *refs):
    rows, n_rows, cap, n_tiles, n_diag = sizes
    inputs, (list_ref, index_ref, place_ref), held, sems = refs[:5], refs[5:8], refs[8:13], refs[13]
    finish(
        started([pltpu.make_async_copy(i, h, sems.at[n]) for n, (i, h) in enumerate(zip(inputs, held))])
    )
    owner_ref, local_ref, tile_ref, diag_ref, group_ref = held
    width_k = owner_ref.shape[0]
    half = n_rows // 2
    row_of = lax.broadcasted_iota(jnp.int32, (rows, rows), 0)
    col_of = lax.broadcasted_iota(jnp.int32, (rows, rows), 1)
    lane = lax.broadcasted_iota(jnp.int32, (rows, LANES), 1)
    owners = lax.broadcasted_iota(jnp.int32, (n_rows, rows), 0)

    def column(row):
        return jnp.sum(jnp.where(row_of == col_of, row, 0), axis=1, keepdims=True)

    def owner_row(k):
        return owner_ref[k : k + 1, :]

    row_ids = lax.broadcasted_iota(jnp.int32, (1, rows), 1)
    owner_columns = [column(owner_row(k)) for k in range(width_k)]
    lists = jnp.zeros((n_rows, LANES), jnp.float32)
    places, half_places = [], []
    for k in range(width_k):
        rank = jnp.zeros((1, rows), jnp.int32)
        for other in range(k + 1):
            match = owner_columns[other] == owner_row(k)
            if other == k:
                match = match & (row_of < col_of)
            rank = rank + jnp.sum(jnp.where(match, 1, 0), axis=0, keepdims=True)
        places.append(owner_row(k) * cap + rank)
        same = (owner_row(k) >= half) == (lax.axis_index("rows") >= half)
        holder = jnp.where(owner_row(k) >= half, owner_row(k) - half, owner_row(k))
        half_places.append(holder * (2 * cap) + rank + jnp.where(same, 0, cap))
        taker = row_ids + rows * (diag_ref[...] + n_diag)
        code = local_ref[k : k + 1, :] + rows * (tile_ref[k : k + 1, :] + n_tiles * taker)
        code, rank = column(code), column(rank)
        mirror = jnp.where(owner_row(k) >= half, owner_row(k) - half, owner_row(k) + half)
        for owner, base in ((owner_row(k), 0), (mirror, LANES // 2)):
            by_rank = jnp.where(lane == rank + base, code, 0).astype(jnp.float32)
            mine = jnp.where(owners == owner, 1.0, 0.0)
            lists = lists + jnp.dot(
                mine, by_rank, precision=HIGH, preferred_element_type=jnp.float32
            )
    lists = (lists + 0.5).astype(jnp.int32)

    def joined(parts, wide):
        spare = wide - len(parts) * rows
        if spare:
            parts = [*parts, jnp.zeros((1, spare), jnp.int32)]
        return jnp.concatenate(parts, axis=1)

    index = [group_ref[...], diag_ref[...]]
    index += [tile_ref[k : k + 1, :] for k in range(width_k + 2)]
    index += [owner_row(k) * rows + local_ref[k : k + 1, :] for k in range(width_k)]
    index = joined(index, index_ref.shape[2])
    index_ref[0] = index
    place_ref[0] = joined(half_places + places, place_ref.shape[2])
    for device in range(n_rows):
        list_ref[device] = jnp.concatenate([lists[device : device + 1, :], index], axis=1)


def copies_of(pairs, sems):
    return started([pltpu.make_async_copy(i, h, sems.at[n]) for n, (i, h) in enumerate(pairs)])


def band_field(rows, width_k, way, n_ways):
    field = (2 + width_k) * rows
    if n_ways == 1:
        return field + jnp.where(lax.axis_index("band") == 0, 0, rows)
    return field + way * rows


def pack_bands(sizes, width_k, product_ref, near_ref, band_refs):
    rows = sizes[0]
    for way, band_ref in enumerate(band_refs):
        field = band_field(rows, width_k, way, len(band_refs))
        for row in range(rows):
            band_ref[row] = product_ref[near_ref[way, 0, field + row] * rows + row]


def table_loads(table_in, table_ref, sems):
    copies = []
    for first in range(0, table_in.shape[0], 2):
        place = pl.ds(first, min(2, table_in.shape[0] - first))
        source, target = table_in.at[place], table_ref.at[place]
        copies.append(pltpu.make_async_copy(source, target, sems.at[first // 2]))
    return started(copies)


def product_kernel(start_in, tile_in, product_out, start_ref, tile_ref, product_ref, sems, tile_sems):
    start = pltpu.make_async_copy(start_in, start_ref, sems.at[0])
    start.start()
    loads = table_loads(tile_in, tile_ref, tile_sems)
    start.wait()
    copies = []

    def done(first, count):
        place = pl.ds(first, count)
        source, target = product_ref.at[place], product_out.at[place]
        copies.extend(started([pltpu.make_async_copy(source, target, sems.at[1 + len(copies)])]))

    rows, n_rhs, states = start_ref.shape
    values = start_ref[...].reshape(rows * n_rhs, states)
    table_products(values, tile_ref, product_ref, done, loads)
    finish(copies)


def first_kernel(sizes, width_k, n_band, *refs):
    rows, n_rows, cap, n_tiles, n_rhs = sizes
    product_in, mirror_ref, tile_ref, list_in, near_in, send_out = refs[:6]
    band_out, refs = refs[6 : 6 + n_band], refs[6 + n_band :]
    product_ref, list_ref, near_ref, send_ref = refs[:4]
    band_refs, (load_sems, meta_sems, send_sems) = refs[4 : 4 + n_band], refs[4 + n_band :]
    half = n_rows // 2
    base = jnp.where(lax.axis_index("rows") >= half, half, 0)
    list_in = list_in.at[pl.ds(base, half), :, pl.ds(0, LANES)]
    metadata = copies_of(((list_in, list_ref), (near_in, near_ref)), meta_sems)
    places = [pl.ds(tile * rows, rows) for tile in range(n_tiles)]
    loads = [(product_in.at[place], product_ref.at[0, place]) for place in places]
    loads = copies_of(loads, load_sems)
    values = mirror_ref[...].reshape(rows * n_rhs, -1)
    table_products(values, tile_ref, product_ref.at[1])
    finish(metadata)
    finish(loads)
    copies = []
    pack_bands(sizes, width_k, product_ref.at[0], near_ref, band_refs)
    for n, (ref, out) in enumerate(zip(band_refs, band_out)):
        copies += started([pltpu.make_async_copy(ref, out, send_sems.at[half + n])])
    for device in range(half):
        for slot in range(2 * cap):
            side, rank = slot // cap, slot % cap
            code = list_ref[device, 0, side * (LANES // 2) + rank]
            send_ref[device, slot] = product_ref[side, below(code, rows * n_tiles)]
        copy = pltpu.make_async_copy(send_ref.at[device], send_out.at[device], send_sems.at[device])
        copies += started([copy])
    finish(copies)


def place(place_ref, values, n_rhs, n_parts):
    per_tile = LANES // n_rhs
    length = place_ref.shape[0] // per_tile
    parts, rest = [], values
    for _ in range(n_parts):
        part = rest.astype(jnp.bfloat16)
        rest = rest - part.astype(jnp.float32)
        parts.append(part)
    parts = jnp.concatenate(parts, axis=1)
    lane = lax.broadcasted_iota(jnp.int32, (length, LANES), 1)
    result = jnp.zeros((length, LANES), jnp.float32)
    placed = jnp.dot(place_ref[...], parts, preferred_element_type=jnp.float32)
    for spot in range(per_tile):
        chosen = placed[spot * length : (spot + 1) * length]
        chosen = sum(chosen[:, n * LANES : (n + 1) * LANES] for n in range(n_parts))
        result = jnp.where((lane >= spot * n_rhs) & (lane < (spot + 1) * n_rhs), chosen, result)
    return result


def spread_values(n_rhs, n_func, functional_ref, blocks, kinds, value_ref, spread_ref, done):
    per_tile = LANES // n_rhs
    lane = lax.broadcasted_iota(jnp.int32, (n_func, LANES), 1)
    columns = slice(done * n_rhs, done * n_rhs + blocks.shape[0])
    value_ref[:, columns] = dot_nt(functional_ref[...], right_operand(blocks))
    for block, kind in enumerate(kinds, done):
        tile, spot = block // per_tile, block % per_tile
        start = pl.multiple_of(kind * n_func, n_func)
        piece = value_ref[pl.ds(start, n_func), tile * LANES : (tile + 1) * LANES]
        piece = jnp.where((lane >= spot * n_rhs) & (lane < (spot + 1) * n_rhs), piece, 0.0)
        spread_ref[block * n_func : (block + 1) * n_func, :] = piece


def one_hot(ids, row):
    return jnp.where(ids == row, 1.0, 0.0).astype(jnp.bfloat16)


def count_kernel(sizes, width_k, n_func, *refs):
    rows, n_rows, cap, n_tiles, n_rhs = sizes
    index_in, right_in, field_ref, list_ref, tile_ref, table_ref, inverse_ref = refs[:7]
    count_out, functional_out, placing_out, partial_out, scale_ref = refs[7:12]
    count_ref, functional_ref, placing_ref, partial_ref = refs[12:16]
    index_ref, right_ref, value_ref, spread_ref, load_sems, sems = refs[16:]
    loads = copies_of(((index_in, index_ref), (right_in, right_ref)), load_sems)
    n_groups = count_ref.shape[0]
    slots, band_rows = n_rows * cap, n_rows * rows
    copies = []

    def send(source, target):
        copies.extend(started([pltpu.make_async_copy(source, target, sems.at[len(copies)])]))

    sums = jnp.sum(tile_ref[...], axis=1)
    line = lax.broadcasted_iota(jnp.int32, (n_func, sums.shape[1]), 0)
    sums = jnp.concatenate([sums, jnp.zeros((n_func - n_tiles, sums.shape[1]), jnp.float32)], axis=0)
    n_diag = inverse_ref.shape[0]
    totals = []
    for d in range(n_diag):
        minus = -jnp.sum(table_ref[d], axis=0, keepdims=True)
        totals.append(-jnp.sum(minus, axis=1, keepdims=True))
        wanted = jnp.where(line == n_tiles, minus, sums)
        high, low = halves(inverse_ref[d])
        right = jnp.concatenate([high, high, low], axis=0)
        solved = jnp.dot(left_operand(wanted), right, preferred_element_type=jnp.float32)
        solved = jnp.where(line == n_tiles + 1, 1.0, solved)
        functional_ref[d * n_func : (d + 1) * n_func, :] = left_operand(solved)
    send(functional_ref, functional_out)

    lists = list_ref[...]
    asker = lax.broadcasted_iota(jnp.int32, lists.shape, 0)
    codes = asker * rows + below(over(lists, rows * n_tiles), rows)
    codes = jnp.where(lists > 0, codes, -1).astype(jnp.float32)
    spread = lax.broadcasted_iota(jnp.int32, (slots, n_rows), 0)
    spread = lax.div(spread, cap) == lax.broadcasted_iota(jnp.int32, (slots, n_rows), 1)
    codes = jnp.dot(
        jnp.where(spread, 1.0, 0.0), codes, precision=HIGH, preferred_element_type=jnp.float32
    )
    rank = lax.rem(lax.broadcasted_iota(jnp.int32, codes.shape, 0), cap)
    lane = lax.broadcasted_iota(jnp.int32, codes.shape, 1)
    asked = jnp.sum(jnp.where(rank == lane, codes, 0.0), axis=1, keepdims=True)
    asked = jnp.where(asked < 0.0, asked - 0.5, asked + 0.5).astype(jnp.int32)
    low, high = asked[: slots // 2], asked[slots // 2 :]
    upper = lax.axis_index("rows") >= n_rows // 2
    asked = jnp.concatenate([jnp.where(upper, high, low), jnp.where(upper, low, high)], axis=0)
    own = lax.axis_index("rows") * rows + lax.broadcasted_iota(jnp.int32, (rows, 1), 0)
    band = lax.axis_index("band")

    def field(n, side):
        return field_ref[n, side : side + 1, :]

    row_ids = lax.broadcasted_iota(jnp.int32, (1, band_rows), 1)
    sides = []
    for side, targets in ((0, jnp.concatenate([asked, own], axis=0)), (1, own)):
        first = band == side
        across = jnp.where(first, field(2 + width_k, 1 - side), field(3 + width_k, 1 - side))
        takers = [field(2 + k, side) * n_groups + field(0, side) for k in range(width_k)]
        takers.append(across * n_groups + field(0, 1 - side))
        takers = jnp.concatenate(takers, axis=1)
        origins = [field(4 + width_k + k, side) for k in range(width_k)] + [row_ids]
        hits = one_hot(targets, jnp.concatenate(origins, axis=1))
        sides.append((takers, hits, field(0, side)))
    pieces, own_pieces = [], []
    ids = lax.broadcasted_iota(jnp.int32, (n_groups, band_rows), 0)
    for t in range(n_tiles + 1):
        found = []
        for takers, hits, groups in sides:
            if t < n_tiles:
                wide = lax.broadcasted_iota(jnp.int32, (n_groups, takers.shape[1]), 0)
                found.append(dot_nt(one_hot(wide + t * n_groups, takers), hits))
            else:
                found.append(dot_nt(one_hot(ids, groups), hits[:, -band_rows:]))
        pieces += [found[0][:, :slots], found[1]]
        own_pieces.append(found[0][:, slots:])
    count_ref[...] = jnp.concatenate(pieces, axis=1).astype(jnp.bfloat16)
    send(count_ref, count_out)

    own_counts = jnp.concatenate([*own_pieces, own_pieces[-1]], axis=1).astype(jnp.bfloat16)
    finish(loads)
    rights = right_ref[...].reshape(rows * n_rhs, -1)
    kinds = [index_ref[0, 0, rows + row] for row in range(rows)]
    spread_values(n_rhs, n_func, functional_ref, rights, kinds, value_ref, spread_ref, 0)
    values = [spread_ref[pl.ds(t, rows, stride=n_func), :] for t in range(n_tiles + 2)]
    values = jnp.concatenate(halves(jnp.concatenate(values, axis=0)), axis=1)
    partial = jnp.dot(own_counts, values, preferred_element_type=jnp.float32)
    partial_ref[...] = partial[:, :LANES] + partial[:, LANES:]
    send(partial_ref, partial_out)

    per_tile = LANES // n_rhs
    depth = rows // per_tile
    length = n_rows * 2 * depth
    order = lax.broadcasted_iota(jnp.int32, (per_tile * length, 1), 0)
    spot, order = lax.div(order, length), lax.rem(order, length)
    device, order = lax.div(order, 2 * depth), lax.rem(order, 2 * depth)
    side, order = lax.div(order, depth), lax.rem(order, depth)
    order = side * band_rows + device * rows + spot * depth + order
    member = [
        one_hot(ids, jnp.where(band == which, field(0, 0), field(0, 1))) for which in range(2)
    ]
    placing = jnp.zeros(placing_ref.shape, jnp.float32)
    for which in range(2):
        placing = placing + dot_nt(one_hot(order, row_ids + which * band_rows), member[which])
    placing_ref[...] = placing.astype(jnp.bfloat16)
    send(placing_ref, placing_out)
    whole = jnp.zeros((n_groups, 1), jnp.float32)
    for side in range(2):
        sums = jnp.zeros((1, band_rows), jnp.float32)
        for d in range(n_diag):
            sums = jnp.where(field(1, side) == d, totals[d], sums)
        weighted = jnp.where(ids == field(0, side), sums, 0.0)
        whole = whole + jnp.sum(weighted, axis=1, keepdims=True)
    scale = place(placing_ref, jnp.broadcast_to(whole, (n_groups, LANES)), n_rhs, 3)
    mine = jnp.zeros(scale_ref.shape, jnp.float32)
    here = lax.axis_index("rows") * 2 + band
    for n in range(2 * n_rows):
        mine = jnp.where(here == n, scale[n * depth : (n + 1) * depth, :], mine)
    scale_ref[...] = mine
    finish(copies)


def gather_solve(sizes, fetch, diags, later, terms, inverse_ref, sum_ref, product_ref):
    rows, n_rows, cap, n_tiles, n_rhs = sizes
    for row in range(rows):
        sum_ref[pl.ds(row * n_rhs, n_rhs), :] = fetch(row)
    finish(later)
    total = sum_ref[...]
    for term in terms:
        total = total + term[...].reshape(total.shape)
    table_products(total, inverse_ref, product_ref)
    for row in range(rows):
        sum_ref[pl.ds(row * n_rhs, n_rhs), :] = product_ref[diags(row) * rows + row]


def arrived_blocks_of(sizes, width_k, place_ref, field, arrived_ref):
    rows, n_rows, cap, n_tiles, n_rhs = sizes
    per = n_rows * cap // arrived_ref.shape[0]

    def fetch(row):
        total = None
        for k in range(width_k):
            slot = place_ref[0, 0, (field + k) * rows + row]
            start = pl.multiple_of(below(slot, per) * n_rhs, n_rhs)
            block = arrived_ref[over(slot, per), pl.ds(start, n_rhs), :]
            total = block if total is None else total + block
        return total

    return fetch


def solve_kernel(sizes, width_k, n_band, field, *refs):
    metadata_in, arrived_ref, inverse_ref = refs[:2], *refs[2:4]
    terms_in, refs = refs[4 : 5 + n_band], refs[5 + n_band :]
    out_ref, metadata, sum_ref, product_ref = refs[0], refs[1:3], *refs[3:5]
    place_ref, index_ref = metadata
    terms, (term_sems, meta_sems) = refs[5 : 6 + n_band], refs[6 + n_band :]
    rows = sizes[0]
    metadata = copies_of(zip(metadata_in, metadata), meta_sems)
    later = copies_of(zip(terms_in, terms), term_sems)
    finish(metadata)
    fetch = arrived_blocks_of(sizes, width_k, place_ref, field, arrived_ref)

    def diags(row):
        return index_ref[0, 0, rows + row]

    gather_solve(sizes, fetch, diags, later, terms, inverse_ref, sum_ref, product_ref)
    out_ref[...] = sum_ref[...].reshape(out_ref.shape)


def pack_kernel(sizes, width_k, n_band, *refs):
    rows, n_rows, cap, n_tiles, n_rhs = sizes
    list_in, near_in, first_ref, tile_ref, send_out = refs[:5]
    band_out, refs = refs[5 : 5 + n_band], refs[5 + n_band :]
    list_ref, near_ref, product_ref, send_ref = refs[:4]
    band_refs, (meta_sems, send_sems) = refs[4 : 4 + n_band], refs[4 + n_band :]
    list_in = list_in.at[:, :, pl.ds(0, LANES)]
    metadata = copies_of(((list_in, list_ref), (near_in, near_ref)), meta_sems)
    table_products(first_ref[...].reshape(rows * n_rhs, -1), tile_ref, product_ref)
    finish(metadata)
    pack_bands(sizes, width_k, product_ref, near_ref, band_refs)
    for owner in range(n_rows):
        for rank in range(cap):
            block = product_ref[below(list_ref[owner, 0, rank], rows * n_tiles)]
            send_ref[owner, rank * n_rhs : (rank + 1) * n_rhs, :] = block
    finish(copies_of(zip((send_ref, *band_refs), (send_out, *band_out)), send_sems))


def own_kernel(sizes, width_k, *refs):
    rows, n_rows, cap, n_tiles, n_rhs = sizes
    metadata_in, first_ref, tile_ref, extra = list(refs[:2]), *refs[2:4], refs[4:8]
    send_out, band_out, metadata, product_ref, send_ref, band_ref = refs[8], refs[9], refs[10:12], *refs[12:15]
    held, value_ref, spread_ref, result_ref, meta_sems, load_sems, send_sems = refs[15:19], *refs[19:]
    list_ref, near_ref = metadata
    metadata_in[0] = metadata_in[0].at[:, :, pl.ds(0, LANES)]
    metadata = copies_of(zip(metadata_in, metadata), meta_sems)
    fetched = copies_of(zip(extra, held), load_sems)
    table_products(first_ref[...].reshape(rows * n_rhs, -1), tile_ref, product_ref)
    finish(metadata)
    copies = []

    def send(source, target):
        copies.extend(started([pltpu.make_async_copy(source, target, send_sems.at[len(copies)])]))

    pack_bands(sizes, width_k, product_ref, near_ref, (band_ref,))
    send(band_ref, band_out)
    body, half = cap * n_rhs, n_rows // 2
    upper = lax.axis_index("rows") >= half
    mine, others = jnp.where(upper, half, 0), jnp.where(upper, 0, half)
    finish(fetched[:1])
    functional_ref, count_ref, place_ref, partial_ref = held
    n_blocks = n_rows * cap + rows
    n_func = spread_ref.shape[0] // n_blocks
    n_diag = functional_ref.shape[0] // n_func

    def spread(done, blocks, kinds):
        spread_values(n_rhs, n_func, functional_ref, blocks, kinds, value_ref, spread_ref, done)

    kinds = [near_ref[0, 0, rows + row] for row in range(rows)]
    spread(n_rows * cap, band_ref[...].reshape(rows * n_rhs, -1), kinds)
    kinds = []
    for order in range(n_rows):
        owner = order % half + (mine if order < half else others)
        for rank in range(cap):
            code = list_ref[owner, 0, rank]
            kinds.append(below(over(code, rows * n_tiles * rows), n_diag))
            block = product_ref[below(code, rows * n_tiles)]
            send_ref[order, rank * n_rhs : (rank + 1) * n_rhs, :] = block
        if order < half:
            send(send_ref.at[order], send_out.at[order, pl.ds(0, body)])
        if order % 2:
            blocks = jnp.concatenate([send_ref[order - 1], send_ref[order]], axis=0)
            spread((order - 1) * cap, blocks, kinds)
            kinds = []
    finish(fetched[1:])
    result = coarse_parts(n_rhs, n_blocks, count_ref, place_ref, partial_ref, spread_ref)
    result_ref[...] = result.reshape(result_ref.shape)
    depth = result_ref.shape[1]
    for n, first in enumerate((mine, others)):
        target = send_out.at[:, pl.ds(body + n * depth, depth)]
        send(result_ref.at[pl.ds(first, half)], target)
    finish(copies)


def mirror_kernel(sizes, list_in, mirror_ref, tile_ref, send_out, list_ref, product_ref, send_ref, sems):
    rows, n_rows, cap, n_tiles, n_rhs = sizes
    half = n_rows // 2
    base = jnp.where(lax.axis_index("rows") >= half, half, 0)
    list_in = list_in.at[pl.ds(base, half), :, pl.ds(0, LANES)]
    metadata = started([pltpu.make_async_copy(list_in, list_ref, sems.at[half])])
    table_products(mirror_ref[...].reshape(rows * n_rhs, -1), tile_ref, product_ref)
    finish(metadata)
    copies = []
    for device in range(half):
        for rank in range(cap):
            code = list_ref[device, 0, LANES // 2 + rank]
            block = product_ref[below(code, rows * n_tiles)]
            send_ref[device, rank * n_rhs : (rank + 1) * n_rhs, :] = block
        copy = pltpu.make_async_copy(send_ref.at[device], send_out.at[device], sems.at[device])
        copies += started([copy])
    finish(copies)


def coarse_parts(n_rhs, n_blocks, count_ref, place_ref, partial_ref, spread_ref):
    n_func = spread_ref.shape[0] // n_blocks
    values = [
        spread_ref[pl.ds(t, n_blocks, stride=n_func), :] for t in range(count_ref.shape[1] // n_blocks)
    ]
    values = jnp.concatenate(values, axis=0)
    partial = jnp.dot(
        count_ref[...], jnp.concatenate(halves(values), axis=1), preferred_element_type=jnp.float32
    )
    partial = partial[:, :LANES] + partial[:, LANES:] + partial_ref[...]
    shift = LANES // 2
    while shift >= n_rhs:
        partial = partial + pltpu.roll(partial, shift, axis=1)
        shift //= 2
    return place(place_ref, partial, n_rhs, 2)


def part_kernel(arrived_ref, keep_ref, give_ref):
    depth = keep_ref.shape[0] // 2
    body = arrived_ref.shape[1] - 4 * depth
    total = arrived_ref[0, body:, :]
    for source in range(1, arrived_ref.shape[0]):
        total = total + arrived_ref[source, body:, :]
    lower = lax.axis_index("band") == 0
    for n in range(2):
        zero, one = (total[(2 * n + m) * depth : (2 * n + m + 1) * depth] for m in range(2))
        keep_ref[n * depth : (n + 1) * depth] = jnp.where(lower, zero, one)
        give_ref[n * depth : (n + 1) * depth] = jnp.where(lower, one, zero)


def half_blocks_of(sizes, width_k, place_ref, arrived_ref, far):
    rows, n_rows, cap, n_tiles, n_rhs = sizes

    def fetch(row):
        total = None
        for k in range(width_k):
            slot = place_ref[0, 0, k * rows + row]
            holder, slot = over(slot, 2 * cap), below(slot, 2 * cap)
            start = pl.ds(pl.multiple_of(below(slot, cap) * n_rhs, n_rhs), n_rhs)
            mine = slot >= cap if far else slot < cap
            block = jnp.where(mine, arrived_ref[holder, start, :], 0.0)
            total = block if total is None else total + block
        return total

    return fetch


def base_kernel(sizes, width_k, *refs):
    metadata_in, own_ref, inverse_ref, terms_in, out_ref = refs[:2], *refs[2:4], refs[4:6], refs[6]
    metadata, sum_ref, product_ref, terms, term_sems, meta_sems = refs[7:9], *refs[9:11], refs[11:13], *refs[13:]
    place_ref, index_ref = metadata
    rows = sizes[0]
    metadata = copies_of(zip(metadata_in, metadata), meta_sems)
    later = copies_of(zip(terms_in, terms), term_sems)
    finish(metadata)
    fetch = half_blocks_of(sizes, width_k, place_ref, own_ref, False)

    def diags(row):
        return index_ref[0, 0, rows + row]

    gather_solve(sizes, fetch, diags, later, terms, inverse_ref, sum_ref, product_ref)
    out_ref[...] = sum_ref[...].reshape(out_ref.shape)


def final_kernel(sizes, width_k, *refs):
    rows, n_rows, cap, n_tiles, n_rhs = sizes
    metadata_in, mirror_ref, inverse_ref, base_ref, near_ref, far_ref, scale_ref = refs[:2], *refs[2:8]
    out_ref, metadata, sum_ref, product_ref, meta_sems = refs[8], refs[9:11], *refs[11:]
    place_ref, index_ref = metadata
    metadata = copies_of(zip(metadata_in, metadata), meta_sems)
    depth = scale_ref.shape[0]
    correction = (near_ref[...] + far_ref[...]) / scale_ref[...]
    padded = jnp.concatenate([correction, jnp.zeros((8 - depth, LANES), jnp.float32)], axis=0)
    turned = padded.T
    finish(metadata)
    fetch = half_blocks_of(sizes, width_k, place_ref, mirror_ref, True)

    def diags(row):
        return index_ref[0, 0, rows + row]

    gather_solve(sizes, fetch, diags, [], [], inverse_ref, sum_ref, product_ref)
    for row in range(rows):
        spot, place = row // depth, row % depth
        column = turned[spot * n_rhs : (spot + 1) * n_rhs, place : place + 1]
        out_ref[row] = (base_ref[row] + column) + sum_ref[pl.ds(row * n_rhs, n_rhs), :]


def shifted(value, axis, steps):
    count = lax.axis_size(axis)
    initial, last = (max(0, -steps), min(count, count - steps))
    return lax.ppermute(value, axis, [(source, source + steps) for source in range(initial, last)])


def to_bands(sends):
    if len(sends) == 1:
        return (lax.ppermute(sends[0], "band", [(0, 1), (1, 0)]),)
    return shifted(sends[0], "band", 1), shifted(sends[1], "band", -1)


def on_device(
    start_iterate,
    right_side,
    diag_table,
    inverse_table,
    coupling_tiles,
    diag_index,
    tile_index,
    source_owner,
    source_local,
    aggregate_map,
):
    rows, n_rhs, states = start_iterate.shape
    width_k = source_owner.shape[1]
    n_tiles, n_diag = coupling_tiles.shape[0], inverse_table.shape[0]
    n_rows, n_bands = lax.axis_size("rows"), lax.axis_size("band")
    n_dev = n_rows * n_bands
    cap = max(2, 2 * width_k * rows // n_rows)
    slots = n_rows * cap
    total_groups = AGG_DEV * n_dev
    per_tile = LANES // n_rhs
    depth = rows // per_tile
    n_func = 16
    dense = (
        n_bands == 2
        and n_dev * rows * total_groups <= DENSE_LIMIT
        and depth == 4
        and n_diag * n_func == LANES
        and n_tiles + 2 <= n_func
    )
    sizes = (rows, n_rows, cap, n_tiles, n_rhs)
    f32, i32 = jnp.float32, jnp.int32
    my_band = lax.axis_index("band")
    my_row = lax.axis_index("rows")

    half = n_rows // 2
    wide = -(-(4 + 2 * width_k) * rows // LANES) * LANES
    place_wide = -(-2 * width_k * rows // LANES) * LANES
    index_shapes = [(width_k, rows), (width_k, rows), (width_k + 2, rows), (1, rows), (1, rows)]
    halves_of_rows = [list(range(half)), list(range(half, n_rows))]
    to_mirror = [(i, (i + half) % n_rows) for i in range(n_rows)]
    mirror = lax.ppermute(start_iterate, "rows", to_mirror)
    lists, index, places = call(
        functools.partial(request_kernel, (rows, n_rows, cap, n_tiles, n_diag)),
        (
            jax.ShapeDtypeStruct((n_rows, 1, LANES + wide), i32),
            jax.ShapeDtypeStruct((1, 1, wide), i32),
            jax.ShapeDtypeStruct((1, 1, place_wide), i32),
        ),
        [HBM] * 5,
        [VMEM] * 3,
        [*[pltpu.VMEM(shape, i32) for shape in index_shapes], pltpu.SemaphoreType.DMA((5,))],
    )(source_owner.T, source_local.T, tile_index.T, diag_index[None], aggregate_map.T)
    lists = lax.all_to_all(lists, "rows", split_axis=0, concat_axis=0, tiled=True)
    if n_bands == 2:
        near = lax.ppermute(index, "band", [(0, 1), (1, 0)])
    else:
        ways = [[(b, (b + step) % n_bands) for b in range(n_bands)] for step in (-1, 1)]
        near = jnp.concatenate([lax.ppermute(index, "band", way) for way in ways], axis=0)

    n_ways = 1 if n_bands == 2 else 2
    block = (rows, n_rhs, states)
    band_shapes = [jax.ShapeDtypeStruct(block, f32)] * n_ways
    band_scratch = [pltpu.VMEM(block, f32)] * n_ways
    term_scratch = [pltpu.VMEM(block, f32)] * (1 + n_ways)
    term_sems = pltpu.SemaphoreType.DMA((1 + n_ways,))
    list_scratch = pltpu.SMEM((half, 1, LANES), i32)
    near_scratch = pltpu.SMEM((n_ways, 1, wide), i32)
    row_scratch = [pltpu.SMEM((1, 1, place_wide), i32), pltpu.SMEM((1, 1, wide), i32)]
    flat = rows * n_rhs
    sums = pltpu.VMEM((flat, states), f32)
    products = pltpu.VMEM((max(n_tiles, n_diag) * rows, n_rhs, states), f32)
    work = 6 * flat * states * states
    made_shape = (n_tiles * rows, n_rhs, states)
    table_scratch = [pltpu.VMEM(coupling_tiles.shape, f32)]
    table_sems = pltpu.SemaphoreType.DMA((-(-n_tiles // 2),))
    made = call(
        product_kernel,
        jax.ShapeDtypeStruct(made_shape, f32),
        [HBM, HBM],
        HBM,
        [
            pltpu.VMEM(block, f32),
            *table_scratch,
            pltpu.VMEM(made_shape, f32),
            pltpu.SemaphoreType.DMA((1 + n_tiles,)),
            table_sems,
        ],
        work * n_tiles,
        4 << 20,
    )(start_iterate, coupling_tiles)
    packed, *bands = call(
        functools.partial(first_kernel, sizes, width_k, n_ways),
        (jax.ShapeDtypeStruct((half, 2 * cap, n_rhs, states), f32), *band_shapes),
        [HBM, VMEM, VMEM, ANY, ANY],
        [HBM] * (1 + n_ways),
        [
            pltpu.VMEM((2, *made_shape), f32),
            list_scratch,
            near_scratch,
            pltpu.VMEM((half, 2 * cap, n_rhs, states), f32),
            *band_scratch,
            pltpu.SemaphoreType.DMA((n_tiles,)),
            pltpu.SemaphoreType.DMA((2,)),
            pltpu.SemaphoreType.DMA((half + n_ways,)),
        ],
        work * n_tiles,
        4 << 20,
    )(made, mirror, coupling_tiles, lists, near)
    packed, late = lax.optimization_barrier((packed, lists))
    if dense:
        across = lax.ppermute(late, "band", [(0, 1), (1, 0)])
        across, *bands = lax.optimization_barrier((across, *bands))
    sends = (packed.reshape(half, 2 * cap * n_rhs, states), *bands)
    halves_of_rows = [list(range(half)), list(range(half, n_rows))]
    def exchange(sends, groups=None):
        arrived = lax.all_to_all(
            sends[0], "rows", split_axis=0, concat_axis=0, tiled=True, axis_index_groups=groups
        )
        return arrived, to_bands(sends[1:])

    arrived_blocks, arrived_bands = exchange(sends, halves_of_rows)

    if dense:
        fields = jnp.stack([late, across])[:, :, 0, LANES:]
        fields = fields.reshape(2, n_rows, -1, rows).transpose(2, 0, 1, 3)
        fields = fields.reshape(-1, 2, n_rows * rows)
        n_blocks = slots + rows
        length = n_dev * depth
        extra_shapes = [
            ((n_diag * n_func, 3 * states), jnp.bfloat16),
            ((total_groups, (n_tiles + 1) * n_blocks), jnp.bfloat16),
            ((per_tile * length, total_groups), jnp.bfloat16),
            ((total_groups, LANES), f32),
        ]
        functional_shape, count_shape, placing_shape, partial_shape = extra_shapes
        counts, functionals, placing, partial, scale = call(
            functools.partial(count_kernel, sizes, width_k, n_func),
            (
                jax.ShapeDtypeStruct(*count_shape),
                jax.ShapeDtypeStruct(*functional_shape),
                jax.ShapeDtypeStruct(*placing_shape),
                jax.ShapeDtypeStruct(*partial_shape),
                jax.ShapeDtypeStruct((depth, LANES), f32),
            ),
            [ANY, HBM] + [VMEM] * 5,
            [HBM] * 4 + [VMEM],
            [
                pltpu.VMEM(*count_shape),
                pltpu.VMEM(*functional_shape),
                pltpu.VMEM(*placing_shape),
                pltpu.VMEM(*partial_shape),
                row_scratch[1],
                pltpu.VMEM(block, f32),
                pltpu.VMEM((n_diag * n_func, flat), f32),
                pltpu.VMEM((rows * n_func, LANES), f32),
                pltpu.SemaphoreType.DMA((2,)),
                pltpu.SemaphoreType.DMA((4,)),
            ],
            4 * total_groups * n_tiles * n_dev * rows * n_blocks,
            4 << 20,
        )(
            index, right_side, fields, late[:, 0, :LANES], coupling_tiles, diag_table, inverse_table
        )
        extra_scratch = [
            *[pltpu.VMEM(*shape) for shape in extra_shapes],
            pltpu.VMEM((n_diag * n_func, n_blocks * n_rhs), f32),
            pltpu.VMEM((n_blocks * n_func, LANES), f32),
            pltpu.VMEM((n_rows, n_bands * depth, LANES), f32),
        ]

        made = (arrived_blocks, functionals, counts, placing, partial, scale)
        made = lax.optimization_barrier(made)
        arrived_blocks, functionals, counts, placing, partial, scale = made

    def solve(field, arrived, bands):
        return call(
            functools.partial(solve_kernel, sizes, width_k, n_ways, field),
            jax.ShapeDtypeStruct(block, f32),
            [ANY] * 2 + [VMEM] * 2 + [HBM] + [ANY] * n_ways,
            VMEM,
            [
                *row_scratch,
                sums,
                products,
                *term_scratch,
                term_sems,
                pltpu.SemaphoreType.DMA((2,)),
            ],
            work * n_diag,
            4 << 20,
        )(places, index, arrived, inverse_table, right_side, *bands)

    first = solve(0, arrived_blocks, arrived_bands)
    body = cap * n_rhs
    full_list = pltpu.SMEM((n_rows, 1, LANES), i32)
    if dense:
        mirror = lax.ppermute(first, "rows", to_mirror)
        own, band = call(
            functools.partial(own_kernel, sizes, width_k),
            (
                jax.ShapeDtypeStruct((half, body + 2 * n_bands * depth, states), f32),
                jax.ShapeDtypeStruct(block, f32),
            ),
            [ANY] * 2 + [VMEM] * 2 + [HBM] * 4,
            [HBM] * 2,
            [
                full_list,
                near_scratch,
                products,
                pltpu.VMEM((n_rows, body, states), f32),
                pltpu.VMEM(block, f32),
                *extra_scratch,
                pltpu.SemaphoreType.DMA((2,)),
                pltpu.SemaphoreType.DMA((4,)),
                pltpu.SemaphoreType.DMA((half + 3,)),
            ],
            2 * work * n_tiles,
            4 << 20,
        )(lists, near, first, coupling_tiles, functionals, counts, placing, partial)
        own, (band,) = exchange((own, band), halves_of_rows)
        packed = call(
            functools.partial(mirror_kernel, sizes),
            jax.ShapeDtypeStruct((half, body, states), f32),
            [ANY] + [VMEM] * 2,
            HBM,
            [
                list_scratch,
                products,
                pltpu.VMEM((half, body, states), f32),
                pltpu.SemaphoreType.DMA((half + 1,)),
            ],
            BEHIND_SWAP * work * n_tiles,
            4 << 20,
        )(lists, mirror, coupling_tiles)
        packed, band = lax.optimization_barrier((packed, band))
        swapped = lax.all_to_all(
            packed, "rows", split_axis=0, concat_axis=0, tiled=True, axis_index_groups=halves_of_rows
        )
        part = jax.ShapeDtypeStruct((2 * depth, LANES), f32)
        keep, give = call(part_kernel, (part, part), [VMEM], [VMEM] * 2)(own)
        keep = keep + lax.ppermute(give, "band", [(0, 1), (1, 0)])
        far = lax.ppermute(keep[depth:], "rows", to_mirror)
        base = call(
            functools.partial(base_kernel, sizes, width_k),
            jax.ShapeDtypeStruct(block, f32),
            [ANY] * 2 + [VMEM] * 2 + [HBM, ANY],
            VMEM,
            [
                *row_scratch,
                sums,
                products,
                *term_scratch,
                term_sems,
                pltpu.SemaphoreType.DMA((2,)),
            ],
            work * n_diag,
            4 << 20,
        )(places, index, own, inverse_table, right_side, band)
        return call(
            functools.partial(final_kernel, sizes, width_k),
            jax.ShapeDtypeStruct(block, f32),
            [ANY] * 2 + [VMEM] * 6,
            VMEM,
            [*row_scratch, sums, products, pltpu.SemaphoreType.DMA((2,))],
            work * n_diag,
            4 << 20,
        )(places, index, swapped, inverse_table, base, keep[:depth], far, scale)

    sends = call(
        functools.partial(pack_kernel, sizes, width_k, n_ways),
        (jax.ShapeDtypeStruct((n_rows, body, states), f32), *band_shapes),
        [ANY] * 2 + [VMEM] * 2,
        [HBM] * (1 + n_ways),
        [
            full_list,
            near_scratch,
            products,
            pltpu.VMEM((n_rows, body, states), f32),
            *band_scratch,
            pltpu.SemaphoreType.DMA((2,)),
            pltpu.SemaphoreType.DMA((1 + n_ways,)),
        ],
        work * n_tiles,
        4 << 20,
    )(lists, near, first, coupling_tiles)
    arrived_blocks, arrived_bands = exchange(sends)
    second = solve(width_k, arrived_blocks, arrived_bands)

    groups = aggregate_map[:, 0]
    own = jnp.arange(rows, dtype=i32)
    index_all = lax.all_gather(index, ("band", "rows"), axis=0, tiled=True)
    index_all = index_all.reshape(n_bands, n_rows, wide)
    groups_all, diags_all = index_all[:, :, :rows], index_all[:, :, rows : 2 * rows]
    codes = lists[:, 0, :cap]
    asked = jnp.arange(n_rows, dtype=i32)[:, None] * rows + codes // (rows * n_tiles) % rows
    asked = jnp.where(codes > 0, asked, -1).reshape(-1)
    table_sums = jnp.sum(diag_table, axis=(1, 2))
    diag_onehot = diags_all.reshape(-1, 1) == jnp.arange(n_diag, dtype=i32)[None]
    block_sums = jnp.sum(jnp.where(diag_onehot, table_sums[None], 0.0), axis=1)
    whole_diag = jnp.sum(
        jnp.where(groups[:, None] == groups_all.reshape(-1)[None], block_sums[None], 0.0), axis=1
    )
    above, below = near[0, 0], near[-1, 0]
    place_of = (2 + width_k) * rows
    band_tiles = jnp.stack([above[place_of : place_of + rows], below[place_of + rows : place_of + 2 * rows]])
    band_groups = jnp.stack([above[:rows], below[:rows]])
    band_valid = jnp.stack([my_band + 1 < n_bands, my_band > 0])
    band_valid = jnp.broadcast_to(band_valid[:, None], (2, rows))
    n_all = n_tiles + n_diag + 1
    code = codes.reshape(-1)
    band_of_mine = lax.dynamic_index_in_dim(groups_all, my_band, 0, keepdims=False).reshape(-1)
    entry_group = jnp.concatenate(
        [jnp.take(band_of_mine, jnp.maximum(asked, 0)), band_groups.reshape(-1), groups, groups]
    )
    entry_func = jnp.concatenate(
        [
            (code % rows) * n_all + (code // rows) % n_tiles,
            (own[None] * n_all + band_tiles).reshape(-1),
            own * n_all + n_tiles + diag_index,
            own * n_all + n_tiles + n_diag,
        ]
    )
    entry_valid = jnp.concatenate([asked >= 0, band_valid.reshape(-1), jnp.ones((2 * rows,), bool)])
    functionals = jnp.concatenate(
        [jnp.sum(coupling_tiles, axis=1), -jnp.sum(diag_table, axis=1)], axis=0
    )
    weights = jnp.einsum("fp,rcp->rfc", functionals, second, precision=HIGH)
    weights = jnp.concatenate([weights, jnp.sum(right_side, axis=2)[:, None]], axis=1)
    chosen = jnp.take(weights.reshape(rows * n_all, n_rhs), entry_func, axis=0)
    chosen = jnp.where(entry_valid[:, None], chosen, 0.0)
    partial = jax.ops.segment_sum(chosen, entry_group, num_segments=total_groups)
    whole = lax.psum(partial, ("band", "rows"))
    correction = jnp.take(whole, groups, axis=0) / whole_diag[:, None]
    return second + correction[:, :, None]


def solution(mesh):
    in_specs = (
        P(("band", "rows"), None, None),
        P(("band", "rows"), None, None),
        P(),
        P(),
        P(),
        P(("band", "rows")),
        P(("band", "rows"), None),
        P(("band", "rows"), None),
        P(("band", "rows"), None),
        P(("band", "rows"), None),
    )
    out_specs = P(("band", "rows"), None, None)
    return jax.shard_map(
        on_device, mesh=mesh, in_specs=in_specs, out_specs=out_specs, check_vma=False
    )
```

```python
import functools

import jax
import jax.numpy as jnp
from jax import lax
from jax.experimental import pallas as pl
from jax.experimental.pallas import tpu as pltpu
from jax.sharding import PartitionSpec as P

AGG_DEV = 8
LANES = 128
DENSE_LIMIT = 1 << 19
BEHIND_SWAP = 100

VMEM = pl.BlockSpec(memory_space=pltpu.VMEM)
SMEM = pl.BlockSpec(memory_space=pltpu.SMEM)
HBM = pl.BlockSpec(memory_space=pltpu.HBM)
ANY = pl.BlockSpec(memory_space=pl.ANY)
HIGH = lax.Precision.HIGHEST


def params():
    return pltpu.CompilerParams(vmem_limit_bytes=24 * 1024 * 1024)


def call(kernel, out_shape, in_specs, out_specs, scratch=(), flops=0, moved=0):
    def shaped(shape, spec):
        return pltpu.HBM(shape.shape, shape.dtype) if spec is HBM else shape

    if isinstance(out_shape, (tuple, list)):
        out_shape = [shaped(*pair) for pair in zip(out_shape, out_specs)]
    else:
        out_shape = shaped(out_shape, out_specs)
    run = pl.pallas_call(
        kernel,
        out_shape=out_shape,
        in_specs=in_specs,
        out_specs=out_specs,
        scratch_shapes=list(scratch),
        compiler_params=params(),
        cost_estimate=pl.CostEstimate(flops=flops, bytes_accessed=moved, transcendentals=0),
    )

    def apply(*args):
        pinned = [
            pltpu.with_memory_space_constraint(arg, pltpu.HBM) if spec is HBM else arg
            for arg, spec in zip(args, in_specs)
        ]
        return run(*pinned)

    return apply


def below(value, bound):
    return value & (bound - 1) if bound & (bound - 1) == 0 else lax.rem(value, bound)


def over(value, bound):
    if bound & (bound - 1) == 0:
        return lax.shift_right_logical(value, bound.bit_length() - 1)
    return lax.div(value, bound)


def halves(value):
    high = value.astype(jnp.bfloat16)
    low = (value - high.astype(jnp.float32)).astype(jnp.bfloat16)
    return high, low


def left_operand(value):
    high, low = halves(value)
    return jnp.concatenate([high, low, high], axis=1)


def right_operand(value):
    high, low = halves(value)
    return jnp.concatenate([high, high, low], axis=1)


def dot_nt(left, right):
    return lax.dot_general(
        left, right, (((1,), (1,)), ((), ())), preferred_element_type=jnp.float32
    )


def table_products(value, table_ref, out_ref, done=None, loads=None):
    left = left_operand(value)
    count, width = table_ref.shape[0], table_ref.shape[1]
    n_rhs = out_ref.shape[1]
    rows = left.shape[0] // n_rhs
    for first in range(0, count, 2):
        last = min(first + 2, count)
        if loads is not None:
            loads[first // 2].wait()
        right = right_operand(table_ref[first:last].reshape((last - first) * width, -1))
        product = dot_nt(left, right)
        for t in range(first, last):
            part = product[:, (t - first) * width : (t - first + 1) * width]
            out_ref[t * rows : (t + 1) * rows] = part.reshape(rows, n_rhs, width)
        if done is not None:
            done(first * rows, (last - first) * rows)


def started(copies):
    for copy in copies:
        copy.start()
    return copies


def finish(copies):
    for copy in copies:
        copy.wait()


def request_kernel(sizes, *refs):
    rows, n_rows, cap, n_tiles, n_diag = sizes
    inputs, (list_ref, index_ref, place_ref), held, sems = refs[:5], refs[5:8], refs[8:13], refs[13]
    finish(
        started([pltpu.make_async_copy(i, h, sems.at[n]) for n, (i, h) in enumerate(zip(inputs, held))])
    )
    owner_ref, local_ref, tile_ref, diag_ref, group_ref = held
    width_k = owner_ref.shape[0]
    half = n_rows // 2
    row_of = lax.broadcasted_iota(jnp.int32, (rows, rows), 0)
    col_of = lax.broadcasted_iota(jnp.int32, (rows, rows), 1)
    lane = lax.broadcasted_iota(jnp.int32, (rows, LANES), 1)
    owners = lax.broadcasted_iota(jnp.int32, (n_rows, rows), 0)

    def column(row):
        return jnp.sum(jnp.where(row_of == col_of, row, 0), axis=1, keepdims=True)

    def owner_row(k):
        return owner_ref[k : k + 1, :]

    row_ids = lax.broadcasted_iota(jnp.int32, (1, rows), 1)
    owner_columns = [column(owner_row(k)) for k in range(width_k)]
    lists = jnp.zeros((n_rows, LANES), jnp.float32)
    places, half_places = [], []
    for k in range(width_k):
        rank = jnp.zeros((1, rows), jnp.int32)
        for other in range(k + 1):
            match = owner_columns[other] == owner_row(k)
            if other == k:
                match = match & (row_of < col_of)
            rank = rank + jnp.sum(jnp.where(match, 1, 0), axis=0, keepdims=True)
        places.append(owner_row(k) * cap + rank)
        same = (owner_row(k) >= half) == (lax.axis_index("rows") >= half)
        holder = jnp.where(owner_row(k) >= half, owner_row(k) - half, owner_row(k))
        half_places.append(holder * (2 * cap) + rank + jnp.where(same, 0, cap))
        taker = row_ids + rows * (diag_ref[...] + n_diag)
        code = local_ref[k : k + 1, :] + rows * (tile_ref[k : k + 1, :] + n_tiles * taker)
        code, rank = column(code), column(rank)
        mirror = jnp.where(owner_row(k) >= half, owner_row(k) - half, owner_row(k) + half)
        for owner, base in ((owner_row(k), 0), (mirror, LANES // 2)):
            by_rank = jnp.where(lane == rank + base, code, 0).astype(jnp.float32)
            mine = jnp.where(owners == owner, 1.0, 0.0)
            lists = lists + jnp.dot(
                mine, by_rank, precision=HIGH, preferred_element_type=jnp.float32
            )
    lists = (lists + 0.5).astype(jnp.int32)

    def joined(parts, wide):
        spare = wide - len(parts) * rows
        if spare:
            parts = [*parts, jnp.zeros((1, spare), jnp.int32)]
        return jnp.concatenate(parts, axis=1)

    index = [group_ref[...], diag_ref[...]]
    index += [tile_ref[k : k + 1, :] for k in range(width_k + 2)]
    index += [owner_row(k) * rows + local_ref[k : k + 1, :] for k in range(width_k)]
    index = joined(index, index_ref.shape[2])
    index_ref[0] = index
    place_ref[0] = joined(half_places + places, place_ref.shape[2])
    for device in range(n_rows):
        list_ref[device] = jnp.concatenate([lists[device : device + 1, :], index], axis=1)


def copies_of(pairs, sems):
    return started([pltpu.make_async_copy(i, h, sems.at[n]) for n, (i, h) in enumerate(pairs)])


def band_field(rows, width_k, way, n_ways):
    field = (2 + width_k) * rows
    if n_ways == 1:
        return field + jnp.where(lax.axis_index("band") == 0, 0, rows)
    return field + way * rows


def pack_bands(sizes, width_k, product_ref, near_ref, band_refs):
    rows = sizes[0]
    for way, band_ref in enumerate(band_refs):
        field = band_field(rows, width_k, way, len(band_refs))
        for row in range(rows):
            band_ref[row] = product_ref[near_ref[way, 0, field + row] * rows + row]


def table_loads(table_in, table_ref, sems):
    copies = []
    for first in range(0, table_in.shape[0], 2):
        place = pl.ds(first, min(2, table_in.shape[0] - first))
        source, target = table_in.at[place], table_ref.at[place]
        copies.append(pltpu.make_async_copy(source, target, sems.at[first // 2]))
    return started(copies)


def product_kernel(start_in, tile_in, product_out, start_ref, tile_ref, product_ref, sems, tile_sems):
    start = pltpu.make_async_copy(start_in, start_ref, sems.at[0])
    start.start()
    loads = table_loads(tile_in, tile_ref, tile_sems)
    start.wait()
    copies = []

    def done(first, count):
        place = pl.ds(first, count)
        source, target = product_ref.at[place], product_out.at[place]
        copies.extend(started([pltpu.make_async_copy(source, target, sems.at[1 + len(copies)])]))

    rows, n_rhs, states = start_ref.shape
    values = start_ref[...].reshape(rows * n_rhs, states)
    table_products(values, tile_ref, product_ref, done, loads)
    finish(copies)


def first_kernel(sizes, width_k, n_band, *refs):
    rows, n_rows, cap, n_tiles, n_rhs = sizes
    product_in, mirror_ref, tile_ref, list_in, near_in, send_out = refs[:6]
    band_out, refs = refs[6 : 6 + n_band], refs[6 + n_band :]
    product_ref, list_ref, near_ref, send_ref = refs[:4]
    band_refs, (load_sems, meta_sems, send_sems) = refs[4 : 4 + n_band], refs[4 + n_band :]
    half = n_rows // 2
    base = jnp.where(lax.axis_index("rows") >= half, half, 0)
    list_in = list_in.at[pl.ds(base, half), :, pl.ds(0, LANES)]
    metadata = copies_of(((list_in, list_ref), (near_in, near_ref)), meta_sems)
    places = [pl.ds(tile * rows, rows) for tile in range(n_tiles)]
    loads = [(product_in.at[place], product_ref.at[0, place]) for place in places]
    loads = copies_of(loads, load_sems)
    values = mirror_ref[...].reshape(rows * n_rhs, -1)
    table_products(values, tile_ref, product_ref.at[1])
    finish(metadata)
    copies = []
    for side in (1, 0):
        if side == 0:
            finish(loads)
        for device in range(half):
            for rank in range(cap):
                code = list_ref[device, 0, side * (LANES // 2) + rank]
                block = product_ref[side, below(code, rows * n_tiles)]
                send_ref[device, side * cap + rank] = block
            place = (device, pl.ds(side * cap, cap))
            copies += started(
                [pltpu.make_async_copy(send_ref.at[place], send_out.at[place], send_sems.at[len(copies)])]
            )
    pack_bands(sizes, width_k, product_ref.at[0], near_ref, band_refs)
    for ref, out in zip(band_refs, band_out):
        copies += started([pltpu.make_async_copy(ref, out, send_sems.at[len(copies)])])
    finish(copies)


def place(place_ref, values, n_rhs, n_parts):
    per_tile = LANES // n_rhs
    length = place_ref.shape[0] // per_tile
    parts, rest = [], values
    for _ in range(n_parts):
        part = rest.astype(jnp.bfloat16)
        rest = rest - part.astype(jnp.float32)
        parts.append(part)
    parts = jnp.concatenate(parts, axis=1)
    lane = lax.broadcasted_iota(jnp.int32, (length, LANES), 1)
    result = jnp.zeros((length, LANES), jnp.float32)
    placed = jnp.dot(place_ref[...], parts, preferred_element_type=jnp.float32)
    for spot in range(per_tile):
        chosen = placed[spot * length : (spot + 1) * length]
        chosen = sum(chosen[:, n * LANES : (n + 1) * LANES] for n in range(n_parts))
        result = jnp.where((lane >= spot * n_rhs) & (lane < (spot + 1) * n_rhs), chosen, result)
    return result


def spread_values(n_rhs, n_func, functional_ref, blocks, kinds, value_ref, spread_ref, done):
    per_tile = LANES // n_rhs
    lane = lax.broadcasted_iota(jnp.int32, (n_func, LANES), 1)
    columns = slice(done * n_rhs, done * n_rhs + blocks.shape[0])
    value_ref[:, columns] = dot_nt(functional_ref[...], right_operand(blocks))
    for block, kind in enumerate(kinds, done):
        tile, spot = block // per_tile, block % per_tile
        start = pl.multiple_of(kind * n_func, n_func)
        piece = value_ref[pl.ds(start, n_func), tile * LANES : (tile + 1) * LANES]
        piece = jnp.where((lane >= spot * n_rhs) & (lane < (spot + 1) * n_rhs), piece, 0.0)
        spread_ref[block * n_func : (block + 1) * n_func, :] = piece


def one_hot(ids, row):
    return jnp.where(ids == row, 1.0, 0.0).astype(jnp.bfloat16)


def count_kernel(sizes, width_k, n_func, *refs):
    rows, n_rows, cap, n_tiles, n_rhs = sizes
    index_in, right_in, field_ref, list_ref, tile_ref, table_ref, inverse_ref = refs[:7]
    count_out, functional_out, placing_out, partial_out, scale_ref = refs[7:12]
    count_ref, functional_ref, placing_ref, partial_ref = refs[12:16]
    index_ref, right_ref, value_ref, spread_ref, load_sems, sems = refs[16:]
    loads = copies_of(((index_in, index_ref), (right_in, right_ref)), load_sems)
    n_groups = count_ref.shape[0]
    slots, band_rows = n_rows * cap, n_rows * rows
    copies = []

    def send(source, target):
        copies.extend(started([pltpu.make_async_copy(source, target, sems.at[len(copies)])]))

    sums = jnp.sum(tile_ref[...], axis=1)
    line = lax.broadcasted_iota(jnp.int32, (n_func, sums.shape[1]), 0)
    sums = jnp.concatenate([sums, jnp.zeros((n_func - n_tiles, sums.shape[1]), jnp.float32)], axis=0)
    n_diag = inverse_ref.shape[0]
    totals = []
    for d in range(n_diag):
        minus = -jnp.sum(table_ref[d], axis=0, keepdims=True)
        totals.append(-jnp.sum(minus, axis=1, keepdims=True))
        wanted = jnp.where(line == n_tiles, minus, sums)
        high, low = halves(inverse_ref[d])
        right = jnp.concatenate([high, high, low], axis=0)
        solved = jnp.dot(left_operand(wanted), right, preferred_element_type=jnp.float32)
        solved = jnp.where(line == n_tiles + 1, 1.0, solved)
        functional_ref[d * n_func : (d + 1) * n_func, :] = left_operand(solved)
    send(functional_ref, functional_out)

    lists = list_ref[...]
    asker = lax.broadcasted_iota(jnp.int32, lists.shape, 0)
    codes = asker * rows + below(over(lists, rows * n_tiles), rows)
    codes = jnp.where(lists > 0, codes, -1).astype(jnp.float32)
    spread = lax.broadcasted_iota(jnp.int32, (slots, n_rows), 0)
    spread = lax.div(spread, cap) == lax.broadcasted_iota(jnp.int32, (slots, n_rows), 1)
    codes = jnp.dot(
        jnp.where(spread, 1.0, 0.0), codes, precision=HIGH, preferred_element_type=jnp.float32
    )
    rank = lax.rem(lax.broadcasted_iota(jnp.int32, codes.shape, 0), cap)
    lane = lax.broadcasted_iota(jnp.int32, codes.shape, 1)
    asked = jnp.sum(jnp.where(rank == lane, codes, 0.0), axis=1, keepdims=True)
    asked = jnp.where(asked < 0.0, asked - 0.5, asked + 0.5).astype(jnp.int32)
    low, high = asked[: slots // 2], asked[slots // 2 :]
    upper = lax.axis_index("rows") >= n_rows // 2
    asked = jnp.concatenate([jnp.where(upper, high, low), jnp.where(upper, low, high)], axis=0)
    own = lax.axis_index("rows") * rows + lax.broadcasted_iota(jnp.int32, (rows, 1), 0)
    band = lax.axis_index("band")

    def field(n, side):
        return field_ref[n, side : side + 1, :]

    row_ids = lax.broadcasted_iota(jnp.int32, (1, band_rows), 1)
    sides = []
    for side, targets in ((0, jnp.concatenate([asked, own], axis=0)), (1, own)):
        first = band == side
        across = jnp.where(first, field(2 + width_k, 1 - side), field(3 + width_k, 1 - side))
        takers = [field(2 + k, side) * n_groups + field(0, side) for k in range(width_k)]
        takers.append(across * n_groups + field(0, 1 - side))
        takers = jnp.concatenate(takers, axis=1)
        origins = [field(4 + width_k + k, side) for k in range(width_k)] + [row_ids]
        hits = one_hot(targets, jnp.concatenate(origins, axis=1))
        sides.append((takers, hits, field(0, side)))
    pieces, own_pieces = [], []
    ids = lax.broadcasted_iota(jnp.int32, (n_groups, band_rows), 0)
    for t in range(n_tiles + 1):
        found = []
        for takers, hits, groups in sides:
            if t < n_tiles:
                wide = lax.broadcasted_iota(jnp.int32, (n_groups, takers.shape[1]), 0)
                found.append(dot_nt(one_hot(wide + t * n_groups, takers), hits))
            else:
                found.append(dot_nt(one_hot(ids, groups), hits[:, -band_rows:]))
        pieces += [found[0][:, :slots], found[1]]
        own_pieces.append(found[0][:, slots:])
    count_ref[...] = jnp.concatenate(pieces, axis=1).astype(jnp.bfloat16)
    send(count_ref, count_out)

    own_counts = jnp.concatenate([*own_pieces, own_pieces[-1]], axis=1).astype(jnp.bfloat16)
    finish(loads)
    rights = right_ref[...].reshape(rows * n_rhs, -1)
    kinds = [index_ref[0, 0, rows + row] for row in range(rows)]
    spread_values(n_rhs, n_func, functional_ref, rights, kinds, value_ref, spread_ref, 0)
    values = [spread_ref[pl.ds(t, rows, stride=n_func), :] for t in range(n_tiles + 2)]
    values = jnp.concatenate(halves(jnp.concatenate(values, axis=0)), axis=1)
    partial = jnp.dot(own_counts, values, preferred_element_type=jnp.float32)
    partial_ref[...] = partial[:, :LANES] + partial[:, LANES:]
    send(partial_ref, partial_out)

    per_tile = LANES // n_rhs
    depth = rows // per_tile
    length = n_rows * 2 * depth
    order = lax.broadcasted_iota(jnp.int32, (per_tile * length, 1), 0)
    spot, order = lax.div(order, length), lax.rem(order, length)
    device, order = lax.div(order, 2 * depth), lax.rem(order, 2 * depth)
    side, order = lax.div(order, depth), lax.rem(order, depth)
    order = side * band_rows + device * rows + spot * depth + order
    member = [
        one_hot(ids, jnp.where(band == which, field(0, 0), field(0, 1))) for which in range(2)
    ]
    placing = jnp.zeros(placing_ref.shape, jnp.float32)
    for which in range(2):
        placing = placing + dot_nt(one_hot(order, row_ids + which * band_rows), member[which])
    placing_ref[...] = placing.astype(jnp.bfloat16)
    send(placing_ref, placing_out)
    whole = jnp.zeros((n_groups, 1), jnp.float32)
    for side in range(2):
        sums = jnp.zeros((1, band_rows), jnp.float32)
        for d in range(n_diag):
            sums = jnp.where(field(1, side) == d, totals[d], sums)
        weighted = jnp.where(ids == field(0, side), sums, 0.0)
        whole = whole + jnp.sum(weighted, axis=1, keepdims=True)
    scale = place(placing_ref, jnp.broadcast_to(whole, (n_groups, LANES)), n_rhs, 3)
    mine = jnp.zeros(scale_ref.shape, jnp.float32)
    here = lax.axis_index("rows") * 2 + band
    for n in range(2 * n_rows):
        mine = jnp.where(here == n, scale[n * depth : (n + 1) * depth, :], mine)
    scale_ref[...] = mine
    finish(copies)


def gather_solve(sizes, fetch, diags, later, terms, inverse_ref, sum_ref, product_ref):
    rows, n_rows, cap, n_tiles, n_rhs = sizes
    for row in range(rows):
        sum_ref[pl.ds(row * n_rhs, n_rhs), :] = fetch(row)
    finish(later)
    total = sum_ref[...]
    for term in terms:
        total = total + term[...].reshape(total.shape)
    table_products(total, inverse_ref, product_ref)
    for row in range(rows):
        sum_ref[pl.ds(row * n_rhs, n_rhs), :] = product_ref[diags(row) * rows + row]


def arrived_blocks_of(sizes, width_k, place_ref, field, arrived_ref):
    rows, n_rows, cap, n_tiles, n_rhs = sizes
    per = n_rows * cap // arrived_ref.shape[0]

    def fetch(row):
        total = None
        for k in range(width_k):
            slot = place_ref[0, 0, (field + k) * rows + row]
            start = pl.multiple_of(below(slot, per) * n_rhs, n_rhs)
            block = arrived_ref[over(slot, per), pl.ds(start, n_rhs), :]
            total = block if total is None else total + block
        return total

    return fetch


def solve_kernel(sizes, width_k, n_band, field, *refs):
    metadata_in, arrived_ref, inverse_ref = refs[:2], *refs[2:4]
    terms_in, refs = refs[4 : 5 + n_band], refs[5 + n_band :]
    out_ref, metadata, sum_ref, product_ref = refs[0], refs[1:3], *refs[3:5]
    place_ref, index_ref = metadata
    terms, (term_sems, meta_sems) = refs[5 : 6 + n_band], refs[6 + n_band :]
    rows = sizes[0]
    metadata = copies_of(zip(metadata_in, metadata), meta_sems)
    later = copies_of(zip(terms_in, terms), term_sems)
    finish(metadata)
    fetch = arrived_blocks_of(sizes, width_k, place_ref, field, arrived_ref)

    def diags(row):
        return index_ref[0, 0, rows + row]

    gather_solve(sizes, fetch, diags, later, terms, inverse_ref, sum_ref, product_ref)
    out_ref[...] = sum_ref[...].reshape(out_ref.shape)


def pack_kernel(sizes, width_k, n_band, *refs):
    rows, n_rows, cap, n_tiles, n_rhs = sizes
    list_in, near_in, first_ref, tile_ref, send_out = refs[:5]
    band_out, refs = refs[5 : 5 + n_band], refs[5 + n_band :]
    list_ref, near_ref, product_ref, send_ref = refs[:4]
    band_refs, (meta_sems, send_sems) = refs[4 : 4 + n_band], refs[4 + n_band :]
    list_in = list_in.at[:, :, pl.ds(0, LANES)]
    metadata = copies_of(((list_in, list_ref), (near_in, near_ref)), meta_sems)
    table_products(first_ref[...].reshape(rows * n_rhs, -1), tile_ref, product_ref)
    finish(metadata)
    pack_bands(sizes, width_k, product_ref, near_ref, band_refs)
    for owner in range(n_rows):
        for rank in range(cap):
            block = product_ref[below(list_ref[owner, 0, rank], rows * n_tiles)]
            send_ref[owner, rank * n_rhs : (rank + 1) * n_rhs, :] = block
    finish(copies_of(zip((send_ref, *band_refs), (send_out, *band_out)), send_sems))


def own_kernel(sizes, width_k, *refs):
    rows, n_rows, cap, n_tiles, n_rhs = sizes
    metadata_in, first_ref, tile_ref, extra = list(refs[:2]), *refs[2:4], refs[4:8]
    send_out, band_out, metadata, product_ref, send_ref, band_ref = refs[8], refs[9], refs[10:12], *refs[12:15]
    held, value_ref, spread_ref, result_ref, meta_sems, load_sems, send_sems = refs[15:19], *refs[19:]
    list_ref, near_ref = metadata
    metadata_in[0] = metadata_in[0].at[:, :, pl.ds(0, LANES)]
    metadata = copies_of(zip(metadata_in, metadata), meta_sems)
    fetched = copies_of(zip(extra, held), load_sems)
    table_products(first_ref[...].reshape(rows * n_rhs, -1), tile_ref, product_ref)
    finish(metadata)
    copies = []

    def send(source, target):
        copies.extend(started([pltpu.make_async_copy(source, target, send_sems.at[len(copies)])]))

    pack_bands(sizes, width_k, product_ref, near_ref, (band_ref,))
    send(band_ref, band_out)
    body, half = cap * n_rhs, n_rows // 2
    upper = lax.axis_index("rows") >= half
    mine, others = jnp.where(upper, half, 0), jnp.where(upper, 0, half)
    finish(fetched[:1])
    functional_ref, count_ref, place_ref, partial_ref = held
    n_blocks = n_rows * cap + rows
    n_func = spread_ref.shape[0] // n_blocks
    n_diag = functional_ref.shape[0] // n_func

    def spread(done, blocks, kinds):
        spread_values(n_rhs, n_func, functional_ref, blocks, kinds, value_ref, spread_ref, done)

    kinds = [near_ref[0, 0, rows + row] for row in range(rows)]
    spread(n_rows * cap, band_ref[...].reshape(rows * n_rhs, -1), kinds)
    kinds = []
    for order in range(n_rows):
        owner = order % half + (mine if order < half else others)
        for rank in range(cap):
            code = list_ref[owner, 0, rank]
            kinds.append(below(over(code, rows * n_tiles * rows), n_diag))
            block = product_ref[below(code, rows * n_tiles)]
            send_ref[order, rank * n_rhs : (rank + 1) * n_rhs, :] = block
        if order < half:
            send(send_ref.at[order], send_out.at[order, pl.ds(0, body)])
        if order % 2:
            blocks = jnp.concatenate([send_ref[order - 1], send_ref[order]], axis=0)
            spread((order - 1) * cap, blocks, kinds)
            kinds = []
    finish(fetched[1:])
    result = coarse_parts(n_rhs, n_blocks, count_ref, place_ref, partial_ref, spread_ref)
    result_ref[...] = result.reshape(result_ref.shape)
    depth = result_ref.shape[1]
    for n, first in enumerate((mine, others)):
        target = send_out.at[:, pl.ds(body + n * depth, depth)]
        send(result_ref.at[pl.ds(first, half)], target)
    finish(copies)


def mirror_kernel(
    sizes, list_in, mirror_ref, tile_ref, inverse_ref, send_out, list_ref, product_ref, block_ref, solved_ref, send_ref, sems
):
    rows, n_rows, cap, n_tiles, n_rhs = sizes
    half, n_diag = n_rows // 2, inverse_ref.shape[0]
    base = jnp.where(lax.axis_index("rows") >= half, half, 0)
    list_in = list_in.at[pl.ds(base, half), :, pl.ds(0, LANES)]
    metadata = started([pltpu.make_async_copy(list_in, list_ref, sems.at[half])])
    table_products(mirror_ref[...].reshape(rows * n_rhs, -1), tile_ref, product_ref)
    finish(metadata)
    codes = [list_ref[n // cap, 0, LANES // 2 + n % cap] for n in range(half * cap)]
    for n, code in enumerate(codes):
        block_ref[n] = product_ref[below(code, rows * n_tiles)]
    values = block_ref[...].reshape(half * cap * n_rhs, -1)
    table_products(values, inverse_ref, solved_ref)
    copies = []
    for n, code in enumerate(codes):
        device, rank = n // cap, n % cap
        kind = below(over(code, rows * n_tiles * rows), n_diag)
        send_ref[device, rank * n_rhs : (rank + 1) * n_rhs, :] = solved_ref[kind * len(codes) + n]
        if rank == cap - 1:
            copy = pltpu.make_async_copy(send_ref.at[device], send_out.at[device], sems.at[device])
            copies += started([copy])
    finish(copies)


def coarse_parts(n_rhs, n_blocks, count_ref, place_ref, partial_ref, spread_ref):
    n_func = spread_ref.shape[0] // n_blocks
    values = [
        spread_ref[pl.ds(t, n_blocks, stride=n_func), :] for t in range(count_ref.shape[1] // n_blocks)
    ]
    values = jnp.concatenate(values, axis=0)
    partial = jnp.dot(
        count_ref[...], jnp.concatenate(halves(values), axis=1), preferred_element_type=jnp.float32
    )
    partial = partial[:, :LANES] + partial[:, LANES:] + partial_ref[...]
    shift = LANES // 2
    while shift >= n_rhs:
        partial = partial + pltpu.roll(partial, shift, axis=1)
        shift //= 2
    return place(place_ref, partial, n_rhs, 2)


def part_kernel(arrived_ref, keep_ref, give_ref):
    depth = keep_ref.shape[0] // 2
    body = arrived_ref.shape[1] - 4 * depth
    total = arrived_ref[0, body:, :]
    for source in range(1, arrived_ref.shape[0]):
        total = total + arrived_ref[source, body:, :]
    lower = lax.axis_index("band") == 0
    for n in range(2):
        zero, one = (total[(2 * n + m) * depth : (2 * n + m + 1) * depth] for m in range(2))
        keep_ref[n * depth : (n + 1) * depth] = jnp.where(lower, zero, one)
        give_ref[n * depth : (n + 1) * depth] = jnp.where(lower, one, zero)


def half_blocks_of(sizes, width_k, place_ref, arrived_ref, far):
    rows, n_rows, cap, n_tiles, n_rhs = sizes

    def fetch(row):
        total = None
        for k in range(width_k):
            slot = place_ref[0, 0, k * rows + row]
            holder, slot = over(slot, 2 * cap), below(slot, 2 * cap)
            start = pl.ds(pl.multiple_of(below(slot, cap) * n_rhs, n_rhs), n_rhs)
            mine = slot >= cap if far else slot < cap
            block = jnp.where(mine, arrived_ref[holder, start, :], 0.0)
            total = block if total is None else total + block
        return total

    return fetch


def base_kernel(sizes, width_k, *refs):
    metadata_in, own_ref, inverse_ref, terms_in, out_ref = refs[:2], *refs[2:4], refs[4:6], refs[6]
    metadata, sum_ref, product_ref, terms, term_sems, meta_sems = refs[7:9], *refs[9:11], refs[11:13], *refs[13:]
    place_ref, index_ref = metadata
    rows = sizes[0]
    metadata = copies_of(zip(metadata_in, metadata), meta_sems)
    later = copies_of(zip(terms_in, terms), term_sems)
    finish(metadata)
    fetch = half_blocks_of(sizes, width_k, place_ref, own_ref, False)

    def diags(row):
        return index_ref[0, 0, rows + row]

    gather_solve(sizes, fetch, diags, later, terms, inverse_ref, sum_ref, product_ref)
    out_ref[...] = sum_ref[...].reshape(out_ref.shape)


def final_kernel(sizes, width_k, *refs):
    place_in, mirror_ref, base_ref, near_ref, far_ref, scale_ref, out_ref, place_ref, sem = refs
    rows, n_rows, cap, n_tiles, n_rhs = sizes
    metadata = pltpu.make_async_copy(place_in, place_ref, sem)
    metadata.start()
    depth = scale_ref.shape[0]
    correction = (near_ref[...] + far_ref[...]) / scale_ref[...]
    padded = jnp.concatenate([correction, jnp.zeros((8 - depth, LANES), jnp.float32)], axis=0)
    turned = padded.T
    metadata.wait()
    fetch = half_blocks_of(sizes, width_k, place_ref, mirror_ref, True)
    for row in range(rows):
        spot, place = row // depth, row % depth
        column = turned[spot * n_rhs : (spot + 1) * n_rhs, place : place + 1]
        out_ref[row] = (base_ref[row] + column) + fetch(row)


def shifted(value, axis, steps):
    count = lax.axis_size(axis)
    initial, last = (max(0, -steps), min(count, count - steps))
    return lax.ppermute(value, axis, [(source, source + steps) for source in range(initial, last)])


def to_bands(sends):
    if len(sends) == 1:
        return (lax.ppermute(sends[0], "band", [(0, 1), (1, 0)]),)
    return shifted(sends[0], "band", 1), shifted(sends[1], "band", -1)


def on_device(
    start_iterate,
    right_side,
    diag_table,
    inverse_table,
    coupling_tiles,
    diag_index,
    tile_index,
    source_owner,
    source_local,
    aggregate_map,
):
    rows, n_rhs, states = start_iterate.shape
    width_k = source_owner.shape[1]
    n_tiles, n_diag = coupling_tiles.shape[0], inverse_table.shape[0]
    n_rows, n_bands = lax.axis_size("rows"), lax.axis_size("band")
    n_dev = n_rows * n_bands
    cap = max(2, 2 * width_k * rows // n_rows)
    slots = n_rows * cap
    total_groups = AGG_DEV * n_dev
    per_tile = LANES // n_rhs
    depth = rows // per_tile
    n_func = 16
    dense = (
        n_bands == 2
        and n_dev * rows * total_groups <= DENSE_LIMIT
        and depth == 4
        and n_diag * n_func == LANES
        and n_tiles + 2 <= n_func
    )
    sizes = (rows, n_rows, cap, n_tiles, n_rhs)
    f32, i32 = jnp.float32, jnp.int32
    my_band = lax.axis_index("band")
    my_row = lax.axis_index("rows")

    half = n_rows // 2
    wide = -(-(4 + 2 * width_k) * rows // LANES) * LANES
    place_wide = -(-2 * width_k * rows // LANES) * LANES
    index_shapes = [(width_k, rows), (width_k, rows), (width_k + 2, rows), (1, rows), (1, rows)]
    halves_of_rows = [list(range(half)), list(range(half, n_rows))]
    to_mirror = [(i, (i + half) % n_rows) for i in range(n_rows)]
    mirror = lax.ppermute(start_iterate, "rows", to_mirror)
    lists, index, places = call(
        functools.partial(request_kernel, (rows, n_rows, cap, n_tiles, n_diag)),
        (
            jax.ShapeDtypeStruct((n_rows, 1, LANES + wide), i32),
            jax.ShapeDtypeStruct((1, 1, wide), i32),
            jax.ShapeDtypeStruct((1, 1, place_wide), i32),
        ),
        [HBM] * 5,
        [VMEM] * 3,
        [*[pltpu.VMEM(shape, i32) for shape in index_shapes], pltpu.SemaphoreType.DMA((5,))],
    )(source_owner.T, source_local.T, tile_index.T, diag_index[None], aggregate_map.T)
    lists = lax.all_to_all(lists, "rows", split_axis=0, concat_axis=0, tiled=True)
    if n_bands == 2:
        near = lax.ppermute(index, "band", [(0, 1), (1, 0)])
    else:
        ways = [[(b, (b + step) % n_bands) for b in range(n_bands)] for step in (-1, 1)]
        near = jnp.concatenate([lax.ppermute(index, "band", way) for way in ways], axis=0)

    n_ways = 1 if n_bands == 2 else 2
    block = (rows, n_rhs, states)
    band_shapes = [jax.ShapeDtypeStruct(block, f32)] * n_ways
    band_scratch = [pltpu.VMEM(block, f32)] * n_ways
    term_scratch = [pltpu.VMEM(block, f32)] * (1 + n_ways)
    term_sems = pltpu.SemaphoreType.DMA((1 + n_ways,))
    list_scratch = pltpu.SMEM((half, 1, LANES), i32)
    near_scratch = pltpu.SMEM((n_ways, 1, wide), i32)
    row_scratch = [pltpu.SMEM((1, 1, place_wide), i32), pltpu.SMEM((1, 1, wide), i32)]
    flat = rows * n_rhs
    sums = pltpu.VMEM((flat, states), f32)
    products = pltpu.VMEM((max(n_tiles, n_diag) * rows, n_rhs, states), f32)
    work = 6 * flat * states * states
    made_shape = (n_tiles * rows, n_rhs, states)
    table_scratch = [pltpu.VMEM(coupling_tiles.shape, f32)]
    table_sems = pltpu.SemaphoreType.DMA((-(-n_tiles // 2),))
    made = call(
        product_kernel,
        jax.ShapeDtypeStruct(made_shape, f32),
        [HBM, HBM],
        HBM,
        [
            pltpu.VMEM(block, f32),
            *table_scratch,
            pltpu.VMEM(made_shape, f32),
            pltpu.SemaphoreType.DMA((1 + n_tiles,)),
            table_sems,
        ],
        work * n_tiles,
        4 << 20,
    )(start_iterate, coupling_tiles)
    packed, *bands = call(
        functools.partial(first_kernel, sizes, width_k, n_ways),
        (jax.ShapeDtypeStruct((half, 2 * cap, n_rhs, states), f32), *band_shapes),
        [HBM, VMEM, VMEM, ANY, ANY],
        [HBM] * (1 + n_ways),
        [
            pltpu.VMEM((2, *made_shape), f32),
            list_scratch,
            near_scratch,
            pltpu.VMEM((half, 2 * cap, n_rhs, states), f32),
            *band_scratch,
            pltpu.SemaphoreType.DMA((n_tiles,)),
            pltpu.SemaphoreType.DMA((2,)),
            pltpu.SemaphoreType.DMA((2 * half + n_ways,)),
        ],
        work * n_tiles,
        4 << 20,
    )(made, mirror, coupling_tiles, lists, near)
    packed, late = lax.optimization_barrier((packed, lists))
    if dense:
        across = lax.ppermute(late, "band", [(0, 1), (1, 0)])
        across, *bands = lax.optimization_barrier((across, *bands))
    sends = (packed.reshape(half, 2 * cap * n_rhs, states), *bands)
    halves_of_rows = [list(range(half)), list(range(half, n_rows))]
    def exchange(sends, groups=None):
        arrived = lax.all_to_all(
            sends[0], "rows", split_axis=0, concat_axis=0, tiled=True, axis_index_groups=groups
        )
        return arrived, to_bands(sends[1:])

    arrived_blocks, arrived_bands = exchange(sends, halves_of_rows)

    if dense:
        fields = jnp.stack([late, across])[:, :, 0, LANES:]
        fields = fields.reshape(2, n_rows, -1, rows).transpose(2, 0, 1, 3)
        fields = fields.reshape(-1, 2, n_rows * rows)
        n_blocks = slots + rows
        length = n_dev * depth
        extra_shapes = [
            ((n_diag * n_func, 3 * states), jnp.bfloat16),
            ((total_groups, (n_tiles + 1) * n_blocks), jnp.bfloat16),
            ((per_tile * length, total_groups), jnp.bfloat16),
            ((total_groups, LANES), f32),
        ]
        functional_shape, count_shape, placing_shape, partial_shape = extra_shapes
        counts, functionals, placing, partial, scale = call(
            functools.partial(count_kernel, sizes, width_k, n_func),
            (
                jax.ShapeDtypeStruct(*count_shape),
                jax.ShapeDtypeStruct(*functional_shape),
                jax.ShapeDtypeStruct(*placing_shape),
                jax.ShapeDtypeStruct(*partial_shape),
                jax.ShapeDtypeStruct((depth, LANES), f32),
            ),
            [ANY, HBM] + [VMEM] * 5,
            [HBM] * 4 + [VMEM],
            [
                pltpu.VMEM(*count_shape),
                pltpu.VMEM(*functional_shape),
                pltpu.VMEM(*placing_shape),
                pltpu.VMEM(*partial_shape),
                row_scratch[1],
                pltpu.VMEM(block, f32),
                pltpu.VMEM((n_diag * n_func, flat), f32),
                pltpu.VMEM((rows * n_func, LANES), f32),
                pltpu.SemaphoreType.DMA((2,)),
                pltpu.SemaphoreType.DMA((4,)),
            ],
            4 * total_groups * n_tiles * n_dev * rows * n_blocks,
            4 << 20,
        )(
            index, right_side, fields, late[:, 0, :LANES], coupling_tiles, diag_table, inverse_table
        )
        extra_scratch = [
            *[pltpu.VMEM(*shape) for shape in extra_shapes],
            pltpu.VMEM((n_diag * n_func, n_blocks * n_rhs), f32),
            pltpu.VMEM((n_blocks * n_func, LANES), f32),
            pltpu.VMEM((n_rows, n_bands * depth, LANES), f32),
        ]

        made = (arrived_blocks, functionals, counts, placing, partial, scale)
        made = lax.optimization_barrier(made)
        arrived_blocks, functionals, counts, placing, partial, scale = made

    def solve(field, arrived, bands):
        return call(
            functools.partial(solve_kernel, sizes, width_k, n_ways, field),
            jax.ShapeDtypeStruct(block, f32),
            [ANY] * 2 + [VMEM] * 2 + [HBM] + [ANY] * n_ways,
            VMEM,
            [
                *row_scratch,
                sums,
                products,
                *term_scratch,
                term_sems,
                pltpu.SemaphoreType.DMA((2,)),
            ],
            work * n_diag,
            4 << 20,
        )(places, index, arrived, inverse_table, right_side, *bands)

    first = solve(0, arrived_blocks, arrived_bands)
    body = cap * n_rhs
    full_list = pltpu.SMEM((n_rows, 1, LANES), i32)
    if dense:
        mirror = lax.ppermute(first, "rows", to_mirror)
        own, band = call(
            functools.partial(own_kernel, sizes, width_k),
            (
                jax.ShapeDtypeStruct((half, body + 2 * n_bands * depth, states), f32),
                jax.ShapeDtypeStruct(block, f32),
            ),
            [ANY] * 2 + [VMEM] * 2 + [HBM] * 4,
            [HBM] * 2,
            [
                full_list,
                near_scratch,
                products,
                pltpu.VMEM((n_rows, body, states), f32),
                pltpu.VMEM(block, f32),
                *extra_scratch,
                pltpu.SemaphoreType.DMA((2,)),
                pltpu.SemaphoreType.DMA((4,)),
                pltpu.SemaphoreType.DMA((half + 3,)),
            ],
            2 * work * n_tiles,
            4 << 20,
        )(lists, near, first, coupling_tiles, functionals, counts, placing, partial)
        own, (band,) = exchange((own, band), halves_of_rows)
        packed = call(
            functools.partial(mirror_kernel, sizes),
            jax.ShapeDtypeStruct((half, body, states), f32),
            [ANY] + [VMEM] * 3,
            HBM,
            [
                list_scratch,
                products,
                pltpu.VMEM((half * cap, n_rhs, states), f32),
                pltpu.VMEM((n_diag * half * cap, n_rhs, states), f32),
                pltpu.VMEM((half, body, states), f32),
                pltpu.SemaphoreType.DMA((half + 1,)),
            ],
            BEHIND_SWAP * work * n_tiles,
            4 << 20,
        )(lists, mirror, coupling_tiles, inverse_table)
        packed, band = lax.optimization_barrier((packed, band))
        swapped = lax.all_to_all(
            packed, "rows", split_axis=0, concat_axis=0, tiled=True, axis_index_groups=halves_of_rows
        )
        part = jax.ShapeDtypeStruct((2 * depth, LANES), f32)
        keep, give = call(part_kernel, (part, part), [VMEM], [VMEM] * 2)(own)
        keep = keep + lax.ppermute(give, "band", [(0, 1), (1, 0)])
        far = lax.ppermute(keep[depth:], "rows", to_mirror)
        base = call(
            functools.partial(base_kernel, sizes, width_k),
            jax.ShapeDtypeStruct(block, f32),
            [ANY] * 2 + [VMEM] * 2 + [HBM, ANY],
            VMEM,
            [
                *row_scratch,
                sums,
                products,
                *term_scratch,
                term_sems,
                pltpu.SemaphoreType.DMA((2,)),
            ],
            work * n_diag,
            4 << 20,
        )(places, index, own, inverse_table, right_side, band)
        return call(
            functools.partial(final_kernel, sizes, width_k),
            jax.ShapeDtypeStruct(block, f32),
            [ANY] + [VMEM] * 5,
            VMEM,
            [row_scratch[0], pltpu.SemaphoreType.DMA],
            0,
            4 << 20,
        )(places, swapped, base, keep[:depth], far, scale)

    sends = call(
        functools.partial(pack_kernel, sizes, width_k, n_ways),
        (jax.ShapeDtypeStruct((n_rows, body, states), f32), *band_shapes),
        [ANY] * 2 + [VMEM] * 2,
        [HBM] * (1 + n_ways),
        [
            full_list,
            near_scratch,
            products,
            pltpu.VMEM((n_rows, body, states), f32),
            *band_scratch,
            pltpu.SemaphoreType.DMA((2,)),
            pltpu.SemaphoreType.DMA((1 + n_ways,)),
        ],
        work * n_tiles,
        4 << 20,
    )(lists, near, first, coupling_tiles)
    arrived_blocks, arrived_bands = exchange(sends)
    second = solve(width_k, arrived_blocks, arrived_bands)

    groups = aggregate_map[:, 0]
    own = jnp.arange(rows, dtype=i32)
    index_all = lax.all_gather(index, ("band", "rows"), axis=0, tiled=True)
    index_all = index_all.reshape(n_bands, n_rows, wide)
    groups_all, diags_all = index_all[:, :, :rows], index_all[:, :, rows : 2 * rows]
    codes = lists[:, 0, :cap]
    asked = jnp.arange(n_rows, dtype=i32)[:, None] * rows + codes // (rows * n_tiles) % rows
    asked = jnp.where(codes > 0, asked, -1).reshape(-1)
    table_sums = jnp.sum(diag_table, axis=(1, 2))
    diag_onehot = diags_all.reshape(-1, 1) == jnp.arange(n_diag, dtype=i32)[None]
    block_sums = jnp.sum(jnp.where(diag_onehot, table_sums[None], 0.0), axis=1)
    whole_diag = jnp.sum(
        jnp.where(groups[:, None] == groups_all.reshape(-1)[None], block_sums[None], 0.0), axis=1
    )
    above, below = near[0, 0], near[-1, 0]
    place_of = (2 + width_k) * rows
    band_tiles = jnp.stack([above[place_of : place_of + rows], below[place_of + rows : place_of + 2 * rows]])
    band_groups = jnp.stack([above[:rows], below[:rows]])
    band_valid = jnp.stack([my_band + 1 < n_bands, my_band > 0])
    band_valid = jnp.broadcast_to(band_valid[:, None], (2, rows))
    n_all = n_tiles + n_diag + 1
    code = codes.reshape(-1)
    band_of_mine = lax.dynamic_index_in_dim(groups_all, my_band, 0, keepdims=False).reshape(-1)
    entry_group = jnp.concatenate(
        [jnp.take(band_of_mine, jnp.maximum(asked, 0)), band_groups.reshape(-1), groups, groups]
    )
    entry_func = jnp.concatenate(
        [
            (code % rows) * n_all + (code // rows) % n_tiles,
            (own[None] * n_all + band_tiles).reshape(-1),
            own * n_all + n_tiles + diag_index,
            own * n_all + n_tiles + n_diag,
        ]
    )
    entry_valid = jnp.concatenate([asked >= 0, band_valid.reshape(-1), jnp.ones((2 * rows,), bool)])
    functionals = jnp.concatenate(
        [jnp.sum(coupling_tiles, axis=1), -jnp.sum(diag_table, axis=1)], axis=0
    )
    weights = jnp.einsum("fp,rcp->rfc", functionals, second, precision=HIGH)
    weights = jnp.concatenate([weights, jnp.sum(right_side, axis=2)[:, None]], axis=1)
    chosen = jnp.take(weights.reshape(rows * n_all, n_rhs), entry_func, axis=0)
    chosen = jnp.where(entry_valid[:, None], chosen, 0.0)
    partial = jax.ops.segment_sum(chosen, entry_group, num_segments=total_groups)
    whole = lax.psum(partial, ("band", "rows"))
    correction = jnp.take(whole, groups, axis=0) / whole_diag[:, None]
    return second + correction[:, :, None]


def solution(mesh):
    in_specs = (
        P(("band", "rows"), None, None),
        P(("band", "rows"), None, None),
        P(),
        P(),
        P(),
        P(("band", "rows")),
        P(("band", "rows"), None),
        P(("band", "rows"), None),
        P(("band", "rows"), None),
        P(("band", "rows"), None),
    )
    out_specs = P(("band", "rows"), None, None)
    return jax.shard_map(
        on_device, mesh=mesh, in_specs=in_specs, out_specs=out_specs, check_vma=False
    )
```

```python
import functools

import jax
import jax.numpy as jnp
from jax import lax
from jax.experimental import pallas as pl
from jax.experimental.pallas import tpu as pltpu
from jax.sharding import PartitionSpec as P

AGG_DEV = 8
LANES = 128
DENSE_LIMIT = 1 << 19
BEHIND_SWAP = 100

VMEM = pl.BlockSpec(memory_space=pltpu.VMEM)
SMEM = pl.BlockSpec(memory_space=pltpu.SMEM)
HBM = pl.BlockSpec(memory_space=pltpu.HBM)
ANY = pl.BlockSpec(memory_space=pl.ANY)
HIGH = lax.Precision.HIGHEST


def params():
    return pltpu.CompilerParams(vmem_limit_bytes=24 * 1024 * 1024)


def call(kernel, out_shape, in_specs, out_specs, scratch=(), flops=0, moved=0):
    def shaped(shape, spec):
        return pltpu.HBM(shape.shape, shape.dtype) if spec is HBM else shape

    if isinstance(out_shape, (tuple, list)):
        out_shape = [shaped(*pair) for pair in zip(out_shape, out_specs)]
    else:
        out_shape = shaped(out_shape, out_specs)
    run = pl.pallas_call(
        kernel,
        out_shape=out_shape,
        in_specs=in_specs,
        out_specs=out_specs,
        scratch_shapes=list(scratch),
        compiler_params=params(),
        cost_estimate=pl.CostEstimate(flops=flops, bytes_accessed=moved, transcendentals=0),
    )

    def apply(*args):
        pinned = [
            pltpu.with_memory_space_constraint(arg, pltpu.HBM) if spec is HBM else arg
            for arg, spec in zip(args, in_specs)
        ]
        return run(*pinned)

    return apply


def below(value, bound):
    return value & (bound - 1) if bound & (bound - 1) == 0 else lax.rem(value, bound)


def over(value, bound):
    if bound & (bound - 1) == 0:
        return lax.shift_right_logical(value, bound.bit_length() - 1)
    return lax.div(value, bound)


def halves(value):
    high = value.astype(jnp.bfloat16)
    low = (value - high.astype(jnp.float32)).astype(jnp.bfloat16)
    return high, low


def left_operand(value):
    high, low = halves(value)
    return jnp.concatenate([high, low, high], axis=1)


def right_operand(value):
    high, low = halves(value)
    return jnp.concatenate([high, high, low], axis=1)


def dot_nt(left, right):
    return lax.dot_general(
        left, right, (((1,), (1,)), ((), ())), preferred_element_type=jnp.float32
    )


def table_products(value, table_ref, out_ref, done=None, loads=None):
    left = left_operand(value)
    count, width = table_ref.shape[0], table_ref.shape[1]
    n_rhs = out_ref.shape[1]
    rows = left.shape[0] // n_rhs
    for first in range(0, count, 2):
        last = min(first + 2, count)
        if loads is not None:
            loads[first // 2].wait()
        right = right_operand(table_ref[first:last].reshape((last - first) * width, -1))
        product = dot_nt(left, right)
        for t in range(first, last):
            part = product[:, (t - first) * width : (t - first + 1) * width]
            out_ref[t * rows : (t + 1) * rows] = part.reshape(rows, n_rhs, width)
        if done is not None:
            done(first * rows, (last - first) * rows)


def started(copies):
    for copy in copies:
        copy.start()
    return copies


def finish(copies):
    for copy in copies:
        copy.wait()


def request_kernel(sizes, *refs):
    rows, n_rows, cap, n_tiles, n_diag = sizes
    inputs, (list_ref, index_ref, place_ref), held, sems = refs[:5], refs[5:8], refs[8:13], refs[13]
    finish(
        started([pltpu.make_async_copy(i, h, sems.at[n]) for n, (i, h) in enumerate(zip(inputs, held))])
    )
    owner_ref, local_ref, tile_ref, diag_ref, group_ref = held
    width_k = owner_ref.shape[0]
    half = n_rows // 2
    row_of = lax.broadcasted_iota(jnp.int32, (rows, rows), 0)
    col_of = lax.broadcasted_iota(jnp.int32, (rows, rows), 1)
    lane = lax.broadcasted_iota(jnp.int32, (rows, LANES), 1)
    owners = lax.broadcasted_iota(jnp.int32, (n_rows, rows), 0)

    def column(row):
        return jnp.sum(jnp.where(row_of == col_of, row, 0), axis=1, keepdims=True)

    def owner_row(k):
        return owner_ref[k : k + 1, :]

    row_ids = lax.broadcasted_iota(jnp.int32, (1, rows), 1)
    owner_columns = [column(owner_row(k)) for k in range(width_k)]
    lists = jnp.zeros((n_rows, LANES), jnp.float32)
    places, half_places = [], []
    for k in range(width_k):
        rank = jnp.zeros((1, rows), jnp.int32)
        for other in range(k + 1):
            match = owner_columns[other] == owner_row(k)
            if other == k:
                match = match & (row_of < col_of)
            rank = rank + jnp.sum(jnp.where(match, 1, 0), axis=0, keepdims=True)
        places.append(owner_row(k) * cap + rank)
        same = (owner_row(k) >= half) == (lax.axis_index("rows") >= half)
        holder = jnp.where(owner_row(k) >= half, owner_row(k) - half, owner_row(k))
        half_places.append(holder * (2 * cap) + rank + jnp.where(same, 0, cap))
        taker = row_ids + rows * (diag_ref[...] + n_diag)
        code = local_ref[k : k + 1, :] + rows * (tile_ref[k : k + 1, :] + n_tiles * taker)
        code, rank = column(code), column(rank)
        mirror = jnp.where(owner_row(k) >= half, owner_row(k) - half, owner_row(k) + half)
        for owner, base in ((owner_row(k), 0), (mirror, LANES // 2)):
            by_rank = jnp.where(lane == rank + base, code, 0).astype(jnp.float32)
            mine = jnp.where(owners == owner, 1.0, 0.0)
            lists = lists + jnp.dot(
                mine, by_rank, precision=HIGH, preferred_element_type=jnp.float32
            )
    lists = (lists + 0.5).astype(jnp.int32)

    def joined(parts, wide):
        spare = wide - len(parts) * rows
        if spare:
            parts = [*parts, jnp.zeros((1, spare), jnp.int32)]
        return jnp.concatenate(parts, axis=1)

    index = [group_ref[...], diag_ref[...]]
    index += [tile_ref[k : k + 1, :] for k in range(width_k + 2)]
    index += [owner_row(k) * rows + local_ref[k : k + 1, :] for k in range(width_k)]
    index = joined(index, index_ref.shape[2])
    index_ref[0] = index
    place_ref[0] = joined(half_places + places, place_ref.shape[2])
    for device in range(n_rows):
        list_ref[device] = jnp.concatenate([lists[device : device + 1, :], index], axis=1)


def copies_of(pairs, sems):
    return started([pltpu.make_async_copy(i, h, sems.at[n]) for n, (i, h) in enumerate(pairs)])


def band_field(rows, width_k, way, n_ways):
    field = (2 + width_k) * rows
    if n_ways == 1:
        return field + jnp.where(lax.axis_index("band") == 0, 0, rows)
    return field + way * rows


def pack_bands(sizes, width_k, product_ref, near_ref, band_refs):
    rows = sizes[0]
    for way, band_ref in enumerate(band_refs):
        field = band_field(rows, width_k, way, len(band_refs))
        for row in range(rows):
            band_ref[row] = product_ref[near_ref[way, 0, field + row] * rows + row]


def table_loads(table_in, table_ref, sems):
    copies = []
    for first in range(0, table_in.shape[0], 2):
        place = pl.ds(first, min(2, table_in.shape[0] - first))
        source, target = table_in.at[place], table_ref.at[place]
        copies.append(pltpu.make_async_copy(source, target, sems.at[first // 2]))
    return started(copies)


def product_kernel(start_in, tile_in, product_ref, start_ref, tile_ref, start_sem, tile_sems):
    start = pltpu.make_async_copy(start_in, start_ref, start_sem)
    start.start()
    loads = table_loads(tile_in, tile_ref, tile_sems)
    start.wait()
    rows, n_rhs, states = start_ref.shape
    values = start_ref[...].reshape(rows * n_rhs, states)
    table_products(values, tile_ref, product_ref, None, loads)


def first_kernel(sizes, width_k, n_band, *refs):
    rows, n_rows, cap, n_tiles, n_rhs = sizes
    own_ref, mirror_ref, tile_ref, list_in, near_in, send_out = refs[:6]
    band_out, refs = refs[6 : 6 + n_band], refs[6 + n_band :]
    product_ref, list_ref, near_ref, send_ref = refs[:4]
    band_refs, (meta_sems, send_sems) = refs[4 : 4 + n_band], refs[4 + n_band :]
    half = n_rows // 2
    base = jnp.where(lax.axis_index("rows") >= half, half, 0)
    list_in = list_in.at[pl.ds(base, half), :, pl.ds(0, LANES)]
    metadata = copies_of(((list_in, list_ref), (near_in, near_ref)), meta_sems)
    values = mirror_ref[...].reshape(rows * n_rhs, -1)
    table_products(values, tile_ref, product_ref)
    finish(metadata)
    copies = []
    for side, blocks_ref in ((0, own_ref), (1, product_ref)):
        for device in range(half):
            for rank in range(cap):
                code = list_ref[device, 0, side * (LANES // 2) + rank]
                block = blocks_ref[below(code, rows * n_tiles)]
                send_ref[device, side * cap + rank] = block
            place = (device, pl.ds(side * cap, cap))
            copies += started(
                [pltpu.make_async_copy(send_ref.at[place], send_out.at[place], send_sems.at[len(copies)])]
            )
    pack_bands(sizes, width_k, own_ref, near_ref, band_refs)
    for ref, out in zip(band_refs, band_out):
        copies += started([pltpu.make_async_copy(ref, out, send_sems.at[len(copies)])])
    finish(copies)


def place(place_ref, values, n_rhs, n_parts):
    per_tile = LANES // n_rhs
    length = place_ref.shape[0] // per_tile
    parts, rest = [], values
    for _ in range(n_parts):
        part = rest.astype(jnp.bfloat16)
        rest = rest - part.astype(jnp.float32)
        parts.append(part)
    parts = jnp.concatenate(parts, axis=1)
    lane = lax.broadcasted_iota(jnp.int32, (length, LANES), 1)
    result = jnp.zeros((length, LANES), jnp.float32)
    placed = jnp.dot(place_ref[...], parts, preferred_element_type=jnp.float32)
    for spot in range(per_tile):
        chosen = placed[spot * length : (spot + 1) * length]
        chosen = sum(chosen[:, n * LANES : (n + 1) * LANES] for n in range(n_parts))
        result = jnp.where((lane >= spot * n_rhs) & (lane < (spot + 1) * n_rhs), chosen, result)
    return result


def spread_values(n_rhs, n_func, functional_ref, blocks, kinds, value_ref, spread_ref, done):
    per_tile = LANES // n_rhs
    lane = lax.broadcasted_iota(jnp.int32, (n_func, LANES), 1)
    columns = slice(done * n_rhs, done * n_rhs + blocks.shape[0])
    value_ref[:, columns] = dot_nt(functional_ref[...], right_operand(blocks))
    for block, kind in enumerate(kinds, done):
        tile, spot = block // per_tile, block % per_tile
        start = pl.multiple_of(kind * n_func, n_func)
        piece = value_ref[pl.ds(start, n_func), tile * LANES : (tile + 1) * LANES]
        piece = jnp.where((lane >= spot * n_rhs) & (lane < (spot + 1) * n_rhs), piece, 0.0)
        spread_ref[block * n_func : (block + 1) * n_func, :] = piece


def one_hot(ids, row):
    return jnp.where(ids == row, 1.0, 0.0).astype(jnp.bfloat16)


def count_kernel(sizes, width_k, n_func, *refs):
    rows, n_rows, cap, n_tiles, n_rhs = sizes
    index_in, right_in, field_ref, list_ref, tile_ref, table_ref, inverse_ref = refs[:7]
    count_out, functional_out, placing_out, partial_out, scale_ref = refs[7:12]
    count_ref, functional_ref, placing_ref, partial_ref = refs[12:16]
    index_ref, right_ref, value_ref, spread_ref, load_sems, sems = refs[16:]
    loads = copies_of(((index_in, index_ref), (right_in, right_ref)), load_sems)
    n_groups = count_ref.shape[0]
    slots, band_rows = n_rows * cap, n_rows * rows
    copies = []

    def send(source, target):
        copies.extend(started([pltpu.make_async_copy(source, target, sems.at[len(copies)])]))

    sums = jnp.sum(tile_ref[...], axis=1)
    line = lax.broadcasted_iota(jnp.int32, (n_func, sums.shape[1]), 0)
    sums = jnp.concatenate([sums, jnp.zeros((n_func - n_tiles, sums.shape[1]), jnp.float32)], axis=0)
    n_diag = inverse_ref.shape[0]
    totals = []
    for d in range(n_diag):
        minus = -jnp.sum(table_ref[d], axis=0, keepdims=True)
        totals.append(-jnp.sum(minus, axis=1, keepdims=True))
        wanted = jnp.where(line == n_tiles, minus, sums)
        high, low = halves(inverse_ref[d])
        right = jnp.concatenate([high, high, low], axis=0)
        solved = jnp.dot(left_operand(wanted), right, preferred_element_type=jnp.float32)
        solved = jnp.where(line == n_tiles + 1, 1.0, solved)
        functional_ref[d * n_func : (d + 1) * n_func, :] = left_operand(solved)
    send(functional_ref, functional_out)

    lists = list_ref[...]
    asker = lax.broadcasted_iota(jnp.int32, lists.shape, 0)
    codes = asker * rows + below(over(lists, rows * n_tiles), rows)
    codes = jnp.where(lists > 0, codes, -1).astype(jnp.float32)
    spread = lax.broadcasted_iota(jnp.int32, (slots, n_rows), 0)
    spread = lax.div(spread, cap) == lax.broadcasted_iota(jnp.int32, (slots, n_rows), 1)
    codes = jnp.dot(
        jnp.where(spread, 1.0, 0.0), codes, precision=HIGH, preferred_element_type=jnp.float32
    )
    rank = lax.rem(lax.broadcasted_iota(jnp.int32, codes.shape, 0), cap)
    lane = lax.broadcasted_iota(jnp.int32, codes.shape, 1)
    asked = jnp.sum(jnp.where(rank == lane, codes, 0.0), axis=1, keepdims=True)
    asked = jnp.where(asked < 0.0, asked - 0.5, asked + 0.5).astype(jnp.int32)
    low, high = asked[: slots // 2], asked[slots // 2 :]
    upper = lax.axis_index("rows") >= n_rows // 2
    asked = jnp.concatenate([jnp.where(upper, high, low), jnp.where(upper, low, high)], axis=0)
    own = lax.axis_index("rows") * rows + lax.broadcasted_iota(jnp.int32, (rows, 1), 0)
    band = lax.axis_index("band")

    def field(n, side):
        return field_ref[n, side : side + 1, :]

    row_ids = lax.broadcasted_iota(jnp.int32, (1, band_rows), 1)
    sides = []
    for side, targets in ((0, jnp.concatenate([asked, own], axis=0)), (1, own)):
        first = band == side
        across = jnp.where(first, field(2 + width_k, 1 - side), field(3 + width_k, 1 - side))
        takers = [field(2 + k, side) * n_groups + field(0, side) for k in range(width_k)]
        takers.append(across * n_groups + field(0, 1 - side))
        takers = jnp.concatenate(takers, axis=1)
        origins = [field(4 + width_k + k, side) for k in range(width_k)] + [row_ids]
        hits = one_hot(targets, jnp.concatenate(origins, axis=1))
        sides.append((takers, hits, field(0, side)))
    pieces, own_pieces = [], []
    ids = lax.broadcasted_iota(jnp.int32, (n_groups, band_rows), 0)
    for t in range(n_tiles + 1):
        found = []
        for takers, hits, groups in sides:
            if t < n_tiles:
                wide = lax.broadcasted_iota(jnp.int32, (n_groups, takers.shape[1]), 0)
                found.append(dot_nt(one_hot(wide + t * n_groups, takers), hits))
            else:
                found.append(dot_nt(one_hot(ids, groups), hits[:, -band_rows:]))
        pieces += [found[0][:, :slots], found[1]]
        own_pieces.append(found[0][:, slots:])
    count_ref[...] = jnp.concatenate(pieces, axis=1).astype(jnp.bfloat16)
    send(count_ref, count_out)

    own_counts = jnp.concatenate([*own_pieces, own_pieces[-1]], axis=1).astype(jnp.bfloat16)
    finish(loads)
    rights = right_ref[...].reshape(rows * n_rhs, -1)
    kinds = [index_ref[0, 0, rows + row] for row in range(rows)]
    spread_values(n_rhs, n_func, functional_ref, rights, kinds, value_ref, spread_ref, 0)
    values = [spread_ref[pl.ds(t, rows, stride=n_func), :] for t in range(n_tiles + 2)]
    values = jnp.concatenate(halves(jnp.concatenate(values, axis=0)), axis=1)
    partial = jnp.dot(own_counts, values, preferred_element_type=jnp.float32)
    partial_ref[...] = partial[:, :LANES] + partial[:, LANES:]
    send(partial_ref, partial_out)

    per_tile = LANES // n_rhs
    depth = rows // per_tile
    length = n_rows * 2 * depth
    order = lax.broadcasted_iota(jnp.int32, (per_tile * length, 1), 0)
    spot, order = lax.div(order, length), lax.rem(order, length)
    device, order = lax.div(order, 2 * depth), lax.rem(order, 2 * depth)
    side, order = lax.div(order, depth), lax.rem(order, depth)
    order = side * band_rows + device * rows + spot * depth + order
    member = [
        one_hot(ids, jnp.where(band == which, field(0, 0), field(0, 1))) for which in range(2)
    ]
    placing = jnp.zeros(placing_ref.shape, jnp.float32)
    for which in range(2):
        placing = placing + dot_nt(one_hot(order, row_ids + which * band_rows), member[which])
    placing_ref[...] = placing.astype(jnp.bfloat16)
    send(placing_ref, placing_out)
    whole = jnp.zeros((n_groups, 1), jnp.float32)
    for side in range(2):
        sums = jnp.zeros((1, band_rows), jnp.float32)
        for d in range(n_diag):
            sums = jnp.where(field(1, side) == d, totals[d], sums)
        weighted = jnp.where(ids == field(0, side), sums, 0.0)
        whole = whole + jnp.sum(weighted, axis=1, keepdims=True)
    scale = place(placing_ref, jnp.broadcast_to(whole, (n_groups, LANES)), n_rhs, 3)
    mine = jnp.zeros(scale_ref.shape, jnp.float32)
    here = lax.axis_index("rows") * 2 + band
    for n in range(2 * n_rows):
        mine = jnp.where(here == n, scale[n * depth : (n + 1) * depth, :], mine)
    scale_ref[...] = mine
    finish(copies)


def gather_solve(sizes, fetch, diags, later, terms, inverse_ref, sum_ref, product_ref):
    rows, n_rows, cap, n_tiles, n_rhs = sizes
    for row in range(rows):
        sum_ref[pl.ds(row * n_rhs, n_rhs), :] = fetch(row)
    finish(later)
    total = sum_ref[...]
    for term in terms:
        total = total + term[...].reshape(total.shape)
    table_products(total, inverse_ref, product_ref)
    for row in range(rows):
        sum_ref[pl.ds(row * n_rhs, n_rhs), :] = product_ref[diags(row) * rows + row]


def arrived_blocks_of(sizes, width_k, place_ref, field, arrived_ref):
    rows, n_rows, cap, n_tiles, n_rhs = sizes
    per = n_rows * cap // arrived_ref.shape[0]

    def fetch(row):
        total = None
        for k in range(width_k):
            slot = place_ref[0, 0, (field + k) * rows + row]
            start = pl.multiple_of(below(slot, per) * n_rhs, n_rhs)
            block = arrived_ref[over(slot, per), pl.ds(start, n_rhs), :]
            total = block if total is None else total + block
        return total

    return fetch


def solve_kernel(sizes, width_k, n_band, field, *refs):
    metadata_in, arrived_ref, inverse_ref = refs[:2], *refs[2:4]
    terms, refs = refs[4 : 5 + n_band], refs[5 + n_band :]
    out_ref, metadata, sum_ref, product_ref, meta_sems = refs[0], refs[1:3], *refs[3:]
    place_ref, index_ref = metadata
    rows = sizes[0]
    finish(copies_of(zip(metadata_in, metadata), meta_sems))
    fetch = arrived_blocks_of(sizes, width_k, place_ref, field, arrived_ref)

    def diags(row):
        return index_ref[0, 0, rows + row]

    gather_solve(sizes, fetch, diags, [], terms, inverse_ref, sum_ref, product_ref)
    out_ref[...] = sum_ref[...].reshape(out_ref.shape)


def pack_kernel(sizes, width_k, n_band, *refs):
    rows, n_rows, cap, n_tiles, n_rhs = sizes
    list_in, near_in, first_ref, tile_ref, send_out = refs[:5]
    band_out, refs = refs[5 : 5 + n_band], refs[5 + n_band :]
    list_ref, near_ref, product_ref, send_ref = refs[:4]
    band_refs, (meta_sems, send_sems) = refs[4 : 4 + n_band], refs[4 + n_band :]
    list_in = list_in.at[:, :, pl.ds(0, LANES)]
    metadata = copies_of(((list_in, list_ref), (near_in, near_ref)), meta_sems)
    table_products(first_ref[...].reshape(rows * n_rhs, -1), tile_ref, product_ref)
    finish(metadata)
    pack_bands(sizes, width_k, product_ref, near_ref, band_refs)
    for owner in range(n_rows):
        for rank in range(cap):
            block = product_ref[below(list_ref[owner, 0, rank], rows * n_tiles)]
            send_ref[owner, rank * n_rhs : (rank + 1) * n_rhs, :] = block
    finish(copies_of(zip((send_ref, *band_refs), (send_out, *band_out)), send_sems))


def own_kernel(sizes, width_k, *refs):
    rows, n_rows, cap, n_tiles, n_rhs = sizes
    metadata_in, first_ref, tile_ref, extra = list(refs[:2]), *refs[2:4], refs[4:8]
    send_out, band_out, metadata, product_ref, send_ref, band_ref = refs[8], refs[9], refs[10:12], *refs[12:15]
    held, value_ref, spread_ref, result_ref, meta_sems, load_sems, send_sems = refs[15:19], *refs[19:]
    list_ref, near_ref = metadata
    metadata_in[0] = metadata_in[0].at[:, :, pl.ds(0, LANES)]
    metadata = copies_of(zip(metadata_in, metadata), meta_sems)
    fetched = copies_of(zip(extra, held), load_sems)
    table_products(first_ref[...].reshape(rows * n_rhs, -1), tile_ref, product_ref)
    finish(metadata)
    copies = []

    def send(source, target):
        copies.extend(started([pltpu.make_async_copy(source, target, send_sems.at[len(copies)])]))

    pack_bands(sizes, width_k, product_ref, near_ref, (band_ref,))
    send(band_ref, band_out)
    body, half = cap * n_rhs, n_rows // 2
    upper = lax.axis_index("rows") >= half
    mine, others = jnp.where(upper, half, 0), jnp.where(upper, 0, half)
    finish(fetched[:1])
    functional_ref, count_ref, place_ref, partial_ref = held
    n_blocks = n_rows * cap + rows
    n_func = spread_ref.shape[0] // n_blocks
    n_diag = functional_ref.shape[0] // n_func

    def spread(done, blocks, kinds):
        spread_values(n_rhs, n_func, functional_ref, blocks, kinds, value_ref, spread_ref, done)

    kinds = [near_ref[0, 0, rows + row] for row in range(rows)]
    spread(n_rows * cap, band_ref[...].reshape(rows * n_rhs, -1), kinds)
    kinds = []
    for order in range(n_rows):
        owner = order % half + (mine if order < half else others)
        for rank in range(cap):
            code = list_ref[owner, 0, rank]
            kinds.append(below(over(code, rows * n_tiles * rows), n_diag))
            block = product_ref[below(code, rows * n_tiles)]
            send_ref[order, rank * n_rhs : (rank + 1) * n_rhs, :] = block
        if order < half:
            send(send_ref.at[order], send_out.at[order, pl.ds(0, body)])
        if order % 2:
            blocks = jnp.concatenate([send_ref[order - 1], send_ref[order]], axis=0)
            spread((order - 1) * cap, blocks, kinds)
            kinds = []
    finish(fetched[1:])
    result = coarse_parts(n_rhs, n_blocks, count_ref, place_ref, partial_ref, spread_ref)
    result_ref[...] = result.reshape(result_ref.shape)
    depth = result_ref.shape[1]
    for n, first in enumerate((mine, others)):
        target = send_out.at[:, pl.ds(body + n * depth, depth)]
        send(result_ref.at[pl.ds(first, half)], target)
    finish(copies)


def mirror_kernel(
    sizes, list_in, mirror_ref, tile_ref, inverse_ref, send_out, list_ref, product_ref, block_ref, solved_ref, send_ref, sems
):
    rows, n_rows, cap, n_tiles, n_rhs = sizes
    half, n_diag = n_rows // 2, inverse_ref.shape[0]
    base = jnp.where(lax.axis_index("rows") >= half, half, 0)
    list_in = list_in.at[pl.ds(base, half), :, pl.ds(0, LANES)]
    metadata = started([pltpu.make_async_copy(list_in, list_ref, sems.at[half])])
    table_products(mirror_ref[...].reshape(rows * n_rhs, -1), tile_ref, product_ref)
    finish(metadata)
    codes = [list_ref[n // cap, 0, LANES // 2 + n % cap] for n in range(half * cap)]
    for n, code in enumerate(codes):
        block_ref[n] = product_ref[below(code, rows * n_tiles)]
    values = block_ref[...].reshape(half * cap * n_rhs, -1)
    table_products(values, inverse_ref, solved_ref)
    copies = []
    for n, code in enumerate(codes):
        device, rank = n // cap, n % cap
        kind = below(over(code, rows * n_tiles * rows), n_diag)
        send_ref[device, rank * n_rhs : (rank + 1) * n_rhs, :] = solved_ref[kind * len(codes) + n]
        if rank == cap - 1:
            copy = pltpu.make_async_copy(send_ref.at[device], send_out.at[device], sems.at[device])
            copies += started([copy])
    finish(copies)


def coarse_parts(n_rhs, n_blocks, count_ref, place_ref, partial_ref, spread_ref):
    n_func = spread_ref.shape[0] // n_blocks
    values = [
        spread_ref[pl.ds(t, n_blocks, stride=n_func), :] for t in range(count_ref.shape[1] // n_blocks)
    ]
    values = jnp.concatenate(values, axis=0)
    partial = jnp.dot(
        count_ref[...], jnp.concatenate(halves(values), axis=1), preferred_element_type=jnp.float32
    )
    partial = partial[:, :LANES] + partial[:, LANES:] + partial_ref[...]
    shift = LANES // 2
    while shift >= n_rhs:
        partial = partial + pltpu.roll(partial, shift, axis=1)
        shift //= 2
    return place(place_ref, partial, n_rhs, 2)


def part_kernel(arrived_ref, keep_ref, give_ref):
    depth = keep_ref.shape[0] // 2
    body = arrived_ref.shape[1] - 4 * depth
    total = arrived_ref[0, body:, :]
    for source in range(1, arrived_ref.shape[0]):
        total = total + arrived_ref[source, body:, :]
    lower = lax.axis_index("band") == 0
    for n in range(2):
        zero, one = (total[(2 * n + m) * depth : (2 * n + m + 1) * depth] for m in range(2))
        keep_ref[n * depth : (n + 1) * depth] = jnp.where(lower, zero, one)
        give_ref[n * depth : (n + 1) * depth] = jnp.where(lower, one, zero)


def half_blocks_of(sizes, width_k, place_ref, arrived_ref, far):
    rows, n_rows, cap, n_tiles, n_rhs = sizes

    def fetch(row):
        total = None
        for k in range(width_k):
            slot = place_ref[0, 0, k * rows + row]
            holder, slot = over(slot, 2 * cap), below(slot, 2 * cap)
            start = pl.ds(pl.multiple_of(below(slot, cap) * n_rhs, n_rhs), n_rhs)
            mine = slot >= cap if far else slot < cap
            block = jnp.where(mine, arrived_ref[holder, start, :], 0.0)
            total = block if total is None else total + block
        return total

    return fetch


def base_kernel(sizes, width_k, *refs):
    metadata_in, own_ref, inverse_ref, terms_in, out_ref = refs[:2], *refs[2:4], refs[4:6], refs[6]
    metadata, sum_ref, product_ref, terms, term_sems, meta_sems = refs[7:9], *refs[9:11], refs[11:13], *refs[13:]
    place_ref, index_ref = metadata
    rows = sizes[0]
    metadata = copies_of(zip(metadata_in, metadata), meta_sems)
    later = copies_of(zip(terms_in, terms), term_sems)
    finish(metadata)
    fetch = half_blocks_of(sizes, width_k, place_ref, own_ref, False)

    def diags(row):
        return index_ref[0, 0, rows + row]

    gather_solve(sizes, fetch, diags, later, terms, inverse_ref, sum_ref, product_ref)
    out_ref[...] = sum_ref[...].reshape(out_ref.shape)


def final_kernel(sizes, width_k, *refs):
    place_in, mirror_ref, base_ref, near_ref, far_ref, scale_ref, out_ref, place_ref, sem = refs
    rows, n_rows, cap, n_tiles, n_rhs = sizes
    metadata = pltpu.make_async_copy(place_in, place_ref, sem)
    metadata.start()
    depth = scale_ref.shape[0]
    correction = (near_ref[...] + far_ref[...]) / scale_ref[...]
    padded = jnp.concatenate([correction, jnp.zeros((8 - depth, LANES), jnp.float32)], axis=0)
    turned = padded.T
    metadata.wait()
    fetch = half_blocks_of(sizes, width_k, place_ref, mirror_ref, True)
    for row in range(rows):
        spot, place = row // depth, row % depth
        column = turned[spot * n_rhs : (spot + 1) * n_rhs, place : place + 1]
        out_ref[row] = (base_ref[row] + column) + fetch(row)


def shifted(value, axis, steps):
    count = lax.axis_size(axis)
    initial, last = (max(0, -steps), min(count, count - steps))
    return lax.ppermute(value, axis, [(source, source + steps) for source in range(initial, last)])


def to_bands(sends):
    if len(sends) == 1:
        return (lax.ppermute(sends[0], "band", [(0, 1), (1, 0)]),)
    return shifted(sends[0], "band", 1), shifted(sends[1], "band", -1)


def on_device(
    start_iterate,
    right_side,
    diag_table,
    inverse_table,
    coupling_tiles,
    diag_index,
    tile_index,
    source_owner,
    source_local,
    aggregate_map,
):
    rows, n_rhs, states = start_iterate.shape
    width_k = source_owner.shape[1]
    n_tiles, n_diag = coupling_tiles.shape[0], inverse_table.shape[0]
    n_rows, n_bands = lax.axis_size("rows"), lax.axis_size("band")
    n_dev = n_rows * n_bands
    cap = max(2, 2 * width_k * rows // n_rows)
    slots = n_rows * cap
    total_groups = AGG_DEV * n_dev
    per_tile = LANES // n_rhs
    depth = rows // per_tile
    n_func = 16
    dense = (
        n_bands == 2
        and n_dev * rows * total_groups <= DENSE_LIMIT
        and depth == 4
        and n_diag * n_func == LANES
        and n_tiles + 2 <= n_func
    )
    sizes = (rows, n_rows, cap, n_tiles, n_rhs)
    f32, i32 = jnp.float32, jnp.int32
    my_band = lax.axis_index("band")
    my_row = lax.axis_index("rows")

    half = n_rows // 2
    wide = -(-(4 + 2 * width_k) * rows // LANES) * LANES
    place_wide = -(-2 * width_k * rows // LANES) * LANES
    index_shapes = [(width_k, rows), (width_k, rows), (width_k + 2, rows), (1, rows), (1, rows)]
    halves_of_rows = [list(range(half)), list(range(half, n_rows))]
    to_mirror = [(i, (i + half) % n_rows) for i in range(n_rows)]
    mirror = lax.ppermute(start_iterate, "rows", to_mirror)
    lists, index, places = call(
        functools.partial(request_kernel, (rows, n_rows, cap, n_tiles, n_diag)),
        (
            jax.ShapeDtypeStruct((n_rows, 1, LANES + wide), i32),
            jax.ShapeDtypeStruct((1, 1, wide), i32),
            jax.ShapeDtypeStruct((1, 1, place_wide), i32),
        ),
        [HBM] * 5,
        [VMEM] * 3,
        [*[pltpu.VMEM(shape, i32) for shape in index_shapes], pltpu.SemaphoreType.DMA((5,))],
    )(source_owner.T, source_local.T, tile_index.T, diag_index[None], aggregate_map.T)
    lists = lax.all_to_all(lists, "rows", split_axis=0, concat_axis=0, tiled=True)
    if n_bands == 2:
        near = lax.ppermute(index, "band", [(0, 1), (1, 0)])
    else:
        ways = [[(b, (b + step) % n_bands) for b in range(n_bands)] for step in (-1, 1)]
        near = jnp.concatenate([lax.ppermute(index, "band", way) for way in ways], axis=0)

    n_ways = 1 if n_bands == 2 else 2
    block = (rows, n_rhs, states)
    band_shapes = [jax.ShapeDtypeStruct(block, f32)] * n_ways
    band_scratch = [pltpu.VMEM(block, f32)] * n_ways
    term_scratch = [pltpu.VMEM(block, f32)] * (1 + n_ways)
    term_sems = pltpu.SemaphoreType.DMA((1 + n_ways,))
    list_scratch = pltpu.SMEM((half, 1, LANES), i32)
    near_scratch = pltpu.SMEM((n_ways, 1, wide), i32)
    row_scratch = [pltpu.SMEM((1, 1, place_wide), i32), pltpu.SMEM((1, 1, wide), i32)]
    flat = rows * n_rhs
    sums = pltpu.VMEM((flat, states), f32)
    products = pltpu.VMEM((max(n_tiles, n_diag) * rows, n_rhs, states), f32)
    work = 6 * flat * states * states
    made_shape = (n_tiles * rows, n_rhs, states)
    table_scratch = [pltpu.VMEM(coupling_tiles.shape, f32)]
    table_sems = pltpu.SemaphoreType.DMA((-(-n_tiles // 2),))
    made = call(
        product_kernel,
        jax.ShapeDtypeStruct(made_shape, f32),
        [HBM, HBM],
        VMEM,
        [
            pltpu.VMEM(block, f32),
            *table_scratch,
            pltpu.SemaphoreType.DMA,
            table_sems,
        ],
        work * n_tiles,
        4 << 20,
    )(start_iterate, coupling_tiles)
    packed, *bands = call(
        functools.partial(first_kernel, sizes, width_k, n_ways),
        (jax.ShapeDtypeStruct((half, 2 * cap, n_rhs, states), f32), *band_shapes),
        [VMEM, VMEM, VMEM, ANY, ANY],
        [HBM] * (1 + n_ways),
        [
            pltpu.VMEM(made_shape, f32),
            list_scratch,
            near_scratch,
            pltpu.VMEM((half, 2 * cap, n_rhs, states), f32),
            *band_scratch,
            pltpu.SemaphoreType.DMA((2,)),
            pltpu.SemaphoreType.DMA((2 * half + n_ways,)),
        ],
        work * n_tiles,
        4 << 20,
    )(made, mirror, coupling_tiles, lists, near)
    packed, late = lax.optimization_barrier((packed, lists))
    if dense:
        across = lax.ppermute(late, "band", [(0, 1), (1, 0)])
        across, *bands = lax.optimization_barrier((across, *bands))
    sends = (packed.reshape(half, 2 * cap * n_rhs, states), *bands)
    halves_of_rows = [list(range(half)), list(range(half, n_rows))]
    def exchange(sends, groups=None):
        arrived = lax.all_to_all(
            sends[0], "rows", split_axis=0, concat_axis=0, tiled=True, axis_index_groups=groups
        )
        return arrived, to_bands(sends[1:])

    arrived_blocks, arrived_bands = exchange(sends, halves_of_rows)

    if dense:
        fields = jnp.stack([late, across])[:, :, 0, LANES:]
        fields = fields.reshape(2, n_rows, -1, rows).transpose(2, 0, 1, 3)
        fields = fields.reshape(-1, 2, n_rows * rows)
        n_blocks = slots + rows
        length = n_dev * depth
        extra_shapes = [
            ((n_diag * n_func, 3 * states), jnp.bfloat16),
            ((total_groups, (n_tiles + 1) * n_blocks), jnp.bfloat16),
            ((per_tile * length, total_groups), jnp.bfloat16),
            ((total_groups, LANES), f32),
        ]
        functional_shape, count_shape, placing_shape, partial_shape = extra_shapes
        counts, functionals, placing, partial, scale = call(
            functools.partial(count_kernel, sizes, width_k, n_func),
            (
                jax.ShapeDtypeStruct(*count_shape),
                jax.ShapeDtypeStruct(*functional_shape),
                jax.ShapeDtypeStruct(*placing_shape),
                jax.ShapeDtypeStruct(*partial_shape),
                jax.ShapeDtypeStruct((depth, LANES), f32),
            ),
            [ANY, HBM] + [VMEM] * 5,
            [HBM] * 4 + [VMEM],
            [
                pltpu.VMEM(*count_shape),
                pltpu.VMEM(*functional_shape),
                pltpu.VMEM(*placing_shape),
                pltpu.VMEM(*partial_shape),
                row_scratch[1],
                pltpu.VMEM(block, f32),
                pltpu.VMEM((n_diag * n_func, flat), f32),
                pltpu.VMEM((rows * n_func, LANES), f32),
                pltpu.SemaphoreType.DMA((2,)),
                pltpu.SemaphoreType.DMA((4,)),
            ],
            4 * total_groups * n_tiles * n_dev * rows * n_blocks,
            4 << 20,
        )(
            index, right_side, fields, late[:, 0, :LANES], coupling_tiles, diag_table, inverse_table
        )
        extra_scratch = [
            *[pltpu.VMEM(*shape) for shape in extra_shapes],
            pltpu.VMEM((n_diag * n_func, n_blocks * n_rhs), f32),
            pltpu.VMEM((n_blocks * n_func, LANES), f32),
            pltpu.VMEM((n_rows, n_bands * depth, LANES), f32),
        ]

        made = (arrived_blocks, functionals, counts, placing, partial, scale)
        made = lax.optimization_barrier(made)
        arrived_blocks, functionals, counts, placing, partial, scale = made

    def solve(field, arrived, bands):
        return call(
            functools.partial(solve_kernel, sizes, width_k, n_ways, field),
            jax.ShapeDtypeStruct(block, f32),
            [ANY] * 2 + [VMEM] * (3 + n_ways),
            VMEM,
            [*row_scratch, sums, products, pltpu.SemaphoreType.DMA((2,))],
            work * n_diag,
            4 << 20,
        )(places, index, arrived, inverse_table, right_side, *bands)

    first = solve(0, arrived_blocks, arrived_bands)
    body = cap * n_rhs
    full_list = pltpu.SMEM((n_rows, 1, LANES), i32)
    if dense:
        mirror = lax.ppermute(first, "rows", to_mirror)
        own, band = call(
            functools.partial(own_kernel, sizes, width_k),
            (
                jax.ShapeDtypeStruct((half, body + 2 * n_bands * depth, states), f32),
                jax.ShapeDtypeStruct(block, f32),
            ),
            [ANY] * 2 + [VMEM] * 2 + [HBM] * 4,
            [HBM] * 2,
            [
                full_list,
                near_scratch,
                products,
                pltpu.VMEM((n_rows, body, states), f32),
                pltpu.VMEM(block, f32),
                *extra_scratch,
                pltpu.SemaphoreType.DMA((2,)),
                pltpu.SemaphoreType.DMA((4,)),
                pltpu.SemaphoreType.DMA((half + 3,)),
            ],
            2 * work * n_tiles,
            4 << 20,
        )(lists, near, first, coupling_tiles, functionals, counts, placing, partial)
        own, (band,) = exchange((own, band), halves_of_rows)
        packed = call(
            functools.partial(mirror_kernel, sizes),
            jax.ShapeDtypeStruct((half, body, states), f32),
            [ANY] + [VMEM] * 3,
            HBM,
            [
                list_scratch,
                products,
                pltpu.VMEM((half * cap, n_rhs, states), f32),
                pltpu.VMEM((n_diag * half * cap, n_rhs, states), f32),
                pltpu.VMEM((half, body, states), f32),
                pltpu.SemaphoreType.DMA((half + 1,)),
            ],
            BEHIND_SWAP * work * n_tiles,
            4 << 20,
        )(lists, mirror, coupling_tiles, inverse_table)
        packed, band = lax.optimization_barrier((packed, band))
        swapped = lax.all_to_all(
            packed, "rows", split_axis=0, concat_axis=0, tiled=True, axis_index_groups=halves_of_rows
        )
        part = jax.ShapeDtypeStruct((2 * depth, LANES), f32)
        keep, give = call(part_kernel, (part, part), [VMEM], [VMEM] * 2)(own)
        keep = keep + lax.ppermute(give, "band", [(0, 1), (1, 0)])
        far = lax.ppermute(keep[depth:], "rows", to_mirror)
        base = call(
            functools.partial(base_kernel, sizes, width_k),
            jax.ShapeDtypeStruct(block, f32),
            [ANY] * 2 + [VMEM] * 2 + [HBM, ANY],
            VMEM,
            [
                *row_scratch,
                sums,
                products,
                *term_scratch,
                term_sems,
                pltpu.SemaphoreType.DMA((2,)),
            ],
            work * n_diag,
            4 << 20,
        )(places, index, own, inverse_table, right_side, band)
        return call(
            functools.partial(final_kernel, sizes, width_k),
            jax.ShapeDtypeStruct(block, f32),
            [ANY] + [VMEM] * 5,
            VMEM,
            [row_scratch[0], pltpu.SemaphoreType.DMA],
            0,
            4 << 20,
        )(places, swapped, base, keep[:depth], far, scale)

    sends = call(
        functools.partial(pack_kernel, sizes, width_k, n_ways),
        (jax.ShapeDtypeStruct((n_rows, body, states), f32), *band_shapes),
        [ANY] * 2 + [VMEM] * 2,
        [HBM] * (1 + n_ways),
        [
            full_list,
            near_scratch,
            products,
            pltpu.VMEM((n_rows, body, states), f32),
            *band_scratch,
            pltpu.SemaphoreType.DMA((2,)),
            pltpu.SemaphoreType.DMA((1 + n_ways,)),
        ],
        work * n_tiles,
        4 << 20,
    )(lists, near, first, coupling_tiles)
    arrived_blocks, arrived_bands = exchange(sends)
    second = solve(width_k, arrived_blocks, arrived_bands)

    groups = aggregate_map[:, 0]
    own = jnp.arange(rows, dtype=i32)
    index_all = lax.all_gather(index, ("band", "rows"), axis=0, tiled=True)
    index_all = index_all.reshape(n_bands, n_rows, wide)
    groups_all, diags_all = index_all[:, :, :rows], index_all[:, :, rows : 2 * rows]
    codes = lists[:, 0, :cap]
    asked = jnp.arange(n_rows, dtype=i32)[:, None] * rows + codes // (rows * n_tiles) % rows
    asked = jnp.where(codes > 0, asked, -1).reshape(-1)
    table_sums = jnp.sum(diag_table, axis=(1, 2))
    diag_onehot = diags_all.reshape(-1, 1) == jnp.arange(n_diag, dtype=i32)[None]
    block_sums = jnp.sum(jnp.where(diag_onehot, table_sums[None], 0.0), axis=1)
    whole_diag = jnp.sum(
        jnp.where(groups[:, None] == groups_all.reshape(-1)[None], block_sums[None], 0.0), axis=1
    )
    above, below = near[0, 0], near[-1, 0]
    place_of = (2 + width_k) * rows
    band_tiles = jnp.stack([above[place_of : place_of + rows], below[place_of + rows : place_of + 2 * rows]])
    band_groups = jnp.stack([above[:rows], below[:rows]])
    band_valid = jnp.stack([my_band + 1 < n_bands, my_band > 0])
    band_valid = jnp.broadcast_to(band_valid[:, None], (2, rows))
    n_all = n_tiles + n_diag + 1
    code = codes.reshape(-1)
    band_of_mine = lax.dynamic_index_in_dim(groups_all, my_band, 0, keepdims=False).reshape(-1)
    entry_group = jnp.concatenate(
        [jnp.take(band_of_mine, jnp.maximum(asked, 0)), band_groups.reshape(-1), groups, groups]
    )
    entry_func = jnp.concatenate(
        [
            (code % rows) * n_all + (code // rows) % n_tiles,
            (own[None] * n_all + band_tiles).reshape(-1),
            own * n_all + n_tiles + diag_index,
            own * n_all + n_tiles + n_diag,
        ]
    )
    entry_valid = jnp.concatenate([asked >= 0, band_valid.reshape(-1), jnp.ones((2 * rows,), bool)])
    functionals = jnp.concatenate(
        [jnp.sum(coupling_tiles, axis=1), -jnp.sum(diag_table, axis=1)], axis=0
    )
    weights = jnp.einsum("fp,rcp->rfc", functionals, second, precision=HIGH)
    weights = jnp.concatenate([weights, jnp.sum(right_side, axis=2)[:, None]], axis=1)
    chosen = jnp.take(weights.reshape(rows * n_all, n_rhs), entry_func, axis=0)
    chosen = jnp.where(entry_valid[:, None], chosen, 0.0)
    partial = jax.ops.segment_sum(chosen, entry_group, num_segments=total_groups)
    whole = lax.psum(partial, ("band", "rows"))
    correction = jnp.take(whole, groups, axis=0) / whole_diag[:, None]
    return second + correction[:, :, None]


def solution(mesh):
    in_specs = (
        P(("band", "rows"), None, None),
        P(("band", "rows"), None, None),
        P(),
        P(),
        P(),
        P(("band", "rows")),
        P(("band", "rows"), None),
        P(("band", "rows"), None),
        P(("band", "rows"), None),
        P(("band", "rows"), None),
    )
    out_specs = P(("band", "rows"), None, None)
    return jax.shard_map(
        on_device, mesh=mesh, in_specs=in_specs, out_specs=out_specs, check_vma=False
    )
```

```python
import functools

import jax
import jax.numpy as jnp
from jax import lax
from jax.experimental import pallas as pl
from jax.experimental.pallas import tpu as pltpu
from jax.sharding import PartitionSpec as P

AGG_DEV = 8
LANES = 128
DENSE_LIMIT = 1 << 19
BEHIND_SWAP = 100

VMEM = pl.BlockSpec(memory_space=pltpu.VMEM)
SMEM = pl.BlockSpec(memory_space=pltpu.SMEM)
HBM = pl.BlockSpec(memory_space=pltpu.HBM)
ANY = pl.BlockSpec(memory_space=pl.ANY)
HIGH = lax.Precision.HIGHEST


def params():
    return pltpu.CompilerParams(vmem_limit_bytes=24 * 1024 * 1024)


def call(kernel, out_shape, in_specs, out_specs, scratch=(), flops=0, moved=0):
    def shaped(shape, spec):
        return pltpu.HBM(shape.shape, shape.dtype) if spec is HBM else shape

    if isinstance(out_shape, (tuple, list)):
        out_shape = [shaped(*pair) for pair in zip(out_shape, out_specs)]
    else:
        out_shape = shaped(out_shape, out_specs)
    run = pl.pallas_call(
        kernel,
        out_shape=out_shape,
        in_specs=in_specs,
        out_specs=out_specs,
        scratch_shapes=list(scratch),
        compiler_params=params(),
        cost_estimate=pl.CostEstimate(flops=flops, bytes_accessed=moved, transcendentals=0),
    )

    def apply(*args):
        pinned = [
            pltpu.with_memory_space_constraint(arg, pltpu.HBM) if spec is HBM else arg
            for arg, spec in zip(args, in_specs)
        ]
        return run(*pinned)

    return apply


def below(value, bound):
    return value & (bound - 1) if bound & (bound - 1) == 0 else lax.rem(value, bound)


def over(value, bound):
    if bound & (bound - 1) == 0:
        return lax.shift_right_logical(value, bound.bit_length() - 1)
    return lax.div(value, bound)


def halves(value):
    high = value.astype(jnp.bfloat16)
    low = (value - high.astype(jnp.float32)).astype(jnp.bfloat16)
    return high, low


def left_operand(value):
    high, low = halves(value)
    return jnp.concatenate([high, low, high], axis=1)


def right_operand(value):
    high, low = halves(value)
    return jnp.concatenate([high, high, low], axis=1)


def dot_nt(left, right):
    return lax.dot_general(
        left, right, (((1,), (1,)), ((), ())), preferred_element_type=jnp.float32
    )


def table_products(value, table_ref, out_ref, done=None, loads=None):
    left = left_operand(value)
    count, width = table_ref.shape[0], table_ref.shape[1]
    n_rhs = out_ref.shape[1]
    rows = left.shape[0] // n_rhs
    for first in range(0, count, 2):
        last = min(first + 2, count)
        if loads is not None:
            loads[first // 2].wait()
        right = right_operand(table_ref[first:last].reshape((last - first) * width, -1))
        product = dot_nt(left, right)
        for t in range(first, last):
            part = product[:, (t - first) * width : (t - first + 1) * width]
            out_ref[t * rows : (t + 1) * rows] = part.reshape(rows, n_rhs, width)
        if done is not None:
            done(first * rows, (last - first) * rows)


def started(copies):
    for copy in copies:
        copy.start()
    return copies


def finish(copies):
    for copy in copies:
        copy.wait()


def request_kernel(sizes, *refs):
    rows, n_rows, cap, n_tiles, n_diag = sizes
    inputs, (list_ref, index_ref, place_ref), held, sems = refs[:5], refs[5:8], refs[8:13], refs[13]
    finish(
        started([pltpu.make_async_copy(i, h, sems.at[n]) for n, (i, h) in enumerate(zip(inputs, held))])
    )
    owner_ref, local_ref, tile_ref, diag_ref, group_ref = held
    width_k = owner_ref.shape[0]
    half = n_rows // 2
    row_of = lax.broadcasted_iota(jnp.int32, (rows, rows), 0)
    col_of = lax.broadcasted_iota(jnp.int32, (rows, rows), 1)
    lane = lax.broadcasted_iota(jnp.int32, (rows, LANES), 1)
    owners = lax.broadcasted_iota(jnp.int32, (n_rows, rows), 0)

    def column(row):
        return jnp.sum(jnp.where(row_of == col_of, row, 0), axis=1, keepdims=True)

    def owner_row(k):
        return owner_ref[k : k + 1, :]

    row_ids = lax.broadcasted_iota(jnp.int32, (1, rows), 1)
    owner_columns = [column(owner_row(k)) for k in range(width_k)]
    lists = jnp.zeros((n_rows, LANES), jnp.float32)
    places, half_places = [], []
    for k in range(width_k):
        rank = jnp.zeros((1, rows), jnp.int32)
        for other in range(k + 1):
            match = owner_columns[other] == owner_row(k)
            if other == k:
                match = match & (row_of < col_of)
            rank = rank + jnp.sum(jnp.where(match, 1, 0), axis=0, keepdims=True)
        places.append(owner_row(k) * cap + rank)
        same = (owner_row(k) >= half) == (lax.axis_index("rows") >= half)
        holder = jnp.where(owner_row(k) >= half, owner_row(k) - half, owner_row(k))
        half_places.append(holder * (2 * cap) + rank + jnp.where(same, 0, cap))
        taker = row_ids + rows * (diag_ref[...] + n_diag)
        code = local_ref[k : k + 1, :] + rows * (tile_ref[k : k + 1, :] + n_tiles * taker)
        code, rank = column(code), column(rank)
        mirror = jnp.where(owner_row(k) >= half, owner_row(k) - half, owner_row(k) + half)
        for owner, base in ((owner_row(k), 0), (mirror, LANES // 2)):
            by_rank = jnp.where(lane == rank + base, code, 0).astype(jnp.float32)
            mine = jnp.where(owners == owner, 1.0, 0.0)
            lists = lists + jnp.dot(
                mine, by_rank, precision=HIGH, preferred_element_type=jnp.float32
            )
    lists = (lists + 0.5).astype(jnp.int32)

    def joined(parts, wide):
        spare = wide - len(parts) * rows
        if spare:
            parts = [*parts, jnp.zeros((1, spare), jnp.int32)]
        return jnp.concatenate(parts, axis=1)

    index = [group_ref[...], diag_ref[...]]
    index += [tile_ref[k : k + 1, :] for k in range(width_k + 2)]
    index += [owner_row(k) * rows + local_ref[k : k + 1, :] for k in range(width_k)]
    index = joined(index, index_ref.shape[2])
    index_ref[0] = index
    place_ref[0] = joined(half_places + places, place_ref.shape[2])
    for device in range(n_rows):
        list_ref[device] = jnp.concatenate([lists[device : device + 1, :], index], axis=1)


def copies_of(pairs, sems):
    return started([pltpu.make_async_copy(i, h, sems.at[n]) for n, (i, h) in enumerate(pairs)])


def band_field(rows, width_k, way, n_ways):
    field = (2 + width_k) * rows
    if n_ways == 1:
        return field + jnp.where(lax.axis_index("band") == 0, 0, rows)
    return field + way * rows


def pack_bands(sizes, width_k, product_ref, near_ref, band_refs):
    rows = sizes[0]
    for way, band_ref in enumerate(band_refs):
        field = band_field(rows, width_k, way, len(band_refs))
        for row in range(rows):
            band_ref[row] = product_ref[near_ref[way, 0, field + row] * rows + row]


def table_loads(table_in, table_ref, sems):
    copies = []
    for first in range(0, table_in.shape[0], 2):
        place = pl.ds(first, min(2, table_in.shape[0] - first))
        source, target = table_in.at[place], table_ref.at[place]
        copies.append(pltpu.make_async_copy(source, target, sems.at[first // 2]))
    return started(copies)


def product_kernel(start_in, tile_in, product_ref, start_ref, tile_ref, start_sem, tile_sems):
    start = pltpu.make_async_copy(start_in, start_ref, start_sem)
    start.start()
    loads = table_loads(tile_in, tile_ref, tile_sems)
    start.wait()
    rows, n_rhs, states = start_ref.shape
    values = start_ref[...].reshape(rows * n_rhs, states)
    table_products(values, tile_ref, product_ref, None, loads)


def first_kernel(sizes, width_k, n_band, *refs):
    rows, n_rows, cap, n_tiles, n_rhs = sizes
    own_ref, mirror_ref, tile_ref, list_in, near_in, send_out = refs[:6]
    band_out, refs = refs[6 : 6 + n_band], refs[6 + n_band :]
    product_ref, list_ref, near_ref, send_ref = refs[:4]
    band_refs, (meta_sems, send_sems) = refs[4 : 4 + n_band], refs[4 + n_band :]
    half = n_rows // 2
    base = jnp.where(lax.axis_index("rows") >= half, half, 0)
    list_in = list_in.at[pl.ds(base, half), :, pl.ds(0, LANES)]
    metadata = copies_of(((list_in, list_ref), (near_in, near_ref)), meta_sems)
    values = mirror_ref[...].reshape(rows * n_rhs, -1)
    table_products(values, tile_ref, product_ref)
    finish(metadata)
    copies = []
    for side, blocks_ref in ((0, own_ref), (1, product_ref)):
        for device in range(half):
            for rank in range(cap):
                code = list_ref[device, 0, side * (LANES // 2) + rank]
                block = blocks_ref[below(code, rows * n_tiles)]
                send_ref[device, side * cap + rank] = block
            place = (device, pl.ds(side * cap, cap))
            copies += started(
                [pltpu.make_async_copy(send_ref.at[place], send_out.at[place], send_sems.at[len(copies)])]
            )
    pack_bands(sizes, width_k, own_ref, near_ref, band_refs)
    for ref, out in zip(band_refs, band_out):
        copies += started([pltpu.make_async_copy(ref, out, send_sems.at[len(copies)])])
    finish(copies)


def place(place_ref, values, n_rhs, n_parts):
    per_tile = LANES // n_rhs
    length = place_ref.shape[0] // per_tile
    parts, rest = [], values
    for _ in range(n_parts):
        part = rest.astype(jnp.bfloat16)
        rest = rest - part.astype(jnp.float32)
        parts.append(part)
    parts = jnp.concatenate(parts, axis=1)
    lane = lax.broadcasted_iota(jnp.int32, (length, LANES), 1)
    result = jnp.zeros((length, LANES), jnp.float32)
    placed = jnp.dot(place_ref[...], parts, preferred_element_type=jnp.float32)
    for spot in range(per_tile):
        chosen = placed[spot * length : (spot + 1) * length]
        chosen = sum(chosen[:, n * LANES : (n + 1) * LANES] for n in range(n_parts))
        result = jnp.where((lane >= spot * n_rhs) & (lane < (spot + 1) * n_rhs), chosen, result)
    return result


def spread_values(n_rhs, n_func, functional_ref, blocks, kinds, value_ref, spread_ref, done):
    per_tile = LANES // n_rhs
    lane = lax.broadcasted_iota(jnp.int32, (n_func, LANES), 1)
    columns = slice(done * n_rhs, done * n_rhs + blocks.shape[0])
    value_ref[:, columns] = dot_nt(functional_ref[...], right_operand(blocks))
    for block, kind in enumerate(kinds, done):
        tile, spot = block // per_tile, block % per_tile
        start = pl.multiple_of(kind * n_func, n_func)
        piece = value_ref[pl.ds(start, n_func), tile * LANES : (tile + 1) * LANES]
        piece = jnp.where((lane >= spot * n_rhs) & (lane < (spot + 1) * n_rhs), piece, 0.0)
        spread_ref[block * n_func : (block + 1) * n_func, :] = piece


def one_hot(ids, row):
    return jnp.where(ids == row, 1.0, 0.0).astype(jnp.bfloat16)


def count_kernel(sizes, width_k, n_func, *refs):
    rows, n_rows, cap, n_tiles, n_rhs = sizes
    index_in, right_in, field_ref, list_ref, tile_ref, table_ref, inverse_ref = refs[:7]
    count_out, functional_out, placing_out, partial_out, scale_ref = refs[7:12]
    count_ref, functional_ref, placing_ref, partial_ref = refs[12:16]
    index_ref, right_ref, value_ref, spread_ref, load_sems, sems = refs[16:]
    loads = copies_of(((index_in, index_ref), (right_in, right_ref)), load_sems)
    n_groups = count_ref.shape[0]
    slots, band_rows = n_rows * cap, n_rows * rows
    copies = []

    def send(source, target):
        copies.extend(started([pltpu.make_async_copy(source, target, sems.at[len(copies)])]))

    sums = jnp.sum(tile_ref[...], axis=1)
    line = lax.broadcasted_iota(jnp.int32, (n_func, sums.shape[1]), 0)
    sums = jnp.concatenate([sums, jnp.zeros((n_func - n_tiles, sums.shape[1]), jnp.float32)], axis=0)
    n_diag = inverse_ref.shape[0]
    totals = []
    for d in range(n_diag):
        minus = -jnp.sum(table_ref[d], axis=0, keepdims=True)
        totals.append(-jnp.sum(minus, axis=1, keepdims=True))
        wanted = jnp.where(line == n_tiles, minus, sums)
        high, low = halves(inverse_ref[d])
        right = jnp.concatenate([high, high, low], axis=0)
        solved = jnp.dot(left_operand(wanted), right, preferred_element_type=jnp.float32)
        solved = jnp.where(line == n_tiles + 1, 1.0, solved)
        functional_ref[d * n_func : (d + 1) * n_func, :] = left_operand(solved)
    send(functional_ref, functional_out)

    lists = list_ref[...]
    asker = lax.broadcasted_iota(jnp.int32, lists.shape, 0)
    codes = asker * rows + below(over(lists, rows * n_tiles), rows)
    codes = jnp.where(lists > 0, codes, -1).astype(jnp.float32)
    spread = lax.broadcasted_iota(jnp.int32, (slots, n_rows), 0)
    spread = lax.div(spread, cap) == lax.broadcasted_iota(jnp.int32, (slots, n_rows), 1)
    codes = jnp.dot(
        jnp.where(spread, 1.0, 0.0), codes, precision=HIGH, preferred_element_type=jnp.float32
    )
    rank = lax.rem(lax.broadcasted_iota(jnp.int32, codes.shape, 0), cap)
    lane = lax.broadcasted_iota(jnp.int32, codes.shape, 1)
    asked = jnp.sum(jnp.where(rank == lane, codes, 0.0), axis=1, keepdims=True)
    asked = jnp.where(asked < 0.0, asked - 0.5, asked + 0.5).astype(jnp.int32)
    low, high = asked[: slots // 2], asked[slots // 2 :]
    upper = lax.axis_index("rows") >= n_rows // 2
    asked = jnp.concatenate([jnp.where(upper, high, low), jnp.where(upper, low, high)], axis=0)
    own = lax.axis_index("rows") * rows + lax.broadcasted_iota(jnp.int32, (rows, 1), 0)
    band = lax.axis_index("band")

    def field(n, side):
        return field_ref[n, side : side + 1, :]

    row_ids = lax.broadcasted_iota(jnp.int32, (1, band_rows), 1)
    sides = []
    for side, targets in ((0, jnp.concatenate([asked, own], axis=0)), (1, own)):
        first = band == side
        across = jnp.where(first, field(2 + width_k, 1 - side), field(3 + width_k, 1 - side))
        takers = [field(2 + k, side) * n_groups + field(0, side) for k in range(width_k)]
        takers.append(across * n_groups + field(0, 1 - side))
        takers = jnp.concatenate(takers, axis=1)
        origins = [field(4 + width_k + k, side) for k in range(width_k)] + [row_ids]
        hits = one_hot(targets, jnp.concatenate(origins, axis=1))
        sides.append((takers, hits, field(0, side)))
    pieces, own_pieces = [], []
    ids = lax.broadcasted_iota(jnp.int32, (n_groups, band_rows), 0)
    for t in range(n_tiles + 1):
        found = []
        for takers, hits, groups in sides:
            if t < n_tiles:
                wide = lax.broadcasted_iota(jnp.int32, (n_groups, takers.shape[1]), 0)
                found.append(dot_nt(one_hot(wide + t * n_groups, takers), hits))
            else:
                found.append(dot_nt(one_hot(ids, groups), hits[:, -band_rows:]))
        pieces += [found[0][:, :slots], found[1]]
        own_pieces.append(found[0][:, slots:])
    count_ref[...] = jnp.concatenate(pieces, axis=1).astype(jnp.bfloat16)
    send(count_ref, count_out)

    own_counts = jnp.concatenate([*own_pieces, own_pieces[-1]], axis=1).astype(jnp.bfloat16)
    finish(loads)
    rights = right_ref[...].reshape(rows * n_rhs, -1)
    kinds = [index_ref[0, 0, rows + row] for row in range(rows)]
    spread_values(n_rhs, n_func, functional_ref, rights, kinds, value_ref, spread_ref, 0)
    values = [spread_ref[pl.ds(t, rows, stride=n_func), :] for t in range(n_tiles + 2)]
    values = jnp.concatenate(halves(jnp.concatenate(values, axis=0)), axis=1)
    partial = jnp.dot(own_counts, values, preferred_element_type=jnp.float32)
    partial_ref[...] = partial[:, :LANES] + partial[:, LANES:]
    send(partial_ref, partial_out)

    per_tile = LANES // n_rhs
    depth = rows // per_tile
    length = n_rows * 2 * depth
    order = lax.broadcasted_iota(jnp.int32, (per_tile * length, 1), 0)
    spot, order = lax.div(order, length), lax.rem(order, length)
    device, order = lax.div(order, 2 * depth), lax.rem(order, 2 * depth)
    side, order = lax.div(order, depth), lax.rem(order, depth)
    order = side * band_rows + device * rows + spot * depth + order
    member = [
        one_hot(ids, jnp.where(band == which, field(0, 0), field(0, 1))) for which in range(2)
    ]
    placing = jnp.zeros(placing_ref.shape, jnp.float32)
    for which in range(2):
        placing = placing + dot_nt(one_hot(order, row_ids + which * band_rows), member[which])
    placing_ref[...] = placing.astype(jnp.bfloat16)
    send(placing_ref, placing_out)
    whole = jnp.zeros((n_groups, 1), jnp.float32)
    for side in range(2):
        sums = jnp.zeros((1, band_rows), jnp.float32)
        for d in range(n_diag):
            sums = jnp.where(field(1, side) == d, totals[d], sums)
        weighted = jnp.where(ids == field(0, side), sums, 0.0)
        whole = whole + jnp.sum(weighted, axis=1, keepdims=True)
    scale = place(placing_ref, jnp.broadcast_to(whole, (n_groups, LANES)), n_rhs, 3)
    mine = jnp.zeros(scale_ref.shape, jnp.float32)
    here = lax.axis_index("rows") * 2 + band
    for n in range(2 * n_rows):
        mine = jnp.where(here == n, scale[n * depth : (n + 1) * depth, :], mine)
    scale_ref[...] = mine
    finish(copies)


def gather_solve(sizes, fetch, diags, later, terms, inverse_ref, sum_ref, product_ref):
    rows, n_rows, cap, n_tiles, n_rhs = sizes
    for row in range(rows):
        sum_ref[pl.ds(row * n_rhs, n_rhs), :] = fetch(row)
    finish(later)
    total = sum_ref[...]
    for term in terms:
        total = total + term[...].reshape(total.shape)
    table_products(total, inverse_ref, product_ref)
    for row in range(rows):
        sum_ref[pl.ds(row * n_rhs, n_rhs), :] = product_ref[diags(row) * rows + row]


def arrived_blocks_of(sizes, width_k, place_ref, field, arrived_ref):
    rows, n_rows, cap, n_tiles, n_rhs = sizes
    per = n_rows * cap // arrived_ref.shape[0]

    def fetch(row):
        total = None
        for k in range(width_k):
            slot = place_ref[0, 0, (field + k) * rows + row]
            start = pl.multiple_of(below(slot, per) * n_rhs, n_rhs)
            block = arrived_ref[over(slot, per), pl.ds(start, n_rhs), :]
            total = block if total is None else total + block
        return total

    return fetch


def solve_kernel(sizes, width_k, n_band, field, *refs):
    metadata_in, arrived_ref, inverse_ref = refs[:2], *refs[2:4]
    terms, refs = refs[4 : 5 + n_band], refs[5 + n_band :]
    out_ref, metadata, sum_ref, product_ref, meta_sems = refs[0], refs[1:3], *refs[3:]
    place_ref, index_ref = metadata
    rows = sizes[0]
    finish(copies_of(zip(metadata_in, metadata), meta_sems))
    fetch = arrived_blocks_of(sizes, width_k, place_ref, field, arrived_ref)

    def diags(row):
        return index_ref[0, 0, rows + row]

    gather_solve(sizes, fetch, diags, [], terms, inverse_ref, sum_ref, product_ref)
    out_ref[...] = sum_ref[...].reshape(out_ref.shape)


def pack_kernel(sizes, width_k, n_band, *refs):
    rows, n_rows, cap, n_tiles, n_rhs = sizes
    list_in, near_in, first_ref, tile_ref, send_out = refs[:5]
    band_out, refs = refs[5 : 5 + n_band], refs[5 + n_band :]
    list_ref, near_ref, product_ref, send_ref = refs[:4]
    band_refs, (meta_sems, send_sems) = refs[4 : 4 + n_band], refs[4 + n_band :]
    list_in = list_in.at[:, :, pl.ds(0, LANES)]
    metadata = copies_of(((list_in, list_ref), (near_in, near_ref)), meta_sems)
    table_products(first_ref[...].reshape(rows * n_rhs, -1), tile_ref, product_ref)
    finish(metadata)
    pack_bands(sizes, width_k, product_ref, near_ref, band_refs)
    for owner in range(n_rows):
        for rank in range(cap):
            block = product_ref[below(list_ref[owner, 0, rank], rows * n_tiles)]
            send_ref[owner, rank * n_rhs : (rank + 1) * n_rhs, :] = block
    finish(copies_of(zip((send_ref, *band_refs), (send_out, *band_out)), send_sems))


def own_kernel(sizes, width_k, *refs):
    rows, n_rows, cap, n_tiles, n_rhs = sizes
    metadata_in, first_ref, tile_ref, extra = list(refs[:2]), *refs[2:4], refs[4:8]
    send_out, band_out, metadata, product_ref, send_ref, band_ref = refs[8], refs[9], refs[10:12], *refs[12:15]
    held, value_ref, spread_ref, result_ref, meta_sems, load_sems, send_sems = refs[15:19], *refs[19:]
    list_ref, near_ref = metadata
    metadata_in[0] = metadata_in[0].at[:, :, pl.ds(0, LANES)]
    metadata = copies_of(zip(metadata_in, metadata), meta_sems)
    fetched = copies_of(zip(extra, held), load_sems)
    table_products(first_ref[...].reshape(rows * n_rhs, -1), tile_ref, product_ref)
    finish(metadata)
    copies = []

    def send(source, target):
        copies.extend(started([pltpu.make_async_copy(source, target, send_sems.at[len(copies)])]))

    pack_bands(sizes, width_k, product_ref, near_ref, (band_ref,))
    send(band_ref, band_out)
    body, half = cap * n_rhs, n_rows // 2
    upper = lax.axis_index("rows") >= half
    mine, others = jnp.where(upper, half, 0), jnp.where(upper, 0, half)
    finish(fetched[:1])
    functional_ref, count_ref, place_ref, partial_ref = held
    n_blocks = n_rows * cap + rows
    n_func = spread_ref.shape[0] // n_blocks
    n_diag = functional_ref.shape[0] // n_func

    def spread(done, blocks, kinds):
        spread_values(n_rhs, n_func, functional_ref, blocks, kinds, value_ref, spread_ref, done)

    kinds = [near_ref[0, 0, rows + row] for row in range(rows)]
    spread(n_rows * cap, band_ref[...].reshape(rows * n_rhs, -1), kinds)
    kinds = []
    for order in range(n_rows):
        owner = order % half + (mine if order < half else others)
        for rank in range(cap):
            code = list_ref[owner, 0, rank]
            kinds.append(below(over(code, rows * n_tiles * rows), n_diag))
            block = product_ref[below(code, rows * n_tiles)]
            send_ref[order, rank * n_rhs : (rank + 1) * n_rhs, :] = block
        if order < half:
            send(send_ref.at[order], send_out.at[order, pl.ds(0, body)])
        if order % 2:
            blocks = jnp.concatenate([send_ref[order - 1], send_ref[order]], axis=0)
            spread((order - 1) * cap, blocks, kinds)
            kinds = []
    finish(fetched[1:])
    result = coarse_parts(n_rhs, n_blocks, count_ref, place_ref, partial_ref, spread_ref)
    result_ref[...] = result.reshape(result_ref.shape)
    depth = result_ref.shape[1]
    for n, first in enumerate((mine, others)):
        target = send_out.at[:, pl.ds(body + n * depth, depth)]
        send(result_ref.at[pl.ds(first, half)], target)
    finish(copies)


def mirror_kernel(
    sizes,
    list_in,
    inner_ref,
    outer_ref,
    tile_ref,
    inverse_ref,
    send_out,
    list_ref,
    product_ref,
    block_ref,
    solved_ref,
    send_ref,
    sems,
):
    rows, n_rows, cap, n_tiles, n_rhs = sizes
    half, n_diag = n_rows // 2, inverse_ref.shape[0]
    base = jnp.where(lax.axis_index("rows") >= half, half, 0)
    list_in = list_in.at[pl.ds(base, half), :, pl.ds(0, LANES)]
    metadata = started([pltpu.make_async_copy(list_in, list_ref, sems.at[half])])
    quarter = lax.div(lax.axis_index("rows") * 4, n_rows)
    mirror = jnp.where((quarter == 1) | (quarter == 2), outer_ref[...], inner_ref[...])
    table_products(mirror.reshape(rows * n_rhs, -1), tile_ref, product_ref)
    finish(metadata)
    codes = [list_ref[n // cap, 0, LANES // 2 + n % cap] for n in range(half * cap)]
    for n, code in enumerate(codes):
        block_ref[n] = product_ref[below(code, rows * n_tiles)]
    values = block_ref[...].reshape(half * cap * n_rhs, -1)
    table_products(values, inverse_ref, solved_ref)
    copies = []
    for n, code in enumerate(codes):
        device, rank = n // cap, n % cap
        kind = below(over(code, rows * n_tiles * rows), n_diag)
        send_ref[device, rank * n_rhs : (rank + 1) * n_rhs, :] = solved_ref[kind * len(codes) + n]
        if rank == cap - 1:
            copy = pltpu.make_async_copy(send_ref.at[device], send_out.at[device], sems.at[device])
            copies += started([copy])
    finish(copies)


def coarse_parts(n_rhs, n_blocks, count_ref, place_ref, partial_ref, spread_ref):
    n_func = spread_ref.shape[0] // n_blocks
    values = [
        spread_ref[pl.ds(t, n_blocks, stride=n_func), :] for t in range(count_ref.shape[1] // n_blocks)
    ]
    values = jnp.concatenate(values, axis=0)
    partial = jnp.dot(
        count_ref[...], jnp.concatenate(halves(values), axis=1), preferred_element_type=jnp.float32
    )
    partial = partial[:, :LANES] + partial[:, LANES:] + partial_ref[...]
    shift = LANES // 2
    while shift >= n_rhs:
        partial = partial + pltpu.roll(partial, shift, axis=1)
        shift //= 2
    return place(place_ref, partial, n_rhs, 2)


def part_kernel(arrived_ref, keep_ref, give_ref):
    depth = keep_ref.shape[0] // 2
    body = arrived_ref.shape[1] - 4 * depth
    total = arrived_ref[0, body:, :]
    for source in range(1, arrived_ref.shape[0]):
        total = total + arrived_ref[source, body:, :]
    lower = lax.axis_index("band") == 0
    for n in range(2):
        zero, one = (total[(2 * n + m) * depth : (2 * n + m + 1) * depth] for m in range(2))
        keep_ref[n * depth : (n + 1) * depth] = jnp.where(lower, zero, one)
        give_ref[n * depth : (n + 1) * depth] = jnp.where(lower, one, zero)


def half_blocks_of(sizes, width_k, place_ref, arrived_ref, far):
    rows, n_rows, cap, n_tiles, n_rhs = sizes

    def fetch(row):
        total = None
        for k in range(width_k):
            slot = place_ref[0, 0, k * rows + row]
            holder, slot = over(slot, 2 * cap), below(slot, 2 * cap)
            start = pl.ds(pl.multiple_of(below(slot, cap) * n_rhs, n_rhs), n_rhs)
            mine = slot >= cap if far else slot < cap
            block = jnp.where(mine, arrived_ref[holder, start, :], 0.0)
            total = block if total is None else total + block
        return total

    return fetch


def base_kernel(sizes, width_k, *refs):
    metadata_in, own_ref, inverse_ref, terms_in, out_ref = refs[:2], *refs[2:4], refs[4:6], refs[6]
    metadata, sum_ref, product_ref, terms, term_sems, meta_sems = refs[7:9], *refs[9:11], refs[11:13], *refs[13:]
    place_ref, index_ref = metadata
    rows = sizes[0]
    metadata = copies_of(zip(metadata_in, metadata), meta_sems)
    later = copies_of(zip(terms_in, terms), term_sems)
    finish(metadata)
    fetch = half_blocks_of(sizes, width_k, place_ref, own_ref, False)

    def diags(row):
        return index_ref[0, 0, rows + row]

    gather_solve(sizes, fetch, diags, later, terms, inverse_ref, sum_ref, product_ref)
    out_ref[...] = sum_ref[...].reshape(out_ref.shape)


def final_kernel(sizes, width_k, *refs):
    place_in, mirror_ref, base_ref, near_ref, far_ref, scale_ref, out_ref, place_ref, sem = refs
    rows, n_rows, cap, n_tiles, n_rhs = sizes
    metadata = pltpu.make_async_copy(place_in, place_ref, sem)
    metadata.start()
    depth = scale_ref.shape[0]
    correction = (near_ref[...] + far_ref[...]) / scale_ref[...]
    padded = jnp.concatenate([correction, jnp.zeros((8 - depth, LANES), jnp.float32)], axis=0)
    turned = padded.T
    metadata.wait()
    fetch = half_blocks_of(sizes, width_k, place_ref, mirror_ref, True)
    for row in range(rows):
        spot, place = row // depth, row % depth
        column = turned[spot * n_rhs : (spot + 1) * n_rhs, place : place + 1]
        out_ref[row] = (base_ref[row] + column) + fetch(row)


def shifted(value, axis, steps):
    count = lax.axis_size(axis)
    initial, last = (max(0, -steps), min(count, count - steps))
    return lax.ppermute(value, axis, [(source, source + steps) for source in range(initial, last)])


def to_bands(sends):
    if len(sends) == 1:
        return (lax.ppermute(sends[0], "band", [(0, 1), (1, 0)]),)
    return shifted(sends[0], "band", 1), shifted(sends[1], "band", -1)


def on_device(
    start_iterate,
    right_side,
    diag_table,
    inverse_table,
    coupling_tiles,
    diag_index,
    tile_index,
    source_owner,
    source_local,
    aggregate_map,
):
    rows, n_rhs, states = start_iterate.shape
    width_k = source_owner.shape[1]
    n_tiles, n_diag = coupling_tiles.shape[0], inverse_table.shape[0]
    n_rows, n_bands = lax.axis_size("rows"), lax.axis_size("band")
    n_dev = n_rows * n_bands
    cap = max(2, 2 * width_k * rows // n_rows)
    slots = n_rows * cap
    total_groups = AGG_DEV * n_dev
    per_tile = LANES // n_rhs
    depth = rows // per_tile
    n_func = 16
    dense = (
        n_bands == 2
        and n_dev * rows * total_groups <= DENSE_LIMIT
        and depth == 4
        and n_rows % 4 == 0
        and n_diag * n_func == LANES
        and n_tiles + 2 <= n_func
    )
    sizes = (rows, n_rows, cap, n_tiles, n_rhs)
    f32, i32 = jnp.float32, jnp.int32
    my_band = lax.axis_index("band")
    my_row = lax.axis_index("rows")

    half = n_rows // 2
    wide = -(-(4 + 2 * width_k) * rows // LANES) * LANES
    place_wide = -(-2 * width_k * rows // LANES) * LANES
    index_shapes = [(width_k, rows), (width_k, rows), (width_k + 2, rows), (1, rows), (1, rows)]
    halves_of_rows = [list(range(half)), list(range(half, n_rows))]
    to_mirror = [(i, (i + half) % n_rows) for i in range(n_rows)]
    mirror = lax.ppermute(start_iterate, "rows", to_mirror)
    lists, index, places = call(
        functools.partial(request_kernel, (rows, n_rows, cap, n_tiles, n_diag)),
        (
            jax.ShapeDtypeStruct((n_rows, 1, LANES + wide), i32),
            jax.ShapeDtypeStruct((1, 1, wide), i32),
            jax.ShapeDtypeStruct((1, 1, place_wide), i32),
        ),
        [HBM] * 5,
        [VMEM] * 3,
        [*[pltpu.VMEM(shape, i32) for shape in index_shapes], pltpu.SemaphoreType.DMA((5,))],
    )(source_owner.T, source_local.T, tile_index.T, diag_index[None], aggregate_map.T)
    lists = lax.all_to_all(lists, "rows", split_axis=0, concat_axis=0, tiled=True)
    if n_bands == 2:
        near = lax.ppermute(index, "band", [(0, 1), (1, 0)])
    else:
        ways = [[(b, (b + step) % n_bands) for b in range(n_bands)] for step in (-1, 1)]
        near = jnp.concatenate([lax.ppermute(index, "band", way) for way in ways], axis=0)

    n_ways = 1 if n_bands == 2 else 2
    block = (rows, n_rhs, states)
    band_shapes = [jax.ShapeDtypeStruct(block, f32)] * n_ways
    band_scratch = [pltpu.VMEM(block, f32)] * n_ways
    term_scratch = [pltpu.VMEM(block, f32)] * (1 + n_ways)
    term_sems = pltpu.SemaphoreType.DMA((1 + n_ways,))
    list_scratch = pltpu.SMEM((half, 1, LANES), i32)
    near_scratch = pltpu.SMEM((n_ways, 1, wide), i32)
    row_scratch = [pltpu.SMEM((1, 1, place_wide), i32), pltpu.SMEM((1, 1, wide), i32)]
    flat = rows * n_rhs
    sums = pltpu.VMEM((flat, states), f32)
    products = pltpu.VMEM((max(n_tiles, n_diag) * rows, n_rhs, states), f32)
    work = 6 * flat * states * states
    made_shape = (n_tiles * rows, n_rhs, states)
    table_scratch = [pltpu.VMEM(coupling_tiles.shape, f32)]
    table_sems = pltpu.SemaphoreType.DMA((-(-n_tiles // 2),))
    made = call(
        product_kernel,
        jax.ShapeDtypeStruct(made_shape, f32),
        [HBM, HBM],
        VMEM,
        [
            pltpu.VMEM(block, f32),
            *table_scratch,
            pltpu.SemaphoreType.DMA,
            table_sems,
        ],
        work * n_tiles,
        4 << 20,
    )(start_iterate, coupling_tiles)
    packed, *bands = call(
        functools.partial(first_kernel, sizes, width_k, n_ways),
        (jax.ShapeDtypeStruct((half, 2 * cap, n_rhs, states), f32), *band_shapes),
        [VMEM, VMEM, VMEM, ANY, ANY],
        [HBM] * (1 + n_ways),
        [
            pltpu.VMEM(made_shape, f32),
            list_scratch,
            near_scratch,
            pltpu.VMEM((half, 2 * cap, n_rhs, states), f32),
            *band_scratch,
            pltpu.SemaphoreType.DMA((2,)),
            pltpu.SemaphoreType.DMA((2 * half + n_ways,)),
        ],
        work * n_tiles,
        4 << 20,
    )(made, mirror, coupling_tiles, lists, near)
    packed, late = lax.optimization_barrier((packed, lists))
    if dense:
        across = lax.ppermute(late, "band", [(0, 1), (1, 0)])
        across, *bands = lax.optimization_barrier((across, *bands))
    sends = (packed.reshape(half, 2 * cap * n_rhs, states), *bands)
    halves_of_rows = [list(range(half)), list(range(half, n_rows))]
    def exchange(sends, groups=None):
        arrived = lax.all_to_all(
            sends[0], "rows", split_axis=0, concat_axis=0, tiled=True, axis_index_groups=groups
        )
        return arrived, to_bands(sends[1:])

    arrived_blocks, arrived_bands = exchange(sends, halves_of_rows)

    if dense:
        fields = jnp.stack([late, across])[:, :, 0, LANES:]
        fields = fields.reshape(2, n_rows, -1, rows).transpose(2, 0, 1, 3)
        fields = fields.reshape(-1, 2, n_rows * rows)
        n_blocks = slots + rows
        length = n_dev * depth
        extra_shapes = [
            ((n_diag * n_func, 3 * states), jnp.bfloat16),
            ((total_groups, (n_tiles + 1) * n_blocks), jnp.bfloat16),
            ((per_tile * length, total_groups), jnp.bfloat16),
            ((total_groups, LANES), f32),
        ]
        functional_shape, count_shape, placing_shape, partial_shape = extra_shapes
        counts, functionals, placing, partial, scale = call(
            functools.partial(count_kernel, sizes, width_k, n_func),
            (
                jax.ShapeDtypeStruct(*count_shape),
                jax.ShapeDtypeStruct(*functional_shape),
                jax.ShapeDtypeStruct(*placing_shape),
                jax.ShapeDtypeStruct(*partial_shape),
                jax.ShapeDtypeStruct((depth, LANES), f32),
            ),
            [ANY, HBM] + [VMEM] * 5,
            [HBM] * 4 + [VMEM],
            [
                pltpu.VMEM(*count_shape),
                pltpu.VMEM(*functional_shape),
                pltpu.VMEM(*placing_shape),
                pltpu.VMEM(*partial_shape),
                row_scratch[1],
                pltpu.VMEM(block, f32),
                pltpu.VMEM((n_diag * n_func, flat), f32),
                pltpu.VMEM((rows * n_func, LANES), f32),
                pltpu.SemaphoreType.DMA((2,)),
                pltpu.SemaphoreType.DMA((4,)),
            ],
            4 * total_groups * n_tiles * n_dev * rows * n_blocks,
            4 << 20,
        )(
            index, right_side, fields, late[:, 0, :LANES], coupling_tiles, diag_table, inverse_table
        )
        extra_scratch = [
            *[pltpu.VMEM(*shape) for shape in extra_shapes],
            pltpu.VMEM((n_diag * n_func, n_blocks * n_rhs), f32),
            pltpu.VMEM((n_blocks * n_func, LANES), f32),
            pltpu.VMEM((n_rows, n_bands * depth, LANES), f32),
        ]

        made = (arrived_blocks, functionals, counts, placing, partial, scale)
        made = lax.optimization_barrier(made)
        arrived_blocks, functionals, counts, placing, partial, scale = made

    def solve(field, arrived, bands):
        return call(
            functools.partial(solve_kernel, sizes, width_k, n_ways, field),
            jax.ShapeDtypeStruct(block, f32),
            [ANY] * 2 + [VMEM] * (3 + n_ways),
            VMEM,
            [*row_scratch, sums, products, pltpu.SemaphoreType.DMA((2,))],
            work * n_diag,
            4 << 20,
        )(places, index, arrived, inverse_table, right_side, *bands)

    first = solve(0, arrived_blocks, arrived_bands)
    body = cap * n_rhs
    full_list = pltpu.SMEM((n_rows, 1, LANES), i32)
    if dense:
        outer = [(i, j) for i, j in to_mirror if i * 4 // n_rows in (0, 3)]
        inner = [(i, j) for i, j in to_mirror if i * 4 // n_rows in (1, 2)]
        inner = lax.ppermute(first, "rows", inner)
        outer = lax.ppermute(first, "rows", outer)
        own, band = call(
            functools.partial(own_kernel, sizes, width_k),
            (
                jax.ShapeDtypeStruct((half, body + 2 * n_bands * depth, states), f32),
                jax.ShapeDtypeStruct(block, f32),
            ),
            [ANY] * 2 + [VMEM] * 2 + [HBM] * 4,
            [HBM] * 2,
            [
                full_list,
                near_scratch,
                products,
                pltpu.VMEM((n_rows, body, states), f32),
                pltpu.VMEM(block, f32),
                *extra_scratch,
                pltpu.SemaphoreType.DMA((2,)),
                pltpu.SemaphoreType.DMA((4,)),
                pltpu.SemaphoreType.DMA((half + 3,)),
            ],
            2 * work * n_tiles,
            4 << 20,
        )(lists, near, first, coupling_tiles, functionals, counts, placing, partial)
        own, (band,) = exchange((own, band), halves_of_rows)
        packed = call(
            functools.partial(mirror_kernel, sizes),
            jax.ShapeDtypeStruct((half, body, states), f32),
            [ANY] + [VMEM] * 4,
            HBM,
            [
                list_scratch,
                products,
                pltpu.VMEM((half * cap, n_rhs, states), f32),
                pltpu.VMEM((n_diag * half * cap, n_rhs, states), f32),
                pltpu.VMEM((half, body, states), f32),
                pltpu.SemaphoreType.DMA((half + 1,)),
            ],
            BEHIND_SWAP * work * n_tiles,
            4 << 20,
        )(lists, inner, outer, coupling_tiles, inverse_table)
        packed, band = lax.optimization_barrier((packed, band))
        swapped = lax.all_to_all(
            packed, "rows", split_axis=0, concat_axis=0, tiled=True, axis_index_groups=halves_of_rows
        )
        part = jax.ShapeDtypeStruct((2 * depth, LANES), f32)
        keep, give = call(part_kernel, (part, part), [VMEM], [VMEM] * 2)(own)
        keep = keep + lax.ppermute(give, "band", [(0, 1), (1, 0)])
        far = lax.ppermute(keep[depth:], "rows", to_mirror)
        base = call(
            functools.partial(base_kernel, sizes, width_k),
            jax.ShapeDtypeStruct(block, f32),
            [ANY] * 2 + [VMEM] * 2 + [HBM, ANY],
            VMEM,
            [
                *row_scratch,
                sums,
                products,
                *term_scratch,
                term_sems,
                pltpu.SemaphoreType.DMA((2,)),
            ],
            work * n_diag,
            4 << 20,
        )(places, index, own, inverse_table, right_side, band)
        return call(
            functools.partial(final_kernel, sizes, width_k),
            jax.ShapeDtypeStruct(block, f32),
            [ANY] + [VMEM] * 5,
            VMEM,
            [row_scratch[0], pltpu.SemaphoreType.DMA],
            0,
            4 << 20,
        )(places, swapped, base, keep[:depth], far, scale)

    sends = call(
        functools.partial(pack_kernel, sizes, width_k, n_ways),
        (jax.ShapeDtypeStruct((n_rows, body, states), f32), *band_shapes),
        [ANY] * 2 + [VMEM] * 2,
        [HBM] * (1 + n_ways),
        [
            full_list,
            near_scratch,
            products,
            pltpu.VMEM((n_rows, body, states), f32),
            *band_scratch,
            pltpu.SemaphoreType.DMA((2,)),
            pltpu.SemaphoreType.DMA((1 + n_ways,)),
        ],
        work * n_tiles,
        4 << 20,
    )(lists, near, first, coupling_tiles)
    arrived_blocks, arrived_bands = exchange(sends)
    second = solve(width_k, arrived_blocks, arrived_bands)

    groups = aggregate_map[:, 0]
    own = jnp.arange(rows, dtype=i32)
    index_all = lax.all_gather(index, ("band", "rows"), axis=0, tiled=True)
    index_all = index_all.reshape(n_bands, n_rows, wide)
    groups_all, diags_all = index_all[:, :, :rows], index_all[:, :, rows : 2 * rows]
    codes = lists[:, 0, :cap]
    asked = jnp.arange(n_rows, dtype=i32)[:, None] * rows + codes // (rows * n_tiles) % rows
    asked = jnp.where(codes > 0, asked, -1).reshape(-1)
    table_sums = jnp.sum(diag_table, axis=(1, 2))
    diag_onehot = diags_all.reshape(-1, 1) == jnp.arange(n_diag, dtype=i32)[None]
    block_sums = jnp.sum(jnp.where(diag_onehot, table_sums[None], 0.0), axis=1)
    whole_diag = jnp.sum(
        jnp.where(groups[:, None] == groups_all.reshape(-1)[None], block_sums[None], 0.0), axis=1
    )
    above, below = near[0, 0], near[-1, 0]
    place_of = (2 + width_k) * rows
    band_tiles = jnp.stack([above[place_of : place_of + rows], below[place_of + rows : place_of + 2 * rows]])
    band_groups = jnp.stack([above[:rows], below[:rows]])
    band_valid = jnp.stack([my_band + 1 < n_bands, my_band > 0])
    band_valid = jnp.broadcast_to(band_valid[:, None], (2, rows))
    n_all = n_tiles + n_diag + 1
    code = codes.reshape(-1)
    band_of_mine = lax.dynamic_index_in_dim(groups_all, my_band, 0, keepdims=False).reshape(-1)
    entry_group = jnp.concatenate(
        [jnp.take(band_of_mine, jnp.maximum(asked, 0)), band_groups.reshape(-1), groups, groups]
    )
    entry_func = jnp.concatenate(
        [
            (code % rows) * n_all + (code // rows) % n_tiles,
            (own[None] * n_all + band_tiles).reshape(-1),
            own * n_all + n_tiles + diag_index,
            own * n_all + n_tiles + n_diag,
        ]
    )
    entry_valid = jnp.concatenate([asked >= 0, band_valid.reshape(-1), jnp.ones((2 * rows,), bool)])
    functionals = jnp.concatenate(
        [jnp.sum(coupling_tiles, axis=1), -jnp.sum(diag_table, axis=1)], axis=0
    )
    weights = jnp.einsum("fp,rcp->rfc", functionals, second, precision=HIGH)
    weights = jnp.concatenate([weights, jnp.sum(right_side, axis=2)[:, None]], axis=1)
    chosen = jnp.take(weights.reshape(rows * n_all, n_rhs), entry_func, axis=0)
    chosen = jnp.where(entry_valid[:, None], chosen, 0.0)
    partial = jax.ops.segment_sum(chosen, entry_group, num_segments=total_groups)
    whole = lax.psum(partial, ("band", "rows"))
    correction = jnp.take(whole, groups, axis=0) / whole_diag[:, None]
    return second + correction[:, :, None]


def solution(mesh):
    in_specs = (
        P(("band", "rows"), None, None),
        P(("band", "rows"), None, None),
        P(),
        P(),
        P(),
        P(("band", "rows")),
        P(("band", "rows"), None),
        P(("band", "rows"), None),
        P(("band", "rows"), None),
        P(("band", "rows"), None),
    )
    out_specs = P(("band", "rows"), None, None)
    return jax.shard_map(
        on_device, mesh=mesh, in_specs=in_specs, out_specs=out_specs, check_vma=False
    )
```

```python
import functools

import jax
import jax.numpy as jnp
from jax import lax
from jax.experimental import pallas as pl
from jax.experimental.pallas import tpu as pltpu
from jax.sharding import PartitionSpec as P

AGG_DEV = 8
LANES = 128
DENSE_LIMIT = 1 << 19
BEHIND_SWAP = 100

VMEM = pl.BlockSpec(memory_space=pltpu.VMEM)
SMEM = pl.BlockSpec(memory_space=pltpu.SMEM)
HBM = pl.BlockSpec(memory_space=pltpu.HBM)
ANY = pl.BlockSpec(memory_space=pl.ANY)
HIGH = lax.Precision.HIGHEST


def params():
    return pltpu.CompilerParams(vmem_limit_bytes=24 * 1024 * 1024)


def call(kernel, out_shape, in_specs, out_specs, scratch=(), flops=0, moved=0):
    def shaped(shape, spec):
        return pltpu.HBM(shape.shape, shape.dtype) if spec is HBM else shape

    if isinstance(out_shape, (tuple, list)):
        out_shape = [shaped(*pair) for pair in zip(out_shape, out_specs)]
    else:
        out_shape = shaped(out_shape, out_specs)
    run = pl.pallas_call(
        kernel,
        out_shape=out_shape,
        in_specs=in_specs,
        out_specs=out_specs,
        scratch_shapes=list(scratch),
        compiler_params=params(),
        cost_estimate=pl.CostEstimate(flops=flops, bytes_accessed=moved, transcendentals=0),
    )

    def apply(*args):
        pinned = [
            pltpu.with_memory_space_constraint(arg, pltpu.HBM) if spec is HBM else arg
            for arg, spec in zip(args, in_specs)
        ]
        return run(*pinned)

    return apply


def below(value, bound):
    return value & (bound - 1) if bound & (bound - 1) == 0 else lax.rem(value, bound)


def over(value, bound):
    if bound & (bound - 1) == 0:
        return lax.shift_right_logical(value, bound.bit_length() - 1)
    return lax.div(value, bound)


def halves(value):
    high = value.astype(jnp.bfloat16)
    low = (value - high.astype(jnp.float32)).astype(jnp.bfloat16)
    return high, low


def left_operand(value):
    high, low = halves(value)
    return jnp.concatenate([high, low, high], axis=1)


def right_operand(value):
    high, low = halves(value)
    return jnp.concatenate([high, high, low], axis=1)


def dot_nt(left, right):
    return lax.dot_general(
        left, right, (((1,), (1,)), ((), ())), preferred_element_type=jnp.float32
    )


def table_products(value, table_ref, out_ref, done=None, loads=None):
    left = left_operand(value)
    count, width = table_ref.shape[0], table_ref.shape[1]
    n_rhs = out_ref.shape[1]
    rows = left.shape[0] // n_rhs
    for first in range(0, count, 2):
        last = min(first + 2, count)
        if loads is not None:
            loads[first // 2].wait()
        right = right_operand(table_ref[first:last].reshape((last - first) * width, -1))
        product = dot_nt(left, right)
        for t in range(first, last):
            part = product[:, (t - first) * width : (t - first + 1) * width]
            out_ref[t * rows : (t + 1) * rows] = part.reshape(rows, n_rhs, width)
        if done is not None:
            done(first * rows, (last - first) * rows)


def started(copies):
    for copy in copies:
        copy.start()
    return copies


def finish(copies):
    for copy in copies:
        copy.wait()


def request_kernel(sizes, *refs):
    rows, n_rows, cap, n_tiles, n_diag = sizes
    inputs, (list_ref, index_ref, place_ref), held, sems = refs[:5], refs[5:8], refs[8:13], refs[13]
    finish(
        started([pltpu.make_async_copy(i, h, sems.at[n]) for n, (i, h) in enumerate(zip(inputs, held))])
    )
    owner_ref, local_ref, tile_ref, diag_ref, group_ref = held
    width_k = owner_ref.shape[0]
    half = n_rows // 2
    row_of = lax.broadcasted_iota(jnp.int32, (rows, rows), 0)
    col_of = lax.broadcasted_iota(jnp.int32, (rows, rows), 1)
    lane = lax.broadcasted_iota(jnp.int32, (rows, LANES), 1)
    owners = lax.broadcasted_iota(jnp.int32, (n_rows, rows), 0)

    def column(row):
        return jnp.sum(jnp.where(row_of == col_of, row, 0), axis=1, keepdims=True)

    def owner_row(k):
        return owner_ref[k : k + 1, :]

    row_ids = lax.broadcasted_iota(jnp.int32, (1, rows), 1)
    owner_columns = [column(owner_row(k)) for k in range(width_k)]
    lists = jnp.zeros((n_rows, LANES), jnp.float32)
    places, half_places = [], []
    for k in range(width_k):
        rank = jnp.zeros((1, rows), jnp.int32)
        for other in range(k + 1):
            match = owner_columns[other] == owner_row(k)
            if other == k:
                match = match & (row_of < col_of)
            rank = rank + jnp.sum(jnp.where(match, 1, 0), axis=0, keepdims=True)
        places.append(owner_row(k) * cap + rank)
        same = (owner_row(k) >= half) == (lax.axis_index("rows") >= half)
        holder = jnp.where(owner_row(k) >= half, owner_row(k) - half, owner_row(k))
        half_places.append(holder * (2 * cap) + rank + jnp.where(same, 0, cap))
        taker = row_ids + rows * (diag_ref[...] + n_diag)
        code = local_ref[k : k + 1, :] + rows * (tile_ref[k : k + 1, :] + n_tiles * taker)
        code, rank = column(code), column(rank)
        mirror = jnp.where(owner_row(k) >= half, owner_row(k) - half, owner_row(k) + half)
        for owner, base in ((owner_row(k), 0), (mirror, LANES // 2)):
            by_rank = jnp.where(lane == rank + base, code, 0).astype(jnp.float32)
            mine = jnp.where(owners == owner, 1.0, 0.0)
            lists = lists + jnp.dot(
                mine, by_rank, precision=HIGH, preferred_element_type=jnp.float32
            )
    lists = (lists + 0.5).astype(jnp.int32)

    def joined(parts, wide):
        spare = wide - len(parts) * rows
        if spare:
            parts = [*parts, jnp.zeros((1, spare), jnp.int32)]
        return jnp.concatenate(parts, axis=1)

    index = [group_ref[...], diag_ref[...]]
    index += [tile_ref[k : k + 1, :] for k in range(width_k + 2)]
    index += [owner_row(k) * rows + local_ref[k : k + 1, :] for k in range(width_k)]
    index = joined(index, index_ref.shape[2])
    index_ref[0] = index
    place_ref[0] = joined(half_places + places, place_ref.shape[2])
    for device in range(n_rows):
        list_ref[device] = jnp.concatenate([lists[device : device + 1, :], index], axis=1)


def copies_of(pairs, sems):
    return started([pltpu.make_async_copy(i, h, sems.at[n]) for n, (i, h) in enumerate(pairs)])


def band_field(rows, width_k, way, n_ways):
    field = (2 + width_k) * rows
    if n_ways == 1:
        return field + jnp.where(lax.axis_index("band") == 0, 0, rows)
    return field + way * rows


def pack_bands(sizes, width_k, product_ref, near_ref, band_refs):
    rows = sizes[0]
    for way, band_ref in enumerate(band_refs):
        field = band_field(rows, width_k, way, len(band_refs))
        for row in range(rows):
            band_ref[row] = product_ref[near_ref[way, 0, field + row] * rows + row]


def table_loads(table_in, table_ref, sems):
    copies = []
    for first in range(0, table_in.shape[0], 2):
        place = pl.ds(first, min(2, table_in.shape[0] - first))
        source, target = table_in.at[place], table_ref.at[place]
        copies.append(pltpu.make_async_copy(source, target, sems.at[first // 2]))
    return started(copies)


def product_kernel(start_in, tile_in, product_ref, start_ref, tile_ref, start_sem, tile_sems):
    start = pltpu.make_async_copy(start_in, start_ref, start_sem)
    start.start()
    loads = table_loads(tile_in, tile_ref, tile_sems)
    start.wait()
    rows, n_rhs, states = start_ref.shape
    values = start_ref[...].reshape(rows * n_rhs, states)
    table_products(values, tile_ref, product_ref, None, loads)


def first_kernel(sizes, width_k, n_band, *refs):
    rows, n_rows, cap, n_tiles, n_rhs = sizes
    own_ref, mirror_ref, tile_ref, list_in, near_in, send_out = refs[:6]
    band_out, refs = refs[6 : 6 + n_band], refs[6 + n_band :]
    product_ref, list_ref, near_ref, send_ref = refs[:4]
    band_refs, (meta_sems, send_sems) = refs[4 : 4 + n_band], refs[4 + n_band :]
    half = n_rows // 2
    base = jnp.where(lax.axis_index("rows") >= half, half, 0)
    list_in = list_in.at[pl.ds(base, half), :, pl.ds(0, LANES)]
    metadata = copies_of(((list_in, list_ref), (near_in, near_ref)), meta_sems)
    values = mirror_ref[...].reshape(rows * n_rhs, -1)
    table_products(values, tile_ref, product_ref)
    finish(metadata)
    copies = []
    for side, blocks_ref in ((0, own_ref), (1, product_ref)):
        for device in range(half):
            for rank in range(cap):
                code = list_ref[device, 0, side * (LANES // 2) + rank]
                block = blocks_ref[below(code, rows * n_tiles)]
                send_ref[device, side * cap + rank] = block
            place = (device, pl.ds(side * cap, cap))
            copies += started(
                [pltpu.make_async_copy(send_ref.at[place], send_out.at[place], send_sems.at[len(copies)])]
            )
    pack_bands(sizes, width_k, own_ref, near_ref, band_refs)
    for ref, out in zip(band_refs, band_out):
        copies += started([pltpu.make_async_copy(ref, out, send_sems.at[len(copies)])])
    finish(copies)


def place(place_ref, values, n_rhs, n_parts):
    per_tile = LANES // n_rhs
    length = place_ref.shape[0] // per_tile
    parts, rest = [], values
    for _ in range(n_parts):
        part = rest.astype(jnp.bfloat16)
        rest = rest - part.astype(jnp.float32)
        parts.append(part)
    parts = jnp.concatenate(parts, axis=1)
    lane = lax.broadcasted_iota(jnp.int32, (length, LANES), 1)
    result = jnp.zeros((length, LANES), jnp.float32)
    placed = jnp.dot(place_ref[...], parts, preferred_element_type=jnp.float32)
    for spot in range(per_tile):
        chosen = placed[spot * length : (spot + 1) * length]
        chosen = sum(chosen[:, n * LANES : (n + 1) * LANES] for n in range(n_parts))
        result = jnp.where((lane >= spot * n_rhs) & (lane < (spot + 1) * n_rhs), chosen, result)
    return result


def spread_values(n_rhs, n_func, functional_ref, blocks, kinds, value_ref, spread_ref, done):
    per_tile = LANES // n_rhs
    lane = lax.broadcasted_iota(jnp.int32, (n_func, LANES), 1)
    columns = slice(done * n_rhs, done * n_rhs + blocks.shape[0])
    value_ref[:, columns] = dot_nt(functional_ref[...], right_operand(blocks))
    for block, kind in enumerate(kinds, done):
        tile, spot = block // per_tile, block % per_tile
        start = pl.multiple_of(kind * n_func, n_func)
        piece = value_ref[pl.ds(start, n_func), tile * LANES : (tile + 1) * LANES]
        piece = jnp.where((lane >= spot * n_rhs) & (lane < (spot + 1) * n_rhs), piece, 0.0)
        spread_ref[block * n_func : (block + 1) * n_func, :] = piece


def one_hot(ids, row):
    return jnp.where(ids == row, 1.0, 0.0).astype(jnp.bfloat16)


def count_kernel(sizes, width_k, n_func, *refs):
    rows, n_rows, cap, n_tiles, n_rhs = sizes
    index_in, right_in, field_ref, list_ref, tile_ref, table_ref, inverse_ref = refs[:7]
    count_out, functional_out, placing_out, partial_out, scale_ref = refs[7:12]
    count_ref, functional_ref, placing_ref, partial_ref = refs[12:16]
    index_ref, right_ref, value_ref, spread_ref, load_sems, sems = refs[16:]
    loads = copies_of(((index_in, index_ref), (right_in, right_ref)), load_sems)
    n_groups = count_ref.shape[0]
    slots, band_rows = n_rows * cap, n_rows * rows
    copies = []

    def send(source, target):
        copies.extend(started([pltpu.make_async_copy(source, target, sems.at[len(copies)])]))

    sums = jnp.sum(tile_ref[...], axis=1)
    line = lax.broadcasted_iota(jnp.int32, (n_func, sums.shape[1]), 0)
    sums = jnp.concatenate([sums, jnp.zeros((n_func - n_tiles, sums.shape[1]), jnp.float32)], axis=0)
    n_diag = inverse_ref.shape[0]
    totals = []
    for d in range(n_diag):
        minus = -jnp.sum(table_ref[d], axis=0, keepdims=True)
        totals.append(-jnp.sum(minus, axis=1, keepdims=True))
        wanted = jnp.where(line == n_tiles, minus, sums)
        high, low = halves(inverse_ref[d])
        right = jnp.concatenate([high, high, low], axis=0)
        solved = jnp.dot(left_operand(wanted), right, preferred_element_type=jnp.float32)
        solved = jnp.where(line == n_tiles + 1, 1.0, solved)
        functional_ref[d * n_func : (d + 1) * n_func, :] = left_operand(solved)
    send(functional_ref, functional_out)

    lists = list_ref[...]
    asker = lax.broadcasted_iota(jnp.int32, lists.shape, 0)
    codes = asker * rows + below(over(lists, rows * n_tiles), rows)
    codes = jnp.where(lists > 0, codes, -1).astype(jnp.float32)
    spread = lax.broadcasted_iota(jnp.int32, (slots, n_rows), 0)
    spread = lax.div(spread, cap) == lax.broadcasted_iota(jnp.int32, (slots, n_rows), 1)
    codes = jnp.dot(
        jnp.where(spread, 1.0, 0.0), codes, precision=HIGH, preferred_element_type=jnp.float32
    )
    rank = lax.rem(lax.broadcasted_iota(jnp.int32, codes.shape, 0), cap)
    lane = lax.broadcasted_iota(jnp.int32, codes.shape, 1)
    asked = jnp.sum(jnp.where(rank == lane, codes, 0.0), axis=1, keepdims=True)
    asked = jnp.where(asked < 0.0, asked - 0.5, asked + 0.5).astype(jnp.int32)
    low, high = asked[: slots // 2], asked[slots // 2 :]
    upper = lax.axis_index("rows") >= n_rows // 2
    asked = jnp.concatenate([jnp.where(upper, high, low), jnp.where(upper, low, high)], axis=0)
    own = lax.axis_index("rows") * rows + lax.broadcasted_iota(jnp.int32, (rows, 1), 0)
    band = lax.axis_index("band")

    def field(n, side):
        return field_ref[n, side : side + 1, :]

    row_ids = lax.broadcasted_iota(jnp.int32, (1, band_rows), 1)
    sides = []
    for side, targets in ((0, jnp.concatenate([asked, own], axis=0)), (1, own)):
        first = band == side
        across = jnp.where(first, field(2 + width_k, 1 - side), field(3 + width_k, 1 - side))
        takers = [field(2 + k, side) * n_groups + field(0, side) for k in range(width_k)]
        takers.append(across * n_groups + field(0, 1 - side))
        takers = jnp.concatenate(takers, axis=1)
        origins = [field(4 + width_k + k, side) for k in range(width_k)] + [row_ids]
        hits = one_hot(targets, jnp.concatenate(origins, axis=1))
        sides.append((takers, hits, field(0, side)))
    pieces, own_pieces = [], []
    ids = lax.broadcasted_iota(jnp.int32, (n_groups, band_rows), 0)
    for t in range(n_tiles + 1):
        found = []
        for takers, hits, groups in sides:
            if t < n_tiles:
                wide = lax.broadcasted_iota(jnp.int32, (n_groups, takers.shape[1]), 0)
                found.append(dot_nt(one_hot(wide + t * n_groups, takers), hits))
            else:
                found.append(dot_nt(one_hot(ids, groups), hits[:, -band_rows:]))
        pieces += [found[0][:, :slots], found[1]]
        own_pieces.append(found[0][:, slots:])
    count_ref[...] = jnp.concatenate(pieces, axis=1).astype(jnp.bfloat16)
    send(count_ref, count_out)

    own_counts = jnp.concatenate([*own_pieces, own_pieces[-1]], axis=1).astype(jnp.bfloat16)
    finish(loads)
    rights = right_ref[...].reshape(rows * n_rhs, -1)
    kinds = [index_ref[0, 0, rows + row] for row in range(rows)]
    spread_values(n_rhs, n_func, functional_ref, rights, kinds, value_ref, spread_ref, 0)
    values = [spread_ref[pl.ds(t, rows, stride=n_func), :] for t in range(n_tiles + 2)]
    values = jnp.concatenate(halves(jnp.concatenate(values, axis=0)), axis=1)
    partial = jnp.dot(own_counts, values, preferred_element_type=jnp.float32)
    partial_ref[...] = partial[:, :LANES] + partial[:, LANES:]
    send(partial_ref, partial_out)

    per_tile = LANES // n_rhs
    depth = rows // per_tile
    length = n_rows * 2 * depth
    order = lax.broadcasted_iota(jnp.int32, (per_tile * length, 1), 0)
    spot, order = lax.div(order, length), lax.rem(order, length)
    device, order = lax.div(order, 2 * depth), lax.rem(order, 2 * depth)
    side, order = lax.div(order, depth), lax.rem(order, depth)
    order = side * band_rows + device * rows + spot * depth + order
    member = [
        one_hot(ids, jnp.where(band == which, field(0, 0), field(0, 1))) for which in range(2)
    ]
    placing = jnp.zeros(placing_ref.shape, jnp.float32)
    for which in range(2):
        placing = placing + dot_nt(one_hot(order, row_ids + which * band_rows), member[which])
    placing_ref[...] = placing.astype(jnp.bfloat16)
    send(placing_ref, placing_out)
    whole = jnp.zeros((n_groups, 1), jnp.float32)
    for side in range(2):
        sums = jnp.zeros((1, band_rows), jnp.float32)
        for d in range(n_diag):
            sums = jnp.where(field(1, side) == d, totals[d], sums)
        weighted = jnp.where(ids == field(0, side), sums, 0.0)
        whole = whole + jnp.sum(weighted, axis=1, keepdims=True)
    scale = place(placing_ref, jnp.broadcast_to(whole, (n_groups, LANES)), n_rhs, 3)
    mine = jnp.zeros(scale_ref.shape, jnp.float32)
    here = lax.axis_index("rows") * 2 + band
    for n in range(2 * n_rows):
        mine = jnp.where(here == n, scale[n * depth : (n + 1) * depth, :], mine)
    scale_ref[...] = mine
    finish(copies)


def gather_solve(sizes, fetch, diags, later, terms, inverse_ref, sum_ref, product_ref):
    rows, n_rows, cap, n_tiles, n_rhs = sizes
    for row in range(rows):
        sum_ref[pl.ds(row * n_rhs, n_rhs), :] = fetch(row)
    finish(later)
    total = sum_ref[...]
    for term in terms:
        total = total + term[...].reshape(total.shape)
    table_products(total, inverse_ref, product_ref)
    for row in range(rows):
        sum_ref[pl.ds(row * n_rhs, n_rhs), :] = product_ref[diags(row) * rows + row]


def arrived_blocks_of(sizes, width_k, place_ref, field, arrived_ref):
    rows, n_rows, cap, n_tiles, n_rhs = sizes
    per = n_rows * cap // arrived_ref.shape[0]

    def fetch(row):
        total = None
        for k in range(width_k):
            slot = place_ref[0, 0, (field + k) * rows + row]
            start = pl.multiple_of(below(slot, per) * n_rhs, n_rhs)
            block = arrived_ref[over(slot, per), pl.ds(start, n_rhs), :]
            total = block if total is None else total + block
        return total

    return fetch


def solve_kernel(sizes, width_k, n_band, field, *refs):
    metadata_in, arrived_ref, inverse_ref = refs[:2], *refs[2:4]
    terms, refs = refs[4 : 5 + n_band], refs[5 + n_band :]
    out_ref, metadata, sum_ref, product_ref, meta_sems = refs[0], refs[1:3], *refs[3:]
    place_ref, index_ref = metadata
    rows = sizes[0]
    metadata = copies_of(zip(metadata_in, metadata), meta_sems)
    total = terms[0][...].reshape(sum_ref.shape)
    for term in terms[1:]:
        total = total + term[...].reshape(sum_ref.shape)
    sum_ref[...] = total
    finish(metadata)
    arrived = arrived_blocks_of(sizes, width_k, place_ref, field, arrived_ref)
    n_rhs = sizes[4]

    def fetch(row):
        return sum_ref[pl.ds(row * n_rhs, n_rhs), :] + arrived(row)

    def diags(row):
        return index_ref[0, 0, rows + row]

    gather_solve(sizes, fetch, diags, [], [], inverse_ref, sum_ref, product_ref)
    out_ref[...] = sum_ref[...].reshape(out_ref.shape)


def pack_kernel(sizes, width_k, n_band, *refs):
    rows, n_rows, cap, n_tiles, n_rhs = sizes
    list_in, near_in, first_ref, tile_ref, send_out = refs[:5]
    band_out, refs = refs[5 : 5 + n_band], refs[5 + n_band :]
    list_ref, near_ref, product_ref, send_ref = refs[:4]
    band_refs, (meta_sems, send_sems) = refs[4 : 4 + n_band], refs[4 + n_band :]
    list_in = list_in.at[:, :, pl.ds(0, LANES)]
    metadata = copies_of(((list_in, list_ref), (near_in, near_ref)), meta_sems)
    table_products(first_ref[...].reshape(rows * n_rhs, -1), tile_ref, product_ref)
    finish(metadata)
    pack_bands(sizes, width_k, product_ref, near_ref, band_refs)
    for owner in range(n_rows):
        for rank in range(cap):
            block = product_ref[below(list_ref[owner, 0, rank], rows * n_tiles)]
            send_ref[owner, rank * n_rhs : (rank + 1) * n_rhs, :] = block
    finish(copies_of(zip((send_ref, *band_refs), (send_out, *band_out)), send_sems))


def own_kernel(sizes, width_k, *refs):
    rows, n_rows, cap, n_tiles, n_rhs = sizes
    metadata_in, first_ref, tile_ref, extra = list(refs[:2]), *refs[2:4], refs[4:8]
    send_out, band_out, metadata, product_ref, send_ref, band_ref = refs[8], refs[9], refs[10:12], *refs[12:15]
    held, value_ref, spread_ref, result_ref, meta_sems, load_sems, send_sems = refs[15:19], *refs[19:]
    list_ref, near_ref = metadata
    metadata_in[0] = metadata_in[0].at[:, :, pl.ds(0, LANES)]
    metadata = copies_of(zip(metadata_in, metadata), meta_sems)
    fetched = copies_of(zip(extra, held), load_sems)
    table_products(first_ref[...].reshape(rows * n_rhs, -1), tile_ref, product_ref)
    finish(metadata)
    copies = []

    def send(source, target):
        copies.extend(started([pltpu.make_async_copy(source, target, send_sems.at[len(copies)])]))

    pack_bands(sizes, width_k, product_ref, near_ref, (band_ref,))
    send(band_ref, band_out)
    body, half = cap * n_rhs, n_rows // 2
    upper = lax.axis_index("rows") >= half
    mine, others = jnp.where(upper, half, 0), jnp.where(upper, 0, half)
    finish(fetched[:1])
    functional_ref, count_ref, place_ref, partial_ref = held
    n_blocks = n_rows * cap + rows
    n_func = spread_ref.shape[0] // n_blocks
    n_diag = functional_ref.shape[0] // n_func

    def spread(done, blocks, kinds):
        spread_values(n_rhs, n_func, functional_ref, blocks, kinds, value_ref, spread_ref, done)

    kinds = [near_ref[0, 0, rows + row] for row in range(rows)]
    spread(n_rows * cap, band_ref[...].reshape(rows * n_rhs, -1), kinds)
    kinds = []
    for order in range(n_rows):
        owner = order % half + (mine if order < half else others)
        for rank in range(cap):
            code = list_ref[owner, 0, rank]
            kinds.append(below(over(code, rows * n_tiles * rows), n_diag))
            block = product_ref[below(code, rows * n_tiles)]
            send_ref[order, rank * n_rhs : (rank + 1) * n_rhs, :] = block
        if order < half:
            send(send_ref.at[order], send_out.at[order, pl.ds(0, body)])
        if order % 2:
            blocks = jnp.concatenate([send_ref[order - 1], send_ref[order]], axis=0)
            spread((order - 1) * cap, blocks, kinds)
            kinds = []
    finish(fetched[1:])
    result = coarse_parts(n_rhs, n_blocks, count_ref, place_ref, partial_ref, spread_ref)
    result_ref[...] = result.reshape(result_ref.shape)
    depth = result_ref.shape[1]
    for n, first in enumerate((mine, others)):
        target = send_out.at[:, pl.ds(body + n * depth, depth)]
        send(result_ref.at[pl.ds(first, half)], target)
    finish(copies)


def mirror_kernel(
    sizes, list_in, mirror_ref, tile_ref, inverse_ref, send_out, list_ref, product_ref, block_ref, solved_ref, send_ref, sems
):
    rows, n_rows, cap, n_tiles, n_rhs = sizes
    half, n_diag = n_rows // 2, inverse_ref.shape[0]
    base = jnp.where(lax.axis_index("rows") >= half, half, 0)
    list_in = list_in.at[pl.ds(base, half), :, pl.ds(0, LANES)]
    metadata = started([pltpu.make_async_copy(list_in, list_ref, sems.at[half])])
    table_products(mirror_ref[...].reshape(rows * n_rhs, -1), tile_ref, product_ref)
    finish(metadata)
    codes = [list_ref[n // cap, 0, LANES // 2 + n % cap] for n in range(half * cap)]
    for n, code in enumerate(codes):
        block_ref[n] = product_ref[below(code, rows * n_tiles)]
    values = block_ref[...].reshape(half * cap * n_rhs, -1)
    table_products(values, inverse_ref, solved_ref)
    copies = []
    for n, code in enumerate(codes):
        device, rank = n // cap, n % cap
        kind = below(over(code, rows * n_tiles * rows), n_diag)
        send_ref[device, rank * n_rhs : (rank + 1) * n_rhs, :] = solved_ref[kind * len(codes) + n]
        if rank == cap - 1:
            copy = pltpu.make_async_copy(send_ref.at[device], send_out.at[device], sems.at[device])
            copies += started([copy])
    finish(copies)


def coarse_parts(n_rhs, n_blocks, count_ref, place_ref, partial_ref, spread_ref):
    n_func = spread_ref.shape[0] // n_blocks
    values = [
        spread_ref[pl.ds(t, n_blocks, stride=n_func), :] for t in range(count_ref.shape[1] // n_blocks)
    ]
    values = jnp.concatenate(values, axis=0)
    partial = jnp.dot(
        count_ref[...], jnp.concatenate(halves(values), axis=1), preferred_element_type=jnp.float32
    )
    partial = partial[:, :LANES] + partial[:, LANES:] + partial_ref[...]
    shift = LANES // 2
    while shift >= n_rhs:
        partial = partial + pltpu.roll(partial, shift, axis=1)
        shift //= 2
    return place(place_ref, partial, n_rhs, 2)


def part_kernel(arrived_ref, keep_ref, give_ref):
    depth = keep_ref.shape[0] // 2
    body = arrived_ref.shape[1] - 4 * depth
    total = arrived_ref[0, body:, :]
    for source in range(1, arrived_ref.shape[0]):
        total = total + arrived_ref[source, body:, :]
    lower = lax.axis_index("band") == 0
    for n in range(2):
        zero, one = (total[(2 * n + m) * depth : (2 * n + m + 1) * depth] for m in range(2))
        keep_ref[n * depth : (n + 1) * depth] = jnp.where(lower, zero, one)
        give_ref[n * depth : (n + 1) * depth] = jnp.where(lower, one, zero)


def half_blocks_of(sizes, width_k, place_ref, arrived_ref, far):
    rows, n_rows, cap, n_tiles, n_rhs = sizes

    def fetch(row):
        total = None
        for k in range(width_k):
            slot = place_ref[0, 0, k * rows + row]
            holder, slot = over(slot, 2 * cap), below(slot, 2 * cap)
            start = pl.ds(pl.multiple_of(below(slot, cap) * n_rhs, n_rhs), n_rhs)
            mine = slot >= cap if far else slot < cap
            block = jnp.where(mine, arrived_ref[holder, start, :], 0.0)
            total = block if total is None else total + block
        return total

    return fetch


def base_kernel(sizes, width_k, *refs):
    metadata_in, own_ref, inverse_ref, terms_in, out_ref = refs[:2], *refs[2:4], refs[4:6], refs[6]
    metadata, sum_ref, product_ref, terms, term_sems, meta_sems = refs[7:9], *refs[9:11], refs[11:13], *refs[13:]
    place_ref, index_ref = metadata
    rows = sizes[0]
    metadata = copies_of(zip(metadata_in, metadata), meta_sems)
    later = copies_of(zip(terms_in, terms), term_sems)
    finish(metadata)
    fetch = half_blocks_of(sizes, width_k, place_ref, own_ref, False)

    def diags(row):
        return index_ref[0, 0, rows + row]

    gather_solve(sizes, fetch, diags, later, terms, inverse_ref, sum_ref, product_ref)
    out_ref[...] = sum_ref[...].reshape(out_ref.shape)


def final_kernel(sizes, width_k, *refs):
    place_in, mirror_ref, base_ref, near_ref, far_ref, scale_ref, out, place_ref, out_ref, sem, out_sems = refs
    rows, n_rows, cap, n_tiles, n_rhs = sizes
    metadata = pltpu.make_async_copy(place_in, place_ref, sem)
    metadata.start()
    depth = scale_ref.shape[0]
    correction = (near_ref[...] + far_ref[...]) / scale_ref[...]
    padded = jnp.concatenate([correction, jnp.zeros((8 - depth, LANES), jnp.float32)], axis=0)
    turned = padded.T
    for row in range(rows):
        spot, place = row // depth, row % depth
        column = turned[spot * n_rhs : (spot + 1) * n_rhs, place : place + 1]
        out_ref[row] = base_ref[row] + column
    metadata.wait()
    fetch = half_blocks_of(sizes, width_k, place_ref, mirror_ref, True)
    step = -(-rows // out_sems.shape[0])
    copies = []
    for first in range(0, rows, step):
        count = min(step, rows - first)
        for row in range(first, first + count):
            out_ref[row] = out_ref[row] + fetch(row)
        place = pl.ds(first, count)
        copy = pltpu.make_async_copy(out_ref.at[place], out.at[place], out_sems.at[len(copies)])
        copies += started([copy])
    finish(copies)


def shifted(value, axis, steps):
    count = lax.axis_size(axis)
    initial, last = (max(0, -steps), min(count, count - steps))
    return lax.ppermute(value, axis, [(source, source + steps) for source in range(initial, last)])


def to_bands(sends):
    if len(sends) == 1:
        return (lax.ppermute(sends[0], "band", [(0, 1), (1, 0)]),)
    return shifted(sends[0], "band", 1), shifted(sends[1], "band", -1)


def on_device(
    start_iterate,
    right_side,
    diag_table,
    inverse_table,
    coupling_tiles,
    diag_index,
    tile_index,
    source_owner,
    source_local,
    aggregate_map,
):
    rows, n_rhs, states = start_iterate.shape
    width_k = source_owner.shape[1]
    n_tiles, n_diag = coupling_tiles.shape[0], inverse_table.shape[0]
    n_rows, n_bands = lax.axis_size("rows"), lax.axis_size("band")
    n_dev = n_rows * n_bands
    cap = max(2, 2 * width_k * rows // n_rows)
    slots = n_rows * cap
    total_groups = AGG_DEV * n_dev
    per_tile = LANES // n_rhs
    depth = rows // per_tile
    n_func = 16
    dense = (
        n_bands == 2
        and n_dev * rows * total_groups <= DENSE_LIMIT
        and depth == 4
        and n_diag * n_func == LANES
        and n_tiles + 2 <= n_func
    )
    sizes = (rows, n_rows, cap, n_tiles, n_rhs)
    f32, i32 = jnp.float32, jnp.int32
    my_band = lax.axis_index("band")
    my_row = lax.axis_index("rows")

    half = n_rows // 2
    wide = -(-(4 + 2 * width_k) * rows // LANES) * LANES
    place_wide = -(-2 * width_k * rows // LANES) * LANES
    index_shapes = [(width_k, rows), (width_k, rows), (width_k + 2, rows), (1, rows), (1, rows)]
    halves_of_rows = [list(range(half)), list(range(half, n_rows))]
    to_mirror = [(i, (i + half) % n_rows) for i in range(n_rows)]
    mirror = lax.ppermute(start_iterate, "rows", to_mirror)
    lists, index, places = call(
        functools.partial(request_kernel, (rows, n_rows, cap, n_tiles, n_diag)),
        (
            jax.ShapeDtypeStruct((n_rows, 1, LANES + wide), i32),
            jax.ShapeDtypeStruct((1, 1, wide), i32),
            jax.ShapeDtypeStruct((1, 1, place_wide), i32),
        ),
        [HBM] * 5,
        [VMEM] * 3,
        [*[pltpu.VMEM(shape, i32) for shape in index_shapes], pltpu.SemaphoreType.DMA((5,))],
    )(source_owner.T, source_local.T, tile_index.T, diag_index[None], aggregate_map.T)
    lists = lax.all_to_all(lists, "rows", split_axis=0, concat_axis=0, tiled=True)
    if n_bands == 2:
        near = lax.ppermute(index, "band", [(0, 1), (1, 0)])
    else:
        ways = [[(b, (b + step) % n_bands) for b in range(n_bands)] for step in (-1, 1)]
        near = jnp.concatenate([lax.ppermute(index, "band", way) for way in ways], axis=0)

    n_ways = 1 if n_bands == 2 else 2
    block = (rows, n_rhs, states)
    band_shapes = [jax.ShapeDtypeStruct(block, f32)] * n_ways
    band_scratch = [pltpu.VMEM(block, f32)] * n_ways
    term_scratch = [pltpu.VMEM(block, f32)] * (1 + n_ways)
    term_sems = pltpu.SemaphoreType.DMA((1 + n_ways,))
    list_scratch = pltpu.SMEM((half, 1, LANES), i32)
    near_scratch = pltpu.SMEM((n_ways, 1, wide), i32)
    row_scratch = [pltpu.SMEM((1, 1, place_wide), i32), pltpu.SMEM((1, 1, wide), i32)]
    flat = rows * n_rhs
    sums = pltpu.VMEM((flat, states), f32)
    products = pltpu.VMEM((max(n_tiles, n_diag) * rows, n_rhs, states), f32)
    work = 6 * flat * states * states
    made_shape = (n_tiles * rows, n_rhs, states)
    table_scratch = [pltpu.VMEM(coupling_tiles.shape, f32)]
    table_sems = pltpu.SemaphoreType.DMA((-(-n_tiles // 2),))
    made = call(
        product_kernel,
        jax.ShapeDtypeStruct(made_shape, f32),
        [HBM, HBM],
        VMEM,
        [
            pltpu.VMEM(block, f32),
            *table_scratch,
            pltpu.SemaphoreType.DMA,
            table_sems,
        ],
        work * n_tiles,
        4 << 20,
    )(start_iterate, coupling_tiles)
    packed, *bands = call(
        functools.partial(first_kernel, sizes, width_k, n_ways),
        (jax.ShapeDtypeStruct((half, 2 * cap, n_rhs, states), f32), *band_shapes),
        [VMEM, VMEM, VMEM, ANY, ANY],
        [HBM] * (1 + n_ways),
        [
            pltpu.VMEM(made_shape, f32),
            list_scratch,
            near_scratch,
            pltpu.VMEM((half, 2 * cap, n_rhs, states), f32),
            *band_scratch,
            pltpu.SemaphoreType.DMA((2,)),
            pltpu.SemaphoreType.DMA((2 * half + n_ways,)),
        ],
        work * n_tiles,
        4 << 20,
    )(made, mirror, coupling_tiles, lists, near)
    packed, late = lax.optimization_barrier((packed, lists))
    if dense:
        across = lax.ppermute(late, "band", [(0, 1), (1, 0)])
        across, *bands = lax.optimization_barrier((across, *bands))
    sends = (packed.reshape(half, 2 * cap * n_rhs, states), *bands)
    halves_of_rows = [list(range(half)), list(range(half, n_rows))]
    def exchange(sends, groups=None):
        arrived = lax.all_to_all(
            sends[0], "rows", split_axis=0, concat_axis=0, tiled=True, axis_index_groups=groups
        )
        return arrived, to_bands(sends[1:])

    arrived_blocks, arrived_bands = exchange(sends, halves_of_rows)

    if dense:
        fields = jnp.stack([late, across])[:, :, 0, LANES:]
        fields = fields.reshape(2, n_rows, -1, rows).transpose(2, 0, 1, 3)
        fields = fields.reshape(-1, 2, n_rows * rows)
        n_blocks = slots + rows
        length = n_dev * depth
        extra_shapes = [
            ((n_diag * n_func, 3 * states), jnp.bfloat16),
            ((total_groups, (n_tiles + 1) * n_blocks), jnp.bfloat16),
            ((per_tile * length, total_groups), jnp.bfloat16),
            ((total_groups, LANES), f32),
        ]
        functional_shape, count_shape, placing_shape, partial_shape = extra_shapes
        counts, functionals, placing, partial, scale = call(
            functools.partial(count_kernel, sizes, width_k, n_func),
            (
                jax.ShapeDtypeStruct(*count_shape),
                jax.ShapeDtypeStruct(*functional_shape),
                jax.ShapeDtypeStruct(*placing_shape),
                jax.ShapeDtypeStruct(*partial_shape),
                jax.ShapeDtypeStruct((depth, LANES), f32),
            ),
            [ANY, HBM] + [VMEM] * 5,
            [HBM] * 4 + [VMEM],
            [
                pltpu.VMEM(*count_shape),
                pltpu.VMEM(*functional_shape),
                pltpu.VMEM(*placing_shape),
                pltpu.VMEM(*partial_shape),
                row_scratch[1],
                pltpu.VMEM(block, f32),
                pltpu.VMEM((n_diag * n_func, flat), f32),
                pltpu.VMEM((rows * n_func, LANES), f32),
                pltpu.SemaphoreType.DMA((2,)),
                pltpu.SemaphoreType.DMA((4,)),
            ],
            4 * total_groups * n_tiles * n_dev * rows * n_blocks,
            4 << 20,
        )(
            index, right_side, fields, late[:, 0, :LANES], coupling_tiles, diag_table, inverse_table
        )
        extra_scratch = [
            *[pltpu.VMEM(*shape) for shape in extra_shapes],
            pltpu.VMEM((n_diag * n_func, n_blocks * n_rhs), f32),
            pltpu.VMEM((n_blocks * n_func, LANES), f32),
            pltpu.VMEM((n_rows, n_bands * depth, LANES), f32),
        ]

        made = (arrived_blocks, functionals, counts, placing, partial, scale)
        made = lax.optimization_barrier(made)
        arrived_blocks, functionals, counts, placing, partial, scale = made

    def solve(field, arrived, bands):
        return call(
            functools.partial(solve_kernel, sizes, width_k, n_ways, field),
            jax.ShapeDtypeStruct(block, f32),
            [ANY] * 2 + [VMEM] * (3 + n_ways),
            VMEM,
            [*row_scratch, sums, products, pltpu.SemaphoreType.DMA((2,))],
            work * n_diag,
            4 << 20,
        )(places, index, arrived, inverse_table, right_side, *bands)

    first = solve(0, arrived_blocks, arrived_bands)
    body = cap * n_rhs
    full_list = pltpu.SMEM((n_rows, 1, LANES), i32)
    if dense:
        mirror = lax.ppermute(first, "rows", to_mirror)
        own, band = call(
            functools.partial(own_kernel, sizes, width_k),
            (
                jax.ShapeDtypeStruct((half, body + 2 * n_bands * depth, states), f32),
                jax.ShapeDtypeStruct(block, f32),
            ),
            [ANY] * 2 + [VMEM] * 2 + [HBM] * 4,
            [HBM] * 2,
            [
                full_list,
                near_scratch,
                products,
                pltpu.VMEM((n_rows, body, states), f32),
                pltpu.VMEM(block, f32),
                *extra_scratch,
                pltpu.SemaphoreType.DMA((2,)),
                pltpu.SemaphoreType.DMA((4,)),
                pltpu.SemaphoreType.DMA((half + 3,)),
            ],
            2 * work * n_tiles,
            4 << 20,
        )(lists, near, first, coupling_tiles, functionals, counts, placing, partial)
        own, (band,) = exchange((own, band), halves_of_rows)
        packed = call(
            functools.partial(mirror_kernel, sizes),
            jax.ShapeDtypeStruct((half, body, states), f32),
            [ANY] + [VMEM] * 3,
            HBM,
            [
                list_scratch,
                products,
                pltpu.VMEM((half * cap, n_rhs, states), f32),
                pltpu.VMEM((n_diag * half * cap, n_rhs, states), f32),
                pltpu.VMEM((half, body, states), f32),
                pltpu.SemaphoreType.DMA((half + 1,)),
            ],
            BEHIND_SWAP * work * n_tiles,
            4 << 20,
        )(lists, mirror, coupling_tiles, inverse_table)
        packed, band = lax.optimization_barrier((packed, band))
        swapped = lax.all_to_all(
            packed, "rows", split_axis=0, concat_axis=0, tiled=True, axis_index_groups=halves_of_rows
        )
        part = jax.ShapeDtypeStruct((2 * depth, LANES), f32)
        keep, give = call(part_kernel, (part, part), [VMEM], [VMEM] * 2)(own)
        keep = keep + lax.ppermute(give, "band", [(0, 1), (1, 0)])
        far = lax.ppermute(keep[depth:], "rows", to_mirror)
        base = call(
            functools.partial(base_kernel, sizes, width_k),
            jax.ShapeDtypeStruct(block, f32),
            [ANY] * 2 + [VMEM] * 2 + [HBM, ANY],
            VMEM,
            [
                *row_scratch,
                sums,
                products,
                *term_scratch,
                term_sems,
                pltpu.SemaphoreType.DMA((2,)),
            ],
            work * n_diag,
            4 << 20,
        )(places, index, own, inverse_table, right_side, band)
        return call(
            functools.partial(final_kernel, sizes, width_k),
            jax.ShapeDtypeStruct(block, f32),
            [ANY] + [VMEM] * 5,
            HBM,
            [
                row_scratch[0],
                pltpu.VMEM(block, f32),
                pltpu.SemaphoreType.DMA,
                pltpu.SemaphoreType.DMA((4,)),
            ],
            0,
            4 << 20,
        )(places, swapped, base, keep[:depth], far, scale)

    sends = call(
        functools.partial(pack_kernel, sizes, width_k, n_ways),
        (jax.ShapeDtypeStruct((n_rows, body, states), f32), *band_shapes),
        [ANY] * 2 + [VMEM] * 2,
        [HBM] * (1 + n_ways),
        [
            full_list,
            near_scratch,
            products,
            pltpu.VMEM((n_rows, body, states), f32),
            *band_scratch,
            pltpu.SemaphoreType.DMA((2,)),
            pltpu.SemaphoreType.DMA((1 + n_ways,)),
        ],
        work * n_tiles,
        4 << 20,
    )(lists, near, first, coupling_tiles)
    arrived_blocks, arrived_bands = exchange(sends)
    second = solve(width_k, arrived_blocks, arrived_bands)

    groups = aggregate_map[:, 0]
    own = jnp.arange(rows, dtype=i32)
    index_all = lax.all_gather(index, ("band", "rows"), axis=0, tiled=True)
    index_all = index_all.reshape(n_bands, n_rows, wide)
    groups_all, diags_all = index_all[:, :, :rows], index_all[:, :, rows : 2 * rows]
    codes = lists[:, 0, :cap]
    asked = jnp.arange(n_rows, dtype=i32)[:, None] * rows + codes // (rows * n_tiles) % rows
    asked = jnp.where(codes > 0, asked, -1).reshape(-1)
    table_sums = jnp.sum(diag_table, axis=(1, 2))
    diag_onehot = diags_all.reshape(-1, 1) == jnp.arange(n_diag, dtype=i32)[None]
    block_sums = jnp.sum(jnp.where(diag_onehot, table_sums[None], 0.0), axis=1)
    whole_diag = jnp.sum(
        jnp.where(groups[:, None] == groups_all.reshape(-1)[None], block_sums[None], 0.0), axis=1
    )
    above, below = near[0, 0], near[-1, 0]
    place_of = (2 + width_k) * rows
    band_tiles = jnp.stack([above[place_of : place_of + rows], below[place_of + rows : place_of + 2 * rows]])
    band_groups = jnp.stack([above[:rows], below[:rows]])
    band_valid = jnp.stack([my_band + 1 < n_bands, my_band > 0])
    band_valid = jnp.broadcast_to(band_valid[:, None], (2, rows))
    n_all = n_tiles + n_diag + 1
    code = codes.reshape(-1)
    band_of_mine = lax.dynamic_index_in_dim(groups_all, my_band, 0, keepdims=False).reshape(-1)
    entry_group = jnp.concatenate(
        [jnp.take(band_of_mine, jnp.maximum(asked, 0)), band_groups.reshape(-1), groups, groups]
    )
    entry_func = jnp.concatenate(
        [
            (code % rows) * n_all + (code // rows) % n_tiles,
            (own[None] * n_all + band_tiles).reshape(-1),
            own * n_all + n_tiles + diag_index,
            own * n_all + n_tiles + n_diag,
        ]
    )
    entry_valid = jnp.concatenate([asked >= 0, band_valid.reshape(-1), jnp.ones((2 * rows,), bool)])
    functionals = jnp.concatenate(
        [jnp.sum(coupling_tiles, axis=1), -jnp.sum(diag_table, axis=1)], axis=0
    )
    weights = jnp.einsum("fp,rcp->rfc", functionals, second, precision=HIGH)
    weights = jnp.concatenate([weights, jnp.sum(right_side, axis=2)[:, None]], axis=1)
    chosen = jnp.take(weights.reshape(rows * n_all, n_rhs), entry_func, axis=0)
    chosen = jnp.where(entry_valid[:, None], chosen, 0.0)
    partial = jax.ops.segment_sum(chosen, entry_group, num_segments=total_groups)
    whole = lax.psum(partial, ("band", "rows"))
    correction = jnp.take(whole, groups, axis=0) / whole_diag[:, None]
    return second + correction[:, :, None]


def solution(mesh):
    in_specs = (
        P(("band", "rows"), None, None),
        P(("band", "rows"), None, None),
        P(),
        P(),
        P(),
        P(("band", "rows")),
        P(("band", "rows"), None),
        P(("band", "rows"), None),
        P(("band", "rows"), None),
        P(("band", "rows"), None),
    )
    out_specs = P(("band", "rows"), None, None)
    return jax.shard_map(
        on_device, mesh=mesh, in_specs=in_specs, out_specs=out_specs, check_vma=False
    )
```

```python
import functools

import jax
import jax.numpy as jnp
from jax import lax
from jax.experimental import pallas as pl
from jax.experimental.pallas import tpu as pltpu
from jax.sharding import PartitionSpec as P

AGG_DEV = 8
LANES = 128
DENSE_LIMIT = 1 << 19
BEHIND_SWAP = 100

VMEM = pl.BlockSpec(memory_space=pltpu.VMEM)
SMEM = pl.BlockSpec(memory_space=pltpu.SMEM)
HBM = pl.BlockSpec(memory_space=pltpu.HBM)
ANY = pl.BlockSpec(memory_space=pl.ANY)
HIGH = lax.Precision.HIGHEST


def params():
    return pltpu.CompilerParams(vmem_limit_bytes=24 * 1024 * 1024)


def call(kernel, out_shape, in_specs, out_specs, scratch=(), flops=0, moved=0):
    def shaped(shape, spec):
        return pltpu.HBM(shape.shape, shape.dtype) if spec is HBM else shape

    if isinstance(out_shape, (tuple, list)):
        out_shape = [shaped(*pair) for pair in zip(out_shape, out_specs)]
    else:
        out_shape = shaped(out_shape, out_specs)
    run = pl.pallas_call(
        kernel,
        out_shape=out_shape,
        in_specs=in_specs,
        out_specs=out_specs,
        scratch_shapes=list(scratch),
        compiler_params=params(),
        cost_estimate=pl.CostEstimate(flops=flops, bytes_accessed=moved, transcendentals=0),
    )

    def apply(*args):
        pinned = [
            pltpu.with_memory_space_constraint(arg, pltpu.HBM) if spec is HBM else arg
            for arg, spec in zip(args, in_specs)
        ]
        return run(*pinned)

    return apply


def below(value, bound):
    return value & (bound - 1) if bound & (bound - 1) == 0 else lax.rem(value, bound)


def over(value, bound):
    if bound & (bound - 1) == 0:
        return lax.shift_right_logical(value, bound.bit_length() - 1)
    return lax.div(value, bound)


def halves(value):
    high = value.astype(jnp.bfloat16)
    low = (value - high.astype(jnp.float32)).astype(jnp.bfloat16)
    return high, low


def left_operand(value):
    high, low = halves(value)
    return jnp.concatenate([high, low, high], axis=1)


def right_operand(value):
    high, low = halves(value)
    return jnp.concatenate([high, high, low], axis=1)


def dot_nt(left, right):
    return lax.dot_general(
        left, right, (((1,), (1,)), ((), ())), preferred_element_type=jnp.float32
    )


def table_products(value, table_ref, out_ref, done=None, loads=None):
    left = left_operand(value)
    count, width = table_ref.shape[0], table_ref.shape[1]
    n_rhs = out_ref.shape[1]
    rows = left.shape[0] // n_rhs
    for first in range(0, count, 2):
        last = min(first + 2, count)
        if loads is not None:
            loads[first // 2].wait()
        right = right_operand(table_ref[first:last].reshape((last - first) * width, -1))
        product = dot_nt(left, right)
        for t in range(first, last):
            part = product[:, (t - first) * width : (t - first + 1) * width]
            out_ref[t * rows : (t + 1) * rows] = part.reshape(rows, n_rhs, width)
        if done is not None:
            done(first * rows, (last - first) * rows)


def started(copies):
    for copy in copies:
        copy.start()
    return copies


def finish(copies):
    for copy in copies:
        copy.wait()


def request_kernel(sizes, *refs):
    rows, n_rows, cap, n_tiles, n_diag = sizes
    inputs, (list_ref, index_ref, place_ref), held, sems = refs[:5], refs[5:8], refs[8:13], refs[13]
    finish(
        started([pltpu.make_async_copy(i, h, sems.at[n]) for n, (i, h) in enumerate(zip(inputs, held))])
    )
    owner_ref, local_ref, tile_ref, diag_ref, group_ref = held
    width_k = owner_ref.shape[0]
    half = n_rows // 2
    row_of = lax.broadcasted_iota(jnp.int32, (rows, rows), 0)
    col_of = lax.broadcasted_iota(jnp.int32, (rows, rows), 1)
    lane = lax.broadcasted_iota(jnp.int32, (rows, LANES), 1)
    owners = lax.broadcasted_iota(jnp.int32, (n_rows, rows), 0)

    def column(row):
        return jnp.sum(jnp.where(row_of == col_of, row, 0), axis=1, keepdims=True)

    def owner_row(k):
        return owner_ref[k : k + 1, :]

    row_ids = lax.broadcasted_iota(jnp.int32, (1, rows), 1)
    owner_columns = [column(owner_row(k)) for k in range(width_k)]
    lists = jnp.zeros((n_rows, LANES), jnp.float32)
    places, half_places = [], []
    for k in range(width_k):
        rank = jnp.zeros((1, rows), jnp.int32)
        for other in range(k + 1):
            match = owner_columns[other] == owner_row(k)
            if other == k:
                match = match & (row_of < col_of)
            rank = rank + jnp.sum(jnp.where(match, 1, 0), axis=0, keepdims=True)
        places.append(owner_row(k) * cap + rank)
        same = (owner_row(k) >= half) == (lax.axis_index("rows") >= half)
        holder = jnp.where(owner_row(k) >= half, owner_row(k) - half, owner_row(k))
        half_places.append(holder * (2 * cap) + rank + jnp.where(same, 0, cap))
        taker = row_ids + rows * (diag_ref[...] + n_diag)
        code = local_ref[k : k + 1, :] + rows * (tile_ref[k : k + 1, :] + n_tiles * taker)
        code, rank = column(code), column(rank)
        mirror = jnp.where(owner_row(k) >= half, owner_row(k) - half, owner_row(k) + half)
        for owner, base in ((owner_row(k), 0), (mirror, LANES // 2)):
            by_rank = jnp.where(lane == rank + base, code, 0).astype(jnp.float32)
            mine = jnp.where(owners == owner, 1.0, 0.0)
            lists = lists + jnp.dot(
                mine, by_rank, precision=HIGH, preferred_element_type=jnp.float32
            )
    lists = (lists + 0.5).astype(jnp.int32)

    def joined(parts, wide):
        spare = wide - len(parts) * rows
        if spare:
            parts = [*parts, jnp.zeros((1, spare), jnp.int32)]
        return jnp.concatenate(parts, axis=1)

    index = [group_ref[...], diag_ref[...]]
    index += [tile_ref[k : k + 1, :] for k in range(width_k + 2)]
    index += [owner_row(k) * rows + local_ref[k : k + 1, :] for k in range(width_k)]
    index = joined(index, index_ref.shape[2])
    index_ref[0] = index
    place_ref[0] = joined(half_places + places, place_ref.shape[2])
    for device in range(n_rows):
        list_ref[device] = jnp.concatenate([lists[device : device + 1, :], index], axis=1)


def copies_of(pairs, sems):
    return started([pltpu.make_async_copy(i, h, sems.at[n]) for n, (i, h) in enumerate(pairs)])


def band_field(rows, width_k, way, n_ways):
    field = (2 + width_k) * rows
    if n_ways == 1:
        return field + jnp.where(lax.axis_index("band") == 0, 0, rows)
    return field + way * rows


def pack_bands(sizes, width_k, product_ref, near_ref, band_refs):
    rows = sizes[0]
    for way, band_ref in enumerate(band_refs):
        field = band_field(rows, width_k, way, len(band_refs))
        for row in range(rows):
            band_ref[row] = product_ref[near_ref[way, 0, field + row] * rows + row]


def table_loads(table_in, table_ref, sems):
    copies = []
    for first in range(0, table_in.shape[0], 2):
        place = pl.ds(first, min(2, table_in.shape[0] - first))
        source, target = table_in.at[place], table_ref.at[place]
        copies.append(pltpu.make_async_copy(source, target, sems.at[first // 2]))
    return started(copies)


def product_kernel(start_in, tile_in, product_ref, start_ref, tile_ref, start_sem, tile_sems):
    start = pltpu.make_async_copy(start_in, start_ref, start_sem)
    start.start()
    loads = table_loads(tile_in, tile_ref, tile_sems)
    start.wait()
    rows, n_rhs, states = start_ref.shape
    values = start_ref[...].reshape(rows * n_rhs, states)
    table_products(values, tile_ref, product_ref, None, loads)


def first_kernel(sizes, width_k, n_band, *refs):
    rows, n_rows, cap, n_tiles, n_rhs = sizes
    own_ref, mirror_ref, tile_ref, list_in, near_in, send_out = refs[:6]
    band_out, refs = refs[6 : 6 + n_band], refs[6 + n_band :]
    product_ref, list_ref, near_ref, send_ref = refs[:4]
    band_refs, (meta_sems, send_sems) = refs[4 : 4 + n_band], refs[4 + n_band :]
    half = n_rows // 2
    base = jnp.where(lax.axis_index("rows") >= half, half, 0)
    list_in = list_in.at[pl.ds(base, half), :, pl.ds(0, LANES)]
    metadata = copies_of(((list_in, list_ref), (near_in, near_ref)), meta_sems)
    values = mirror_ref[...].reshape(rows * n_rhs, -1)
    table_products(values, tile_ref, product_ref)
    finish(metadata)
    copies = []
    def send(source, target):
        copies.extend(started([pltpu.make_async_copy(source, target, send_sems.at[len(copies)])]))

    for side, blocks_ref in ((0, own_ref), (1, product_ref)):
        for device in range(half):
            for rank in range(cap):
                code = list_ref[device, 0, side * (LANES // 2) + rank]
                send_ref[device, side * cap + rank] = blocks_ref[below(code, rows * n_tiles)]
        place = (slice(None), pl.ds(side * cap, cap))
        send(send_ref.at[place], send_out.at[place])
        if side == 0:
            pack_bands(sizes, width_k, own_ref, near_ref, band_refs)
            for ref, out in zip(band_refs, band_out):
                send(ref, out)
    finish(copies)


def place(place_ref, values, n_rhs, n_parts):
    per_tile = LANES // n_rhs
    length = place_ref.shape[0] // per_tile
    parts, rest = [], values
    for _ in range(n_parts):
        part = rest.astype(jnp.bfloat16)
        rest = rest - part.astype(jnp.float32)
        parts.append(part)
    parts = jnp.concatenate(parts, axis=1)
    lane = lax.broadcasted_iota(jnp.int32, (length, LANES), 1)
    result = jnp.zeros((length, LANES), jnp.float32)
    placed = jnp.dot(place_ref[...], parts, preferred_element_type=jnp.float32)
    for spot in range(per_tile):
        chosen = placed[spot * length : (spot + 1) * length]
        chosen = sum(chosen[:, n * LANES : (n + 1) * LANES] for n in range(n_parts))
        result = jnp.where((lane >= spot * n_rhs) & (lane < (spot + 1) * n_rhs), chosen, result)
    return result


def spread_values(n_rhs, n_func, functional_ref, blocks, kinds, value_ref, spread_ref, done):
    per_tile = LANES // n_rhs
    lane = lax.broadcasted_iota(jnp.int32, (n_func, LANES), 1)
    columns = slice(done * n_rhs, done * n_rhs + blocks.shape[0])
    value_ref[:, columns] = dot_nt(functional_ref[...], right_operand(blocks))
    for block, kind in enumerate(kinds, done):
        tile, spot = block // per_tile, block % per_tile
        start = pl.multiple_of(kind * n_func, n_func)
        piece = value_ref[pl.ds(start, n_func), tile * LANES : (tile + 1) * LANES]
        piece = jnp.where((lane >= spot * n_rhs) & (lane < (spot + 1) * n_rhs), piece, 0.0)
        spread_ref[block * n_func : (block + 1) * n_func, :] = piece


def one_hot(ids, row):
    return jnp.where(ids == row, 1.0, 0.0).astype(jnp.bfloat16)


def count_kernel(sizes, width_k, n_func, *refs):
    rows, n_rows, cap, n_tiles, n_rhs = sizes
    index_in, right_in, field_ref, list_ref, tile_ref, table_ref, inverse_ref = refs[:7]
    count_out, functional_out, placing_out, partial_out, scale_ref = refs[7:12]
    count_ref, functional_ref, placing_ref, partial_ref = refs[12:16]
    index_ref, right_ref, value_ref, spread_ref, load_sems, sems = refs[16:]
    loads = copies_of(((index_in, index_ref), (right_in, right_ref)), load_sems)
    n_groups = count_ref.shape[0]
    slots, band_rows = n_rows * cap, n_rows * rows
    copies = []

    def send(source, target):
        copies.extend(started([pltpu.make_async_copy(source, target, sems.at[len(copies)])]))

    sums = jnp.sum(tile_ref[...], axis=1)
    line = lax.broadcasted_iota(jnp.int32, (n_func, sums.shape[1]), 0)
    sums = jnp.concatenate([sums, jnp.zeros((n_func - n_tiles, sums.shape[1]), jnp.float32)], axis=0)
    n_diag = inverse_ref.shape[0]
    totals = []
    for d in range(n_diag):
        minus = -jnp.sum(table_ref[d], axis=0, keepdims=True)
        totals.append(-jnp.sum(minus, axis=1, keepdims=True))
        wanted = jnp.where(line == n_tiles, minus, sums)
        high, low = halves(inverse_ref[d])
        right = jnp.concatenate([high, high, low], axis=0)
        solved = jnp.dot(left_operand(wanted), right, preferred_element_type=jnp.float32)
        solved = jnp.where(line == n_tiles + 1, 1.0, solved)
        functional_ref[d * n_func : (d + 1) * n_func, :] = left_operand(solved)
    send(functional_ref, functional_out)

    lists = list_ref[...]
    asker = lax.broadcasted_iota(jnp.int32, lists.shape, 0)
    codes = asker * rows + below(over(lists, rows * n_tiles), rows)
    codes = jnp.where(lists > 0, codes, -1).astype(jnp.float32)
    spread = lax.broadcasted_iota(jnp.int32, (slots, n_rows), 0)
    spread = lax.div(spread, cap) == lax.broadcasted_iota(jnp.int32, (slots, n_rows), 1)
    codes = jnp.dot(
        jnp.where(spread, 1.0, 0.0), codes, precision=HIGH, preferred_element_type=jnp.float32
    )
    rank = lax.rem(lax.broadcasted_iota(jnp.int32, codes.shape, 0), cap)
    lane = lax.broadcasted_iota(jnp.int32, codes.shape, 1)
    asked = jnp.sum(jnp.where(rank == lane, codes, 0.0), axis=1, keepdims=True)
    asked = jnp.where(asked < 0.0, asked - 0.5, asked + 0.5).astype(jnp.int32)
    low, high = asked[: slots // 2], asked[slots // 2 :]
    upper = lax.axis_index("rows") >= n_rows // 2
    asked = jnp.concatenate([jnp.where(upper, high, low), jnp.where(upper, low, high)], axis=0)
    own = lax.axis_index("rows") * rows + lax.broadcasted_iota(jnp.int32, (rows, 1), 0)
    band = lax.axis_index("band")

    def field(n, side):
        return field_ref[n, side : side + 1, :]

    row_ids = lax.broadcasted_iota(jnp.int32, (1, band_rows), 1)
    sides = []
    for side, targets in ((0, jnp.concatenate([asked, own], axis=0)), (1, own)):
        first = band == side
        across = jnp.where(first, field(2 + width_k, 1 - side), field(3 + width_k, 1 - side))
        takers = [field(2 + k, side) * n_groups + field(0, side) for k in range(width_k)]
        takers.append(across * n_groups + field(0, 1 - side))
        takers = jnp.concatenate(takers, axis=1)
        origins = [field(4 + width_k + k, side) for k in range(width_k)] + [row_ids]
        hits = one_hot(targets, jnp.concatenate(origins, axis=1))
        sides.append((takers, hits, field(0, side)))
    pieces, own_pieces = [], []
    ids = lax.broadcasted_iota(jnp.int32, (n_groups, band_rows), 0)
    for t in range(n_tiles + 1):
        found = []
        for takers, hits, groups in sides:
            if t < n_tiles:
                wide = lax.broadcasted_iota(jnp.int32, (n_groups, takers.shape[1]), 0)
                found.append(dot_nt(one_hot(wide + t * n_groups, takers), hits))
            else:
                found.append(dot_nt(one_hot(ids, groups), hits[:, -band_rows:]))
        pieces += [found[0][:, :slots], found[1]]
        own_pieces.append(found[0][:, slots:])
    count_ref[...] = jnp.concatenate(pieces, axis=1).astype(jnp.bfloat16)
    send(count_ref, count_out)

    own_counts = jnp.concatenate([*own_pieces, own_pieces[-1]], axis=1).astype(jnp.bfloat16)
    finish(loads)
    rights = right_ref[...].reshape(rows * n_rhs, -1)
    kinds = [index_ref[0, 0, rows + row] for row in range(rows)]
    spread_values(n_rhs, n_func, functional_ref, rights, kinds, value_ref, spread_ref, 0)
    values = [spread_ref[pl.ds(t, rows, stride=n_func), :] for t in range(n_tiles + 2)]
    values = jnp.concatenate(halves(jnp.concatenate(values, axis=0)), axis=1)
    partial = jnp.dot(own_counts, values, preferred_element_type=jnp.float32)
    partial_ref[...] = partial[:, :LANES] + partial[:, LANES:]
    send(partial_ref, partial_out)

    per_tile = LANES // n_rhs
    depth = rows // per_tile
    length = n_rows * 2 * depth
    order = lax.broadcasted_iota(jnp.int32, (per_tile * length, 1), 0)
    spot, order = lax.div(order, length), lax.rem(order, length)
    device, order = lax.div(order, 2 * depth), lax.rem(order, 2 * depth)
    side, order = lax.div(order, depth), lax.rem(order, depth)
    order = side * band_rows + device * rows + spot * depth + order
    member = [
        one_hot(ids, jnp.where(band == which, field(0, 0), field(0, 1))) for which in range(2)
    ]
    placing = jnp.zeros(placing_ref.shape, jnp.float32)
    for which in range(2):
        placing = placing + dot_nt(one_hot(order, row_ids + which * band_rows), member[which])
    placing_ref[...] = placing.astype(jnp.bfloat16)
    send(placing_ref, placing_out)
    whole = jnp.zeros((n_groups, 1), jnp.float32)
    for side in range(2):
        sums = jnp.zeros((1, band_rows), jnp.float32)
        for d in range(n_diag):
            sums = jnp.where(field(1, side) == d, totals[d], sums)
        weighted = jnp.where(ids == field(0, side), sums, 0.0)
        whole = whole + jnp.sum(weighted, axis=1, keepdims=True)
    scale = place(placing_ref, jnp.broadcast_to(whole, (n_groups, LANES)), n_rhs, 3)
    mine = jnp.zeros(scale_ref.shape, jnp.float32)
    here = lax.axis_index("rows") * 2 + band
    for n in range(2 * n_rows):
        mine = jnp.where(here == n, scale[n * depth : (n + 1) * depth, :], mine)
    scale_ref[...] = mine
    finish(copies)


def gather_solve(sizes, fetch, diags, later, terms, inverse_ref, sum_ref, product_ref):
    rows, n_rows, cap, n_tiles, n_rhs = sizes
    for row in range(rows):
        sum_ref[pl.ds(row * n_rhs, n_rhs), :] = fetch(row)
    finish(later)
    total = sum_ref[...]
    for term in terms:
        total = total + term[...].reshape(total.shape)
    table_products(total, inverse_ref, product_ref)
    for row in range(rows):
        sum_ref[pl.ds(row * n_rhs, n_rhs), :] = product_ref[diags(row) * rows + row]


def arrived_blocks_of(sizes, width_k, place_ref, field, arrived_ref):
    rows, n_rows, cap, n_tiles, n_rhs = sizes
    per = n_rows * cap // arrived_ref.shape[0]

    def fetch(row):
        total = None
        for k in range(width_k):
            slot = place_ref[0, 0, (field + k) * rows + row]
            start = pl.multiple_of(below(slot, per) * n_rhs, n_rhs)
            block = arrived_ref[over(slot, per), pl.ds(start, n_rhs), :]
            total = block if total is None else total + block
        return total

    return fetch


def solve_kernel(sizes, width_k, n_band, field, *refs):
    metadata_in, arrived_ref, inverse_ref = refs[:2], *refs[2:4]
    terms, refs = refs[4 : 5 + n_band], refs[5 + n_band :]
    out_ref, metadata, sum_ref, product_ref, meta_sems = refs[0], refs[1:3], *refs[3:]
    place_ref, index_ref = metadata
    rows = sizes[0]
    metadata = copies_of(zip(metadata_in, metadata), meta_sems)
    total = terms[0][...].reshape(sum_ref.shape)
    for term in terms[1:]:
        total = total + term[...].reshape(sum_ref.shape)
    sum_ref[...] = total
    finish(metadata)
    arrived = arrived_blocks_of(sizes, width_k, place_ref, field, arrived_ref)
    n_rhs = sizes[4]

    def fetch(row):
        return sum_ref[pl.ds(row * n_rhs, n_rhs), :] + arrived(row)

    def diags(row):
        return index_ref[0, 0, rows + row]

    gather_solve(sizes, fetch, diags, [], [], inverse_ref, sum_ref, product_ref)
    out_ref[...] = sum_ref[...].reshape(out_ref.shape)


def pack_kernel(sizes, width_k, n_band, *refs):
    rows, n_rows, cap, n_tiles, n_rhs = sizes
    list_in, near_in, first_ref, tile_ref, send_out = refs[:5]
    band_out, refs = refs[5 : 5 + n_band], refs[5 + n_band :]
    list_ref, near_ref, product_ref, send_ref = refs[:4]
    band_refs, (meta_sems, send_sems) = refs[4 : 4 + n_band], refs[4 + n_band :]
    list_in = list_in.at[:, :, pl.ds(0, LANES)]
    metadata = copies_of(((list_in, list_ref), (near_in, near_ref)), meta_sems)
    table_products(first_ref[...].reshape(rows * n_rhs, -1), tile_ref, product_ref)
    finish(metadata)
    pack_bands(sizes, width_k, product_ref, near_ref, band_refs)
    for owner in range(n_rows):
        for rank in range(cap):
            block = product_ref[below(list_ref[owner, 0, rank], rows * n_tiles)]
            send_ref[owner, rank * n_rhs : (rank + 1) * n_rhs, :] = block
    finish(copies_of(zip((send_ref, *band_refs), (send_out, *band_out)), send_sems))


def own_kernel(sizes, width_k, *refs):
    rows, n_rows, cap, n_tiles, n_rhs = sizes
    metadata_in, first_ref, tile_ref, extra = list(refs[:2]), *refs[2:4], refs[4:8]
    send_out, band_out, metadata, product_ref, send_ref, band_ref = refs[8], refs[9], refs[10:12], *refs[12:15]
    held, value_ref, spread_ref, result_ref, meta_sems, load_sems, send_sems = refs[15:19], *refs[19:]
    list_ref, near_ref = metadata
    metadata_in[0] = metadata_in[0].at[:, :, pl.ds(0, LANES)]
    metadata = copies_of(zip(metadata_in, metadata), meta_sems)
    fetched = copies_of(zip(extra, held), load_sems)
    table_products(first_ref[...].reshape(rows * n_rhs, -1), tile_ref, product_ref)
    finish(metadata)
    copies = []

    def send(source, target):
        copies.extend(started([pltpu.make_async_copy(source, target, send_sems.at[len(copies)])]))

    pack_bands(sizes, width_k, product_ref, near_ref, (band_ref,))
    send(band_ref, band_out)
    body, half = cap * n_rhs, n_rows // 2
    upper = lax.axis_index("rows") >= half
    mine, others = jnp.where(upper, half, 0), jnp.where(upper, 0, half)
    finish(fetched[:1])
    functional_ref, count_ref, place_ref, partial_ref = held
    n_blocks = n_rows * cap + rows
    n_func = spread_ref.shape[0] // n_blocks
    n_diag = functional_ref.shape[0] // n_func

    def spread(done, blocks, kinds):
        spread_values(n_rhs, n_func, functional_ref, blocks, kinds, value_ref, spread_ref, done)

    kinds = [near_ref[0, 0, rows + row] for row in range(rows)]
    spread(n_rows * cap, band_ref[...].reshape(rows * n_rhs, -1), kinds)
    kinds = []
    for order in range(n_rows):
        owner = order % half + (mine if order < half else others)
        for rank in range(cap):
            code = list_ref[owner, 0, rank]
            kinds.append(below(over(code, rows * n_tiles * rows), n_diag))
            block = product_ref[below(code, rows * n_tiles)]
            send_ref[order, rank * n_rhs : (rank + 1) * n_rhs, :] = block
        if order < half:
            send(send_ref.at[order], send_out.at[order, pl.ds(0, body)])
        if order % 2:
            blocks = jnp.concatenate([send_ref[order - 1], send_ref[order]], axis=0)
            spread((order - 1) * cap, blocks, kinds)
            kinds = []
    finish(fetched[1:])
    result = coarse_parts(n_rhs, n_blocks, count_ref, place_ref, partial_ref, spread_ref)
    result_ref[...] = result.reshape(result_ref.shape)
    depth = result_ref.shape[1]
    for n, first in enumerate((mine, others)):
        target = send_out.at[:, pl.ds(body + n * depth, depth)]
        send(result_ref.at[pl.ds(first, half)], target)
    finish(copies)


def mirror_kernel(
    sizes, list_in, mirror_ref, tile_ref, inverse_ref, send_out, list_ref, product_ref, block_ref, solved_ref, send_ref, sems
):
    rows, n_rows, cap, n_tiles, n_rhs = sizes
    half, n_diag = n_rows // 2, inverse_ref.shape[0]
    base = jnp.where(lax.axis_index("rows") >= half, half, 0)
    list_in = list_in.at[pl.ds(base, half), :, pl.ds(0, LANES)]
    metadata = started([pltpu.make_async_copy(list_in, list_ref, sems.at[half])])
    table_products(mirror_ref[...].reshape(rows * n_rhs, -1), tile_ref, product_ref)
    finish(metadata)
    codes = [list_ref[n // cap, 0, LANES // 2 + n % cap] for n in range(half * cap)]
    for n, code in enumerate(codes):
        block_ref[n] = product_ref[below(code, rows * n_tiles)]
    values = block_ref[...].reshape(half * cap * n_rhs, -1)
    table_products(values, inverse_ref, solved_ref)
    copies = []
    for n, code in enumerate(codes):
        device, rank = n // cap, n % cap
        kind = below(over(code, rows * n_tiles * rows), n_diag)
        send_ref[device, rank * n_rhs : (rank + 1) * n_rhs, :] = solved_ref[kind * len(codes) + n]
        if rank == cap - 1:
            copy = pltpu.make_async_copy(send_ref.at[device], send_out.at[device], sems.at[device])
            copies += started([copy])
    finish(copies)


def coarse_parts(n_rhs, n_blocks, count_ref, place_ref, partial_ref, spread_ref):
    n_func = spread_ref.shape[0] // n_blocks
    values = [
        spread_ref[pl.ds(t, n_blocks, stride=n_func), :] for t in range(count_ref.shape[1] // n_blocks)
    ]
    values = jnp.concatenate(values, axis=0)
    partial = jnp.dot(
        count_ref[...], jnp.concatenate(halves(values), axis=1), preferred_element_type=jnp.float32
    )
    partial = partial[:, :LANES] + partial[:, LANES:] + partial_ref[...]
    shift = LANES // 2
    while shift >= n_rhs:
        partial = partial + pltpu.roll(partial, shift, axis=1)
        shift //= 2
    return place(place_ref, partial, n_rhs, 2)


def part_kernel(arrived_ref, keep_ref, give_ref):
    depth = keep_ref.shape[0] // 2
    body = arrived_ref.shape[1] - 4 * depth
    total = arrived_ref[0, body:, :]
    for source in range(1, arrived_ref.shape[0]):
        total = total + arrived_ref[source, body:, :]
    lower = lax.axis_index("band") == 0
    for n in range(2):
        zero, one = (total[(2 * n + m) * depth : (2 * n + m + 1) * depth] for m in range(2))
        keep_ref[n * depth : (n + 1) * depth] = jnp.where(lower, zero, one)
        give_ref[n * depth : (n + 1) * depth] = jnp.where(lower, one, zero)


def half_blocks_of(sizes, width_k, place_ref, arrived_ref, far):
    rows, n_rows, cap, n_tiles, n_rhs = sizes

    def fetch(row):
        total = None
        for k in range(width_k):
            slot = place_ref[0, 0, k * rows + row]
            holder, slot = over(slot, 2 * cap), below(slot, 2 * cap)
            start = pl.ds(pl.multiple_of(below(slot, cap) * n_rhs, n_rhs), n_rhs)
            mine = slot >= cap if far else slot < cap
            block = jnp.where(mine, arrived_ref[holder, start, :], 0.0)
            total = block if total is None else total + block
        return total

    return fetch


def base_kernel(sizes, width_k, *refs):
    metadata_in, own_ref, inverse_ref, terms_in, out_ref = refs[:2], *refs[2:4], refs[4:6], refs[6]
    metadata, sum_ref, product_ref, terms, term_sems, meta_sems = refs[7:9], *refs[9:11], refs[11:13], *refs[13:]
    place_ref, index_ref = metadata
    rows = sizes[0]
    metadata = copies_of(zip(metadata_in, metadata), meta_sems)
    later = copies_of(zip(terms_in, terms), term_sems)
    finish(metadata)
    fetch = half_blocks_of(sizes, width_k, place_ref, own_ref, False)

    def diags(row):
        return index_ref[0, 0, rows + row]

    gather_solve(sizes, fetch, diags, later, terms, inverse_ref, sum_ref, product_ref)
    out_ref[...] = sum_ref[...].reshape(out_ref.shape)


def final_kernel(sizes, width_k, *refs):
    place_in, mirror_ref, base_ref, near_ref, far_ref, scale_ref, out, place_ref, out_ref, sem, out_sems = refs
    rows, n_rows, cap, n_tiles, n_rhs = sizes
    metadata = pltpu.make_async_copy(place_in, place_ref, sem)
    metadata.start()
    depth = scale_ref.shape[0]
    correction = (near_ref[...] + far_ref[...]) / scale_ref[...]
    padded = jnp.concatenate([correction, jnp.zeros((8 - depth, LANES), jnp.float32)], axis=0)
    turned = padded.T
    for row in range(rows):
        spot, place = row // depth, row % depth
        column = turned[spot * n_rhs : (spot + 1) * n_rhs, place : place + 1]
        out_ref[row] = base_ref[row] + column
    metadata.wait()
    fetch = half_blocks_of(sizes, width_k, place_ref, mirror_ref, True)
    step = -(-rows // out_sems.shape[0])
    copies = []
    for first in range(0, rows, step):
        count = min(step, rows - first)
        for row in range(first, first + count):
            out_ref[row] = out_ref[row] + fetch(row)
        place = pl.ds(first, count)
        copy = pltpu.make_async_copy(out_ref.at[place], out.at[place], out_sems.at[len(copies)])
        copies += started([copy])
    finish(copies)


def shifted(value, axis, steps):
    count = lax.axis_size(axis)
    initial, last = (max(0, -steps), min(count, count - steps))
    return lax.ppermute(value, axis, [(source, source + steps) for source in range(initial, last)])


def to_bands(sends):
    if len(sends) == 1:
        return (lax.ppermute(sends[0], "band", [(0, 1), (1, 0)]),)
    return shifted(sends[0], "band", 1), shifted(sends[1], "band", -1)


def on_device(
    start_iterate,
    right_side,
    diag_table,
    inverse_table,
    coupling_tiles,
    diag_index,
    tile_index,
    source_owner,
    source_local,
    aggregate_map,
):
    rows, n_rhs, states = start_iterate.shape
    width_k = source_owner.shape[1]
    n_tiles, n_diag = coupling_tiles.shape[0], inverse_table.shape[0]
    n_rows, n_bands = lax.axis_size("rows"), lax.axis_size("band")
    n_dev = n_rows * n_bands
    cap = max(2, 2 * width_k * rows // n_rows)
    slots = n_rows * cap
    total_groups = AGG_DEV * n_dev
    per_tile = LANES // n_rhs
    depth = rows // per_tile
    n_func = 16
    dense = (
        n_bands == 2
        and n_dev * rows * total_groups <= DENSE_LIMIT
        and depth == 4
        and n_diag * n_func == LANES
        and n_tiles + 2 <= n_func
    )
    sizes = (rows, n_rows, cap, n_tiles, n_rhs)
    f32, i32 = jnp.float32, jnp.int32
    my_band = lax.axis_index("band")
    my_row = lax.axis_index("rows")

    half = n_rows // 2
    wide = -(-(4 + 2 * width_k) * rows // LANES) * LANES
    place_wide = -(-2 * width_k * rows // LANES) * LANES
    index_shapes = [(width_k, rows), (width_k, rows), (width_k + 2, rows), (1, rows), (1, rows)]
    halves_of_rows = [list(range(half)), list(range(half, n_rows))]
    to_mirror = [(i, (i + half) % n_rows) for i in range(n_rows)]
    mirror = lax.ppermute(start_iterate, "rows", to_mirror)
    lists, index, places = call(
        functools.partial(request_kernel, (rows, n_rows, cap, n_tiles, n_diag)),
        (
            jax.ShapeDtypeStruct((n_rows, 1, LANES + wide), i32),
            jax.ShapeDtypeStruct((1, 1, wide), i32),
            jax.ShapeDtypeStruct((1, 1, place_wide), i32),
        ),
        [HBM] * 5,
        [VMEM] * 3,
        [*[pltpu.VMEM(shape, i32) for shape in index_shapes], pltpu.SemaphoreType.DMA((5,))],
    )(source_owner.T, source_local.T, tile_index.T, diag_index[None], aggregate_map.T)
    lists = lax.all_to_all(lists, "rows", split_axis=0, concat_axis=0, tiled=True)
    if n_bands == 2:
        near = lax.ppermute(index, "band", [(0, 1), (1, 0)])
    else:
        ways = [[(b, (b + step) % n_bands) for b in range(n_bands)] for step in (-1, 1)]
        near = jnp.concatenate([lax.ppermute(index, "band", way) for way in ways], axis=0)

    n_ways = 1 if n_bands == 2 else 2
    block = (rows, n_rhs, states)
    band_shapes = [jax.ShapeDtypeStruct(block, f32)] * n_ways
    band_scratch = [pltpu.VMEM(block, f32)] * n_ways
    term_scratch = [pltpu.VMEM(block, f32)] * (1 + n_ways)
    term_sems = pltpu.SemaphoreType.DMA((1 + n_ways,))
    list_scratch = pltpu.SMEM((half, 1, LANES), i32)
    near_scratch = pltpu.SMEM((n_ways, 1, wide), i32)
    row_scratch = [pltpu.SMEM((1, 1, place_wide), i32), pltpu.SMEM((1, 1, wide), i32)]
    flat = rows * n_rhs
    sums = pltpu.VMEM((flat, states), f32)
    products = pltpu.VMEM((max(n_tiles, n_diag) * rows, n_rhs, states), f32)
    work = 6 * flat * states * states
    made_shape = (n_tiles * rows, n_rhs, states)
    table_scratch = [pltpu.VMEM(coupling_tiles.shape, f32)]
    table_sems = pltpu.SemaphoreType.DMA((-(-n_tiles // 2),))
    made = call(
        product_kernel,
        jax.ShapeDtypeStruct(made_shape, f32),
        [HBM, HBM],
        VMEM,
        [
            pltpu.VMEM(block, f32),
            *table_scratch,
            pltpu.SemaphoreType.DMA,
            table_sems,
        ],
        work * n_tiles,
        4 << 20,
    )(start_iterate, coupling_tiles)
    packed, *bands = call(
        functools.partial(first_kernel, sizes, width_k, n_ways),
        (jax.ShapeDtypeStruct((half, 2 * cap, n_rhs, states), f32), *band_shapes),
        [VMEM, VMEM, VMEM, ANY, ANY],
        [HBM] * (1 + n_ways),
        [
            pltpu.VMEM(made_shape, f32),
            list_scratch,
            near_scratch,
            pltpu.VMEM((half, 2 * cap, n_rhs, states), f32),
            *band_scratch,
            pltpu.SemaphoreType.DMA((2,)),
            pltpu.SemaphoreType.DMA((2 * half + n_ways,)),
        ],
        work * n_tiles,
        4 << 20,
    )(made, mirror, coupling_tiles, lists, near)
    packed, late = lax.optimization_barrier((packed, lists))
    if dense:
        across = lax.ppermute(late, "band", [(0, 1), (1, 0)])
        across, *bands = lax.optimization_barrier((across, *bands))
    sends = (packed.reshape(half, 2 * cap * n_rhs, states), *bands)
    halves_of_rows = [list(range(half)), list(range(half, n_rows))]
    def exchange(sends, groups=None):
        arrived = lax.all_to_all(
            sends[0], "rows", split_axis=0, concat_axis=0, tiled=True, axis_index_groups=groups
        )
        return arrived, to_bands(sends[1:])

    arrived_blocks, arrived_bands = exchange(sends, halves_of_rows)

    if dense:
        fields = jnp.stack([late, across])[:, :, 0, LANES:]
        fields = fields.reshape(2, n_rows, -1, rows).transpose(2, 0, 1, 3)
        fields = fields.reshape(-1, 2, n_rows * rows)
        n_blocks = slots + rows
        length = n_dev * depth
        extra_shapes = [
            ((n_diag * n_func, 3 * states), jnp.bfloat16),
            ((total_groups, (n_tiles + 1) * n_blocks), jnp.bfloat16),
            ((per_tile * length, total_groups), jnp.bfloat16),
            ((total_groups, LANES), f32),
        ]
        functional_shape, count_shape, placing_shape, partial_shape = extra_shapes
        counts, functionals, placing, partial, scale = call(
            functools.partial(count_kernel, sizes, width_k, n_func),
            (
                jax.ShapeDtypeStruct(*count_shape),
                jax.ShapeDtypeStruct(*functional_shape),
                jax.ShapeDtypeStruct(*placing_shape),
                jax.ShapeDtypeStruct(*partial_shape),
                jax.ShapeDtypeStruct((depth, LANES), f32),
            ),
            [ANY, HBM] + [VMEM] * 5,
            [HBM] * 4 + [VMEM],
            [
                pltpu.VMEM(*count_shape),
                pltpu.VMEM(*functional_shape),
                pltpu.VMEM(*placing_shape),
                pltpu.VMEM(*partial_shape),
                row_scratch[1],
                pltpu.VMEM(block, f32),
                pltpu.VMEM((n_diag * n_func, flat), f32),
                pltpu.VMEM((rows * n_func, LANES), f32),
                pltpu.SemaphoreType.DMA((2,)),
                pltpu.SemaphoreType.DMA((4,)),
            ],
            4 * total_groups * n_tiles * n_dev * rows * n_blocks,
            4 << 20,
        )(
            index, right_side, fields, late[:, 0, :LANES], coupling_tiles, diag_table, inverse_table
        )
        extra_scratch = [
            *[pltpu.VMEM(*shape) for shape in extra_shapes],
            pltpu.VMEM((n_diag * n_func, n_blocks * n_rhs), f32),
            pltpu.VMEM((n_blocks * n_func, LANES), f32),
            pltpu.VMEM((n_rows, n_bands * depth, LANES), f32),
        ]

        made = (arrived_blocks, functionals, counts, placing, partial, scale)
        made = lax.optimization_barrier(made)
        arrived_blocks, functionals, counts, placing, partial, scale = made

    def solve(field, arrived, bands):
        return call(
            functools.partial(solve_kernel, sizes, width_k, n_ways, field),
            jax.ShapeDtypeStruct(block, f32),
            [ANY] * 2 + [VMEM] * (3 + n_ways),
            VMEM,
            [*row_scratch, sums, products, pltpu.SemaphoreType.DMA((2,))],
            work * n_diag,
            4 << 20,
        )(places, index, arrived, inverse_table, right_side, *bands)

    first = solve(0, arrived_blocks, arrived_bands)
    body = cap * n_rhs
    full_list = pltpu.SMEM((n_rows, 1, LANES), i32)
    if dense:
        mirror = lax.ppermute(first, "rows", to_mirror)
        own, band = call(
            functools.partial(own_kernel, sizes, width_k),
            (
                jax.ShapeDtypeStruct((half, body + 2 * n_bands * depth, states), f32),
                jax.ShapeDtypeStruct(block, f32),
            ),
            [ANY] * 2 + [VMEM] * 2 + [HBM] * 4,
            [HBM] * 2,
            [
                full_list,
                near_scratch,
                products,
                pltpu.VMEM((n_rows, body, states), f32),
                pltpu.VMEM(block, f32),
                *extra_scratch,
                pltpu.SemaphoreType.DMA((2,)),
                pltpu.SemaphoreType.DMA((4,)),
                pltpu.SemaphoreType.DMA((half + 3,)),
            ],
            2 * work * n_tiles,
            4 << 20,
        )(lists, near, first, coupling_tiles, functionals, counts, placing, partial)
        own, (band,) = exchange((own, band), halves_of_rows)
        packed = call(
            functools.partial(mirror_kernel, sizes),
            jax.ShapeDtypeStruct((half, body, states), f32),
            [ANY] + [VMEM] * 3,
            HBM,
            [
                list_scratch,
                products,
                pltpu.VMEM((half * cap, n_rhs, states), f32),
                pltpu.VMEM((n_diag * half * cap, n_rhs, states), f32),
                pltpu.VMEM((half, body, states), f32),
                pltpu.SemaphoreType.DMA((half + 1,)),
            ],
            BEHIND_SWAP * work * n_tiles,
            4 << 20,
        )(lists, mirror, coupling_tiles, inverse_table)
        packed, band = lax.optimization_barrier((packed, band))
        swapped = lax.all_to_all(
            packed, "rows", split_axis=0, concat_axis=0, tiled=True, axis_index_groups=halves_of_rows
        )
        part = jax.ShapeDtypeStruct((2 * depth, LANES), f32)
        keep, give = call(part_kernel, (part, part), [VMEM], [VMEM] * 2)(own)
        keep = keep + lax.ppermute(give, "band", [(0, 1), (1, 0)])
        far = lax.ppermute(keep[depth:], "rows", to_mirror)
        base = call(
            functools.partial(base_kernel, sizes, width_k),
            jax.ShapeDtypeStruct(block, f32),
            [ANY] * 2 + [VMEM] * 2 + [HBM, ANY],
            VMEM,
            [
                *row_scratch,
                sums,
                products,
                *term_scratch,
                term_sems,
                pltpu.SemaphoreType.DMA((2,)),
            ],
            work * n_diag,
            4 << 20,
        )(places, index, own, inverse_table, right_side, band)
        return call(
            functools.partial(final_kernel, sizes, width_k),
            jax.ShapeDtypeStruct(block, f32),
            [ANY] + [VMEM] * 5,
            HBM,
            [
                row_scratch[0],
                pltpu.VMEM(block, f32),
                pltpu.SemaphoreType.DMA,
                pltpu.SemaphoreType.DMA((4,)),
            ],
            0,
            4 << 20,
        )(places, swapped, base, keep[:depth], far, scale)

    sends = call(
        functools.partial(pack_kernel, sizes, width_k, n_ways),
        (jax.ShapeDtypeStruct((n_rows, body, states), f32), *band_shapes),
        [ANY] * 2 + [VMEM] * 2,
        [HBM] * (1 + n_ways),
        [
            full_list,
            near_scratch,
            products,
            pltpu.VMEM((n_rows, body, states), f32),
            *band_scratch,
            pltpu.SemaphoreType.DMA((2,)),
            pltpu.SemaphoreType.DMA((1 + n_ways,)),
        ],
        work * n_tiles,
        4 << 20,
    )(lists, near, first, coupling_tiles)
    arrived_blocks, arrived_bands = exchange(sends)
    second = solve(width_k, arrived_blocks, arrived_bands)

    groups = aggregate_map[:, 0]
    own = jnp.arange(rows, dtype=i32)
    index_all = lax.all_gather(index, ("band", "rows"), axis=0, tiled=True)
    index_all = index_all.reshape(n_bands, n_rows, wide)
    groups_all, diags_all = index_all[:, :, :rows], index_all[:, :, rows : 2 * rows]
    codes = lists[:, 0, :cap]
    asked = jnp.arange(n_rows, dtype=i32)[:, None] * rows + codes // (rows * n_tiles) % rows
    asked = jnp.where(codes > 0, asked, -1).reshape(-1)
    table_sums = jnp.sum(diag_table, axis=(1, 2))
    diag_onehot = diags_all.reshape(-1, 1) == jnp.arange(n_diag, dtype=i32)[None]
    block_sums = jnp.sum(jnp.where(diag_onehot, table_sums[None], 0.0), axis=1)
    whole_diag = jnp.sum(
        jnp.where(groups[:, None] == groups_all.reshape(-1)[None], block_sums[None], 0.0), axis=1
    )
    above, below = near[0, 0], near[-1, 0]
    place_of = (2 + width_k) * rows
    band_tiles = jnp.stack([above[place_of : place_of + rows], below[place_of + rows : place_of + 2 * rows]])
    band_groups = jnp.stack([above[:rows], below[:rows]])
    band_valid = jnp.stack([my_band + 1 < n_bands, my_band > 0])
    band_valid = jnp.broadcast_to(band_valid[:, None], (2, rows))
    n_all = n_tiles + n_diag + 1
    code = codes.reshape(-1)
    band_of_mine = lax.dynamic_index_in_dim(groups_all, my_band, 0, keepdims=False).reshape(-1)
    entry_group = jnp.concatenate(
        [jnp.take(band_of_mine, jnp.maximum(asked, 0)), band_groups.reshape(-1), groups, groups]
    )
    entry_func = jnp.concatenate(
        [
            (code % rows) * n_all + (code // rows) % n_tiles,
            (own[None] * n_all + band_tiles).reshape(-1),
            own * n_all + n_tiles + diag_index,
            own * n_all + n_tiles + n_diag,
        ]
    )
    entry_valid = jnp.concatenate([asked >= 0, band_valid.reshape(-1), jnp.ones((2 * rows,), bool)])
    functionals = jnp.concatenate(
        [jnp.sum(coupling_tiles, axis=1), -jnp.sum(diag_table, axis=1)], axis=0
    )
    weights = jnp.einsum("fp,rcp->rfc", functionals, second, precision=HIGH)
    weights = jnp.concatenate([weights, jnp.sum(right_side, axis=2)[:, None]], axis=1)
    chosen = jnp.take(weights.reshape(rows * n_all, n_rhs), entry_func, axis=0)
    chosen = jnp.where(entry_valid[:, None], chosen, 0.0)
    partial = jax.ops.segment_sum(chosen, entry_group, num_segments=total_groups)
    whole = lax.psum(partial, ("band", "rows"))
    correction = jnp.take(whole, groups, axis=0) / whole_diag[:, None]
    return second + correction[:, :, None]


def solution(mesh):
    in_specs = (
        P(("band", "rows"), None, None),
        P(("band", "rows"), None, None),
        P(),
        P(),
        P(),
        P(("band", "rows")),
        P(("band", "rows"), None),
        P(("band", "rows"), None),
        P(("band", "rows"), None),
        P(("band", "rows"), None),
    )
    out_specs = P(("band", "rows"), None, None)
    return jax.shard_map(
        on_device, mesh=mesh, in_specs=in_specs, out_specs=out_specs, check_vma=False
    )
```
